32 devices in a mesh: dp: 8 (over z, core), fsdp: 4 (over y, x).
Axes of the slice: x: 2, y: 2, z: 4, core: 2. Of those that a mesh axis runs over, the one named last changes fastest.
Arguments:
- patches: bfloat16 [6400, 1024], P(('dp', 'fsdp')), may hold values from -6 to 6
- out_grad: bfloat16 [6400, 1024], P(('dp', 'fsdp')), may hold values from -6 to 6
- norm_gain: bfloat16 [2, 2, 1024], P(None, None, ('dp', 'fsdp')), may hold values from 0.099609375 to 1.8984375
- norm_shift: bfloat16 [2, 2, 1024], P(None, None, ('dp', 'fsdp')), may hold values from -4 to 4
- qkv_weight: bfloat16 [2, 1024, 3072], P(None, ('dp', 'fsdp')), may hold values from -0.1875 to 0.1875
- qv_bias: bfloat16 [2, 2048], P(None, ('dp', 'fsdp')), may hold values from -6 to 6
- rel_table: bfloat16 [2, 361, 32], replicated, may hold values from -6 to 6
- proj_weight: bfloat16 [2, 1024, 1024], P(None, ('dp', 'fsdp')), may hold values from -0.75 to 0.75
- proj_bias: bfloat16 [2, 1024], P(None, ('dp', 'fsdp')), may hold values from -4 to 4
- up_weight: bfloat16 [2, 1024, 4096], P(None, ('dp', 'fsdp')), may hold values from -0.1875 to 0.1875
- up_bias: bfloat16 [2, 4096], P(None, ('dp', 'fsdp')), may hold values from -6 to 6
- down_weight: bfloat16 [2, 4096, 1024], P(None, ('dp', 'fsdp')), may hold values from -0.09375 to 0.09375
- down_bias: bfloat16 [2, 1024], P(None, ('dp', 'fsdp')), may hold values from -4 to 4
- tile_perm: int32 [64], replicated, may hold values from 0 to 63, as said below
- window_slot: int32 [64], replicated, may hold values from 0 to 63, as said below
- mask_ids: int32 [64], replicated, may hold values from 0 to 3
- bias_index: int32 [100, 100], replicated, may hold values from 0 to 360, as said below
Outputs:
- block_out: bfloat16 [6400, 1024], P(('dp', 'fsdp'))
- patches_grad: float32 [6400, 1024], P(('dp', 'fsdp'))
- norm_gain_grad: float32 [2, 2, 1024], P(None, None, ('dp', 'fsdp'))
- norm_shift_grad: float32 [2, 2, 1024], P(None, None, ('dp', 'fsdp'))
- qkv_weight_grad: float32 [2, 1024, 3072], P(None, ('dp', 'fsdp'))
- qv_bias_grad: float32 [2, 2048], P(None, ('dp', 'fsdp'))
- rel_table_grad: float32 [2, 361, 32], replicated
- proj_weight_grad: float32 [2, 1024, 1024], P(None, ('dp', 'fsdp'))
- proj_bias_grad: float32 [2, 1024], P(None, ('dp', 'fsdp'))
- up_weight_grad: float32 [2, 1024, 4096], P(None, ('dp', 'fsdp'))
- up_bias_grad: float32 [2, 4096], P(None, ('dp', 'fsdp'))
- down_weight_grad: float32 [2, 4096, 1024], P(None, ('dp', 'fsdp'))
- down_bias_grad: float32 [2, 1024], P(None, ('dp', 'fsdp'))
The draws below stay inside these ranges and needn't reach their ends.
Inputs may be any that keep to these rules, and one draw needn't show every extreme that they name: A permutation of the 64 windows; slots window_slot[w] and window_slot[tile_perm[w]] lie on devices of the same index along dp; for any two devices, at most 1 windows w held on the second have window tile_perm[w] held on the first, and some pair of devices has exactly 1. `window_slot`: a permutation of the 64 slots. `bias_index`: entry (i, j) depends only on the offset between positions i and j of the window, and different offsets have different entries.
All inputs are finite; a program needn't handle non-finite values.
Results may differ from the reference program's by a relative error of at most 0.015.
Values may be sent and summed in bfloat16 or wider, within the bound.
A program may use at most 320 MiB of HBM per device.

```python
import jax
import jax.numpy as jnp
from jax import lax

D = 1024
FF = 4096
HEADS = 32
SIDE = 10
WIN_DEV = 2
WIN = 100
BUCKETS = 361
PEERS = 4
TOTAL = 64
TOKENS = 6400


def tile_layout(key):
    group_count = TOTAL // (PEERS * WIN_DEV)
    keys = jax.random.split(key, 3)

    def offset_row(subkey):
        moved = 1 + jax.random.permutation(subkey, PEERS - 1).astype(jnp.int32)
        return jnp.concatenate([moved, jnp.zeros((1,), jnp.int32)])
    offsets = jax.vmap(offset_row)(jax.random.split(keys[0], group_count))
    slot_peer = jnp.arange(WIN_DEV, dtype=jnp.int32) % PEERS
    source_peer = jnp.arange(PEERS, dtype=jnp.int32)
    target_peer = (source_peer[None, :, None] + offsets[:, slot_peer][:, None, :]) % PEERS

    def order_row(subkey):
        return jax.random.permutation(subkey, WIN_DEV).astype(jnp.int32)
    orders = jax.vmap(order_row)(jax.random.split(keys[1], group_count * PEERS)).reshape(group_count, PEERS, WIN_DEV)
    target_place = jnp.take_along_axis(orders, target_peer, axis=1)
    group_base = jnp.arange(group_count, dtype=jnp.int32)[:, None, None] * (PEERS * WIN_DEV)
    target_slot = (group_base + target_peer * WIN_DEV + target_place).reshape(-1)
    source_of = jnp.zeros((TOTAL,), jnp.int32).at[target_slot].set(jnp.arange(TOTAL, dtype=jnp.int32))
    window_slot = jax.random.permutation(keys[2], TOTAL).astype(jnp.int32)
    return (source_of, window_slot)


def draw_tile_perm(key, part):
    source_of, window_slot = tile_layout(key)
    window_of = jnp.zeros((TOTAL,), jnp.int32).at[window_slot].set(jnp.arange(TOTAL, dtype=jnp.int32))
    return window_of[source_of[window_slot]]


def draw_window_slot(key, part):
    source_of, window_slot = tile_layout(key)
    return window_slot


def draw_bias_index(key, part):
    key = jax.random.fold_in(key, 7)
    bucket_order = jax.random.permutation(key, BUCKETS).astype(jnp.int32)
    position = jnp.arange(WIN, dtype=jnp.int32)
    row_of = position // SIDE
    column_of = position % SIDE
    offset = (row_of[:, None] - row_of[None, :] + SIDE - 1) * (2 * SIDE - 1) + (column_of[:, None] - column_of[None, :] + SIDE - 1)
    return bucket_order[offset]


def place_ends(drawn, stream_key, smallest, high):
    shape = drawn.shape
    place = [jax.random.randint(jax.random.fold_in(stream_key, axis), (), 0, shape[axis]) for axis in range(len(shape))]
    drawn = drawn.at[tuple(place)].set(smallest)
    longest = shape.index(max(shape))
    place[longest] = (place[longest] + 1) % shape[longest]
    return drawn.at[tuple(place)].set(high)


def levels(stream_key, shape, cuts, smallest, top_value):
    level, own = 1.0, jax.random.fold_in(stream_key, 6)
    for dim, shards_of in cuts:
        heights = jnp.exp(jax.random.uniform(jax.random.fold_in(own, dim), (shards_of,), jnp.float32, smallest / len(cuts), top_value / len(cuts)))
        level = level * jnp.repeat(heights, shape[dim] // shards_of).reshape([-1 if axis == dim else 1 for axis in range(len(shape))])
    return level


def gaussian(own_key, shape, width, reach, cuts=(), kind=jnp.bfloat16):
    array = width * jax.random.normal(own_key, shape, jnp.float32)
    if cuts:
        array = array * levels(own_key, shape, cuts, -0.22, 0.18)
    return jnp.clip(array, -reach, reach).astype(kind)


def setup_inputs(seed: int = 0) -> dict:
    splits = jax.random.split(jax.random.key(seed), 18)
    return {
        "patches": gaussian(splits[0], (TOKENS, D), 1.0, 6.0, ((0, 32),)),
        "out_grad": gaussian(splits[1], (TOKENS, D), 1.0, 6.0, ((0, 32),)),
        "norm_gain": jnp.clip(1.0 + 0.18 * jax.random.normal(splits[2], (2, 2, D), jnp.float32), 0.099609375, 1.8984375).astype(jnp.bfloat16),
        "norm_shift": gaussian(splits[3], (2, 2, D), 0.3, 4.0, ((2, 32),)),
        "qkv_weight": gaussian(splits[4], (2, D, 3 * D), D ** -0.5, 0.1875, ((1, 32),)),
        "qv_bias": gaussian(splits[5], (2, 2 * D), 0.5, 6.0, ((1, 32),)),
        "rel_table": gaussian(splits[6], (2, BUCKETS, HEADS), 1.0, 6.0),
        "proj_weight": gaussian(splits[7], (2, D, D), (D // 16) ** -0.5, 0.75, ((1, 32),)),
        "proj_bias": gaussian(splits[8], (2, D), 0.3, 4.0, ((1, 32),)),
        "up_weight": gaussian(splits[9], (2, D, FF), D ** -0.5, 0.1875, ((1, 32),)),
        "up_bias": gaussian(splits[10], (2, FF), 0.5, 6.0, ((1, 32),)),
        "down_weight": gaussian(splits[11], (2, FF, D), FF ** -0.5, 0.09375, ((1, 32),)),
        "down_bias": gaussian(splits[12], (2, D), 0.3, 4.0, ((1, 32),)),
        "tile_perm": draw_tile_perm(jax.random.fold_in(splits[17], 71), 0),
        "window_slot": draw_window_slot(jax.random.fold_in(splits[17], 71), 0),
        "mask_ids": place_ends(jax.random.randint(splits[15], (TOTAL,), 0, 4), jax.random.fold_in(splits[15], 1), 0, 3).astype(jnp.int32),
        "bias_index": draw_bias_index(jax.random.fold_in(splits[17], 71), 0),
    }


epsilon = 1e-05
masked_score = -1000000000.0
highest = lax.Precision.HIGHEST

@jax.custom_vjp
def low(v):
    return lax.optimization_barrier(v.astype(jnp.bfloat16)).astype(jnp.float32)

@jax.custom_vjp
def low_back(v):
    return v

def low_keep(v):
    return (low(v), None)

def low_pass(kept, grad):
    return (grad,)

def back_keep(v):
    return (v, None)

def back_low(kept, grad):
    return (low(grad),)
low.defvjp(low_keep, low_pass)
low_back.defvjp(back_keep, back_low)

def both_ways(values):
    return low_back(low(values))

def layer_norm(inputs, gain, shift):
    mean_value = lax.optimization_barrier(jnp.mean(inputs, axis=-1, keepdims=True))
    centered = inputs - mean_value
    variance = lax.optimization_barrier(jnp.mean(centered * centered, axis=-1, keepdims=True))
    return centered * lax.rsqrt(variance + epsilon) * gain + shift

def region_mask(region_ids):
    position = jnp.arange(WIN, dtype=jnp.int32)
    cut_point = SIDE - SIDE // 2
    right_half = (position % SIDE >= cut_point).astype(jnp.int32)
    lower_half = (position // SIDE >= cut_point).astype(jnp.int32)
    labels = region_ids[:, None] % 2 * right_half[None] + 2 * (region_ids[:, None] // 2) * lower_half[None]
    same_label = labels[:, :, None] == labels[:, None, :]
    return jnp.where(same_label, 0.0, masked_score).astype(jnp.float32)[:, None]

def position_table(table, bias_index):
    return jnp.transpose(table[bias_index], (2, 0, 1))

def block_apply(tiles, params, position_bias, regions):
    norm_gains, norm_shifts, w_qkv, qv_bias, w_proj, b_proj, w_up, b_up, w_down, b_down = params
    group_size = tiles.shape[0]
    model_width = tiles.shape[-1]
    head_size = model_width // HEADS
    normed = low(layer_norm(tiles, norm_gains[0], norm_shifts[0]))
    bias_full = jnp.concatenate([qv_bias[:model_width], jnp.zeros((model_width,), jnp.float32), qv_bias[model_width:]])
    qkv = both_ways(jnp.einsum('wpd,de->wpe', normed, w_qkv, precision=highest) + bias_full)
    qkv_parts = qkv.reshape(group_size, WIN, 3, HEADS, head_size)
    scores = jnp.einsum('wqhd,wkhd->whqk', qkv_parts[:, :, 0], qkv_parts[:, :, 1], precision=highest) * head_size ** (-0.5) + position_bias[None] + regions
    scores = low_back(scores)
    row_max = lax.optimization_barrier(jnp.max(scores, axis=-1, keepdims=True))
    shifted_exp = jnp.exp(scores - row_max)
    soft = low(shifted_exp / lax.optimization_barrier(jnp.sum(shifted_exp, axis=-1, keepdims=True)))
    attended = jnp.einsum('whqk,wkhd->wqhd', soft, qkv_parts[:, :, 2], precision=highest).reshape(tiles.shape)
    attended = both_ways(attended)
    branch = low_back(jnp.einsum('wpc,cd->wpd', attended, w_proj, precision=highest) + b_proj)
    middle = tiles + branch
    normed_two = low(layer_norm(middle, norm_gains[1], norm_shifts[1]))
    hidden = low_back(jnp.einsum('wpd,df->wpf', normed_two, w_up, precision=highest) + b_up)
    activated = low(jax.nn.gelu(hidden, approximate=False))
    return middle + low_back(jnp.einsum('wpf,fd->wpd', activated, w_down, precision=highest) + b_down)

def run_block(tiles, params, position_bias, regions):
    count = tiles.shape[0]
    grouped = (tiles.reshape(count // 32, 32, WIN, tiles.shape[-1]), regions.reshape(count // 32, 32, 1, WIN, WIN))

    def one_group(members):
        return block_apply(members[0], params, position_bias, members[1])
    return lax.map(jax.checkpoint(one_group), grouped).reshape(tiles.shape)

def reference(patches, out_grad, norm_gain, norm_shift, qkv_weight, qv_bias, rel_table, proj_weight, proj_bias, up_weight, up_bias, down_weight, down_bias, tile_perm, window_slot, mask_ids, bias_index):
    slot_ids = jnp.arange(TOTAL, dtype=jnp.int32)
    source_of = jnp.zeros((TOTAL,), jnp.int32).at[window_slot].set(window_slot[tile_perm].astype(jnp.int32))
    target_of = jnp.zeros((TOTAL,), jnp.int32).at[source_of].set(slot_ids)
    region_slot = jnp.zeros((TOTAL,), jnp.int32).at[window_slot].set(mask_ids.astype(jnp.int32))
    regions = region_mask(region_slot)
    no_mask = jnp.zeros_like(regions)
    weights = tuple((argument.astype(jnp.float32) for argument in (norm_gain, norm_shift, qkv_weight, qv_bias, rel_table, proj_weight, proj_bias, up_weight, up_bias, down_weight, down_bias)))

    def forward(inputs, params):
        gains_all, shifts_all, qkv_all, qv_all, table_all, proj_all, proj_bias_all, up_all, up_bias_all, down_all, down_bias_all = params

        def layer_params(layer_index):
            return (gains_all[layer_index], shifts_all[layer_index], qkv_all[layer_index], qv_all[layer_index], proj_all[layer_index], proj_bias_all[layer_index], up_all[layer_index], up_bias_all[layer_index], down_all[layer_index], down_bias_all[layer_index])
        tiles = inputs.reshape(TOTAL, WIN, D)
        out_one = run_block(tiles, layer_params(0), position_table(table_all[0], bias_index), no_mask)
        moved = both_ways(out_one)[source_of]
        out_two = run_block(moved, layer_params(1), position_table(table_all[1], bias_index), regions)
        return low(out_two)[target_of].reshape(TOKENS, D)
    result, pullback = jax.vjp(forward, patches.astype(jnp.float32), weights)
    grad_patches, grads = pullback(out_grad.astype(jnp.float32))
    return (result.astype(jnp.bfloat16), grad_patches, grads[0], grads[1], grads[2], grads[3], grads[4], grads[5], grads[6], grads[7], grads[8], grads[9], grads[10])
```

```python
import functools

import jax
import jax.numpy as jnp
from jax import lax
from jax.experimental import pallas as pl
from jax.experimental.pallas import tpu as pltpu
from jax.sharding import PartitionSpec as P

HEADS = 32
SIDE = 10
WIN = 100


epsilon = 1e-05
masked_score = -1000000000.0


def layer_norm(inputs, gain, shift):
    mean_value = jnp.mean(inputs, axis=-1, keepdims=True)
    centered = inputs - mean_value
    inverse = lax.rsqrt(jnp.mean(centered * centered, axis=-1, keepdims=True) + epsilon)
    normal_part = centered * inverse
    return (normal_part * gain + shift, normal_part, inverse)


def norm_back(grad_out, normal_part, inverse, gain):
    scaled = grad_out * gain
    grad_in = inverse * (
        scaled
        - jnp.mean(scaled, axis=-1, keepdims=True)
        - normal_part * jnp.mean(scaled * normal_part, axis=-1, keepdims=True)
    )
    return (grad_in, jnp.sum(grad_out * normal_part, axis=0), jnp.sum(grad_out, axis=0))


def gelu_exact(hidden):
    return jax.nn.gelu(hidden, approximate=False)


def region_mask(region_ids):
    position = jnp.arange(WIN, dtype=jnp.int32)
    cut_point = SIDE - SIDE // 2
    right_half = (position % SIDE >= cut_point).astype(jnp.int32)
    lower_half = (position // SIDE >= cut_point).astype(jnp.int32)
    labels = (
        region_ids[:, None] % 2 * right_half[None]
        + 2 * (region_ids[:, None] // 2) * lower_half[None]
    )
    same_label = labels[:, :, None] == labels[:, None, :]
    return jnp.where(same_label, 0.0, masked_score).astype(jnp.float32)[:, None]


MESH = pl.DeviceIdType.MESH
ANY = pl.BlockSpec(memory_space=pl.ANY)
VMEM = pl.BlockSpec(memory_space=pltpu.VMEM)
WIDE = 1024
LOOK = 2


def ring_position(peer, peers):
    column, row = lax.rem(peer, 2), lax.div(peer, 2)
    return column * (peers - 1 - row) + (1 - column) * row


def ring_member(place, peers):
    place = lax.rem(place + peers, peers)
    far = lax.div(place, peers // 2)
    return (1 - far) * 2 * place + far * (2 * (peers - 1 - place) + 1)


class Place:
    def __init__(self, depths, peers):
        self.depths, self.peers, self.half = depths, peers, peers // 2
        outer = lax.axis_index("dp")
        self.depth, self.core = lax.div(outer, 2), lax.rem(outer, 2)
        self.peer = lax.axis_index("fsdp")
        self.spot = ring_position(self.peer, peers)
        self.index = outer * peers + self.peer
        self.total = depths * 2 * peers

    def sibling(self):
        return (self.depth * 2 + 1 - self.core, self.peer)

    def around(self, step):
        return ring_member(self.spot + step, self.peers)

    def neighbour(self, step):
        return (self.depth * 2 + self.core, self.around(step))

    def at_depth(self, step):
        return lax.rem(self.depth + step + self.depths, self.depths)

    def deep(self, step):
        return (self.at_depth(step) * 2 + self.core, self.peer)

    def other(self, step):
        index = lax.rem(self.index + step, self.total)
        return (lax.div(index, self.peers), lax.rem(index, self.peers))

    def greet(self):
        barrier = pltpu.get_barrier_semaphore()

        def signal(step, carry):
            pl.semaphore_signal(barrier, inc=1, device_id=self.other(step), device_id_type=MESH)
            return carry

        lax.fori_loop(1, self.total, signal, 0)
        pl.semaphore_wait(barrier, self.total - 1)

    def greet_near(self):
        barrier = pltpu.get_barrier_semaphore()
        near = [self.sibling(), self.neighbour(1), self.neighbour(-1)]
        near += [self.deep(step) for step in range(1, self.depths)]
        for device in near:
            pl.semaphore_signal(barrier, inc=1, device_id=device, device_id_type=MESH)
        pl.semaphore_wait(barrier, len(near))


def remote(source, target, send, receive, device):
    return pltpu.make_async_remote_copy(
        src_ref=source,
        dst_ref=target,
        send_sem=send,
        recv_sem=receive,
        device_id=device,
        device_id_type=MESH,
    )


class Spread:
    def __init__(self, place, source, target, send, receive, local):
        self.place, self.source, self.target = place, source, target
        self.send, self.receive, self.local = send, receive, local

    def own(self):
        return pltpu.make_async_copy(self.source, self.target.at[self.place.index], self.local)

    def start(self):
        def copy(step, carry):
            remote(
                self.source,
                self.target.at[self.place.index],
                self.send,
                self.receive,
                self.place.other(step),
            ).start()
            return carry

        lax.fori_loop(1, self.place.total, copy, 0)
        self.own().start()

    def wait(self):
        rest = self.target.at[pl.ds(0, self.place.total - 1)]
        both = remote(rest, rest, self.send, self.receive, self.place.other(1))
        both.wait_send()
        both.wait_recv()
        self.own().wait()


def gather_kernel(chunks, depths, peers, count, *refs):
    blocks, small = refs[:count], refs[count]
    fulls, small_full = refs[count + 1 : 2 * count + 1], refs[2 * count + 1]
    (z_send, z_recv, r_send, r_recv, c_send, c_recv, own_sem, s_send, s_recv, s_own) = refs[
        2 * count + 2 :
    ]
    place = Place(depths, peers)
    half = place.half
    core, cut = place.core, depths // 2

    def view(i, depth, peer):
        array, layer, rows, columns = chunks[i]
        return fulls[array].at[depth, core, peer, rows, columns]

    def block(i):
        array, layer, rows, columns = chunks[i]
        return blocks[array].at[layer, rows, columns]

    def own(i):
        return pltpu.make_async_copy(block(i), view(i, place.depth, place.peer), own_sem.at[i])

    def deep(i, step):
        return remote(
            block(i),
            view(i, place.depth, place.peer),
            z_send.at[i, step - 1],
            z_recv.at[i, step - 1],
            place.deep(step),
        )

    def part(step, way):
        if step < half:
            return slice(None)
        return slice(0, cut) if way == 0 else slice(cut, depths)

    def ring(i, step, way):
        turn = 1 if way == 0 else -1
        here = view(i, part(step, way), place.around(-turn * (step - 1)))
        return remote(
            here,
            here,
            r_send.at[i, step - 1, way],
            r_recv.at[i, step - 1, way],
            place.neighbour(turn),
        )

    def across(i, slot):
        step = (slot + 1) // 2
        turn = 1 if slot % 2 else -1
        here = view(i, slice(None), place.around(-turn * step))
        return remote(here, here, c_send.at[i, slot], c_recv.at[i, slot], place.sibling())

    slots = 2 * half
    total = len(chunks)

    def begin(i):
        for step in range(1, depths):
            deep(i, step).start()
        own(i).start()

    def first(i):
        own(i).wait()
        for step in range(1, depths):
            deep(i, step).wait_recv()
        ring(i, 1, 0).start()
        ring(i, 1, 1).start()
        across(i, 0).start()

    def later(i, step):
        ring(i, step, 0).wait_recv()
        ring(i, step, 1).wait_recv()
        if step < half:
            ring(i, step + 1, 0).start()
            ring(i, step + 1, 1).start()
            across(i, 2 * step - 1).start()
            across(i, 2 * step).start()
        else:
            across(i, 2 * step - 1).start()

    place.greet()
    begin(0)
    spread = Spread(place, small, small_full, s_send, s_recv, s_own)
    spread.start()
    for i in range(1, min(LOOK, total)):
        begin(i)
    for tick in range(total + half):
        if tick + LOOK < total:
            begin(tick + LOOK)
        if tick < total:
            first(tick)
        for step in range(1, half + 1):
            if 0 <= tick - step < total:
                later(tick - step, step)
    spread.wait()
    for i in range(total):
        for slot in range(slots):
            across(i, slot).wait()
        for step in range(1, depths):
            deep(i, step).wait_send()
        for step in range(1, half + 1):
            for way in range(2):
                ring(i, step, way).wait_send()


def chunk_list(shapes, layers):
    chunks = []
    for layer in layers:
        for which, (rows, columns) in enumerate(shapes):
            array = layer * len(shapes) + which
            if columns > WIDE:
                for start in range(0, columns, WIDE):
                    chunks.append((which, array, layer, slice(None), slice(start, start + WIDE)))
            else:
                size = rows // 4 if rows % 64 == 0 and rows > 64 else rows
                for start in range(0, rows, size):
                    chunks.append((which, array, layer, slice(start, start + size), slice(None)))
    return chunks


def gather_all(blocks, small, depths, peers):
    shapes = [b.shape[1:] for b in blocks]
    half = peers // 2
    count = 2 * len(blocks)
    plan = [(array, layer, rows, cols) for _, array, layer, rows, cols in chunk_list(shapes, (0, 1))]
    total = len(plan)

    outs = [
        jax.ShapeDtypeStruct((depths, 2, peers) + shape, jnp.bfloat16)
        for _ in range(2)
        for shape in shapes
    ]
    outs.append(jax.ShapeDtypeStruct((depths * 2 * peers,) + small.shape, small.dtype))
    dma = pltpu.SemaphoreType.DMA
    doubled = list(blocks) + list(blocks)
    return pl.pallas_call(
        functools.partial(gather_kernel, plan, depths, peers, count),
        out_shape=outs,
        in_specs=[ANY] * (count + 1),
        out_specs=[ANY] * (count + 1),
        scratch_shapes=[
            dma((total, depths - 1)),
            dma((total, depths - 1)),
            dma((total, half, 2)),
            dma((total, half, 2)),
            dma((total, 2 * half)),
            dma((total, 2 * half)),
            dma((total,)),
            dma(()),
            dma(()),
            dma(()),
        ],
        compiler_params=pltpu.CompilerParams(
            collective_id=0, has_side_effects=True, vmem_limit_bytes=60 * 2**20
        ),
    )(*doubled, small)


def sum_kernel(plan, depths, peers, count, with_small, *refs):
    lefts, rights, rest = refs[:count], refs[count : 2 * count], refs[2 * count :]
    if with_small:
        small, rest = rest[0], rest[1:]
    outs, rest = rest[:count], rest[count:]
    if with_small:
        small_all, rest = rest[0], rest[1:]
    left_bufs, right_bufs, rest = rest[:count], rest[count : 2 * count], rest[2 * count :]
    (half_send, half_recv, full_send, full_recv, z_out, z_in, own_part, x_send, x_recv, x_own) = rest[:10]
    (r_send, r_recv, z_send, z_recv) = rest[10:14]
    if with_small:
        small_in, small_sum, a_send, a_recv, a_own, b_send, b_recv, b_own = rest[14:]
    place = Place(depths, peers)
    half, core = place.half, place.core
    rows = z_out.shape[2]
    tall = depths * rows
    cut = tall // 2

    def swap(k):
        array = k // 2
        if k % 2 == 0:
            mine, theirs = lefts[array].at[core], lefts[array].at[1 - core]
            buf = left_bufs[array]
        else:
            mine = theirs = rights[array]
            buf = right_bufs[array]
        return (
            pltpu.make_async_copy(mine, buf.at[0], x_own.at[k]),
            remote(theirs, buf.at[1], x_send.at[k], x_recv.at[k], place.sibling()),
        )

    def product(i, peer):
        array, row_part, start, _ = plan[i]
        columns = pl.ds(start, WIDE)
        return jnp.dot(
            left_bufs[array][0, row_part, peer],
            right_bufs[array][0, :, columns],
            preferred_element_type=jnp.float32,
        ) + jnp.dot(
            left_bufs[array][1, row_part, peer],
            right_bufs[array][1, :, columns],
            preferred_element_type=jnp.float32,
        )

    def ring(i, step, way):
        if step == 1:
            source, target = half_send.at[i, way], half_recv.at[i, way]
        else:
            source, target = full_send.at[i, step - 2, way], full_recv.at[i, step - 2, way]
        return remote(
            source,
            target,
            r_send.at[i, step - 1, way],
            r_recv.at[i, step - 1, way],
            place.neighbour(1 if way == 0 else -1),
        )

    def deep(i, step):
        return remote(
            z_out.at[i, place.at_depth(step)],
            z_in.at[i, step - 1],
            z_send.at[i, step - 1],
            z_recv.at[i, step - 1],
            place.deep(step),
        )

    def first(i):
        found = product(i, place.around(half)).astype(jnp.bfloat16)
        half_send[i, 0] = found[:cut]
        half_send[i, 1] = found[cut:]
        ring(i, 1, 0).start()
        ring(i, 1, 1).start()

    def next_step(i, step):
        for way in range(2):
            turn = 1 if way == 0 else -1
            found = product(i, place.around(turn * (half - step + 1)))
            ring(i, step - 1, way).wait_recv()
            if step == 2:
                came = half_recv[i, way].astype(jnp.float32)
                low = found[:cut] + came if way == 0 else found[:cut]
                high = found[cut:] if way == 0 else found[cut:] + came
                full_send[i, 0, way, :cut] = low.astype(jnp.bfloat16)
                full_send[i, 0, way, cut:] = high.astype(jnp.bfloat16)
            else:
                came = full_recv[i, step - 3, way].astype(jnp.float32)
                full_send[i, step - 2, way] = (found + came).astype(jnp.bfloat16)
            ring(i, step, way).start()

    def plane(i):
        found = product(i, place.peer)
        for way in range(2):
            ring(i, half, way).wait_recv()
            found += full_recv[i, half - 2, way].astype(jnp.float32)
        for depth in range(depths):
            piece = found[depth * rows : (depth + 1) * rows]
            z_out[i, depth] = piece.astype(jnp.bfloat16)

            @pl.when(depth == place.depth)
            def _():
                own_part[i] = piece

        for step in range(1, depths):
            deep(i, step).start()

    def finish(i):
        array, _, start, out_rows = plan[i]
        found = own_part[i]
        for step in range(1, depths):
            deep(i, step).wait_recv()
            found += z_in[i, step - 1].astype(jnp.float32)
        outs[array][out_rows, pl.ds(start, WIDE)] = found

    if with_small:
        place.greet()
    else:
        place.greet_near()
    for k in reversed(range(2 * count)):
        for copy in swap(k):
            copy.start()
    if with_small:

        def send_small(step, carry):
            outer, peer = place.other(step)
            remote(
                small.at[outer * peers + peer],
                small_in.at[place.index],
                a_send,
                a_recv,
                (outer, peer),
            ).start()
            return carry

        lax.fori_loop(1, place.total, send_small, 0)
        own_small = pltpu.make_async_copy(small.at[place.index], small_in.at[place.index], a_own)
        own_small.start()
        spread = Spread(place, small_sum, small_all, b_send, b_recv, b_own)

    total = len(plan)
    ready = set()
    for tick in range(total + half + 1):
        if tick < total:
            array = plan[tick][0]
            if array not in ready:
                ready.add(array)
                for k in (2 * array + 1, 2 * array):
                    kept, sent = swap(k)
                    kept.wait()
                    sent.wait_recv()
            first(tick)
        for step in range(2, half + 1):
            if 0 <= tick - step + 1 < total:
                next_step(tick - step + 1, step)
        if 0 <= tick - half < total:
            plane(tick - half)
        if 0 <= tick - half - 1 < total:
            finish(tick - half - 1)
        if with_small and tick == 4:
            rest_in = small_in.at[pl.ds(0, place.total - 1)]
            both = remote(rest_in, rest_in, a_send, a_recv, place.other(1))
            both.wait_send()
            both.wait_recv()
            own_small.wait()
            small_sum[...] = jnp.sum(small_in[...], axis=0)
            spread.start()
    if with_small:
        spread.wait()
    for k in range(2 * count):
        swap(k)[1].wait_send()
    for i in range(total):
        for step in range(1, half + 1):
            for way in range(2):
                ring(i, step, way).wait_send()
        for step in range(1, depths):
            deep(i, step).wait_send()


def sum_all(pairs, shapes, depths, peers, call, small=None):
    half, count = peers // 2, len(pairs)
    tokens = pairs[0][0].shape[0]
    padded = -(-tokens // 128) * 128
    unit = min(shape[0] for shape in shapes)
    lefts, rights, plan = [], [], []
    for array, ((left, right), shape) in enumerate(zip(pairs, shapes)):
        parts = shape[0] // unit
        turned = jnp.pad(left, ((0, padded - tokens), (0, 0))).T
        turned = turned.reshape(depths, 2, peers, parts, unit, padded)
        lefts.append(
            turned.transpose(1, 3, 2, 0, 4, 5).reshape(2, parts, peers, depths * unit, padded)
        )
        rights.append(jnp.pad(right, ((0, padded - tokens), (0, 0))))
        for part in range(parts):
            for start in range(0, shape[1], WIDE):
                plan.append((array, part, start, pl.ds(part * unit, unit)))
    plan = plan[::-1]
    total, tall = len(plan), depths * unit
    dma = pltpu.SemaphoreType.DMA
    low = jnp.bfloat16
    scratch = [pltpu.VMEM((2,) + a.shape[1:], low) for a in lefts]
    scratch += [pltpu.VMEM((2,) + a.shape, low) for a in rights]
    scratch += [
        pltpu.VMEM((total, 2, tall // 2, WIDE), low),
        pltpu.VMEM((total, 2, tall // 2, WIDE), low),
        pltpu.VMEM((total, half - 1, 2, tall, WIDE), low),
        pltpu.VMEM((total, half - 1, 2, tall, WIDE), low),
        pltpu.VMEM((total, depths, unit, WIDE), low),
        pltpu.VMEM((total, depths - 1, unit, WIDE), low),
        pltpu.VMEM((total, unit, WIDE), jnp.float32),
        dma((2 * count,)),
        dma((2 * count,)),
        dma((2 * count,)),
        dma((total, half, 2)),
        dma((total, half, 2)),
        dma((total, depths - 1)),
        dma((total, depths - 1)),
    ]
    args = [*lefts, *rights]
    in_specs = [ANY] * (2 * count)
    out_shape = [jax.ShapeDtypeStruct(shape, jnp.float32) for shape in shapes]
    out_specs = [VMEM] * count
    if small is not None:
        args.append(small)
        in_specs.append(ANY)
        out_shape.append(jax.ShapeDtypeStruct(small.shape, jnp.float32))
        out_specs.append(VMEM)
        scratch += [
            pltpu.VMEM(small.shape, jnp.float32),
            pltpu.VMEM(small.shape[1:], jnp.float32),
        ] + [dma(())] * 6
    return pl.pallas_call(
        functools.partial(sum_kernel, plan, depths, peers, count, small is not None),
        out_shape=out_shape,
        in_specs=in_specs,
        out_specs=out_specs,
        scratch_shapes=scratch,
        compiler_params=pltpu.CompilerParams(
            collective_id=call, has_side_effects=True, vmem_limit_bytes=60 * 2**20
        ),
    )(*args)


def attention_scores(qkv_parts, position_bias, mask_add):
    head_scale = qkv_parts.shape[-1] ** (-0.5)
    scores = (
        jnp.einsum(
            "wqhd,wkhd->whqk",
            qkv_parts[:, :, 0],
            qkv_parts[:, :, 1],
            preferred_element_type=jnp.float32,
        )
        * head_scale
        + position_bias[None]
    )
    if mask_add is not None:
        scores = scores + mask_add
    return scores


def block_forward(inputs, weights, position_bias, mask_add, windows):
    norm_gains, norm_shifts, w_qkv, qv_bias, w_proj, b_proj, w_up, b_up, w_down, b_down = weights
    model_width = inputs.shape[1]
    norm_gains = norm_gains.astype(jnp.float32)
    norm_shifts = norm_shifts.astype(jnp.float32)
    normed, normal_one, inverse_one = layer_norm(inputs, norm_gains[0], norm_shifts[0])
    normed_low = normed.astype(jnp.bfloat16)
    qv_float = qv_bias.astype(jnp.float32)
    bias_full = jnp.concatenate(
        [qv_float[:model_width], jnp.zeros((model_width,), jnp.float32), qv_float[model_width:]]
    )
    qkv_low = (jnp.dot(normed_low, w_qkv, preferred_element_type=jnp.float32) + bias_full).astype(
        jnp.bfloat16
    )
    qkv_parts = qkv_low.reshape(windows, WIN, 3, HEADS, -1)
    scores = attention_scores(qkv_parts, position_bias, mask_add)
    row_max = jnp.max(scores, axis=-1, keepdims=True)
    shifted_exp = jnp.exp(scores - row_max)
    row_total = jnp.sum(shifted_exp, axis=-1, keepdims=True)
    soft_low = (shifted_exp / row_total).astype(jnp.bfloat16)
    log_total = row_max + jnp.log(row_total)
    attended = jnp.einsum(
        "whqk,wkhd->wqhd", soft_low, qkv_parts[:, :, 2], preferred_element_type=jnp.float32
    )
    attended_low = attended.reshape(inputs.shape).astype(jnp.bfloat16)
    middle = inputs + (
        jnp.dot(attended_low, w_proj, preferred_element_type=jnp.float32)
        + b_proj.astype(jnp.float32)
    )
    normed_two, normal_two, inverse_two = layer_norm(middle, norm_gains[1], norm_shifts[1])
    normed_two_low = normed_two.astype(jnp.bfloat16)
    hidden = jnp.dot(normed_two_low, w_up, preferred_element_type=jnp.float32) + b_up.astype(
        jnp.float32
    )
    activated_low = gelu_exact(hidden).astype(jnp.bfloat16)
    output = middle + (
        jnp.dot(activated_low, w_down, preferred_element_type=jnp.float32)
        + b_down.astype(jnp.float32)
    )
    kept_state = (
        normal_one,
        inverse_one,
        normed_low,
        qkv_low,
        log_total,
        attended_low,
        normal_two,
        inverse_two,
        normed_two_low,
        hidden,
        activated_low,
    )
    return (output, kept_state)


def block_backward(grad_out, weights, kept_state, position_bias, mask_add, bucket_table, windows):
    norm_gains, norm_shifts, w_qkv, qv_bias, w_proj, b_proj, w_up, b_up, w_down, b_down = weights
    (
        normal_one,
        inverse_one,
        normed_low,
        qkv_low,
        log_total,
        attended_low,
        normal_two,
        inverse_two,
        normed_two_low,
        hidden,
        activated_low,
    ) = kept_state
    model_width = grad_out.shape[1]
    norm_gains = norm_gains.astype(jnp.float32)
    grad_down_low = grad_out.astype(jnp.bfloat16)
    down_bias_grad = jnp.sum(grad_down_low, axis=0, dtype=jnp.float32)
    grad_act = jnp.einsum("rd,fd->rf", grad_down_low, w_down, preferred_element_type=jnp.float32)
    gelu_back = jax.vjp(gelu_exact, hidden)[1]
    grad_hidden_low = gelu_back(grad_act)[0].astype(jnp.bfloat16)
    up_bias_grad = jnp.sum(grad_hidden_low, axis=0, dtype=jnp.float32)
    grad_normed_two = jnp.einsum(
        "rf,df->rd", grad_hidden_low, w_up, preferred_element_type=jnp.float32
    )
    grad_mid_norm, gain_two_grad, shift_two_grad = norm_back(
        grad_normed_two, normal_two, inverse_two, norm_gains[1]
    )
    grad_middle = grad_out + grad_mid_norm
    grad_branch_low = grad_middle.astype(jnp.bfloat16)
    proj_bias_grad = jnp.sum(grad_branch_low, axis=0, dtype=jnp.float32)
    grad_attended_low = jnp.einsum(
        "rd,cd->rc", grad_branch_low, w_proj, preferred_element_type=jnp.float32
    ).astype(jnp.bfloat16)
    qkv_parts = qkv_low.reshape(windows, WIN, 3, HEADS, -1)
    scores = attention_scores(qkv_parts, position_bias, mask_add)
    soft = jnp.exp(scores - log_total)
    soft_low = soft.astype(jnp.bfloat16)
    grad_heads = grad_attended_low.reshape(windows, WIN, HEADS, -1)
    grad_value = jnp.einsum(
        "whqk,wqhd->wkhd", soft_low, grad_heads, preferred_element_type=jnp.float32
    )
    grad_soft = jnp.einsum(
        "wqhd,wkhd->whqk", grad_heads, qkv_parts[:, :, 2], preferred_element_type=jnp.float32
    )
    grad_scores_low = (
        soft * (grad_soft - jnp.sum(soft * grad_soft, axis=-1, keepdims=True))
    ).astype(jnp.bfloat16)
    head_scale = qkv_parts.shape[-1] ** (-0.5)
    grad_query = (
        jnp.einsum(
            "whqk,wkhd->wqhd",
            grad_scores_low,
            qkv_parts[:, :, 1],
            preferred_element_type=jnp.float32,
        )
        * head_scale
    )
    grad_key = (
        jnp.einsum(
            "whqk,wqhd->wkhd",
            grad_scores_low,
            qkv_parts[:, :, 0],
            preferred_element_type=jnp.float32,
        )
        * head_scale
    )
    score_sum = jnp.sum(grad_scores_low, axis=0, dtype=jnp.float32).reshape(HEADS, -1)
    table_grad = jnp.einsum("hn,nb->bh", score_sum, bucket_table, precision=lax.Precision.HIGHEST)
    grad_qkv_low = (
        jnp.stack([grad_query, grad_key, grad_value], axis=2)
        .reshape(qkv_low.shape)
        .astype(jnp.bfloat16)
    )
    column_sums = jnp.sum(grad_qkv_low, axis=0, dtype=jnp.float32)
    qv_grad = jnp.concatenate([column_sums[:model_width], column_sums[2 * model_width :]])
    grad_normed = jnp.einsum("re,de->rd", grad_qkv_low, w_qkv, preferred_element_type=jnp.float32)
    grad_in_norm, gain_one_grad, shift_one_grad = norm_back(
        grad_normed, normal_one, inverse_one, norm_gains[0]
    )
    grad_input = grad_middle + grad_in_norm
    grads = (
        jnp.stack([gain_one_grad, gain_two_grad]),
        jnp.stack([shift_one_grad, shift_two_grad]),
        qv_grad,
        proj_bias_grad,
        up_bias_grad,
        down_bias_grad,
    )
    pairs = (
        (normed_low, grad_qkv_low),
        (attended_low, grad_branch_low),
        (normed_two_low, grad_hidden_low),
        (activated_low, grad_down_low),
    )
    return (grad_input, grads, table_grad, pairs)


def shards(
    outer_count,
    peer_count,
    patches,
    out_grad,
    norm_gain,
    norm_shift,
    qkv_weight,
    qv_bias,
    rel_table,
    proj_weight,
    proj_bias,
    up_weight,
    up_bias,
    down_weight,
    down_bias,
    tile_perm,
    window_slot,
    mask_ids,
    bias_index,
):
    windows = patches.shape[0] // WIN
    model_width = patches.shape[1]
    depths = outer_count // 2
    devices = outer_count * peer_count
    capacity = (windows + peer_count - 1) // peer_count
    device_index = lax.axis_index(("dp", "fsdp"))
    total_windows = tile_perm.shape[0]
    slot_ids = jnp.arange(total_windows, dtype=jnp.int32)

    def one_hot_pick(keys, values):
        return jnp.sum(jnp.where(keys[None, :] == slot_ids[:, None], values[None, :], 0), axis=1)

    def look_up(values, at):
        hit = at[:, None] == jnp.arange(values.shape[0], dtype=jnp.int32)[None, :]
        return jnp.sum(jnp.where(hit, values[None, :], 0), axis=1)

    source_of = one_hot_pick(window_slot, look_up(window_slot, tile_perm))
    target_of = one_hot_pick(source_of, slot_ids)
    region_slot = one_hot_pick(window_slot, mask_ids)
    own_slots = device_index * windows + jnp.arange(windows, dtype=jnp.int32)

    def rank_of(slots, device_of):
        grid_view = device_of.reshape(-1, windows)
        earlier = jnp.arange(windows)[None, :] < jnp.arange(windows)[:, None]
        same_peer = grid_view[:, :, None] == grid_view[:, None, :]
        ranks = jnp.sum(same_peer & earlier[None], axis=2).reshape(-1)
        return look_up(ranks, slots)

    def peer_of(slots):
        return slots // windows % peer_count

    own_source = look_up(source_of, own_slots)
    own_target = look_up(target_of, own_slots)
    forward_send = peer_of(own_target) * capacity + rank_of(own_slots, target_of // windows)
    forward_take = peer_of(own_source) * capacity + rank_of(own_source, target_of // windows)
    backward_send = peer_of(own_source) * capacity + rank_of(own_slots, source_of // windows)
    backward_take = peer_of(own_target) * capacity + rank_of(own_target, source_of // windows)
    mask_add = region_mask(look_up(region_slot, own_slots))
    bucket_table = (
        bias_index.reshape(-1)[:, None] == jnp.arange(rel_table.shape[1], dtype=jnp.int32)[None, :]
    ).astype(jnp.float32)
    tables = rel_table.astype(jnp.float32)
    bias_one = jnp.einsum(
        "nb,bh->hn", bucket_table, tables[0], precision=lax.Precision.HIGHEST
    ).reshape(HEADS, WIN, WIN)
    bias_two = jnp.einsum(
        "nb,bh->hn", bucket_table, tables[1], precision=lax.Precision.HIGHEST
    ).reshape(HEADS, WIN, WIN)

    def choose(rows, at, count):
        spots = jnp.arange(count, dtype=jnp.int32)
        hit = spots[:, None] == at[None, :]
        return sum(
            jnp.where(hit[:, w][:, None, None], rows[w][None], jnp.zeros((), rows.dtype))
            for w in range(rows.shape[0])
        )

    def take(rows, at):
        hit = at[:, None] == jnp.arange(rows.shape[0], dtype=jnp.int32)[None, :]
        return sum(
            jnp.where(hit[:, w][:, None, None], rows[w][None], jnp.zeros((), rows.dtype))
            for w in range(rows.shape[0])
        )

    def move(rows_low, send, fetch):
        parts = rows_low.reshape(windows, WIN, model_width)
        sectioning = choose(parts, send, peer_count * capacity)
        arrived = lax.all_to_all(sectioning, "fsdp", split_axis=0, concat_axis=0, tiled=True)
        return take(arrived, fetch).reshape(rows_low.shape)

    def to_shifted(rows_low):
        return move(rows_low, forward_send, forward_take)

    def from_shifted(rows_low):
        return move(rows_low, backward_send, backward_take)

    vectors = (norm_gain, norm_shift, qv_bias, proj_bias, up_bias, down_bias)
    flat = jnp.concatenate([v.reshape(-1) for v in vectors])
    small = jnp.pad(flat, (0, -flat.shape[0] % 2048)).reshape(-1, 128)
    matrices = (qkv_weight, proj_weight, up_weight, down_weight)
    *fulls, small_full = gather_all(matrices, small, depths, peer_count)
    small_full = small_full.reshape(devices, -1)
    whole, offset = [], 0
    for v in vectors:
        size = v.size
        piece = small_full[:, offset : offset + size].reshape((devices,) + v.shape)
        offset += size
        piece = jnp.moveaxis(piece, 0, -2)
        whole.append(piece.reshape(v.shape[:-1] + (-1,)))

    def weights_of(layer):
        gains, shifts, qv, proj_b, up_b, down_b = [v[layer] for v in whole]
        w_qkv, w_proj, w_up, w_down = [
            fulls[4 * layer + k].reshape(-1, matrices[k].shape[-1]) for k in range(4)
        ]
        return (gains, shifts, w_qkv, qv, w_proj, proj_b, w_up, up_b, w_down, down_b)

    first_weights, second_weights = weights_of(0), weights_of(1)
    grad_two = to_shifted(out_grad)
    output_one, state_one = block_forward(
        patches.astype(jnp.float32), first_weights, bias_one, None, windows
    )
    second_input = to_shifted(output_one.astype(jnp.bfloat16))
    output_two, state_two = block_forward(
        second_input.astype(jnp.float32), second_weights, bias_two, mask_add, windows
    )
    block_out = from_shifted(output_two.astype(jnp.bfloat16))
    shapes = [m.shape[1:] for m in matrices]
    grad_input_two, grads_two, table_two, pairs_two = block_backward(
        grad_two.astype(jnp.float32), second_weights, state_two, bias_two, mask_add, bucket_table, windows
    )
    sums_two = sum_all(pairs_two, shapes, depths, peer_count, 1)
    grad_one = from_shifted(grad_input_two.astype(jnp.bfloat16))
    grad_patches, grads_one, table_one, pairs_one = block_backward(
        grad_one.astype(jnp.float32), first_weights, state_one, bias_one, None, bucket_table, windows
    )
    small_grads = []
    for one, two, v in zip(grads_one, grads_two, vectors):
        both = jnp.stack([one, two]).reshape(v.shape[:-1] + (devices, v.shape[-1]))
        small_grads.append(jnp.moveaxis(both, -2, 0).reshape(devices, -1))
    table = jnp.stack([table_one, table_two]).reshape(-1)
    table = jnp.pad(table, (0, -table.shape[0] % devices)).reshape(devices, -1)
    packed = jnp.concatenate(small_grads + [table], axis=1)
    width = packed.shape[1]
    packed = jnp.pad(packed, ((0, 0), (0, -width % 1024))).reshape(devices, -1, 128)
    *sums_one, small_all = sum_all(pairs_one, shapes, depths, peer_count, 2, packed)
    small_all = small_all.reshape(devices, -1)
    mine = lax.dynamic_index_in_dim(small_all, device_index, 0, keepdims=False)
    vector_grads, offset = [], 0
    for v in vectors:
        vector_grads.append(mine[offset : offset + v.size].reshape(v.shape))
        offset += v.size
    table_total = small_all[:, offset:width].reshape(-1)[: rel_table.size].reshape(rel_table.shape)
    grad_qkv, grad_proj, grad_up, grad_down = [
        jnp.stack([one, two]) for one, two in zip(sums_one, sums_two)
    ]
    return (
        block_out,
        grad_patches,
        vector_grads[0],
        vector_grads[1],
        grad_qkv,
        vector_grads[2],
        table_total,
        grad_proj,
        vector_grads[3],
        grad_up,
        vector_grads[4],
        grad_down,
        vector_grads[5],
    )


def solution(mesh):
    placed = (
        P(("dp", "fsdp"), None),
        P(("dp", "fsdp"), None),
        P(None, None, ("dp", "fsdp")),
        P(None, None, ("dp", "fsdp")),
        P(None, ("dp", "fsdp"), None),
        P(None, ("dp", "fsdp")),
        P(),
        P(None, ("dp", "fsdp"), None),
        P(None, ("dp", "fsdp")),
        P(None, ("dp", "fsdp"), None),
        P(None, ("dp", "fsdp")),
        P(None, ("dp", "fsdp"), None),
        P(None, ("dp", "fsdp")),
        P(),
        P(),
        P(),
        P(),
    )
    return jax.shard_map(
        functools.partial(shards, mesh.shape["dp"], mesh.shape["fsdp"]),
        mesh=mesh,
        in_specs=placed,
        out_specs=(
            P(("dp", "fsdp"), None),
            P(("dp", "fsdp"), None),
            P(None, None, ("dp", "fsdp")),
            P(None, None, ("dp", "fsdp")),
            P(None, ("dp", "fsdp"), None),
            P(None, ("dp", "fsdp")),
            P(),
            P(None, ("dp", "fsdp"), None),
            P(None, ("dp", "fsdp")),
            P(None, ("dp", "fsdp"), None),
            P(None, ("dp", "fsdp")),
            P(None, ("dp", "fsdp"), None),
            P(None, ("dp", "fsdp")),
        ),
        check_vma=False,
    )
```

```python
import functools
import types

import jax
import jax.numpy as jnp
from jax import lax
from jax.experimental import pallas as pl
from jax.experimental.pallas import tpu as pltpu
from jax.sharding import PartitionSpec as P

HEADS = 32
SIDE = 10
WIN = 100


epsilon = 1e-05
masked_score = -1000000000.0


def layer_norm(inputs, gain, shift):
    mean_value = jnp.mean(inputs, axis=-1, keepdims=True)
    centered = inputs - mean_value
    inverse = lax.rsqrt(jnp.mean(centered * centered, axis=-1, keepdims=True) + epsilon)
    normal_part = centered * inverse
    return (normal_part * gain + shift, normal_part, inverse)


def norm_back(grad_out, normal_part, inverse, gain):
    scaled = grad_out * gain
    grad_in = inverse * (
        scaled
        - jnp.mean(scaled, axis=-1, keepdims=True)
        - normal_part * jnp.mean(scaled * normal_part, axis=-1, keepdims=True)
    )
    return (grad_in, jnp.sum(grad_out * normal_part, axis=0), jnp.sum(grad_out, axis=0))


def gelu_exact(hidden):
    return jax.nn.gelu(hidden, approximate=False)


def region_mask(region_ids):
    position = jnp.arange(WIN, dtype=jnp.int32)
    cut_point = SIDE - SIDE // 2
    right_half = (position % SIDE >= cut_point).astype(jnp.int32)
    lower_half = (position // SIDE >= cut_point).astype(jnp.int32)
    labels = (
        region_ids[:, None] % 2 * right_half[None]
        + 2 * (region_ids[:, None] // 2) * lower_half[None]
    )
    same_label = labels[:, :, None] == labels[:, None, :]
    return jnp.where(same_label, 0.0, masked_score).astype(jnp.float32)[:, None]


MESH = pl.DeviceIdType.MESH
ANY = pl.BlockSpec(memory_space=pl.ANY)
VMEM = pl.BlockSpec(memory_space=pltpu.VMEM)
WIDE = 1024
LOOK = 2


def ring_position(peer, peers):
    column, row = lax.rem(peer, 2), lax.div(peer, 2)
    return column * (peers - 1 - row) + (1 - column) * row


def ring_member(place, peers):
    place = lax.rem(place + peers, peers)
    far = lax.div(place, peers // 2)
    return (1 - far) * 2 * place + far * (2 * (peers - 1 - place) + 1)


class Place:
    def __init__(self, depths, peers):
        self.depths, self.peers, self.half = depths, peers, peers // 2
        outer = lax.axis_index("dp")
        self.depth, self.core = lax.div(outer, 2), lax.rem(outer, 2)
        self.peer = lax.axis_index("fsdp")
        self.spot = ring_position(self.peer, peers)
        self.index = outer * peers + self.peer
        self.total = depths * 2 * peers

    def sibling(self):
        return (self.depth * 2 + 1 - self.core, self.peer)

    def around(self, step):
        return ring_member(self.spot + step, self.peers)

    def neighbour(self, step):
        return (self.depth * 2 + self.core, self.around(step))

    def at_depth(self, step):
        return lax.rem(self.depth + step + self.depths, self.depths)

    def deep(self, step):
        return (self.at_depth(step) * 2 + self.core, self.peer)

    def other(self, step):
        index = lax.rem(self.index + step, self.total)
        return (lax.div(index, self.peers), lax.rem(index, self.peers))

    def greet(self):
        barrier = pltpu.get_barrier_semaphore()

        def signal(step, carry):
            pl.semaphore_signal(barrier, inc=1, device_id=self.other(step), device_id_type=MESH)
            return carry

        lax.fori_loop(1, self.total, signal, 0)
        pl.semaphore_wait(barrier, self.total - 1)

    def greet_near(self):
        barrier = pltpu.get_barrier_semaphore()
        near = [self.sibling(), self.neighbour(1), self.neighbour(-1)]
        near += [self.deep(step) for step in range(1, self.depths)]
        for device in near:
            pl.semaphore_signal(barrier, inc=1, device_id=device, device_id_type=MESH)
        pl.semaphore_wait(barrier, len(near))


def remote(source, target, send, receive, device):
    return pltpu.make_async_remote_copy(
        src_ref=source,
        dst_ref=target,
        send_sem=send,
        recv_sem=receive,
        device_id=device,
        device_id_type=MESH,
    )


class Spread:
    def __init__(self, place, source, target, send, receive, local):
        self.place, self.source, self.target = place, source, target
        self.send, self.receive, self.local = send, receive, local

    def own(self):
        return pltpu.make_async_copy(self.source, self.target.at[self.place.index], self.local)

    def start(self):
        def copy(step, carry):
            remote(
                self.source,
                self.target.at[self.place.index],
                self.send,
                self.receive,
                self.place.other(step),
            ).start()
            return carry

        lax.fori_loop(1, self.place.total, copy, 0)
        self.own().start()

    def wait(self):
        rest = self.target.at[pl.ds(0, self.place.total - 1)]
        both = remote(rest, rest, self.send, self.receive, self.place.other(1))
        both.wait_send()
        both.wait_recv()
        self.own().wait()


def gather_kernel(chunks, depths, peers, count, *refs):
    blocks, small = refs[:count], refs[count]
    fulls, small_full = refs[count + 1 : 2 * count + 1], refs[2 * count + 1]
    (z_send, z_recv, r_send, r_recv, c_send, c_recv, own_sem, s_send, s_recv, s_own) = refs[
        2 * count + 2 :
    ]
    place = Place(depths, peers)
    half = place.half
    core, cut = place.core, depths // 2

    def view(i, depth, peer):
        array, layer, rows, columns = chunks[i]
        return fulls[array].at[depth, core, peer, rows, columns]

    def block(i):
        array, layer, rows, columns = chunks[i]
        return blocks[array].at[layer, rows, columns]

    def own(i):
        return pltpu.make_async_copy(block(i), view(i, place.depth, place.peer), own_sem.at[i])

    def deep(i, step):
        return remote(
            block(i),
            view(i, place.depth, place.peer),
            z_send.at[i, step - 1],
            z_recv.at[i, step - 1],
            place.deep(step),
        )

    def part(step, way):
        if step < half:
            return slice(None)
        return slice(0, cut) if way == 0 else slice(cut, depths)

    def ring(i, step, way):
        turn = 1 if way == 0 else -1
        here = view(i, part(step, way), place.around(-turn * (step - 1)))
        return remote(
            here,
            here,
            r_send.at[i, step - 1, way],
            r_recv.at[i, step - 1, way],
            place.neighbour(turn),
        )

    def across(i, slot):
        step = (slot + 1) // 2
        turn = 1 if slot % 2 else -1
        here = view(i, slice(None), place.around(-turn * step))
        return remote(here, here, c_send.at[i, slot], c_recv.at[i, slot], place.sibling())

    slots = 2 * half
    total = len(chunks)

    def begin(i):
        for step in range(1, depths):
            deep(i, step).start()
        own(i).start()

    def first(i):
        own(i).wait()
        for step in range(1, depths):
            deep(i, step).wait_recv()
        ring(i, 1, 0).start()
        ring(i, 1, 1).start()
        across(i, 0).start()

    def later(i, step):
        ring(i, step, 0).wait_recv()
        ring(i, step, 1).wait_recv()
        if step < half:
            ring(i, step + 1, 0).start()
            ring(i, step + 1, 1).start()
            across(i, 2 * step - 1).start()
            across(i, 2 * step).start()
        else:
            across(i, 2 * step - 1).start()

    place.greet()
    begin(0)
    spread = Spread(place, small, small_full, s_send, s_recv, s_own)
    spread.start()
    for i in range(1, min(LOOK, total)):
        begin(i)
    for tick in range(total + half):
        if tick + LOOK < total:
            begin(tick + LOOK)
        if tick < total:
            first(tick)
        for step in range(1, half + 1):
            if 0 <= tick - step < total:
                later(tick - step, step)
    spread.wait()
    for i in range(total):
        for slot in range(slots):
            across(i, slot).wait()
        for step in range(1, depths):
            deep(i, step).wait_send()
        for step in range(1, half + 1):
            for way in range(2):
                ring(i, step, way).wait_send()


def chunk_list(shapes, layers):
    chunks = []
    for layer in layers:
        for which, (rows, columns) in enumerate(shapes):
            array = layer * len(shapes) + which
            if columns > WIDE:
                for start in range(0, columns, WIDE):
                    chunks.append((which, array, layer, slice(None), slice(start, start + WIDE)))
            else:
                size = rows // 4 if rows % 64 == 0 and rows > 64 else rows
                for start in range(0, rows, size):
                    chunks.append((which, array, layer, slice(start, start + size), slice(None)))
    return chunks


def gather_all(blocks, small, depths, peers):
    shapes = [b.shape[1:] for b in blocks]
    half = peers // 2
    count = 2 * len(blocks)
    plan = [(array, layer, rows, cols) for _, array, layer, rows, cols in chunk_list(shapes, (0, 1))]
    total = len(plan)

    outs = [
        jax.ShapeDtypeStruct((depths, 2, peers) + shape, jnp.bfloat16)
        for _ in range(2)
        for shape in shapes
    ]
    outs.append(jax.ShapeDtypeStruct((depths * 2 * peers,) + small.shape, small.dtype))
    dma = pltpu.SemaphoreType.DMA
    doubled = list(blocks) + list(blocks)
    return pl.pallas_call(
        functools.partial(gather_kernel, plan, depths, peers, count),
        out_shape=outs,
        in_specs=[ANY] * (count + 1),
        out_specs=[ANY] * (count + 1),
        scratch_shapes=[
            dma((total, depths - 1)),
            dma((total, depths - 1)),
            dma((total, half, 2)),
            dma((total, half, 2)),
            dma((total, 2 * half)),
            dma((total, 2 * half)),
            dma((total,)),
            dma(()),
            dma(()),
            dma(()),
        ],
        compiler_params=pltpu.CompilerParams(
            collective_id=0, has_side_effects=True, vmem_limit_bytes=60 * 2**20
        ),
    )(*doubled, small)


def sum_kernel(plan, depths, peers, count, with_small, *refs):
    lefts, rights, rest = refs[:count], refs[count : 2 * count], refs[2 * count :]
    if with_small:
        small, rest = rest[0], rest[1:]
    outs, rest = rest[:count], rest[count:]
    if with_small:
        small_all, rest = rest[0], rest[1:]
    left_bufs, right_bufs, rest = rest[:count], rest[count : 2 * count], rest[2 * count :]
    (half_send, half_recv, full_send, full_recv, z_out, z_in, own_part, x_send, x_recv, x_own) = rest[:10]
    (r_send, r_recv, z_send, z_recv) = rest[10:14]
    if with_small:
        small_in, small_sum, a_send, a_recv, a_own, b_send, b_recv, b_own = rest[14:]
    place = Place(depths, peers)
    half, core = place.half, place.core
    rows = z_out.shape[2]
    tall = depths * rows
    cut = tall // 2

    def swap(k):
        array = k // 2
        if k % 2 == 0:
            mine, theirs = lefts[array].at[core], lefts[array].at[1 - core]
            buf = left_bufs[array]
        else:
            mine = theirs = rights[array]
            buf = right_bufs[array]
        return (
            pltpu.make_async_copy(mine, buf.at[0], x_own.at[k]),
            remote(theirs, buf.at[1], x_send.at[k], x_recv.at[k], place.sibling()),
        )

    def product(i, peer):
        array, row_part, start, _ = plan[i]
        columns = pl.ds(start, WIDE)
        return jnp.dot(
            left_bufs[array][0, row_part, peer],
            right_bufs[array][0, :, columns],
            preferred_element_type=jnp.float32,
        ) + jnp.dot(
            left_bufs[array][1, row_part, peer],
            right_bufs[array][1, :, columns],
            preferred_element_type=jnp.float32,
        )

    def ring(i, step, way):
        if step == 1:
            source, target = half_send.at[i, way], half_recv.at[i, way]
        else:
            source, target = full_send.at[i, step - 2, way], full_recv.at[i, step - 2, way]
        return remote(
            source,
            target,
            r_send.at[i, step - 1, way],
            r_recv.at[i, step - 1, way],
            place.neighbour(1 if way == 0 else -1),
        )

    def deep(i, step):
        return remote(
            z_out.at[i, place.at_depth(step)],
            z_in.at[i, step - 1],
            z_send.at[i, step - 1],
            z_recv.at[i, step - 1],
            place.deep(step),
        )

    def first(i):
        found = product(i, place.around(half)).astype(jnp.bfloat16)
        half_send[i, 0] = found[:cut]
        half_send[i, 1] = found[cut:]
        ring(i, 1, 0).start()
        ring(i, 1, 1).start()

    def next_step(i, step):
        for way in range(2):
            turn = 1 if way == 0 else -1
            found = product(i, place.around(turn * (half - step + 1)))
            ring(i, step - 1, way).wait_recv()
            if step == 2:
                came = half_recv[i, way].astype(jnp.float32)
                low = found[:cut] + came if way == 0 else found[:cut]
                high = found[cut:] if way == 0 else found[cut:] + came
                full_send[i, 0, way, :cut] = low.astype(jnp.bfloat16)
                full_send[i, 0, way, cut:] = high.astype(jnp.bfloat16)
            else:
                came = full_recv[i, step - 3, way].astype(jnp.float32)
                full_send[i, step - 2, way] = (found + came).astype(jnp.bfloat16)
            ring(i, step, way).start()

    def plane(i):
        found = product(i, place.peer)
        for way in range(2):
            ring(i, half, way).wait_recv()
            found += full_recv[i, half - 2, way].astype(jnp.float32)
        for depth in range(depths):
            piece = found[depth * rows : (depth + 1) * rows]
            z_out[i, depth] = piece.astype(jnp.bfloat16)

            @pl.when(depth == place.depth)
            def _():
                own_part[i] = piece

        for step in range(1, depths):
            deep(i, step).start()

    def finish(i):
        array, _, start, out_rows = plan[i]
        found = own_part[i]
        for step in range(1, depths):
            deep(i, step).wait_recv()
            found += z_in[i, step - 1].astype(jnp.float32)
        outs[array][out_rows, pl.ds(start, WIDE)] = found

    if with_small:
        place.greet()
    else:
        place.greet_near()
    for k in reversed(range(2 * count)):
        for copy in swap(k):
            copy.start()
    if with_small:

        def send_small(step, carry):
            outer, peer = place.other(step)
            remote(
                small.at[outer * peers + peer],
                small_in.at[place.index],
                a_send,
                a_recv,
                (outer, peer),
            ).start()
            return carry

        lax.fori_loop(1, place.total, send_small, 0)
        own_small = pltpu.make_async_copy(small.at[place.index], small_in.at[place.index], a_own)
        own_small.start()
        spread = Spread(place, small_sum, small_all, b_send, b_recv, b_own)

    total = len(plan)
    ready = set()
    for tick in range(total + half + 1):
        if tick < total:
            array = plan[tick][0]
            if array not in ready:
                ready.add(array)
                for k in (2 * array + 1, 2 * array):
                    kept, sent = swap(k)
                    kept.wait()
                    sent.wait_recv()
            first(tick)
        for step in range(2, half + 1):
            if 0 <= tick - step + 1 < total:
                next_step(tick - step + 1, step)
        if 0 <= tick - half < total:
            plane(tick - half)
        if 0 <= tick - half - 1 < total:
            finish(tick - half - 1)
        if with_small and tick == 4:
            rest_in = small_in.at[pl.ds(0, place.total - 1)]
            both = remote(rest_in, rest_in, a_send, a_recv, place.other(1))
            both.wait_send()
            both.wait_recv()
            own_small.wait()
            small_sum[...] = jnp.sum(small_in[...], axis=0)
            spread.start()
    if with_small:
        spread.wait()
    for k in range(2 * count):
        swap(k)[1].wait_send()
    for i in range(total):
        for step in range(1, half + 1):
            for way in range(2):
                ring(i, step, way).wait_send()
        for step in range(1, depths):
            deep(i, step).wait_send()


def sum_all(pairs, shapes, depths, peers, call, small=None):
    half, count = peers // 2, len(pairs)
    tokens = pairs[0][0].shape[0]
    padded = -(-tokens // 128) * 128
    unit = min(shape[0] for shape in shapes)
    lefts, rights, plan = [], [], []
    for array, ((left, right), shape) in enumerate(zip(pairs, shapes)):
        parts = shape[0] // unit
        turned = jnp.pad(left, ((0, padded - tokens), (0, 0))).T
        turned = turned.reshape(depths, 2, peers, parts, unit, padded)
        lefts.append(
            turned.transpose(1, 3, 2, 0, 4, 5).reshape(2, parts, peers, depths * unit, padded)
        )
        rights.append(jnp.pad(right, ((0, padded - tokens), (0, 0))))
        for part in range(parts):
            for start in range(0, shape[1], WIDE):
                plan.append((array, part, start, pl.ds(part * unit, unit)))
    plan = plan[::-1]
    total, tall = len(plan), depths * unit
    dma = pltpu.SemaphoreType.DMA
    low = jnp.bfloat16
    scratch = [pltpu.VMEM((2,) + a.shape[1:], low) for a in lefts]
    scratch += [pltpu.VMEM((2,) + a.shape, low) for a in rights]
    scratch += [
        pltpu.VMEM((total, 2, tall // 2, WIDE), low),
        pltpu.VMEM((total, 2, tall // 2, WIDE), low),
        pltpu.VMEM((total, half - 1, 2, tall, WIDE), low),
        pltpu.VMEM((total, half - 1, 2, tall, WIDE), low),
        pltpu.VMEM((total, depths, unit, WIDE), low),
        pltpu.VMEM((total, depths - 1, unit, WIDE), low),
        pltpu.VMEM((total, unit, WIDE), jnp.float32),
        dma((2 * count,)),
        dma((2 * count,)),
        dma((2 * count,)),
        dma((total, half, 2)),
        dma((total, half, 2)),
        dma((total, depths - 1)),
        dma((total, depths - 1)),
    ]
    args = [*lefts, *rights]
    in_specs = [ANY] * (2 * count)
    out_shape = [jax.ShapeDtypeStruct(shape, jnp.float32) for shape in shapes]
    out_specs = [VMEM] * count
    if small is not None:
        args.append(small)
        in_specs.append(ANY)
        out_shape.append(jax.ShapeDtypeStruct(small.shape, jnp.float32))
        out_specs.append(VMEM)
        scratch += [
            pltpu.VMEM(small.shape, jnp.float32),
            pltpu.VMEM(small.shape[1:], jnp.float32),
        ] + [dma(())] * 6
    return pl.pallas_call(
        functools.partial(sum_kernel, plan, depths, peers, count, small is not None),
        out_shape=out_shape,
        in_specs=in_specs,
        out_specs=out_specs,
        scratch_shapes=scratch,
        compiler_params=pltpu.CompilerParams(
            collective_id=call, has_side_effects=True, vmem_limit_bytes=60 * 2**20
        ),
    )(*args)


def attention_scores(qkv_parts, position_bias, mask_add):
    head_scale = qkv_parts.shape[-1] ** (-0.5)
    scores = (
        jnp.einsum(
            "wqhd,wkhd->whqk",
            qkv_parts[:, :, 0],
            qkv_parts[:, :, 1],
            preferred_element_type=jnp.float32,
        )
        * head_scale
        + position_bias[None]
    )
    if mask_add is not None:
        scores = scores + mask_add
    return scores


def block_forward(inputs, weights, position_bias, mask_add, windows):
    norm_gains, norm_shifts, w_qkv, qv_bias, w_proj, b_proj, w_up, b_up, w_down, b_down = weights
    model_width = inputs.shape[1]
    norm_gains = norm_gains.astype(jnp.float32)
    norm_shifts = norm_shifts.astype(jnp.float32)
    normed, normal_one, inverse_one = layer_norm(inputs, norm_gains[0], norm_shifts[0])
    normed_low = normed.astype(jnp.bfloat16)
    qv_float = qv_bias.astype(jnp.float32)
    bias_full = jnp.concatenate(
        [qv_float[:model_width], jnp.zeros((model_width,), jnp.float32), qv_float[model_width:]]
    )
    qkv_low = (jnp.dot(normed_low, w_qkv, preferred_element_type=jnp.float32) + bias_full).astype(
        jnp.bfloat16
    )
    qkv_parts = qkv_low.reshape(windows, WIN, 3, HEADS, -1)
    scores = attention_scores(qkv_parts, position_bias, mask_add)
    row_max = jnp.max(scores, axis=-1, keepdims=True)
    shifted_exp = jnp.exp(scores - row_max)
    row_total = jnp.sum(shifted_exp, axis=-1, keepdims=True)
    soft_low = (shifted_exp / row_total).astype(jnp.bfloat16)
    log_total = row_max + jnp.log(row_total)
    attended = jnp.einsum(
        "whqk,wkhd->wqhd", soft_low, qkv_parts[:, :, 2], preferred_element_type=jnp.float32
    )
    attended_low = attended.reshape(inputs.shape).astype(jnp.bfloat16)
    middle = inputs + (
        jnp.dot(attended_low, w_proj, preferred_element_type=jnp.float32)
        + b_proj.astype(jnp.float32)
    )
    normed_two, normal_two, inverse_two = layer_norm(middle, norm_gains[1], norm_shifts[1])
    normed_two_low = normed_two.astype(jnp.bfloat16)
    hidden = jnp.dot(normed_two_low, w_up, preferred_element_type=jnp.float32) + b_up.astype(
        jnp.float32
    )
    activated_low = gelu_exact(hidden).astype(jnp.bfloat16)
    output = middle + (
        jnp.dot(activated_low, w_down, preferred_element_type=jnp.float32)
        + b_down.astype(jnp.float32)
    )
    kept_state = (
        normal_one,
        inverse_one,
        normed_low,
        qkv_low,
        log_total,
        attended_low,
        normal_two,
        inverse_two,
        normed_two_low,
        hidden,
        activated_low,
    )
    return (output, kept_state)


def block_backward(grad_out, weights, kept_state, position_bias, mask_add, bucket_table, windows):
    norm_gains, norm_shifts, w_qkv, qv_bias, w_proj, b_proj, w_up, b_up, w_down, b_down = weights
    (
        normal_one,
        inverse_one,
        normed_low,
        qkv_low,
        log_total,
        attended_low,
        normal_two,
        inverse_two,
        normed_two_low,
        hidden,
        activated_low,
    ) = kept_state
    model_width = grad_out.shape[1]
    norm_gains = norm_gains.astype(jnp.float32)
    grad_down_low = grad_out.astype(jnp.bfloat16)
    down_bias_grad = jnp.sum(grad_down_low, axis=0, dtype=jnp.float32)
    grad_act = jnp.einsum("rd,fd->rf", grad_down_low, w_down, preferred_element_type=jnp.float32)
    gelu_back = jax.vjp(gelu_exact, hidden)[1]
    grad_hidden_low = gelu_back(grad_act)[0].astype(jnp.bfloat16)
    up_bias_grad = jnp.sum(grad_hidden_low, axis=0, dtype=jnp.float32)
    grad_normed_two = jnp.einsum(
        "rf,df->rd", grad_hidden_low, w_up, preferred_element_type=jnp.float32
    )
    grad_mid_norm, gain_two_grad, shift_two_grad = norm_back(
        grad_normed_two, normal_two, inverse_two, norm_gains[1]
    )
    grad_middle = grad_out + grad_mid_norm
    grad_branch_low = grad_middle.astype(jnp.bfloat16)
    proj_bias_grad = jnp.sum(grad_branch_low, axis=0, dtype=jnp.float32)
    grad_attended_low = jnp.einsum(
        "rd,cd->rc", grad_branch_low, w_proj, preferred_element_type=jnp.float32
    ).astype(jnp.bfloat16)
    qkv_parts = qkv_low.reshape(windows, WIN, 3, HEADS, -1)
    scores = attention_scores(qkv_parts, position_bias, mask_add)
    soft = jnp.exp(scores - log_total)
    soft_low = soft.astype(jnp.bfloat16)
    grad_heads = grad_attended_low.reshape(windows, WIN, HEADS, -1)
    grad_value = jnp.einsum(
        "whqk,wqhd->wkhd", soft_low, grad_heads, preferred_element_type=jnp.float32
    )
    grad_soft = jnp.einsum(
        "wqhd,wkhd->whqk", grad_heads, qkv_parts[:, :, 2], preferred_element_type=jnp.float32
    )
    grad_scores_low = (
        soft * (grad_soft - jnp.sum(soft * grad_soft, axis=-1, keepdims=True))
    ).astype(jnp.bfloat16)
    head_scale = qkv_parts.shape[-1] ** (-0.5)
    grad_query = (
        jnp.einsum(
            "whqk,wkhd->wqhd",
            grad_scores_low,
            qkv_parts[:, :, 1],
            preferred_element_type=jnp.float32,
        )
        * head_scale
    )
    grad_key = (
        jnp.einsum(
            "whqk,wqhd->wkhd",
            grad_scores_low,
            qkv_parts[:, :, 0],
            preferred_element_type=jnp.float32,
        )
        * head_scale
    )
    score_sum = jnp.sum(grad_scores_low, axis=0, dtype=jnp.float32).reshape(HEADS, -1)
    table_grad = jnp.einsum("hn,nb->bh", score_sum, bucket_table, precision=lax.Precision.HIGHEST)
    grad_qkv_low = (
        jnp.stack([grad_query, grad_key, grad_value], axis=2)
        .reshape(qkv_low.shape)
        .astype(jnp.bfloat16)
    )
    column_sums = jnp.sum(grad_qkv_low, axis=0, dtype=jnp.float32)
    qv_grad = jnp.concatenate([column_sums[:model_width], column_sums[2 * model_width :]])
    grad_normed = jnp.einsum("re,de->rd", grad_qkv_low, w_qkv, preferred_element_type=jnp.float32)
    grad_in_norm, gain_one_grad, shift_one_grad = norm_back(
        grad_normed, normal_one, inverse_one, norm_gains[0]
    )
    grad_input = grad_middle + grad_in_norm
    grads = (
        jnp.stack([gain_one_grad, gain_two_grad]),
        jnp.stack([shift_one_grad, shift_two_grad]),
        qv_grad,
        proj_bias_grad,
        up_bias_grad,
        down_bias_grad,
    )
    pairs = (
        (normed_low, grad_qkv_low),
        (attended_low, grad_branch_low),
        (normed_two_low, grad_hidden_low),
        (activated_low, grad_down_low),
    )
    return (grad_input, grads, table_grad, pairs)


def shards(
    outer_count,
    peer_count,
    patches,
    out_grad,
    norm_gain,
    norm_shift,
    qkv_weight,
    qv_bias,
    rel_table,
    proj_weight,
    proj_bias,
    up_weight,
    up_bias,
    down_weight,
    down_bias,
    tile_perm,
    window_slot,
    mask_ids,
    bias_index,
):
    windows = patches.shape[0] // WIN
    model_width = patches.shape[1]
    depths = outer_count // 2
    devices = outer_count * peer_count
    capacity = (windows + peer_count - 1) // peer_count
    device_index = lax.axis_index(("dp", "fsdp"))
    total_windows = tile_perm.shape[0]
    slot_ids = jnp.arange(total_windows, dtype=jnp.int32)

    def one_hot_pick(keys, values):
        return jnp.sum(jnp.where(keys[None, :] == slot_ids[:, None], values[None, :], 0), axis=1)

    def look_up(values, at):
        hit = at[:, None] == jnp.arange(values.shape[0], dtype=jnp.int32)[None, :]
        return jnp.sum(jnp.where(hit, values[None, :], 0), axis=1)

    source_of = one_hot_pick(window_slot, look_up(window_slot, tile_perm))
    target_of = one_hot_pick(source_of, slot_ids)
    region_slot = one_hot_pick(window_slot, mask_ids)
    own_slots = device_index * windows + jnp.arange(windows, dtype=jnp.int32)

    def rank_of(slots, device_of):
        grid_view = device_of.reshape(-1, windows)
        earlier = jnp.arange(windows)[None, :] < jnp.arange(windows)[:, None]
        same_peer = grid_view[:, :, None] == grid_view[:, None, :]
        ranks = jnp.sum(same_peer & earlier[None], axis=2).reshape(-1)
        return look_up(ranks, slots)

    def peer_of(slots):
        return slots // windows % peer_count

    own_source = look_up(source_of, own_slots)
    own_target = look_up(target_of, own_slots)
    forward_send = peer_of(own_target) * capacity + rank_of(own_slots, target_of // windows)
    forward_take = peer_of(own_source) * capacity + rank_of(own_source, target_of // windows)
    backward_send = peer_of(own_source) * capacity + rank_of(own_slots, source_of // windows)
    backward_take = peer_of(own_target) * capacity + rank_of(own_target, source_of // windows)
    mask_add = region_mask(look_up(region_slot, own_slots))
    bucket_table = (
        bias_index.reshape(-1)[:, None] == jnp.arange(rel_table.shape[1], dtype=jnp.int32)[None, :]
    ).astype(jnp.float32)
    tables = rel_table.astype(jnp.float32)
    bias_one = jnp.einsum(
        "nb,bh->hn", bucket_table, tables[0], precision=lax.Precision.HIGHEST
    ).reshape(HEADS, WIN, WIN)
    bias_two = jnp.einsum(
        "nb,bh->hn", bucket_table, tables[1], precision=lax.Precision.HIGHEST
    ).reshape(HEADS, WIN, WIN)

    def choose(rows, at, count):
        spots = jnp.arange(count, dtype=jnp.int32)
        hit = spots[:, None] == at[None, :]
        return sum(
            jnp.where(hit[:, w][:, None, None], rows[w][None], jnp.zeros((), rows.dtype))
            for w in range(rows.shape[0])
        )

    def take(rows, at):
        hit = at[:, None] == jnp.arange(rows.shape[0], dtype=jnp.int32)[None, :]
        return sum(
            jnp.where(hit[:, w][:, None, None], rows[w][None], jnp.zeros((), rows.dtype))
            for w in range(rows.shape[0])
        )

    def move(rows_low, send, fetch):
        parts = rows_low.reshape(windows, WIN, model_width)
        sectioning = choose(parts, send, peer_count * capacity)
        arrived = lax.all_to_all(sectioning, "fsdp", split_axis=0, concat_axis=0, tiled=True)
        return take(arrived, fetch).reshape(rows_low.shape)

    def to_shifted(rows_low):
        return move(rows_low, forward_send, forward_take)

    def from_shifted(rows_low):
        return move(rows_low, backward_send, backward_take)

    vectors = (norm_gain, norm_shift, qv_bias, proj_bias, up_bias, down_bias)
    flat = jnp.concatenate([v.reshape(-1) for v in vectors])
    small = jnp.pad(flat, (0, -flat.shape[0] % 2048)).reshape(-1, 128)
    matrices = (qkv_weight, proj_weight, up_weight, down_weight)
    *fulls, small_full = gather_all(matrices, small, depths, peer_count)
    small_full = small_full.reshape(devices, -1)
    whole, offset = [], 0
    for v in vectors:
        size = v.size
        piece = small_full[:, offset : offset + size].reshape((devices,) + v.shape)
        offset += size
        piece = jnp.moveaxis(piece, 0, -2)
        whole.append(piece.reshape(v.shape[:-1] + (-1,)))

    def weights_of(layer):
        gains, shifts, qv, proj_b, up_b, down_b = [v[layer] for v in whole]
        w_qkv, w_proj, w_up, w_down = [
            fulls[4 * layer + k].reshape(-1, matrices[k].shape[-1]) for k in range(4)
        ]
        return (gains, shifts, w_qkv, qv, w_proj, proj_b, w_up, up_b, w_down, down_b)

    first_weights, second_weights = weights_of(0), weights_of(1)
    grad_two = to_shifted(out_grad)
    output_one, state_one = block_forward(
        patches.astype(jnp.float32), first_weights, bias_one, None, windows
    )
    second_input = to_shifted(output_one.astype(jnp.bfloat16))
    output_two, state_two = block_forward(
        second_input.astype(jnp.float32), second_weights, bias_two, mask_add, windows
    )
    block_out = from_shifted(output_two.astype(jnp.bfloat16))
    shapes = [m.shape[1:] for m in matrices]
    grad_input_two, grads_two, table_two, pairs_two = block_backward(
        grad_two.astype(jnp.float32), second_weights, state_two, bias_two, mask_add, bucket_table, windows
    )
    sums_two = sum_all(pairs_two, shapes, depths, peer_count, 1)
    grad_one = from_shifted(grad_input_two.astype(jnp.bfloat16))
    grad_patches, grads_one, table_one, pairs_one = block_backward(
        grad_one.astype(jnp.float32), first_weights, state_one, bias_one, None, bucket_table, windows
    )
    small_grads = []
    for one, two, v in zip(grads_one, grads_two, vectors):
        both = jnp.stack([one, two]).reshape(v.shape[:-1] + (devices, v.shape[-1]))
        small_grads.append(jnp.moveaxis(both, -2, 0).reshape(devices, -1))
    table = jnp.stack([table_one, table_two]).reshape(-1)
    table = jnp.pad(table, (0, -table.shape[0] % devices)).reshape(devices, -1)
    packed = jnp.concatenate(small_grads + [table], axis=1)
    width = packed.shape[1]
    packed = jnp.pad(packed, ((0, 0), (0, -width % 1024))).reshape(devices, -1, 128)
    *sums_one, small_all = sum_all(pairs_one, shapes, depths, peer_count, 2, packed)
    small_all = small_all.reshape(devices, -1)
    mine = lax.dynamic_index_in_dim(small_all, device_index, 0, keepdims=False)
    vector_grads, offset = [], 0
    for v in vectors:
        vector_grads.append(mine[offset : offset + v.size].reshape(v.shape))
        offset += v.size
    table_total = small_all[:, offset:width].reshape(-1)[: rel_table.size].reshape(rel_table.shape)
    grad_qkv, grad_proj, grad_up, grad_down = [
        jnp.stack([one, two]) for one, two in zip(sums_one, sums_two)
    ]
    return (
        block_out,
        grad_patches,
        vector_grads[0],
        vector_grads[1],
        grad_qkv,
        vector_grads[2],
        table_total,
        grad_proj,
        vector_grads[3],
        grad_up,
        vector_grads[4],
        grad_down,
        vector_grads[5],
    )


ROWS = 112
GAP = 2
AHEAD = 4
F_BUDGET, B_BUDGET = 5.0, 5.0
KEYS = 128
GROUP = 4
SCALE = 32**-0.5
LOW = jnp.bfloat16
WHOLE = jnp.float32
NEVER = -1e30


def names(words, refs):
    return types.SimpleNamespace(**dict(zip(words, refs, strict=True)))


class Queue:
    def __init__(self, budget):
        self.pieces, self.budget = [], budget

    def add(self, tick, cost, work, *arguments):
        self.pieces.append((tick, cost, work, arguments))

    def run(self, tick, after, all_of_it=False):
        left = self.budget
        while self.pieces and self.pieces[0][0] <= tick and (left > 0 or all_of_it):
            left -= self.step(after)

    def step(self, after):
        _, cost, work, arguments = self.pieces.pop(0)
        work(*arguments)
        after()
        return cost


def row_loop(count, size, body):
    def step(i, carry):
        body(pl.multiple_of(i * size, size))
        return carry

    lax.fori_loop(0, count // size, step, 0)


def lane_mask(rows, head):
    lane = lax.broadcasted_iota(jnp.int32, (rows, 128), 1)
    return lane // 32 == head


def per_head(value):
    tall = jnp.concatenate([value, jnp.zeros((KEYS - ROWS, 128), value.dtype)], axis=0)
    zero = jnp.zeros((), value.dtype)
    return jnp.concatenate(
        [jnp.where(lane_mask(KEYS, head), tall, zero) for head in range(GROUP)], axis=0
    )


def dot(a, b, over=(1, 0)):
    return lax.dot_general(
        a, b, (((over[0],), (over[1],)), ((), ())), preferred_element_type=jnp.float32
    )


def normal_parts(block):
    mean = jnp.mean(block, axis=1, keepdims=True)
    centered = block - mean
    inverse = lax.rsqrt(jnp.mean(centered * centered, axis=1, keepdims=True) + epsilon)
    return centered * inverse, inverse


class Exchange:
    def __init__(self, place, out, into, send, receive, parts):
        self.place, self.out, self.into = place, out, into
        self.send, self.receive = send, receive
        self.width = out.shape[-1] // parts

    def columns(self, part):
        return slice(part * self.width, (part + 1) * self.width)

    def copy(self, part, step):
        place = self.place
        peer = lax.rem(place.peer + step, place.peers)
        return remote(
            self.out.at[peer, :, self.columns(part)],
            self.into.at[place.peer, :, self.columns(part)],
            self.send.at[part, step - 1],
            self.receive.at[part, step - 1],
            (place.depth * 2 + place.core, peer),
        )

    def give(self, part, tiles, chosen):
        columns = self.columns(part)
        for peer in range(self.place.peers):
            self.out[peer, :, columns] = tiles[chosen[peer], :, columns]
        self.into[self.place.peer, :, columns] = self.out[self.place.peer, :, columns]
        for step in range(1, self.place.peers):
            self.copy(part, step).start()

    def await_part(self, part):
        for step in range(1, self.place.peers):
            self.copy(part, step).wait_recv()

    def finish(self, parts):
        for part in range(parts):
            for step in range(1, self.place.peers):
                self.copy(part, step).wait_send()


class Gather:
    def __init__(self, place, chunks, blocks, fulls, sems):
        self.place, self.chunks, self.blocks, self.fulls = place, chunks, blocks, fulls
        (self.z_send, self.z_recv, self.r_send, self.r_recv, self.c_send, self.c_recv, self.own_sem) = sems
        self.half, self.cut = place.half, place.depths // 2

    def view(self, i, depth, peer):
        array, layer, columns = self.chunks[i]
        return self.fulls[layer * len(self.blocks) + array].at[
            depth, self.place.core, peer, :, columns
        ]

    def block(self, i):
        array, layer, columns = self.chunks[i]
        return self.blocks[array].at[layer, :, columns]

    def own(self, i):
        place = self.place
        return pltpu.make_async_copy(
            self.block(i), self.view(i, place.depth, place.peer), self.own_sem.at[i]
        )

    def deep(self, i, step):
        place = self.place
        return remote(
            self.block(i),
            self.view(i, place.depth, place.peer),
            self.z_send.at[i, step - 1],
            self.z_recv.at[i, step - 1],
            place.deep(step),
        )

    def part(self, step, way):
        if step < self.half:
            return slice(None)
        return slice(0, self.cut) if way == 0 else slice(self.cut, self.place.depths)

    def ring(self, i, step, way):
        turn = 1 if way == 0 else -1
        here = self.view(i, self.part(step, way), self.place.around(-turn * (step - 1)))
        return remote(
            here,
            here,
            self.r_send.at[i, step - 1, way],
            self.r_recv.at[i, step - 1, way],
            self.place.neighbour(turn),
        )

    def across(self, i, slot):
        step = (slot + 1) // 2
        turn = 1 if slot % 2 else -1
        here = self.view(i, slice(None), self.place.around(-turn * step))
        return remote(
            here, here, self.c_send.at[i, slot], self.c_recv.at[i, slot], self.place.sibling()
        )

    def begin(self, i):
        for step in range(1, self.place.depths):
            self.deep(i, step).start()
        self.own(i).start()

    def first(self, i):
        self.own(i).wait()
        for step in range(1, self.place.depths):
            self.deep(i, step).wait_recv()
        self.ring(i, 1, 0).start()
        self.ring(i, 1, 1).start()
        self.across(i, 0).start()

    def later(self, i, step):
        self.ring(i, step, 0).wait_recv()
        self.ring(i, step, 1).wait_recv()
        if step < self.half:
            self.ring(i, step + 1, 0).start()
            self.ring(i, step + 1, 1).start()
            self.across(i, 2 * step - 1).start()
            self.across(i, 2 * step).start()
        else:
            self.across(i, 2 * step - 1).start()

    def tick(self, tick):
        total = len(self.chunks)
        if tick + AHEAD < total:
            self.begin(tick + AHEAD)
        if tick < total:
            self.first(tick)
        for step in range(1, self.half + 1):
            if 0 <= tick - step * GAP < total:
                self.later(tick - step * GAP, step)

    def await_across(self, i):
        for slot in range(2 * self.half):
            self.across(i, slot).wait_recv()

    def finish(self):
        for i in range(len(self.chunks)):
            for slot in range(2 * self.half):
                self.across(i, slot).wait_send()
            for step in range(1, self.place.depths):
                self.deep(i, step).wait_send()
            for step in range(1, self.half + 1):
                for way in range(2):
                    self.ring(i, step, way).wait_send()


F_IN = (
    "w0", "w1", "w2", "w3", "small", "x0", "grads", "tables", "index", "mask", "forward_send", "forward_take",
    "backward_send", "backward_take",
)
F_OUT = (
    "f0", "f1", "f2", "f3", "f4", "f5", "f6", "f7", "moved_grad", "result", "left0", "left1", "left2",
    "left3", "low_x", "middle", "qkv", "probs", "slope", "vec32",
)
F_SCRATCH = (
    "small_full", "bias", "x", "x0w", "normed", "att", "normed_two", "act", "mid", "q_s", "p_s", "slope_s", "wide_a",
    "wide_b", "total", "sib_a", "sib_b", "turned", "left_a", "left_b", "g_out", "g_in", "x_out", "x_in",
    "y_out", "y_in", "vec64", "vec128", "z_send", "z_recv", "r_send", "r_recv", "c_send", "c_recv", "own_sem",
    "s_send", "s_recv", "s_own", "load", "save", "swap_send", "swap_recv", "eg_send", "eg_recv", "ex_send",
    "ex_recv", "ey_send", "ey_recv",
)


def forward_kernel(chunks, depths, peers, *refs):
    r = names(F_IN + F_OUT + F_SCRATCH, refs)
    place = Place(depths, peers)
    gather = Gather(
        place,
        chunks,
        (r.w0, r.w1, r.w2, r.w3),
        (r.f0, r.f1, r.f2, r.f3, r.f4, r.f5, r.f6, r.f7),
        (r.z_send, r.z_recv, r.r_send, r.r_recv, r.c_send, r.c_recv, r.own_sem),
    )
    spread = Spread(place, r.small, r.small_full, r.s_send, r.s_recv, r.s_own)
    eg = Exchange(place, r.g_out, r.g_in, r.eg_send, r.eg_recv, 1)
    ex = Exchange(place, r.x_out, r.x_in, r.ex_send, r.ex_recv, 4)
    ey = Exchange(place, r.y_out, r.y_in, r.ey_send, r.ey_recv, 4)
    windows = 2
    tall = windows * ROWS
    per_layer = len(chunks) // 2
    total = len(chunks)
    queue = Queue(F_BUDGET)
    saved, loaded, used = [], [], set()

    def spill(source, target):
        copy = pltpu.make_async_copy(source, target, r.save.at[len(saved)])
        copy.start()
        saved.append(copy)

    def staged(i):
        array, layer, columns = chunks[i]
        count = sum(1 for c in chunks[:i] if (c[0] == 3) == (array == 3))
        return (r.wide_b if array == 3 else r.wide_a).at[count % 2]

    def load(i):
        array, layer, columns = chunks[i]
        source = gather.fulls[layer * 4 + array].at[:, :, :, :, columns]
        return pltpu.make_async_copy(source, staged(i), r.load.at[i])

    def weight(i):
        assert i in loaded
        used.add(i)
        load(i).wait()
        value = staged(i)[...]
        return value.reshape(-1, value.shape[-1])

    def fetch(i):
        gather.await_across(i)
        load(i).start()

    def unpack():
        spread.wait()
        count = place.total
        row = lax.broadcasted_iota(jnp.int32, (count, 128), 0)
        lane = lax.broadcasted_iota(jnp.int32, (count, 128), 1)

        def spread_lanes(line, member, size):
            each = 128 // size
            found = jnp.zeros((count, 128), WHOLE)
            for turn in range(each):
                spot = (member + turn) % each
                rolled = line if turn == 0 else pltpu.roll(line, turn * size, 1)
                found += jnp.where((lane // size == spot) & (row % each == spot), rolled, 0.0)
            blocks = [
                jnp.sum(found[each * b : each * (b + 1)], axis=0, keepdims=True)
                for b in range(count // each)
            ]
            return jnp.concatenate(blocks, axis=1)

        for k in range(3):
            line = r.small_full[:, k, :].astype(WHOLE)
            for member in range(4):
                r.vec32[4 * k + member : 4 * k + member + 1, :] = spread_lanes(line, member, 32)
        line = r.small_full[:, 3, :].astype(WHOLE)
        for member in range(2):
            r.vec64[member : member + 1, :] = spread_lanes(line, member, 64)
        for member in range(2):
            line = r.small_full[:, 4 + member, :].astype(WHOLE)
            r.vec128[member : member + 1, :] = jnp.concatenate(
                [line[d : d + 1] for d in range(count)], axis=1
            )

    def bias_rows(start, stop):
        buckets = lax.broadcasted_iota(jnp.int32, (384, KEYS), 0)

        def step(i, carry):
            rows = pl.ds(pl.multiple_of(i * 8, 8), 8)
            lines = r.index[rows, :]
            found = []
            for row in range(8):
                hot = jnp.where(buckets == lines[row : row + 1], 1.0, 0.0).astype(LOW)
                found.append(dot(r.tables[...], hot))
            for k in range(2 * HEADS):
                layer, head, g = k // HEADS, k // 8 % GROUP, k % 8
                block = jnp.concatenate([one[k : k + 1] for one in found], axis=0)
                r.bias[layer, g, rows, head * KEYS : (head + 1) * KEYS] = block
            return carry

        lax.fori_loop(start, stop, step, 0)

    def vec(k):
        return r.vec32[k : k + 1, :]

    def norm(source, target, layer, k):
        gain, shift = vec(2 * layer + k), vec(4 + 2 * layer + k)

        def body(start):
            rows = pl.ds(start, 32)
            parts, _ = normal_parts(source[rows, :].astype(WHOLE))
            target[rows, :] = (parts * gain + shift).astype(LOW)

        row_loop(tall, 32, body)

    def enter(layer):
        x = r.x.at[layer]
        if layer == 0:
            x[...] = r.x0[...]
        else:
            for part in range(4):
                ex.await_part(part)
            for w in range(windows):
                x[w * ROWS : (w + 1) * ROWS, :] = r.x_in[r.forward_take[w]]
        spill(x, r.low_x.at[layer])
        norm(x, r.normed.at[layer], layer, 0)
        swap(layer, 0).start()

    def project(layer, i):
        part = i % per_layer
        found = dot(r.normed[layer], weight(i))
        if part != 1:
            half = part // 2
            found = found + r.vec64[layer : layer + 1, half * 1024 : (half + 1) * 1024]
        r.q_s[layer, :, part * 1024 : (part + 1) * 1024] = found.astype(LOW)

    def attend(layer, w):
        def step(g, carry):
            rows = slice(w * ROWS, (w + 1) * ROWS)
            start = pl.multiple_of(g * 128, 128)
            q = r.q_s[layer, rows, pl.ds(start, 128)]
            k = r.q_s[layer, rows, pl.ds(start + 1024, 128)]
            v = r.q_s[layer, rows, pl.ds(start + 2048, 128)]
            scores = dot(q, per_head(k), (1, 1)) * SCALE + r.bias[layer, g]
            heads = []
            for head in range(GROUP):
                one = scores[:, head * KEYS : (head + 1) * KEYS]
                if layer == 1:
                    one = one + r.mask[w]
                shifted = jnp.exp(one - jnp.max(one, axis=1, keepdims=True))
                heads.append(
                    (shifted * (1.0 / jnp.sum(shifted, axis=1, keepdims=True))).astype(LOW)
                )
            found = jnp.concatenate(heads, axis=1)
            r.p_s[layer, w * 8 + g] = found
            r.att[layer, rows, pl.ds(start, 128)] = dot(found, per_head(v)).astype(LOW)
            return carry

        lax.fori_loop(0, 8, step, 0)

    def branch(layer, i):
        spill(r.q_s.at[layer], r.qkv.at[layer])
        spill(r.p_s.at[layer], r.probs.at[layer])
        swap(layer, 1).start()
        found = dot(r.att[layer], weight(i)) + vec(8 + layer)
        r.mid[layer] = r.x[layer].astype(WHOLE) + found
        spill(r.mid.at[layer], r.middle.at[layer])

    def second_norm(layer):
        norm(r.mid.at[layer], r.normed_two.at[layer], layer, 1)
        swap(layer, 2).start()

    def widen(layer, i):
        part = i % per_layer - 4
        columns = slice(part * 1024, (part + 1) * 1024)
        r.total[...] = dot(r.normed_two[layer], weight(i)) + r.vec128[layer : layer + 1, columns]

        def body(start):
            rows = pl.ds(start, 16)
            v = r.total[rows, :]
            spread_half = 0.5 * (1.0 + lax.erf(v * (2.0**-0.5)))
            density = jnp.exp(-0.5 * v * v) * 0.3989422804014327
            r.act[layer, rows, columns] = (v * spread_half).astype(LOW)
            r.slope_s[layer, rows, columns] = (spread_half + v * density).astype(LOW)

        row_loop(tall, 16, body)
        if part == 3:
            spill(r.slope_s.at[layer], r.slope.at[layer])
            swap(layer, 3).start()

    def narrow(layer, i):
        part = i % per_layer - 8
        columns = slice(part * 256, (part + 1) * 256)
        found = dot(r.act[layer], weight(i)) + vec(10 + layer)[:, columns]
        found = (r.mid[layer, :, columns] + found).astype(LOW)
        for w in range(windows):
            r.x0w[w, :, columns] = found[w * ROWS : (w + 1) * ROWS]
        if layer == 0:
            ex.give(part, r.x0w, r.forward_send)
        else:
            ey.give(part, r.x0w, r.backward_send)

    sources = (r.normed, r.att, r.normed_two, r.act)

    def swap(layer, array):
        target = (r.sib_b if array == 3 else r.sib_a.at[array]).at[layer]
        return remote(
            sources[array].at[layer],
            target,
            r.swap_send.at[layer, array],
            r.swap_recv.at[layer, array],
            place.sibling(),
        )

    def turn(layer, array):
        swap(layer, array).wait_recv()
        mine = sources[array].at[layer]
        theirs = (r.sib_b if array == 3 else r.sib_a.at[array]).at[layer]
        unit = r.left0.shape[-2] // depths
        pad = jnp.zeros((256 - tall, 128), WHOLE)
        rounds = peers if array == 3 else 1
        for f in range(rounds):
            for depth in range(depths):
                start = (depth * 2 + place.core) * rounds * 128 + f * 128
                columns = pl.ds(pl.multiple_of(start, 128), 128)
                for side, ref in enumerate((mine, theirs)):
                    block = jnp.concatenate([ref[:, columns].astype(WHOLE), pad], axis=0)
                    r.turned[depth, :, side * 256 : (side + 1) * 256] = block.T
            for part in range(4):
                found = jnp.concatenate(
                    [r.turned[depth, part * unit : (part + 1) * unit] for depth in range(depths)],
                    axis=0,
                ).astype(LOW)
                if array == 3:
                    r.left_b[layer, part, f] = found
                else:
                    r.left_a[layer, array, part] = found
        if array == 3:
            spill(r.left_b.at[layer], r.left3.at[layer])
        else:
            spill(r.left_a.at[layer, array], (r.left0, r.left1, r.left2)[array].at[layer])

    place.greet()
    gather.begin(0)
    spread.start()
    eg.give(0, r.grads, r.forward_send)
    for i in range(1, AHEAD):
        gather.begin(i)

    whole_at = GAP * place.half + 1
    lag = whole_at + 1
    queue.add(0, 5, bias_rows, 0, 7)
    queue.add(0, 5, bias_rows, 7, ROWS // 8)
    queue.add(2, 1, unpack)
    for layer in range(2):
        base = layer * per_layer
        late = base + lag
        queue.add(2 if layer == 0 else late + 1, 2, enter, layer)
        for part in range(3):
            queue.add(late + part, 1.5, project, layer, base + part)
        for w in range(windows):
            queue.add(late + 2, 5, attend, layer, w)
        queue.add(late + 3, 1.5, branch, layer, base + 3)
        queue.add(late + 3, 1.5, second_norm, layer)
        for part in range(4):
            queue.add(late + 4 + part, 3.5, widen, layer, base + 4 + part)
            if part < 3:
                queue.add(late + 4 + part, 1, turn, layer, part)
        for part in range(4):
            queue.add(late + 8 + part, 1.5, narrow, layer, base + 8 + part)
        queue.add(late + 12, 4, turn, layer, 3)

    last = total - 1 + lag
    state = types.SimpleNamespace(tick=0)

    def pump():
        while len(loaded) < total and len(loaded) <= state.tick - whole_at:
            i = len(loaded)
            same = [j for j in range(i) if (chunks[j][0] == 3) == (chunks[i][0] == 3)]
            if len(same) > 1 and same[-2] not in used:
                break
            fetch(i)
            loaded.append(i)

    for tick in range(last + 1):
        state.tick = tick
        gather.tick(tick)
        pump()
        queue.run(tick, pump)
        if tick == 3:
            eg.await_part(0)
            for w in range(windows):
                r.moved_grad[w] = r.g_in[r.forward_take[w]]
    queue.run(last + total, pump, True)
    for part in range(4):
        ey.await_part(part)
    for w in range(windows):
        r.result[w] = r.y_in[r.backward_take[w]]
    eg.finish(1)
    ex.finish(4)
    ey.finish(4)
    gather.finish()
    for layer in range(2):
        for array in range(4):
            swap(layer, array).wait_send()
    for copy in saved:
        copy.wait()


def forward_all(blocks, small, x0, grads, tables, index, mask, moves, depths, peers):
    count = depths * 2 * peers
    width = x0.shape[-1]
    hidden = blocks[2].shape[-1]
    tall = x0.shape[0]
    half = peers // 2
    chunks = []
    for layer in range(2):
        for array, block in enumerate(blocks):
            size = 256 if array == 3 else 1024
            for start in range(0, block.shape[-1], size):
                chunks.append((array, layer, slice(start, start + size)))
    total = len(chunks)
    unit = blocks[0].shape[1]
    dma = pltpu.SemaphoreType.DMA
    vmem = pltpu.VMEM
    smem = pl.BlockSpec(memory_space=pltpu.SMEM)
    shape = jax.ShapeDtypeStruct
    tiles = (2, ROWS, width)
    left = (2, peers, depths * unit, 512)
    outs = [shape((depths, 2, peers) + b.shape[1:], LOW) for _ in range(2) for b in blocks]
    outs += [shape(tiles, LOW), shape(tiles, LOW)]
    outs += [shape(left, LOW)] * 3 + [shape((2, 4) + left[1:], LOW)]
    outs += [
        shape((2, tall, width), LOW),
        shape((2, tall, width), WHOLE),
        shape((2, tall, 3 * width), LOW),
        shape((2, 16, ROWS, GROUP * KEYS), LOW),
        shape((2, tall, hidden), LOW),
        shape((12, width), WHOLE),
    ]
    exchange = (peers,) + tiles[1:]
    scratch = [
        vmem((count,) + small.shape, WHOLE),
        vmem((2, 8, ROWS, GROUP * KEYS), WHOLE),
        vmem((2, tall, width), LOW),
        vmem(tiles, LOW),
        vmem((2, tall, width), LOW),
        vmem((2, tall, width), LOW),
        vmem((2, tall, width), LOW),
        vmem((2, tall, hidden), LOW),
        vmem((2, tall, width), WHOLE),
        vmem((2, tall, 3 * width), LOW),
        vmem((2, 16, ROWS, GROUP * KEYS), LOW),
        vmem((2, tall, hidden), LOW),
        vmem((2, depths, 2, peers, unit, 1024), LOW),
        vmem((2, depths, 2, peers, 4 * unit, 256), LOW),
        vmem((tall, 1024), WHOLE),
        vmem((3, 2, tall, width), LOW),
        vmem((2, tall, hidden), LOW),
        vmem((depths, 128, 512), WHOLE),
        vmem((2, 3) + left[1:], LOW),
        vmem((2, 4) + left[1:], LOW),
        *[vmem(exchange, LOW)] * 6,
        vmem((2, 2 * width), WHOLE),
        vmem((2, hidden), WHOLE),
        dma((total, depths - 1)),
        dma((total, depths - 1)),
        dma((total, half, 2)),
        dma((total, half, 2)),
        dma((total, 2 * half)),
        dma((total, 2 * half)),
        dma((total,)),
        dma(()),
        dma(()),
        dma(()),
        dma((total,)),
        dma((32,)),
        dma((2, 4)),
        dma((2, 4)),
        dma((1, peers - 1)),
        dma((1, peers - 1)),
        *[dma((4, peers - 1))] * 4,
    ]
    return pl.pallas_call(
        functools.partial(forward_kernel, chunks, depths, peers),
        out_shape=outs,
        in_specs=[ANY] * 4 + [VMEM] * 6 + [smem] * 4,
        out_specs=[ANY] * 8 + [VMEM] * 2 + [ANY] * 9 + [VMEM],
        scratch_shapes=scratch,
        compiler_params=pltpu.CompilerParams(
            collective_id=3, has_side_effects=True, vmem_limit_bytes=63 * 2**20
        ),
    )(*blocks, small, x0, grads, tables, index, mask, *moves)


SLOTS = 6


class Reduce:
    def __init__(self, place, plan, product, keep, bufs, sems):
        self.place, self.plan, self.product, self.keep = place, plan, product, keep
        (self.half_send, self.half_recv, self.full_send, self.full_recv, self.z_out, self.z_in, self.own_part) = bufs
        self.r_send, self.r_recv, self.z_send, self.z_recv = sems
        self.half = place.half
        self.rows = self.z_out.shape[2]
        self.cut = place.depths * self.rows // 2

    def ring(self, i, step, way):
        slot = i % SLOTS
        if step == 1:
            source, target = self.half_send.at[slot, way], self.half_recv.at[slot, way]
        else:
            source = self.full_send.at[slot, step - 2, way]
            target = self.full_recv.at[slot, step - 2, way]
        return remote(
            source,
            target,
            self.r_send.at[slot, step - 1, way],
            self.r_recv.at[slot, step - 1, way],
            self.place.neighbour(1 if way == 0 else -1),
        )

    def deep(self, i, step):
        slot = i % SLOTS
        return remote(
            self.z_out.at[slot, self.place.at_depth(step)],
            self.z_in.at[slot, step - 1],
            self.z_send.at[slot, step - 1],
            self.z_recv.at[slot, step - 1],
            self.place.deep(step),
        )

    def sent(self, i):
        for way in range(2):
            for step in range(1, self.half + 1):
                self.ring(i, step, way).wait_send()
        for step in range(1, self.place.depths):
            self.deep(i, step).wait_send()

    def first(self, i):
        if i >= SLOTS:
            self.sent(i - SLOTS)
        slot = i % SLOTS
        found = self.product(i, self.place.around(self.half)).astype(LOW)
        for way in range(2):
            self.half_send[slot, way] = found[: self.cut] if way == 0 else found[self.cut :]
            self.ring(i, 1, way).start()

    def next_step(self, i, step):
        slot = i % SLOTS
        cut = self.cut
        for way in range(2):
            turn = 1 if way == 0 else -1
            found = self.product(i, self.place.around(turn * (self.half - step + 1)))
            self.ring(i, step - 1, way).wait_recv()
            target = self.full_send.at[slot, step - 2, way]
            if step == 2:
                came = self.half_recv[slot, way].astype(WHOLE)
                low = found[:cut] + came if way == 0 else found[:cut]
                high = found[cut:] if way == 0 else found[cut:] + came
                target[:cut] = low.astype(LOW)
                target[cut:] = high.astype(LOW)
            else:
                came = self.full_recv[slot, step - 3, way].astype(WHOLE)
                target[...] = (found + came).astype(LOW)
            self.ring(i, step, way).start()

    def plane(self, i):
        slot, rows = i % SLOTS, self.rows
        found = self.product(i, self.place.peer)
        for way in range(2):
            self.ring(i, self.half, way).wait_recv()
            found += self.full_recv[slot, self.half - 2, way].astype(WHOLE)
        for depth in range(self.place.depths):
            piece = found[depth * rows : (depth + 1) * rows]
            self.z_out[slot, depth] = piece.astype(LOW)

            @pl.when(depth == self.place.depth)
            def _():
                self.own_part[slot] = piece

        for step in range(1, self.place.depths):
            self.deep(i, step).start()

    def finish(self, i):
        slot = i % SLOTS
        found = self.own_part[slot]
        for step in range(1, self.place.depths):
            self.deep(i, step).wait_recv()
            found += self.z_in[slot, step - 1].astype(WHOLE)
        self.keep(i, found)


B_IN = (
    "f0", "f1", "f2", "f3", "f4", "f5", "f6", "f7", "moved_grad", "left0", "left1", "left2", "left3", "low_x",
    "middle", "qkv", "probs", "slope", "vec32", "index", "backward_send", "backward_take",
)
B_OUT = (
    "patches_grad", "g_qkv", "g_proj", "g_up", "g_down", "small_all", "own",
)
B_SCRATCH = (
    "half_send", "half_recv", "full_send", "full_recv", "z_out", "z_in", "own_part", "left_a", "left_b",
    "right0", "right1", "right2", "right3", "wide_a", "wide_b", "slope_s", "p_s", "q_s", "mid", "x", "grad",
    "att_grad", "total", "g_mid", "score_sum", "tiles", "e_out", "e_in", "small_mine", "small_in",
    "small_sum", "r_send", "r_recv", "z_send", "z_recv", "swap_send", "swap_recv", "credit", "load", "state",
    "e_send", "e_recv", "a_send", "a_recv", "a_own", "b_send", "b_recv", "b_own",
)
SMALL_ROWS = 96


def backward_kernel(plan, depths, peers, *refs):
    r = names(B_IN + B_OUT + B_SCRATCH, refs)
    place = Place(depths, peers)
    fulls = (r.f0, r.f1, r.f2, r.f3, r.f4, r.f5, r.f6, r.f7)
    rights = (r.right0, r.right1, r.right2, r.right3)
    outs = (r.g_qkv, r.g_proj, r.g_up, r.g_down)
    windows, tall = 2, 2 * ROWS
    total = len(plan)
    queue = Queue(B_BUDGET)
    done, used, loaded = set(), set(), []
    unit = r.z_out.shape[2]

    def product(i, peer):
        layer, array, part, start = plan[i]
        left = r.left_b[layer, part, peer] if array == 3 else r.left_a[layer, array, peer]
        return dot(left, rights[array][:, start : start + WIDE])

    def keep(i, found):
        layer, array, part, start = plan[i]
        outs[array][layer, part * unit : (part + 1) * unit, start : start + WIDE] = found

    reduce = Reduce(
        place,
        plan,
        product,
        keep,
        (r.half_send, r.half_recv, r.full_send, r.full_recv, r.z_out, r.z_in, r.own_part),
        (r.r_send, r.r_recv, r.z_send, r.z_recv),
    )
    exchange = Exchange(place, r.e_out, r.e_in, r.e_send, r.e_recv, 1)

    order = [(layer, array, part) for layer in (1, 0) for array, parts in ((3, 4), (2, 4), (1, 1), (0, 3)) for part in range(parts)]

    def slot_of(k):
        down = order[k][1] == 3
        return sum(1 for o in order[:k] if (o[1] == 3) == down) % 2

    def load(k):
        layer, array, part = order[k]
        full = fulls[layer * 4 + array]
        if array == 3:
            return pltpu.make_async_copy(full.at[part], r.wide_b.at[slot_of(k)], r.load.at[k])
        source = full.at[:, :, :, :, part * 1024 : (part + 1) * 1024]
        return pltpu.make_async_copy(source, r.wide_a.at[slot_of(k)], r.load.at[k])

    def pump():
        while len(loaded) < len(order):
            k = len(loaded)
            same = [j for j in range(k) if (order[j][1] == 3) == (order[k][1] == 3)]
            if len(same) > 1 and same[-2] not in used:
                break
            load(k).start()
            loaded.append(k)

    def weight(layer, array, part):
        k = order.index((layer, array, part))
        assert k in loaded
        used.add(k)
        load(k).wait()
        value = (r.wide_b if array == 3 else r.wide_a)[slot_of(k)]
        return value.reshape(-1, value.shape[-1])

    def swap(layer, array, part):
        columns = slice(part * 1024, (part + 1) * 1024)
        right = rights[array]
        return remote(
            right.at[0:tall, columns],
            right.at[256 : 256 + tall, columns],
            r.swap_send.at[array, part],
            r.swap_recv.at[array, part],
            place.sibling(),
        )

    def free(array):
        pl.semaphore_signal(r.credit.at[array], inc=1, device_id=place.sibling(), device_id_type=MESH)

    def hand_over(layer, array, part):
        if layer == 0 and part == 0:
            pl.semaphore_wait(r.credit.at[array], 1)
        swap(layer, array, part).start()

    def ready(layer, array, part):
        if layer == 0:
            assert (array, "freed") in done
            swap(1, array, part).wait_send()

    def put(layer, row, vector):
        for k in range(vector.shape[1] // 128):
            line = layer * SMALL_ROWS + row + k
            r.small_mine[line : line + 1, :] = vector[:, k * 128 : (k + 1) * 128]

    def column_sums(layer, row, value):
        ones = jnp.ones((8, tall), LOW)
        put(layer, row, dot(ones, value)[:1])

    states = (("slope_s", "slope"), ("p_s", "probs"), ("q_s", "qkv"), ("mid", "middle"), ("x", "low_x"))

    def state_copy(layer, k):
        here, there = states[k]
        return pltpu.make_async_copy(
            getattr(r, there).at[layer], getattr(r, here), r.state.at[layer, k]
        )

    def left_copies(layer):
        sources = (r.left0, r.left1, r.left2)
        found = [
            pltpu.make_async_copy(
                sources[k].at[layer], r.left_a.at[layer, k], r.state.at[layer, 5 + k]
            )
            for k in range(3)
        ]
        return found + [
            pltpu.make_async_copy(r.left3.at[layer], r.left_b.at[layer], r.state.at[layer, 8])
        ]

    def vec(k):
        return r.vec32[k : k + 1, :]

    def take_grad(layer):
        if layer == 1:
            for w in range(windows):
                r.grad[w * ROWS : (w + 1) * ROWS, :] = r.moved_grad[w]
        else:
            exchange.await_part(0)
            for w in range(windows):
                r.grad[w * ROWS : (w + 1) * ROWS, :] = r.e_in[r.backward_take[w]]
        ready(layer, 3, 0)
        value = r.grad[...]
        r.right3[0:tall, :] = value
        hand_over(layer, 3, 0)
        column_sums(layer, 88, value)

    def hidden_grad(layer, part):
        if part == 0:
            state_copy(layer, 0).wait()
        columns = slice(part * 1024, (part + 1) * 1024)
        ready(layer, 2, part)
        found = dot(r.grad[...], weight(layer, 3, part), (1, 1))
        low = (found * r.slope_s[:, columns].astype(WHOLE)).astype(LOW)
        r.right2[0:tall, columns] = low
        hand_over(layer, 2, part)
        column_sums(layer, 56 + 8 * part, low)
        if part == 3 and layer == 1:
            state_copy(0, 0).start()

    def add_back(layer, array, part, columns):
        found = dot(rights[array][0:tall, columns], weight(layer, array, part), (1, 1))
        if part == 0:
            r.total[...] = found
        else:
            r.total[...] += found

    def up_back(layer, part):
        add_back(layer, 2, part, slice(part * 1024, (part + 1) * 1024))

    def norm_loop(source, layer, k, finish):
        gain = vec(2 * layer + k)

        def body(i, carry):
            start = pl.multiple_of(i * 16, 16)
            rows = pl.ds(start, 16)
            parts, inverse = normal_parts(source[rows, :].astype(WHOLE))
            g = r.total[rows, :]
            e = g * gain
            mean = jnp.mean(e, axis=1, keepdims=True)
            along = jnp.mean(e * parts, axis=1, keepdims=True)
            finish(rows, inverse * (e - mean - parts * along))
            by_gain, by_shift = carry
            return (
                by_gain + jnp.sum(g * parts, axis=0, keepdims=True),
                by_shift + jnp.sum(g, axis=0, keepdims=True),
            )

        zero = jnp.zeros((1, source.shape[-1]), WHOLE)
        by_gain, by_shift = lax.fori_loop(0, tall // 16, body, (zero, zero))
        put(layer, 8 * k, by_gain)
        put(layer, 16 + 8 * k, by_shift)

    def middle_grad(layer):
        state_copy(layer, 3).wait()
        ready(layer, 1, 0)

        def finish(rows, found):
            whole = r.grad[rows, :].astype(WHOLE) + found
            r.g_mid[rows, :] = whole
            r.right1[rows, :] = whole.astype(LOW)

        norm_loop(r.mid, layer, 1, finish)
        hand_over(layer, 1, 0)
        column_sums(layer, 48, r.right1[0:tall, :])
        if layer == 1:
            state_copy(0, 3).start()

    def attended_grad(layer):
        r.att_grad[...] = dot(r.right1[0:tall, :], weight(layer, 1, 0), (1, 1)).astype(LOW)

    def fold(value):
        return sum(
            jnp.where(lane_mask(KEYS, head), value[head * KEYS : (head + 1) * KEYS], 0.0)
            for head in range(GROUP)
        )[:ROWS]

    def attend_back(layer, w):
        if w == 0:
            state_copy(layer, 1).wait()
            state_copy(layer, 2).wait()
            for part in range(3):
                ready(layer, 0, part)

        def step(g, carry):
            rows = slice(w * ROWS, (w + 1) * ROWS)
            start = pl.multiple_of(g * 128, 128)
            q = r.q_s[rows, pl.ds(start, 128)]
            k = r.q_s[rows, pl.ds(start + 1024, 128)]
            v = r.q_s[rows, pl.ds(start + 2048, 128)]
            out_grad = r.att_grad[rows, pl.ds(start, 128)]
            low = r.p_s[w * 8 + g]
            prob_grad = dot(out_grad, per_head(v), (1, 1))
            pieces = []
            for head in range(GROUP):
                one = slice(head * KEYS, (head + 1) * KEYS)
                probs = low[:, one].astype(WHOLE)
                weighed = probs * prob_grad[:, one]
                pieces.append(weighed - probs * jnp.sum(weighed, axis=1, keepdims=True))
            score_grad = jnp.concatenate(pieces, axis=1).astype(LOW)
            if w == 0:
                r.score_sum[g] = score_grad.astype(WHOLE)
            else:
                r.score_sum[g] += score_grad.astype(WHOLE)
            by_query = dot(score_grad, per_head(k)) * SCALE
            by_key = fold(dot(score_grad, q, (0, 0))) * SCALE
            by_value = fold(dot(low, out_grad, (0, 0)))
            for part, found in enumerate((by_query, by_key, by_value)):
                r.right0[rows, pl.ds(start + part * 1024, 128)] = found.astype(LOW)
            return carry

        lax.fori_loop(0, 8, step, 0)
        if w == windows - 1:
            for part in range(3):
                hand_over(layer, 0, part)
            column_sums(layer, 32, r.right0[0:tall, 0:1024])
            column_sums(layer, 40, r.right0[0:tall, 2048:3072])
            if layer == 1:
                state_copy(0, 1).start()
                state_copy(0, 2).start()

    def qkv_back(layer, part):
        add_back(layer, 0, part, slice(part * 1024, (part + 1) * 1024))

    def input_grad(layer):
        state_copy(layer, 4).wait()

        def finish(rows, found):
            r.g_mid[rows, :] = r.g_mid[rows, :] + found

        norm_loop(r.x, layer, 0, finish)
        if layer == 1:
            state_copy(0, 4).start()
            for w in range(windows):
                r.tiles[w] = r.g_mid[w * ROWS : (w + 1) * ROWS, :].astype(LOW)
            exchange.give(0, r.tiles, r.backward_send)
        else:
            for w in range(windows):
                r.patches_grad[w * WIN : (w + 1) * WIN, :] = r.g_mid[w * ROWS : w * ROWS + WIN, :]

    def table_grad(layer):
        buckets = lax.broadcasted_iota(jnp.int32, (384, KEYS), 0)

        def step(i, found):
            line = r.index[pl.ds(i, 1), :]
            hot = jnp.where(buckets == line, 1.0, 0.0).astype(LOW)
            value = r.score_sum[:, pl.ds(i, 1), :].reshape(8, GROUP * KEYS)
            value = jnp.concatenate(
                [value[:, head * KEYS : (head + 1) * KEYS] for head in range(GROUP)], axis=0
            )
            high = value.astype(LOW)
            rest = (value - high.astype(WHOLE)).astype(LOW)
            return found + dot(jnp.concatenate([high, rest], axis=0), hot, (1, 1))

        found = lax.fori_loop(0, 100, step, jnp.zeros((64, 384), WHOLE))
        found = found[:32] + found[32:]
        base = 2 * SMALL_ROWS + layer * SMALL_ROWS
        for k in range(3):
            r.small_mine[base + 32 * k : base + 32 * (k + 1), :] = found[:, 128 * k : 128 * (k + 1)]

    def send_small():
        def step(k, carry):
            outer, peer = place.other(k)
            remote(
                r.small_mine.at[pl.ds(pl.multiple_of((outer * peers + peer) * 16, 16), 16)],
                r.small_in.at[place.index],
                r.a_send,
                r.a_recv,
                (outer, peer),
            ).start()
            return carry

        lax.fori_loop(1, place.total, step, 0)
        own_small().start()

    def own_small():
        mine = r.small_mine.at[pl.ds(pl.multiple_of(place.index * 16, 16), 16)]
        return pltpu.make_async_copy(mine, r.small_in.at[place.index], r.a_own)

    spread = Spread(place, r.small_sum, r.small_all, r.b_send, r.b_recv, r.b_own)

    def sum_small():
        rest = r.small_in.at[pl.ds(0, place.total - 1)]
        both = remote(rest, rest, r.a_send, r.a_recv, place.other(1))
        both.wait_send()
        both.wait_recv()
        own_small().wait()
        r.small_sum[...] = jnp.sum(r.small_in[...], axis=0)
        spread.start()

    def own_vectors():
        starts = ((0, 4), (8, 4), (16, 4), (24, 4), (32, 2), (48, 4), (56, 1), (88, 4))
        for layer in range(2):
            for k, (row, each) in enumerate(starts):
                line = layer * SMALL_ROWS + row + lax.div(place.index, each)
                found = r.small_all[lax.div(line, 16), pl.ds(lax.rem(line, 16), 1), :]
                back = lax.rem(each - lax.rem(place.index, each), each) * (128 // each)
                r.own[8 * layer + k : 8 * layer + k + 1, :] = pltpu.roll(found, back, 1)

    def note(work, *what):
        work(*what)
        done.add((work.__name__, *what))

    def add(tick, cost, work, *what):
        queue.add(tick, cost, note, work, *what)

    for k in range(5):
        state_copy(1, k).start()
    for layer in (1, 0):
        for copy in left_copies(layer):
            copy.start()
    for right in rights:
        zero = jnp.zeros((256 - tall, right.shape[1]), LOW)
        right[tall:256, :] = zero
        right[256 + tall : 512, :] = zero
    r.small_mine[...] = jnp.zeros(r.small_mine.shape, WHOLE)
    pump()
    place.greet()

    add(0, 1, take_grad, 1)
    last_use = {
        array: max(i for i, p in enumerate(plan) if p[0] == 1 and p[1] == array) for array in range(4)
    }
    after = {array: last_use[array] + GAP * place.half for array in range(4)}
    for layer in (1, 0):
        late = 9 if layer == 0 else 0
        if layer == 0:
            add(0, 5, table_grad, 1)
            add(late, 1, take_grad, 0)
        for part in range(4):
            add(late and after[2], 2, hidden_grad, layer, part)
        for part in range(4):
            add(late, 2, up_back, layer, part)
        add(late and after[1], 3, middle_grad, layer)
        add(late, 1.5, attended_grad, layer)
        for w in range(windows):
            add(late and after[0], 7, attend_back, layer, w)
        for part in range(3):
            add(late, 1.5, qkv_back, layer, part)
        add(late, 3, input_grad, layer)
    add(0, 5, table_grad, 0)
    add(0, 1, send_small)

    needs = {3: ("take_grad",), 2: ("hidden_grad",), 1: ("middle_grad",), 0: ("attend_back",)}

    def wanted(i):
        layer, array, part, start = plan[i]
        what = needs[array] + (layer,)
        if array == 2:
            what += (start // 1024,)
        if array == 0:
            what += (windows - 1,)
        return what

    received, lefts_in = set(), set()
    half = place.half
    for tick in range(total + GAP * (half + 1)):
        if tick < total:
            layer, array, part, start = plan[tick]
            while wanted(tick) not in done:
                queue.step(pump)
            if layer not in lefts_in:
                lefts_in.add(layer)
                for copy in left_copies(layer):
                    copy.wait()
            key = (layer, array, start // 1024)
            if key not in received:
                received.add(key)
                swap(*key).wait_recv()
            reduce.first(tick)
        for step in range(2, half + 1):
            i = tick - GAP * (step - 1)
            if 0 <= i < total:
                reduce.next_step(i, step)
        i = tick - GAP * half
        if 0 <= i < total:
            reduce.plane(i)
            for array, last in last_use.items():
                if i == last:
                    free(array)
                    done.add((array, "freed"))
        i = tick - GAP * (half + 1)
        if 0 <= i < total:
            reduce.finish(i)
        queue.run(tick, pump)
        if ("send_small",) in done and ("sum_small",) not in done and tick >= total - 1:
            note(sum_small)
    assert not queue.pieces
    if ("sum_small",) not in done:
        sum_small()
    spread.wait()
    own_vectors()
    exchange.finish(1)
    for array, parts in ((3, 1), (2, 4), (1, 1), (0, 3)):
        for part in range(parts):
            swap(0, array, part).wait_send()
    for i in range(total - SLOTS, total):
        reduce.sent(i)


def backward_all(fulls, state, index, moves, depths, peers):
    moved_grad, left0, left1, left2, left3, low_x, middle, qkv, probs, slope, vec32 = state
    count = depths * 2 * peers
    tall, width = low_x.shape[1:]
    hidden = slope.shape[-1]
    unit = width // count
    half = peers // 2
    plan = []
    for layer in (1, 0):
        plan += [(layer, 3, part, 0) for part in range(4)]
        plan += [(layer, 2, 0, start) for start in range(0, hidden, WIDE)]
        plan += [(layer, 1, 0, 0)]
        plan += [(layer, 0, 0, start) for start in range(0, 3 * width, WIDE)]
    dma = pltpu.SemaphoreType.DMA
    vmem = pltpu.VMEM
    smem = pl.BlockSpec(memory_space=pltpu.SMEM)
    shape = jax.ShapeDtypeStruct
    flat = depths * unit
    outs = [
        shape((2 * WIN, width), WHOLE),
        shape((2, unit, 3 * width), WHOLE),
        shape((2, unit, width), WHOLE),
        shape((2, unit, hidden), WHOLE),
        shape((2, 4 * unit, width), WHOLE),
        shape((count, 16, 128), WHOLE),
        shape((16, 128), WHOLE),
    ]
    scratch = [
        vmem((SLOTS, 2, flat // 2, WIDE), LOW),
        vmem((SLOTS, 2, flat // 2, WIDE), LOW),
        vmem((SLOTS, half - 1, 2, flat, WIDE), LOW),
        vmem((SLOTS, half - 1, 2, flat, WIDE), LOW),
        vmem((SLOTS, depths, unit, WIDE), LOW),
        vmem((SLOTS, depths - 1, unit, WIDE), LOW),
        vmem((SLOTS, unit, WIDE), WHOLE),
        vmem((2, 3) + left0.shape[1:], LOW),
        vmem(left3.shape, LOW),
        vmem((512, 3 * width), LOW),
        vmem((512, width), LOW),
        vmem((512, hidden), LOW),
        vmem((512, width), LOW),
        vmem((2, depths, 2, peers, unit, 1024), LOW),
        vmem((2, 2, peers, 4 * unit, width), LOW),
        vmem((tall, hidden), LOW),
        vmem(probs.shape[1:], LOW),
        vmem((tall, 3 * width), LOW),
        vmem((tall, width), WHOLE),
        vmem((tall, width), LOW),
        vmem((tall, width), LOW),
        vmem((tall, width), LOW),
        vmem((tall, width), WHOLE),
        vmem((tall, width), WHOLE),
        vmem((8, ROWS, GROUP * KEYS), WHOLE),
        vmem((2, ROWS, width), LOW),
        vmem((peers, ROWS, width), LOW),
        vmem((peers, ROWS, width), LOW),
        vmem((count * 16, 128), WHOLE),
        vmem((count, 16, 128), WHOLE),
        vmem((16, 128), WHOLE),
        dma((SLOTS, half, 2)),
        dma((SLOTS, half, 2)),
        dma((SLOTS, depths - 1)),
        dma((SLOTS, depths - 1)),
        dma((4, 4)),
        dma((4, 4)),
        pltpu.SemaphoreType.REGULAR((4,)),
        dma((24,)),
        dma((2, 9)),
        dma((1, peers - 1)),
        dma((1, peers - 1)),
        *[dma(())] * 6,
    ]
    return pl.pallas_call(
        functools.partial(backward_kernel, plan, depths, peers),
        out_shape=outs,
        in_specs=[ANY] * 8 + [VMEM] + [ANY] * 9 + [VMEM] * 2 + [smem] * 2,
        out_specs=[VMEM] * 7,
        scratch_shapes=scratch,
        compiler_params=pltpu.CompilerParams(
            collective_id=4, has_side_effects=True, vmem_limit_bytes=63 * 2**20
        ),
    )(*fulls, *state, index, *moves)


def whole_shards(
    outer_count,
    peer_count,
    patches,
    out_grad,
    norm_gain,
    norm_shift,
    qkv_weight,
    qv_bias,
    rel_table,
    proj_weight,
    proj_bias,
    up_weight,
    up_bias,
    down_weight,
    down_bias,
    tile_perm,
    window_slot,
    mask_ids,
    bias_index,
):
    windows = patches.shape[0] // WIN
    width = patches.shape[1]
    depths = outer_count // 2
    device_index = lax.axis_index(("dp", "fsdp"))
    slot_ids = jnp.arange(tile_perm.shape[0], dtype=jnp.int32)

    def one_hot_pick(keys, values):
        return jnp.sum(jnp.where(keys[None, :] == slot_ids[:, None], values[None, :], 0), axis=1)

    def look_up(values, at):
        hit = at[:, None] == jnp.arange(values.shape[0], dtype=jnp.int32)[None, :]
        return jnp.sum(jnp.where(hit, values[None, :], 0), axis=1)

    source_of = one_hot_pick(window_slot, look_up(window_slot, tile_perm))
    target_of = one_hot_pick(source_of, slot_ids)
    region_slot = one_hot_pick(window_slot, mask_ids)
    own_slots = device_index * windows + jnp.arange(windows, dtype=jnp.int32)
    forward_take = look_up(source_of, own_slots) // windows % peer_count
    backward_take = look_up(target_of, own_slots) // windows % peer_count
    spots = jnp.arange(peer_count, dtype=jnp.int32)
    numbers = jnp.arange(windows, dtype=jnp.int32)

    def window_for(peers):
        return jnp.sum(jnp.where(peers[None, :] == spots[:, None], numbers[None, :], 0), axis=1)

    moves = (window_for(backward_take), forward_take, window_for(forward_take), backward_take)
    mask = region_mask(look_up(region_slot, own_slots))[:, 0]
    mask = jnp.pad(mask, ((0, 0), (0, ROWS - WIN), (0, KEYS - WIN)))
    index = jnp.pad(
        bias_index, ((0, ROWS - WIN), (0, KEYS - WIN)), constant_values=rel_table.shape[1]
    )
    tables = rel_table.reshape(2, -1, HEADS // GROUP, GROUP).transpose(0, 3, 2, 1)
    tables = tables.reshape(2 * HEADS, -1)
    tables = jnp.pad(tables, ((0, 0), (0, 384 - tables.shape[1])), constant_values=NEVER)

    each = width // (outer_count * peer_count)
    small = jnp.concatenate(
        [
            norm_gain.reshape(1, 4 * each),
            norm_shift.reshape(1, 4 * each),
            jnp.concatenate([proj_bias, down_bias], axis=0).reshape(1, 4 * each),
            qv_bias.reshape(1, 4 * each),
            up_bias,
            jnp.zeros((2, 4 * each), LOW),
        ],
        axis=0,
    ).astype(jnp.float32)

    def padded(rows):
        return jnp.pad(rows.reshape(windows, WIN, width), ((0, 0), (0, ROWS - WIN), (0, 0)))

    found = forward_all(
        (qkv_weight, proj_weight, up_weight, down_weight),
        small,
        padded(patches).reshape(windows * ROWS, width),
        padded(out_grad),
        tables,
        index,
        mask,
        moves,
        depths,
        peer_count,
    )
    fulls, moved_grad, result, state = found[:8], found[8], found[9], found[10:]
    grad_patches, grad_qkv, grad_proj, grad_up, grad_down, small_all, own = backward_all(
        fulls, (moved_grad, *state), index, moves[2:], depths, peer_count
    )

    def trimmed(rows):
        return rows.reshape(windows, ROWS, width)[:, :WIN].reshape(windows * WIN, width)

    flat = small_all.reshape(-1)
    per_layer = SMALL_ROWS * 128
    own = own.reshape(2, 8, 128)
    gain_grad, shift_grad = own[:, 0:2, :each], own[:, 2:4, :each]
    qv_grad, proj_b_grad = own[:, 4, : 2 * each], own[:, 5, :each]
    up_b_grad, down_b_grad = own[:, 6], own[:, 7, :each]
    table = flat[2 * per_layer : 4 * per_layer].reshape(2, 3, GROUP, HEADS // GROUP, 128)
    table = table.transpose(0, 1, 4, 3, 2).reshape(2, 3 * 128, HEADS)[:, : rel_table.shape[1]]
    return (
        trimmed(result),
        grad_patches,
        gain_grad,
        shift_grad,
        grad_qkv,
        qv_grad,
        table,
        grad_proj,
        proj_b_grad,
        grad_up,
        up_b_grad,
        grad_down,
        down_b_grad,
    )


def solution(mesh):
    outer_count, peer_count = mesh.shape["dp"], mesh.shape["fsdp"]
    fused = outer_count == 8 and peer_count == 4
    placed = (
        P(("dp", "fsdp"), None),
        P(("dp", "fsdp"), None),
        P(None, None, ("dp", "fsdp")),
        P(None, None, ("dp", "fsdp")),
        P(None, ("dp", "fsdp"), None),
        P(None, ("dp", "fsdp")),
        P(),
        P(None, ("dp", "fsdp"), None),
        P(None, ("dp", "fsdp")),
        P(None, ("dp", "fsdp"), None),
        P(None, ("dp", "fsdp")),
        P(None, ("dp", "fsdp"), None),
        P(None, ("dp", "fsdp")),
        P(),
        P(),
        P(),
        P(),
    )
    return jax.shard_map(
        functools.partial(whole_shards if fused else shards, outer_count, peer_count),
        mesh=mesh,
        in_specs=placed,
        out_specs=(
            P(("dp", "fsdp"), None),
            P(("dp", "fsdp"), None),
            P(None, None, ("dp", "fsdp")),
            P(None, None, ("dp", "fsdp")),
            P(None, ("dp", "fsdp"), None),
            P(None, ("dp", "fsdp")),
            P(),
            P(None, ("dp", "fsdp"), None),
            P(None, ("dp", "fsdp")),
            P(None, ("dp", "fsdp"), None),
            P(None, ("dp", "fsdp")),
            P(None, ("dp", "fsdp"), None),
            P(None, ("dp", "fsdp")),
        ),
        check_vma=False,
    )
```

```python
import functools
import types

import jax
import jax.numpy as jnp
from jax import lax
from jax.experimental import pallas as pl
from jax.experimental.pallas import tpu as pltpu
from jax.sharding import PartitionSpec as P

HEADS = 32
SIDE = 10
WIN = 100


epsilon = 1e-05
masked_score = -1000000000.0


def layer_norm(inputs, gain, shift):
    mean_value = jnp.mean(inputs, axis=-1, keepdims=True)
    centered = inputs - mean_value
    inverse = lax.rsqrt(jnp.mean(centered * centered, axis=-1, keepdims=True) + epsilon)
    normal_part = centered * inverse
    return (normal_part * gain + shift, normal_part, inverse)


def norm_back(grad_out, normal_part, inverse, gain):
    scaled = grad_out * gain
    grad_in = inverse * (
        scaled
        - jnp.mean(scaled, axis=-1, keepdims=True)
        - normal_part * jnp.mean(scaled * normal_part, axis=-1, keepdims=True)
    )
    return (grad_in, jnp.sum(grad_out * normal_part, axis=0), jnp.sum(grad_out, axis=0))


def gelu_exact(hidden):
    return jax.nn.gelu(hidden, approximate=False)


def region_mask(region_ids):
    position = jnp.arange(WIN, dtype=jnp.int32)
    cut_point = SIDE - SIDE // 2
    right_half = (position % SIDE >= cut_point).astype(jnp.int32)
    lower_half = (position // SIDE >= cut_point).astype(jnp.int32)
    labels = (
        region_ids[:, None] % 2 * right_half[None]
        + 2 * (region_ids[:, None] // 2) * lower_half[None]
    )
    same_label = labels[:, :, None] == labels[:, None, :]
    return jnp.where(same_label, 0.0, masked_score).astype(jnp.float32)[:, None]


MESH = pl.DeviceIdType.MESH
ANY = pl.BlockSpec(memory_space=pl.ANY)
VMEM = pl.BlockSpec(memory_space=pltpu.VMEM)
WIDE = 1024
LOOK = 2


def ring_position(peer, peers):
    column, row = lax.rem(peer, 2), lax.div(peer, 2)
    return column * (peers - 1 - row) + (1 - column) * row


def ring_member(place, peers):
    place = lax.rem(place + peers, peers)
    far = lax.div(place, peers // 2)
    return (1 - far) * 2 * place + far * (2 * (peers - 1 - place) + 1)


class Place:
    def __init__(self, depths, peers):
        self.depths, self.peers, self.half = depths, peers, peers // 2
        outer = lax.axis_index("dp")
        self.depth, self.core = lax.div(outer, 2), lax.rem(outer, 2)
        self.peer = lax.axis_index("fsdp")
        self.spot = ring_position(self.peer, peers)
        self.index = outer * peers + self.peer
        self.total = depths * 2 * peers

    def sibling(self):
        return (self.depth * 2 + 1 - self.core, self.peer)

    def around(self, step):
        return ring_member(self.spot + step, self.peers)

    def neighbour(self, step):
        return (self.depth * 2 + self.core, self.around(step))

    def at_depth(self, step):
        return lax.rem(self.depth + step + self.depths, self.depths)

    def deep(self, step):
        return (self.at_depth(step) * 2 + self.core, self.peer)

    def other(self, step):
        index = lax.rem(self.index + step, self.total)
        return (lax.div(index, self.peers), lax.rem(index, self.peers))

    def greet(self):
        barrier = pltpu.get_barrier_semaphore()

        def signal(step, carry):
            pl.semaphore_signal(barrier, inc=1, device_id=self.other(step), device_id_type=MESH)
            return carry

        lax.fori_loop(1, self.total, signal, 0)
        pl.semaphore_wait(barrier, self.total - 1)

    def greet_near(self):
        barrier = pltpu.get_barrier_semaphore()
        near = [self.sibling(), self.neighbour(1), self.neighbour(-1)]
        near += [self.deep(step) for step in range(1, self.depths)]
        for device in near:
            pl.semaphore_signal(barrier, inc=1, device_id=device, device_id_type=MESH)
        pl.semaphore_wait(barrier, len(near))


def remote(source, target, send, receive, device):
    return pltpu.make_async_remote_copy(
        src_ref=source,
        dst_ref=target,
        send_sem=send,
        recv_sem=receive,
        device_id=device,
        device_id_type=MESH,
    )


class Spread:
    def __init__(self, place, source, target, send, receive, local):
        self.place, self.source, self.target = place, source, target
        self.send, self.receive, self.local = send, receive, local

    def own(self):
        return pltpu.make_async_copy(self.source, self.target.at[self.place.index], self.local)

    def start(self):
        def copy(step, carry):
            remote(
                self.source,
                self.target.at[self.place.index],
                self.send,
                self.receive,
                self.place.other(step),
            ).start()
            return carry

        lax.fori_loop(1, self.place.total, copy, 0)
        self.own().start()

    def wait(self):
        rest = self.target.at[pl.ds(0, self.place.total - 1)]
        both = remote(rest, rest, self.send, self.receive, self.place.other(1))
        both.wait_send()
        both.wait_recv()
        self.own().wait()


def gather_kernel(chunks, depths, peers, count, *refs):
    blocks, small = refs[:count], refs[count]
    fulls, small_full = refs[count + 1 : 2 * count + 1], refs[2 * count + 1]
    (z_send, z_recv, r_send, r_recv, c_send, c_recv, own_sem, s_send, s_recv, s_own) = refs[
        2 * count + 2 :
    ]
    place = Place(depths, peers)
    half = place.half
    core, cut = place.core, depths // 2

    def view(i, depth, peer):
        array, layer, rows, columns = chunks[i]
        return fulls[array].at[depth, core, peer, rows, columns]

    def block(i):
        array, layer, rows, columns = chunks[i]
        return blocks[array].at[layer, rows, columns]

    def own(i):
        return pltpu.make_async_copy(block(i), view(i, place.depth, place.peer), own_sem.at[i])

    def deep(i, step):
        return remote(
            block(i),
            view(i, place.depth, place.peer),
            z_send.at[i, step - 1],
            z_recv.at[i, step - 1],
            place.deep(step),
        )

    def part(step, way):
        if step < half:
            return slice(None)
        return slice(0, cut) if way == 0 else slice(cut, depths)

    def ring(i, step, way):
        turn = 1 if way == 0 else -1
        here = view(i, part(step, way), place.around(-turn * (step - 1)))
        return remote(
            here,
            here,
            r_send.at[i, step - 1, way],
            r_recv.at[i, step - 1, way],
            place.neighbour(turn),
        )

    def across(i, slot):
        step = (slot + 1) // 2
        turn = 1 if slot % 2 else -1
        here = view(i, slice(None), place.around(-turn * step))
        return remote(here, here, c_send.at[i, slot], c_recv.at[i, slot], place.sibling())

    slots = 2 * half
    total = len(chunks)

    def begin(i):
        for step in range(1, depths):
            deep(i, step).start()
        own(i).start()

    def first(i):
        own(i).wait()
        for step in range(1, depths):
            deep(i, step).wait_recv()
        ring(i, 1, 0).start()
        ring(i, 1, 1).start()
        across(i, 0).start()

    def later(i, step):
        ring(i, step, 0).wait_recv()
        ring(i, step, 1).wait_recv()
        if step < half:
            ring(i, step + 1, 0).start()
            ring(i, step + 1, 1).start()
            across(i, 2 * step - 1).start()
            across(i, 2 * step).start()
        else:
            across(i, 2 * step - 1).start()

    place.greet()
    begin(0)
    spread = Spread(place, small, small_full, s_send, s_recv, s_own)
    spread.start()
    for i in range(1, min(LOOK, total)):
        begin(i)
    for tick in range(total + half):
        if tick + LOOK < total:
            begin(tick + LOOK)
        if tick < total:
            first(tick)
        for step in range(1, half + 1):
            if 0 <= tick - step < total:
                later(tick - step, step)
    spread.wait()
    for i in range(total):
        for slot in range(slots):
            across(i, slot).wait()
        for step in range(1, depths):
            deep(i, step).wait_send()
        for step in range(1, half + 1):
            for way in range(2):
                ring(i, step, way).wait_send()


def chunk_list(shapes, layers):
    chunks = []
    for layer in layers:
        for which, (rows, columns) in enumerate(shapes):
            array = layer * len(shapes) + which
            if columns > WIDE:
                for start in range(0, columns, WIDE):
                    chunks.append((which, array, layer, slice(None), slice(start, start + WIDE)))
            else:
                size = rows // 4 if rows % 64 == 0 and rows > 64 else rows
                for start in range(0, rows, size):
                    chunks.append((which, array, layer, slice(start, start + size), slice(None)))
    return chunks


def gather_all(blocks, small, depths, peers):
    shapes = [b.shape[1:] for b in blocks]
    half = peers // 2
    count = 2 * len(blocks)
    plan = [(array, layer, rows, cols) for _, array, layer, rows, cols in chunk_list(shapes, (0, 1))]
    total = len(plan)

    outs = [
        jax.ShapeDtypeStruct((depths, 2, peers) + shape, jnp.bfloat16)
        for _ in range(2)
        for shape in shapes
    ]
    outs.append(jax.ShapeDtypeStruct((depths * 2 * peers,) + small.shape, small.dtype))
    dma = pltpu.SemaphoreType.DMA
    doubled = list(blocks) + list(blocks)
    return pl.pallas_call(
        functools.partial(gather_kernel, plan, depths, peers, count),
        out_shape=outs,
        in_specs=[ANY] * (count + 1),
        out_specs=[ANY] * (count + 1),
        scratch_shapes=[
            dma((total, depths - 1)),
            dma((total, depths - 1)),
            dma((total, half, 2)),
            dma((total, half, 2)),
            dma((total, 2 * half)),
            dma((total, 2 * half)),
            dma((total,)),
            dma(()),
            dma(()),
            dma(()),
        ],
        compiler_params=pltpu.CompilerParams(
            collective_id=0, has_side_effects=True, vmem_limit_bytes=60 * 2**20
        ),
    )(*doubled, small)


def sum_kernel(plan, depths, peers, count, with_small, *refs):
    lefts, rights, rest = refs[:count], refs[count : 2 * count], refs[2 * count :]
    if with_small:
        small, rest = rest[0], rest[1:]
    outs, rest = rest[:count], rest[count:]
    if with_small:
        small_all, rest = rest[0], rest[1:]
    left_bufs, right_bufs, rest = rest[:count], rest[count : 2 * count], rest[2 * count :]
    (half_send, half_recv, full_send, full_recv, z_out, z_in, own_part, x_send, x_recv, x_own) = rest[:10]
    (r_send, r_recv, z_send, z_recv) = rest[10:14]
    if with_small:
        small_in, small_sum, a_send, a_recv, a_own, b_send, b_recv, b_own = rest[14:]
    place = Place(depths, peers)
    half, core = place.half, place.core
    rows = z_out.shape[2]
    tall = depths * rows
    cut = tall // 2

    def swap(k):
        array = k // 2
        if k % 2 == 0:
            mine, theirs = lefts[array].at[core], lefts[array].at[1 - core]
            buf = left_bufs[array]
        else:
            mine = theirs = rights[array]
            buf = right_bufs[array]
        return (
            pltpu.make_async_copy(mine, buf.at[0], x_own.at[k]),
            remote(theirs, buf.at[1], x_send.at[k], x_recv.at[k], place.sibling()),
        )

    def product(i, peer):
        array, row_part, start, _ = plan[i]
        columns = pl.ds(start, WIDE)
        return jnp.dot(
            left_bufs[array][0, row_part, peer],
            right_bufs[array][0, :, columns],
            preferred_element_type=jnp.float32,
        ) + jnp.dot(
            left_bufs[array][1, row_part, peer],
            right_bufs[array][1, :, columns],
            preferred_element_type=jnp.float32,
        )

    def ring(i, step, way):
        if step == 1:
            source, target = half_send.at[i, way], half_recv.at[i, way]
        else:
            source, target = full_send.at[i, step - 2, way], full_recv.at[i, step - 2, way]
        return remote(
            source,
            target,
            r_send.at[i, step - 1, way],
            r_recv.at[i, step - 1, way],
            place.neighbour(1 if way == 0 else -1),
        )

    def deep(i, step):
        return remote(
            z_out.at[i, place.at_depth(step)],
            z_in.at[i, step - 1],
            z_send.at[i, step - 1],
            z_recv.at[i, step - 1],
            place.deep(step),
        )

    def first(i):
        found = product(i, place.around(half)).astype(jnp.bfloat16)
        half_send[i, 0] = found[:cut]
        half_send[i, 1] = found[cut:]
        ring(i, 1, 0).start()
        ring(i, 1, 1).start()

    def next_step(i, step):
        for way in range(2):
            turn = 1 if way == 0 else -1
            found = product(i, place.around(turn * (half - step + 1)))
            ring(i, step - 1, way).wait_recv()
            if step == 2:
                came = half_recv[i, way].astype(jnp.float32)
                low = found[:cut] + came if way == 0 else found[:cut]
                high = found[cut:] if way == 0 else found[cut:] + came
                full_send[i, 0, way, :cut] = low.astype(jnp.bfloat16)
                full_send[i, 0, way, cut:] = high.astype(jnp.bfloat16)
            else:
                came = full_recv[i, step - 3, way].astype(jnp.float32)
                full_send[i, step - 2, way] = (found + came).astype(jnp.bfloat16)
            ring(i, step, way).start()

    def plane(i):
        found = product(i, place.peer)
        for way in range(2):
            ring(i, half, way).wait_recv()
            found += full_recv[i, half - 2, way].astype(jnp.float32)
        for depth in range(depths):
            piece = found[depth * rows : (depth + 1) * rows]
            z_out[i, depth] = piece.astype(jnp.bfloat16)

            @pl.when(depth == place.depth)
            def _():
                own_part[i] = piece

        for step in range(1, depths):
            deep(i, step).start()

    def finish(i):
        array, _, start, out_rows = plan[i]
        found = own_part[i]
        for step in range(1, depths):
            deep(i, step).wait_recv()
            found += z_in[i, step - 1].astype(jnp.float32)
        outs[array][out_rows, pl.ds(start, WIDE)] = found

    if with_small:
        place.greet()
    else:
        place.greet_near()
    for k in reversed(range(2 * count)):
        for copy in swap(k):
            copy.start()
    if with_small:

        def send_small(step, carry):
            outer, peer = place.other(step)
            remote(
                small.at[outer * peers + peer],
                small_in.at[place.index],
                a_send,
                a_recv,
                (outer, peer),
            ).start()
            return carry

        lax.fori_loop(1, place.total, send_small, 0)
        own_small = pltpu.make_async_copy(small.at[place.index], small_in.at[place.index], a_own)
        own_small.start()
        spread = Spread(place, small_sum, small_all, b_send, b_recv, b_own)

    total = len(plan)
    ready = set()
    for tick in range(total + half + 1):
        if tick < total:
            array = plan[tick][0]
            if array not in ready:
                ready.add(array)
                for k in (2 * array + 1, 2 * array):
                    kept, sent = swap(k)
                    kept.wait()
                    sent.wait_recv()
            first(tick)
        for step in range(2, half + 1):
            if 0 <= tick - step + 1 < total:
                next_step(tick - step + 1, step)
        if 0 <= tick - half < total:
            plane(tick - half)
        if 0 <= tick - half - 1 < total:
            finish(tick - half - 1)
        if with_small and tick == 4:
            rest_in = small_in.at[pl.ds(0, place.total - 1)]
            both = remote(rest_in, rest_in, a_send, a_recv, place.other(1))
            both.wait_send()
            both.wait_recv()
            own_small.wait()
            small_sum[...] = jnp.sum(small_in[...], axis=0)
            spread.start()
    if with_small:
        spread.wait()
    for k in range(2 * count):
        swap(k)[1].wait_send()
    for i in range(total):
        for step in range(1, half + 1):
            for way in range(2):
                ring(i, step, way).wait_send()
        for step in range(1, depths):
            deep(i, step).wait_send()


def sum_all(pairs, shapes, depths, peers, call, small=None):
    half, count = peers // 2, len(pairs)
    tokens = pairs[0][0].shape[0]
    padded = -(-tokens // 128) * 128
    unit = min(shape[0] for shape in shapes)
    lefts, rights, plan = [], [], []
    for array, ((left, right), shape) in enumerate(zip(pairs, shapes)):
        parts = shape[0] // unit
        turned = jnp.pad(left, ((0, padded - tokens), (0, 0))).T
        turned = turned.reshape(depths, 2, peers, parts, unit, padded)
        lefts.append(
            turned.transpose(1, 3, 2, 0, 4, 5).reshape(2, parts, peers, depths * unit, padded)
        )
        rights.append(jnp.pad(right, ((0, padded - tokens), (0, 0))))
        for part in range(parts):
            for start in range(0, shape[1], WIDE):
                plan.append((array, part, start, pl.ds(part * unit, unit)))
    plan = plan[::-1]
    total, tall = len(plan), depths * unit
    dma = pltpu.SemaphoreType.DMA
    low = jnp.bfloat16
    scratch = [pltpu.VMEM((2,) + a.shape[1:], low) for a in lefts]
    scratch += [pltpu.VMEM((2,) + a.shape, low) for a in rights]
    scratch += [
        pltpu.VMEM((total, 2, tall // 2, WIDE), low),
        pltpu.VMEM((total, 2, tall // 2, WIDE), low),
        pltpu.VMEM((total, half - 1, 2, tall, WIDE), low),
        pltpu.VMEM((total, half - 1, 2, tall, WIDE), low),
        pltpu.VMEM((total, depths, unit, WIDE), low),
        pltpu.VMEM((total, depths - 1, unit, WIDE), low),
        pltpu.VMEM((total, unit, WIDE), jnp.float32),
        dma((2 * count,)),
        dma((2 * count,)),
        dma((2 * count,)),
        dma((total, half, 2)),
        dma((total, half, 2)),
        dma((total, depths - 1)),
        dma((total, depths - 1)),
    ]
    args = [*lefts, *rights]
    in_specs = [ANY] * (2 * count)
    out_shape = [jax.ShapeDtypeStruct(shape, jnp.float32) for shape in shapes]
    out_specs = [VMEM] * count
    if small is not None:
        args.append(small)
        in_specs.append(ANY)
        out_shape.append(jax.ShapeDtypeStruct(small.shape, jnp.float32))
        out_specs.append(VMEM)
        scratch += [
            pltpu.VMEM(small.shape, jnp.float32),
            pltpu.VMEM(small.shape[1:], jnp.float32),
        ] + [dma(())] * 6
    return pl.pallas_call(
        functools.partial(sum_kernel, plan, depths, peers, count, small is not None),
        out_shape=out_shape,
        in_specs=in_specs,
        out_specs=out_specs,
        scratch_shapes=scratch,
        compiler_params=pltpu.CompilerParams(
            collective_id=call, has_side_effects=True, vmem_limit_bytes=60 * 2**20
        ),
    )(*args)


def attention_scores(qkv_parts, position_bias, mask_add):
    head_scale = qkv_parts.shape[-1] ** (-0.5)
    scores = (
        jnp.einsum(
            "wqhd,wkhd->whqk",
            qkv_parts[:, :, 0],
            qkv_parts[:, :, 1],
            preferred_element_type=jnp.float32,
        )
        * head_scale
        + position_bias[None]
    )
    if mask_add is not None:
        scores = scores + mask_add
    return scores


def block_forward(inputs, weights, position_bias, mask_add, windows):
    norm_gains, norm_shifts, w_qkv, qv_bias, w_proj, b_proj, w_up, b_up, w_down, b_down = weights
    model_width = inputs.shape[1]
    norm_gains = norm_gains.astype(jnp.float32)
    norm_shifts = norm_shifts.astype(jnp.float32)
    normed, normal_one, inverse_one = layer_norm(inputs, norm_gains[0], norm_shifts[0])
    normed_low = normed.astype(jnp.bfloat16)
    qv_float = qv_bias.astype(jnp.float32)
    bias_full = jnp.concatenate(
        [qv_float[:model_width], jnp.zeros((model_width,), jnp.float32), qv_float[model_width:]]
    )
    qkv_low = (jnp.dot(normed_low, w_qkv, preferred_element_type=jnp.float32) + bias_full).astype(
        jnp.bfloat16
    )
    qkv_parts = qkv_low.reshape(windows, WIN, 3, HEADS, -1)
    scores = attention_scores(qkv_parts, position_bias, mask_add)
    row_max = jnp.max(scores, axis=-1, keepdims=True)
    shifted_exp = jnp.exp(scores - row_max)
    row_total = jnp.sum(shifted_exp, axis=-1, keepdims=True)
    soft_low = (shifted_exp / row_total).astype(jnp.bfloat16)
    log_total = row_max + jnp.log(row_total)
    attended = jnp.einsum(
        "whqk,wkhd->wqhd", soft_low, qkv_parts[:, :, 2], preferred_element_type=jnp.float32
    )
    attended_low = attended.reshape(inputs.shape).astype(jnp.bfloat16)
    middle = inputs + (
        jnp.dot(attended_low, w_proj, preferred_element_type=jnp.float32)
        + b_proj.astype(jnp.float32)
    )
    normed_two, normal_two, inverse_two = layer_norm(middle, norm_gains[1], norm_shifts[1])
    normed_two_low = normed_two.astype(jnp.bfloat16)
    hidden = jnp.dot(normed_two_low, w_up, preferred_element_type=jnp.float32) + b_up.astype(
        jnp.float32
    )
    activated_low = gelu_exact(hidden).astype(jnp.bfloat16)
    output = middle + (
        jnp.dot(activated_low, w_down, preferred_element_type=jnp.float32)
        + b_down.astype(jnp.float32)
    )
    kept_state = (
        normal_one,
        inverse_one,
        normed_low,
        qkv_low,
        log_total,
        attended_low,
        normal_two,
        inverse_two,
        normed_two_low,
        hidden,
        activated_low,
    )
    return (output, kept_state)


def block_backward(grad_out, weights, kept_state, position_bias, mask_add, bucket_table, windows):
    norm_gains, norm_shifts, w_qkv, qv_bias, w_proj, b_proj, w_up, b_up, w_down, b_down = weights
    (
        normal_one,
        inverse_one,
        normed_low,
        qkv_low,
        log_total,
        attended_low,
        normal_two,
        inverse_two,
        normed_two_low,
        hidden,
        activated_low,
    ) = kept_state
    model_width = grad_out.shape[1]
    norm_gains = norm_gains.astype(jnp.float32)
    grad_down_low = grad_out.astype(jnp.bfloat16)
    down_bias_grad = jnp.sum(grad_down_low, axis=0, dtype=jnp.float32)
    grad_act = jnp.einsum("rd,fd->rf", grad_down_low, w_down, preferred_element_type=jnp.float32)
    gelu_back = jax.vjp(gelu_exact, hidden)[1]
    grad_hidden_low = gelu_back(grad_act)[0].astype(jnp.bfloat16)
    up_bias_grad = jnp.sum(grad_hidden_low, axis=0, dtype=jnp.float32)
    grad_normed_two = jnp.einsum(
        "rf,df->rd", grad_hidden_low, w_up, preferred_element_type=jnp.float32
    )
    grad_mid_norm, gain_two_grad, shift_two_grad = norm_back(
        grad_normed_two, normal_two, inverse_two, norm_gains[1]
    )
    grad_middle = grad_out + grad_mid_norm
    grad_branch_low = grad_middle.astype(jnp.bfloat16)
    proj_bias_grad = jnp.sum(grad_branch_low, axis=0, dtype=jnp.float32)
    grad_attended_low = jnp.einsum(
        "rd,cd->rc", grad_branch_low, w_proj, preferred_element_type=jnp.float32
    ).astype(jnp.bfloat16)
    qkv_parts = qkv_low.reshape(windows, WIN, 3, HEADS, -1)
    scores = attention_scores(qkv_parts, position_bias, mask_add)
    soft = jnp.exp(scores - log_total)
    soft_low = soft.astype(jnp.bfloat16)
    grad_heads = grad_attended_low.reshape(windows, WIN, HEADS, -1)
    grad_value = jnp.einsum(
        "whqk,wqhd->wkhd", soft_low, grad_heads, preferred_element_type=jnp.float32
    )
    grad_soft = jnp.einsum(
        "wqhd,wkhd->whqk", grad_heads, qkv_parts[:, :, 2], preferred_element_type=jnp.float32
    )
    grad_scores_low = (
        soft * (grad_soft - jnp.sum(soft * grad_soft, axis=-1, keepdims=True))
    ).astype(jnp.bfloat16)
    head_scale = qkv_parts.shape[-1] ** (-0.5)
    grad_query = (
        jnp.einsum(
            "whqk,wkhd->wqhd",
            grad_scores_low,
            qkv_parts[:, :, 1],
            preferred_element_type=jnp.float32,
        )
        * head_scale
    )
    grad_key = (
        jnp.einsum(
            "whqk,wqhd->wkhd",
            grad_scores_low,
            qkv_parts[:, :, 0],
            preferred_element_type=jnp.float32,
        )
        * head_scale
    )
    score_sum = jnp.sum(grad_scores_low, axis=0, dtype=jnp.float32).reshape(HEADS, -1)
    table_grad = jnp.einsum("hn,nb->bh", score_sum, bucket_table, precision=lax.Precision.HIGHEST)
    grad_qkv_low = (
        jnp.stack([grad_query, grad_key, grad_value], axis=2)
        .reshape(qkv_low.shape)
        .astype(jnp.bfloat16)
    )
    column_sums = jnp.sum(grad_qkv_low, axis=0, dtype=jnp.float32)
    qv_grad = jnp.concatenate([column_sums[:model_width], column_sums[2 * model_width :]])
    grad_normed = jnp.einsum("re,de->rd", grad_qkv_low, w_qkv, preferred_element_type=jnp.float32)
    grad_in_norm, gain_one_grad, shift_one_grad = norm_back(
        grad_normed, normal_one, inverse_one, norm_gains[0]
    )
    grad_input = grad_middle + grad_in_norm
    grads = (
        jnp.stack([gain_one_grad, gain_two_grad]),
        jnp.stack([shift_one_grad, shift_two_grad]),
        qv_grad,
        proj_bias_grad,
        up_bias_grad,
        down_bias_grad,
    )
    pairs = (
        (normed_low, grad_qkv_low),
        (attended_low, grad_branch_low),
        (normed_two_low, grad_hidden_low),
        (activated_low, grad_down_low),
    )
    return (grad_input, grads, table_grad, pairs)


def shards(
    outer_count,
    peer_count,
    patches,
    out_grad,
    norm_gain,
    norm_shift,
    qkv_weight,
    qv_bias,
    rel_table,
    proj_weight,
    proj_bias,
    up_weight,
    up_bias,
    down_weight,
    down_bias,
    tile_perm,
    window_slot,
    mask_ids,
    bias_index,
):
    windows = patches.shape[0] // WIN
    model_width = patches.shape[1]
    depths = outer_count // 2
    devices = outer_count * peer_count
    capacity = (windows + peer_count - 1) // peer_count
    device_index = lax.axis_index(("dp", "fsdp"))
    total_windows = tile_perm.shape[0]
    slot_ids = jnp.arange(total_windows, dtype=jnp.int32)

    def one_hot_pick(keys, values):
        return jnp.sum(jnp.where(keys[None, :] == slot_ids[:, None], values[None, :], 0), axis=1)

    def look_up(values, at):
        hit = at[:, None] == jnp.arange(values.shape[0], dtype=jnp.int32)[None, :]
        return jnp.sum(jnp.where(hit, values[None, :], 0), axis=1)

    source_of = one_hot_pick(window_slot, look_up(window_slot, tile_perm))
    target_of = one_hot_pick(source_of, slot_ids)
    region_slot = one_hot_pick(window_slot, mask_ids)
    own_slots = device_index * windows + jnp.arange(windows, dtype=jnp.int32)

    def rank_of(slots, device_of):
        grid_view = device_of.reshape(-1, windows)
        earlier = jnp.arange(windows)[None, :] < jnp.arange(windows)[:, None]
        same_peer = grid_view[:, :, None] == grid_view[:, None, :]
        ranks = jnp.sum(same_peer & earlier[None], axis=2).reshape(-1)
        return look_up(ranks, slots)

    def peer_of(slots):
        return slots // windows % peer_count

    own_source = look_up(source_of, own_slots)
    own_target = look_up(target_of, own_slots)
    forward_send = peer_of(own_target) * capacity + rank_of(own_slots, target_of // windows)
    forward_take = peer_of(own_source) * capacity + rank_of(own_source, target_of // windows)
    backward_send = peer_of(own_source) * capacity + rank_of(own_slots, source_of // windows)
    backward_take = peer_of(own_target) * capacity + rank_of(own_target, source_of // windows)
    mask_add = region_mask(look_up(region_slot, own_slots))
    bucket_table = (
        bias_index.reshape(-1)[:, None] == jnp.arange(rel_table.shape[1], dtype=jnp.int32)[None, :]
    ).astype(jnp.float32)
    tables = rel_table.astype(jnp.float32)
    bias_one = jnp.einsum(
        "nb,bh->hn", bucket_table, tables[0], precision=lax.Precision.HIGHEST
    ).reshape(HEADS, WIN, WIN)
    bias_two = jnp.einsum(
        "nb,bh->hn", bucket_table, tables[1], precision=lax.Precision.HIGHEST
    ).reshape(HEADS, WIN, WIN)

    def choose(rows, at, count):
        spots = jnp.arange(count, dtype=jnp.int32)
        hit = spots[:, None] == at[None, :]
        return sum(
            jnp.where(hit[:, w][:, None, None], rows[w][None], jnp.zeros((), rows.dtype))
            for w in range(rows.shape[0])
        )

    def take(rows, at):
        hit = at[:, None] == jnp.arange(rows.shape[0], dtype=jnp.int32)[None, :]
        return sum(
            jnp.where(hit[:, w][:, None, None], rows[w][None], jnp.zeros((), rows.dtype))
            for w in range(rows.shape[0])
        )

    def move(rows_low, send, fetch):
        parts = rows_low.reshape(windows, WIN, model_width)
        sectioning = choose(parts, send, peer_count * capacity)
        arrived = lax.all_to_all(sectioning, "fsdp", split_axis=0, concat_axis=0, tiled=True)
        return take(arrived, fetch).reshape(rows_low.shape)

    def to_shifted(rows_low):
        return move(rows_low, forward_send, forward_take)

    def from_shifted(rows_low):
        return move(rows_low, backward_send, backward_take)

    vectors = (norm_gain, norm_shift, qv_bias, proj_bias, up_bias, down_bias)
    flat = jnp.concatenate([v.reshape(-1) for v in vectors])
    small = jnp.pad(flat, (0, -flat.shape[0] % 2048)).reshape(-1, 128)
    matrices = (qkv_weight, proj_weight, up_weight, down_weight)
    *fulls, small_full = gather_all(matrices, small, depths, peer_count)
    small_full = small_full.reshape(devices, -1)
    whole, offset = [], 0
    for v in vectors:
        size = v.size
        piece = small_full[:, offset : offset + size].reshape((devices,) + v.shape)
        offset += size
        piece = jnp.moveaxis(piece, 0, -2)
        whole.append(piece.reshape(v.shape[:-1] + (-1,)))

    def weights_of(layer):
        gains, shifts, qv, proj_b, up_b, down_b = [v[layer] for v in whole]
        w_qkv, w_proj, w_up, w_down = [
            fulls[4 * layer + k].reshape(-1, matrices[k].shape[-1]) for k in range(4)
        ]
        return (gains, shifts, w_qkv, qv, w_proj, proj_b, w_up, up_b, w_down, down_b)

    first_weights, second_weights = weights_of(0), weights_of(1)
    grad_two = to_shifted(out_grad)
    output_one, state_one = block_forward(
        patches.astype(jnp.float32), first_weights, bias_one, None, windows
    )
    second_input = to_shifted(output_one.astype(jnp.bfloat16))
    output_two, state_two = block_forward(
        second_input.astype(jnp.float32), second_weights, bias_two, mask_add, windows
    )
    block_out = from_shifted(output_two.astype(jnp.bfloat16))
    shapes = [m.shape[1:] for m in matrices]
    grad_input_two, grads_two, table_two, pairs_two = block_backward(
        grad_two.astype(jnp.float32), second_weights, state_two, bias_two, mask_add, bucket_table, windows
    )
    sums_two = sum_all(pairs_two, shapes, depths, peer_count, 1)
    grad_one = from_shifted(grad_input_two.astype(jnp.bfloat16))
    grad_patches, grads_one, table_one, pairs_one = block_backward(
        grad_one.astype(jnp.float32), first_weights, state_one, bias_one, None, bucket_table, windows
    )
    small_grads = []
    for one, two, v in zip(grads_one, grads_two, vectors):
        both = jnp.stack([one, two]).reshape(v.shape[:-1] + (devices, v.shape[-1]))
        small_grads.append(jnp.moveaxis(both, -2, 0).reshape(devices, -1))
    table = jnp.stack([table_one, table_two]).reshape(-1)
    table = jnp.pad(table, (0, -table.shape[0] % devices)).reshape(devices, -1)
    packed = jnp.concatenate(small_grads + [table], axis=1)
    width = packed.shape[1]
    packed = jnp.pad(packed, ((0, 0), (0, -width % 1024))).reshape(devices, -1, 128)
    *sums_one, small_all = sum_all(pairs_one, shapes, depths, peer_count, 2, packed)
    small_all = small_all.reshape(devices, -1)
    mine = lax.dynamic_index_in_dim(small_all, device_index, 0, keepdims=False)
    vector_grads, offset = [], 0
    for v in vectors:
        vector_grads.append(mine[offset : offset + v.size].reshape(v.shape))
        offset += v.size
    table_total = small_all[:, offset:width].reshape(-1)[: rel_table.size].reshape(rel_table.shape)
    grad_qkv, grad_proj, grad_up, grad_down = [
        jnp.stack([one, two]) for one, two in zip(sums_one, sums_two)
    ]
    return (
        block_out,
        grad_patches,
        vector_grads[0],
        vector_grads[1],
        grad_qkv,
        vector_grads[2],
        table_total,
        grad_proj,
        vector_grads[3],
        grad_up,
        vector_grads[4],
        grad_down,
        vector_grads[5],
    )


ROWS = 112
GAP, F_GAP = 2, 1
EARLY = {12: 1, 20: 9}
F_BUDGET, B_BUDGET = 5.0, 5.0
KEYS = 128
GROUP = 4
SCALE = 32**-0.5
LOW = jnp.bfloat16
WHOLE = jnp.float32
NEVER = -1e30


class Queue:
    def __init__(self, budget):
        self.pieces, self.budget = [], budget

    def add(self, tick, cost, work, *arguments):
        self.pieces.append((tick, cost, work, arguments))

    def run(self, tick, after, all_of_it=False):
        left = self.budget
        while self.pieces and self.pieces[0][0] <= tick and (left > 0 or all_of_it):
            left -= self.step(after)

    def step(self, after):
        _, cost, work, arguments = self.pieces.pop(0)
        work(*arguments)
        after()
        return cost


def row_loop(count, size, body):
    def step(i, carry):
        body(pl.multiple_of(i * size, size))
        return carry

    lax.fori_loop(0, count // size, step, 0)


def lane_mask(rows, head):
    lane = lax.broadcasted_iota(jnp.int32, (rows, 128), 1)
    return lane // 32 == head


def per_head(value):
    tall = jnp.concatenate([value, jnp.zeros((KEYS - ROWS, 128), value.dtype)], axis=0)
    zero = jnp.zeros((), value.dtype)
    return jnp.concatenate(
        [jnp.where(lane_mask(KEYS, head), tall, zero) for head in range(GROUP)], axis=0
    )


def dot(a, b, over=(1, 0)):
    return lax.dot_general(
        a, b, (((over[0],), (over[1],)), ((), ())), preferred_element_type=jnp.float32
    )


def normal_parts(block):
    mean = jnp.mean(block, axis=1, keepdims=True)
    centered = block - mean
    inverse = lax.rsqrt(jnp.mean(centered * centered, axis=1, keepdims=True) + epsilon)
    return centered * inverse, inverse


class Exchange:
    def __init__(self, place, out, into, send, receive, parts):
        self.place, self.out, self.into = place, out, into
        self.send, self.receive = send, receive
        self.width = out.shape[-1] // parts

    def columns(self, part):
        return slice(part * self.width, (part + 1) * self.width)

    def copy(self, part, step):
        place = self.place
        peer = lax.rem(place.peer + step, place.peers)
        return remote(
            self.out.at[peer, :, self.columns(part)],
            self.into.at[place.peer, :, self.columns(part)],
            self.send.at[part, step - 1],
            self.receive.at[part, step - 1],
            (place.depth * 2 + place.core, peer),
        )

    def give(self, part, tiles, chosen):
        columns = self.columns(part)
        for peer in range(self.place.peers):
            self.out[peer, :, columns] = tiles[chosen[peer], :, columns]
        self.into[self.place.peer, :, columns] = self.out[self.place.peer, :, columns]
        for step in range(1, self.place.peers):
            self.copy(part, step).start()

    def await_part(self, part):
        for step in range(1, self.place.peers):
            self.copy(part, step).wait_recv()

    def finish(self, parts):
        for part in range(parts):
            for step in range(1, self.place.peers):
                self.copy(part, step).wait_send()


class Gather:
    def __init__(self, place, chunks, early, blocks, fulls, sems):
        self.place, self.chunks, self.blocks, self.fulls = place, chunks, blocks, fulls
        (self.z_send, self.z_recv, self.r_send, self.r_recv, self.c_send, self.c_recv, self.own_sem) = sems
        self.half, self.cut = place.half, place.depths // 2
        self.early = early
        self.late = [i for i in range(len(chunks)) if i not in early]
        self.begun = 0
        self.gone = len(self.late) - 1 + F_GAP * self.half
        assert place.depths == 2 * self.half

    def whole_at(self, i):
        if i in self.early:
            return max(self.whole_at(i - 1), self.early[i] + 2 * self.half + 2 * self.place.depths - 1)
        return self.late.index(i) + F_GAP * self.half

    def full(self, i):
        array, layer, columns = self.chunks[i]
        return self.fulls[layer * len(self.blocks) + array]

    def view(self, i, depth, peer, rows=slice(None)):
        return self.full(i).at[depth, self.place.core, peer, rows, self.chunks[i][2]]

    def plane(self, i, depth):
        return self.full(i).at[depth, self.place.core, :, :, self.chunks[i][2]]

    def block(self, i, rows=slice(None)):
        array, layer, columns = self.chunks[i]
        return self.blocks[array].at[layer, rows, columns]

    def own(self, i):
        place = self.place
        return pltpu.make_async_copy(
            self.block(i), self.view(i, place.depth, place.peer), self.own_sem.at[i]
        )

    def deep(self, i, step):
        place = self.place
        if i in self.early:
            source = target = self.plane(i, place.depth)
        else:
            source, target = self.block(i), self.view(i, place.depth, place.peer)
        return remote(
            source,
            target,
            self.z_send.at[i, step - 1],
            self.z_recv.at[i, step - 1],
            place.deep(step),
        )

    def ring(self, i, step, way):
        place = self.place
        turn = 1 if way == 0 else -1
        peer = place.around(-turn * (step - 1))
        if i in self.early:
            rows = slice(None)
            if step == self.half:
                cut = self.full(i).shape[3] // 2
                rows = slice(0, cut) if way == 0 else slice(cut, 2 * cut)
            target = self.view(i, place.depth, peer, rows)
            source = self.block(i, rows) if step == 1 else target
        else:
            depths = slice(None)
            if step == self.half:
                depths = slice(0, self.cut) if way == 0 else slice(self.cut, place.depths)
            source = target = self.view(i, depths, peer)
        return remote(
            source,
            target,
            self.r_send.at[i, step - 1, way],
            self.r_recv.at[i, step - 1, way],
            place.neighbour(turn),
        )

    def across(self, i, slot):
        place = self.place
        if i in self.early:
            here = self.plane(i, place.at_depth(-slot))
        else:
            step = (slot + 1) // 2
            turn = 1 if slot % 2 else -1
            here = self.view(i, slice(None), place.around(-turn * step))
        return remote(here, here, self.c_send.at[i, slot], self.c_recv.at[i, slot], place.sibling())

    def begin(self, i):
        for step in range(1, self.place.depths):
            self.deep(i, step).start()
        self.own(i).start()

    def start_ring(self, i):
        self.ring(i, 1, 0).start()
        self.ring(i, 1, 1).start()

    def first(self, i):
        self.own(i).wait()
        for step in range(1, self.place.depths):
            self.deep(i, step).wait_recv()
        self.start_ring(i)
        self.across(i, 0).start()

    def later(self, i, step):
        self.ring(i, step, 0).wait_recv()
        self.ring(i, step, 1).wait_recv()
        early = i in self.early
        if step < self.half:
            self.ring(i, step + 1, 0).start()
            self.ring(i, step + 1, 1).start()
            if not early:
                self.across(i, 2 * step - 1).start()
                self.across(i, 2 * step).start()
        elif early:
            self.own(i).wait()
            self.across(i, 0).start()
        else:
            self.across(i, 2 * step - 1).start()

    def spread_planes(self, i):
        for step in range(1, self.place.depths):
            self.deep(i, step).wait_recv()
            self.across(i, step).start()

    def tick(self, tick):
        late = self.late
        for i, start in self.early.items():
            if tick == start:
                self.own(i).start()
                self.start_ring(i)
            step, odd = divmod(tick - start, 2)
            if 1 <= step <= self.half and not odd:
                self.later(i, step)
            if 0 <= step - self.half < self.place.depths - 1 and not odd:
                self.deep(i, step - self.half + 1).start()
            if tick == self.whole_at(i):
                self.spread_planes(i)
        while self.begun < min(len(late), tick + 1 + min(2 + (tick + 1) // 2, 6)):
            self.begin(late[self.begun])
            self.begun += 1
        if tick < len(late):
            self.first(late[tick])
        for step in range(1, self.half + 1):
            if 0 <= tick - step * F_GAP < len(late):
                self.later(late[tick - step * F_GAP], step)

    def await_across(self, i):
        for slot in range(2 * self.half):
            self.across(i, slot).wait_recv()

    def finish(self):
        for i in range(len(self.chunks)):
            for slot in range(2 * self.half):
                self.across(i, slot).wait_send()
            for step in range(1, self.place.depths):
                self.deep(i, step).wait_send()
            for step in range(1, self.half + 1):
                for way in range(2):
                    self.ring(i, step, way).wait_send()


def forward_kernel(chunks, depths, peers, *refs):
    r = types.SimpleNamespace()
    (
        r.w0, r.w1, r.w2, r.w3, r.small, r.x0, r.grads, r.tables, r.index, r.mask, r.forward_send,
        r.forward_take, r.backward_send, r.backward_take, r.f0, r.f1, r.f2, r.f3, r.f4, r.f5, r.f6, r.f7,
        r.moved_grad, r.result, r.left0, r.left1, r.left2, r.left3, r.low_x, r.middle, r.qkv, r.probs,
        r.slope, r.vec32, r.small_full, r.bias, r.x, r.x0w, r.normed, r.att, r.normed_two, r.act, r.mid,
        r.q_s, r.p_s, r.slope_s, r.wide_a, r.wide_b, r.total, r.sib_a, r.sib_b, r.turned, r.left_a, r.left_b,
        r.g_out, r.g_in, r.x_out, r.x_in, r.y_out, r.y_in, r.vec64, r.vec128, r.z_send, r.z_recv, r.r_send,
        r.r_recv, r.c_send, r.c_recv, r.own_sem, r.s_send, r.s_recv, r.s_own, r.load, r.save, r.swap_send,
        r.swap_recv, r.eg_send, r.eg_recv, r.ex_send, r.ex_recv, r.ey_send, r.ey_recv,
    ) = refs
    place = Place(depths, peers)
    gather = Gather(
        place,
        chunks,
        EARLY,
        (r.w0, r.w1, r.w2, r.w3),
        (r.f0, r.f1, r.f2, r.f3, r.f4, r.f5, r.f6, r.f7),
        (r.z_send, r.z_recv, r.r_send, r.r_recv, r.c_send, r.c_recv, r.own_sem),
    )
    spread = Spread(place, r.small, r.small_full, r.s_send, r.s_recv, r.s_own)
    eg = Exchange(place, r.g_out, r.g_in, r.eg_send, r.eg_recv, 1)
    ex = Exchange(place, r.x_out, r.x_in, r.ex_send, r.ex_recv, 4)
    ey = Exchange(place, r.y_out, r.y_in, r.ey_send, r.ey_recv, 4)
    windows = 2
    tall = windows * ROWS
    per_layer = len(chunks) // 2
    total = len(chunks)
    queue = Queue(F_BUDGET)
    saved, loaded, used = [], [], set()

    def spill(source, target):
        copy = pltpu.make_async_copy(source, target, r.save.at[len(saved)])
        copy.start()
        saved.append(copy)

    def staged(i):
        array, layer, columns = chunks[i]
        count = sum(1 for c in chunks[:i] if (c[0] == 3) == (array == 3))
        return (r.wide_b if array == 3 else r.wide_a).at[count % 2]

    def load(i):
        array, layer, columns = chunks[i]
        source = gather.fulls[layer * 4 + array].at[:, :, :, :, columns]
        return pltpu.make_async_copy(source, staged(i), r.load.at[i])

    def weight(i):
        assert i in loaded
        used.add(i)
        load(i).wait()
        value = staged(i)[...]
        return value.reshape(-1, value.shape[-1])

    def fetch(i):
        gather.await_across(i)
        load(i).start()

    def unpack():
        spread.wait()
        count = place.total
        row = lax.broadcasted_iota(jnp.int32, (count, 128), 0)
        lane = lax.broadcasted_iota(jnp.int32, (count, 128), 1)

        def spread_lanes(line, member, size):
            each = 128 // size
            found = jnp.zeros((count, 128), WHOLE)
            for turn in range(each):
                spot = (member + turn) % each
                rolled = line if turn == 0 else pltpu.roll(line, turn * size, 1)
                found += jnp.where((lane // size == spot) & (row % each == spot), rolled, 0.0)
            blocks = [
                jnp.sum(found[each * b : each * (b + 1)], axis=0, keepdims=True)
                for b in range(count // each)
            ]
            return jnp.concatenate(blocks, axis=1)

        for k in range(3):
            line = r.small_full[:, k, :].astype(WHOLE)
            for member in range(4):
                r.vec32[4 * k + member : 4 * k + member + 1, :] = spread_lanes(line, member, 32)
        line = r.small_full[:, 3, :].astype(WHOLE)
        for member in range(2):
            r.vec64[member : member + 1, :] = spread_lanes(line, member, 64)
        for member in range(2):
            line = r.small_full[:, 4 + member, :].astype(WHOLE)
            r.vec128[member : member + 1, :] = jnp.concatenate(
                [line[d : d + 1] for d in range(count)], axis=1
            )

    def bias_rows(start, stop):
        buckets = lax.broadcasted_iota(jnp.int32, (384, KEYS), 0)

        def step(i, carry):
            rows = pl.ds(pl.multiple_of(i * 8, 8), 8)
            lines = r.index[rows, :]
            found = []
            for row in range(8):
                hot = jnp.where(buckets == lines[row : row + 1], 1.0, 0.0).astype(LOW)
                found.append(dot(r.tables[...], hot))
            for k in range(2 * HEADS):
                layer, head, g = k // HEADS, k // 8 % GROUP, k % 8
                block = jnp.concatenate([one[k : k + 1] for one in found], axis=0)
                r.bias[layer, g, rows, head * KEYS : (head + 1) * KEYS] = block
            return carry

        lax.fori_loop(start, stop, step, 0)

    def vec(k):
        return r.vec32[k : k + 1, :]

    def pad_windows(source):
        flat = r.mid.at[1]
        flat[0 : windows * WIN, :] = source[...].astype(WHOLE)
        r.total[...] = jnp.zeros(r.total.shape, WHOLE)
        for w in range(windows):
            r.total[w * ROWS : w * ROWS + WIN, :] = flat[w * WIN : (w + 1) * WIN, :]

    def norm(source, target, layer, k):
        gain, shift = vec(2 * layer + k), vec(4 + 2 * layer + k)

        def body(start):
            rows = pl.ds(start, 32)
            parts, _ = normal_parts(source[rows, :].astype(WHOLE))
            target[rows, :] = (parts * gain + shift).astype(LOW)

        row_loop(tall, 32, body)

    def enter(layer):
        x = r.x.at[layer]
        if layer == 0:
            pad_windows(r.x0)
            x[...] = r.total[...].astype(LOW)
        else:
            for part in range(4):
                ex.await_part(part)
            for w in range(windows):
                x[w * ROWS : (w + 1) * ROWS, :] = r.x_in[r.forward_take[w]]
        spill(x, r.low_x.at[layer])
        norm(x, r.normed.at[layer], layer, 0)
        swap(layer, 0).start()

    def project(layer, i):
        part = i % per_layer
        found = dot(r.normed[layer], weight(i))
        if part != 1:
            half = part // 2
            found = found + r.vec64[layer : layer + 1, half * 1024 : (half + 1) * 1024]
        r.q_s[layer, :, part * 1024 : (part + 1) * 1024] = found.astype(LOW)

    def attend(layer, w):
        def step(g, carry):
            rows = slice(w * ROWS, (w + 1) * ROWS)
            start = pl.multiple_of(g * 128, 128)
            q = r.q_s[layer, rows, pl.ds(start, 128)]
            k = r.q_s[layer, rows, pl.ds(start + 1024, 128)]
            v = r.q_s[layer, rows, pl.ds(start + 2048, 128)]
            scores = dot(q, per_head(k), (1, 1)) * SCALE + r.bias[layer, g]
            heads = []
            for head in range(GROUP):
                one = scores[:, head * KEYS : (head + 1) * KEYS]
                if layer == 1:
                    one = one + r.mask[w]
                shifted = jnp.exp(one - jnp.max(one, axis=1, keepdims=True))
                heads.append(
                    (shifted * (1.0 / jnp.sum(shifted, axis=1, keepdims=True))).astype(LOW)
                )
            found = jnp.concatenate(heads, axis=1)
            r.p_s[layer, w * 8 + g] = found
            r.att[layer, rows, pl.ds(start, 128)] = dot(found, per_head(v)).astype(LOW)
            return carry

        lax.fori_loop(0, 8, step, 0)

    def branch(layer, i):
        spill(r.q_s.at[layer], r.qkv.at[layer])
        spill(r.p_s.at[layer], r.probs.at[layer])
        swap(layer, 1).start()
        found = dot(r.att[layer], weight(i)) + vec(8 + layer)
        r.mid[layer] = r.x[layer].astype(WHOLE) + found
        spill(r.mid.at[layer], r.middle.at[layer])

    def second_norm(layer):
        norm(r.mid.at[layer], r.normed_two.at[layer], layer, 1)
        swap(layer, 2).start()

    def widen(layer, i):
        part = i % per_layer - 4
        columns = slice(part * 1024, (part + 1) * 1024)
        r.total[...] = dot(r.normed_two[layer], weight(i)) + r.vec128[layer : layer + 1, columns]

        def body(start):
            rows = pl.ds(start, 16)
            v = r.total[rows, :]
            spread_half = 0.5 * (1.0 + lax.erf(v * (2.0**-0.5)))
            density = jnp.exp(-0.5 * v * v) * 0.3989422804014327
            r.act[layer, rows, columns] = (v * spread_half).astype(LOW)
            r.slope_s[layer, rows, columns] = (spread_half + v * density).astype(LOW)

        row_loop(tall, 16, body)
        if part == 3:
            spill(r.slope_s.at[layer], r.slope.at[layer])
            swap(layer, 3).start()

    def narrow(layer, i):
        part = i % per_layer - 8
        columns = slice(part * 256, (part + 1) * 256)
        found = dot(r.act[layer], weight(i)) + vec(10 + layer)[:, columns]
        found = (r.mid[layer, :, columns] + found).astype(LOW)
        for w in range(windows):
            r.x0w[w, :, columns] = found[w * ROWS : (w + 1) * ROWS]
        if layer == 0:
            ex.give(part, r.x0w, r.forward_send)
        else:
            ey.give(part, r.x0w, r.backward_send)

    sources = (r.normed, r.att, r.normed_two, r.act)

    def swap(layer, array):
        target = (r.sib_b if array == 3 else r.sib_a.at[array]).at[layer]
        return remote(
            sources[array].at[layer],
            target,
            r.swap_send.at[layer, array],
            r.swap_recv.at[layer, array],
            place.sibling(),
        )

    def turn(layer, array):
        swap(layer, array).wait_recv()
        mine = sources[array].at[layer]
        theirs = (r.sib_b if array == 3 else r.sib_a.at[array]).at[layer]
        unit = r.left0.shape[-2] // depths
        pad = jnp.zeros((256 - tall, 128), WHOLE)
        rounds = peers if array == 3 else 1
        for f in range(rounds):
            for depth in range(depths):
                start = (depth * 2 + place.core) * rounds * 128 + f * 128
                columns = pl.ds(pl.multiple_of(start, 128), 128)
                for side, ref in enumerate((mine, theirs)):
                    block = jnp.concatenate([ref[:, columns].astype(WHOLE), pad], axis=0)
                    r.turned[depth, :, side * 256 : (side + 1) * 256] = block.T
            for part in range(4):
                found = jnp.concatenate(
                    [r.turned[depth, part * unit : (part + 1) * unit] for depth in range(depths)],
                    axis=0,
                ).astype(LOW)
                if array == 3:
                    r.left_b[layer, part, f] = found
                else:
                    r.left_a[layer, array, part] = found
        if array == 3:
            spill(r.left_b.at[layer], r.left3.at[layer])
        else:
            spill(r.left_a.at[layer, array], (r.left0, r.left1, r.left2)[array].at[layer])

    place.greet()
    for i in range(2):
        gather.begin(gather.late[i])
        gather.begun += 1
    pad_windows(r.grads)
    for w in range(windows):
        r.x0w[w] = r.total[w * ROWS : (w + 1) * ROWS, :].astype(LOW)
    eg.give(0, r.x0w, r.forward_send)
    spread.start()

    def at(layer, part):
        return gather.whole_at(layer * per_layer + part) + 2

    queue.add(0, 5, bias_rows, 0, 7)
    queue.add(0, 5, bias_rows, 7, ROWS // 8)
    queue.add(2, 1, unpack)
    for layer in range(2):
        base = layer * per_layer
        queue.add(2 if layer == 0 else at(0, 11) + 1, 2, enter, layer)
        for part in range(3):
            queue.add(at(layer, part), 1.5, project, layer, base + part)
        for w in range(windows):
            queue.add(at(layer, 2), 5, attend, layer, w)
        queue.add(at(layer, 3), 1.5, branch, layer, base + 3)
        queue.add(at(layer, 3), 1.5, second_norm, layer)
        for part in range(4):
            queue.add(at(layer, 4 + part), 3.5, widen, layer, base + 4 + part)
            if part < 3:
                queue.add(at(layer, 4 + part), 1, turn, layer, part)
        for part in range(4):
            queue.add(at(layer, 8 + part), 1.5, narrow, layer, base + 8 + part)
        queue.add(at(layer, 11) + 1, 4, turn, layer, 3)

    last = gather.gone + 2
    state = types.SimpleNamespace(tick=0)

    def pump():
        while len(loaded) < total and gather.whole_at(len(loaded)) < state.tick:
            i = len(loaded)
            same = [j for j in range(i) if (chunks[j][0] == 3) == (chunks[i][0] == 3)]
            if len(same) > 1 and same[-2] not in used:
                break
            fetch(i)
            loaded.append(i)

    for tick in range(last + 1):
        state.tick = tick
        gather.tick(tick)
        pump()
        queue.run(tick, pump)
        if tick == 3:
            eg.await_part(0)
            for w in range(windows):
                r.moved_grad[w] = r.g_in[r.forward_take[w]]
    queue.run(last + total, pump, True)
    for part in range(4):
        ey.await_part(part)
    for w in range(windows):
        tile = r.y_in[r.backward_take[w]].astype(WHOLE)
        r.total[w * WIN : (w + 1) * WIN, :] = tile[:WIN]
    r.result[...] = r.total[0 : windows * WIN, :].astype(LOW)
    eg.finish(1)
    ex.finish(4)
    ey.finish(4)
    gather.finish()
    for layer in range(2):
        for array in range(4):
            swap(layer, array).wait_send()
    for copy in saved:
        copy.wait()


def forward_all(blocks, small, x0, grads, tables, index, mask, moves, depths, peers):
    count = depths * 2 * peers
    width = x0.shape[-1]
    hidden = blocks[2].shape[-1]
    tall = 2 * ROWS
    half = peers // 2
    chunks = []
    for layer in range(2):
        for array, block in enumerate(blocks):
            size = 256 if array == 3 else 1024
            for start in range(0, block.shape[-1], size):
                chunks.append((array, layer, slice(start, start + size)))
    total = len(chunks)
    unit = blocks[0].shape[1]
    dma = pltpu.SemaphoreType.DMA
    vmem = pltpu.VMEM
    smem = pl.BlockSpec(memory_space=pltpu.SMEM)
    shape = jax.ShapeDtypeStruct
    tiles = (2, ROWS, width)
    left = (2, peers, depths * unit, 512)
    outs = [shape((depths, 2, peers) + b.shape[1:], LOW) for _ in range(2) for b in blocks]
    outs += [shape(tiles, LOW), shape(x0.shape, LOW)]
    outs += [shape(left, LOW)] * 3 + [shape((2, 4) + left[1:], LOW)]
    outs += [
        shape((2, tall, width), LOW),
        shape((2, tall, width), WHOLE),
        shape((2, tall, 3 * width), LOW),
        shape((2, 16, ROWS, GROUP * KEYS), LOW),
        shape((2, tall, hidden), LOW),
        shape((12, width), WHOLE),
    ]
    exchange = (peers,) + tiles[1:]
    scratch = [
        vmem((count,) + small.shape, WHOLE),
        vmem((2, 8, ROWS, GROUP * KEYS), WHOLE),
        vmem((2, tall, width), LOW),
        vmem(tiles, LOW),
        vmem((2, tall, width), LOW),
        vmem((2, tall, width), LOW),
        vmem((2, tall, width), LOW),
        vmem((2, tall, hidden), LOW),
        vmem((2, tall, width), WHOLE),
        vmem((2, tall, 3 * width), LOW),
        vmem((2, 16, ROWS, GROUP * KEYS), LOW),
        vmem((2, tall, hidden), LOW),
        vmem((2, depths, 2, peers, unit, 1024), LOW),
        vmem((2, depths, 2, peers, 4 * unit, 256), LOW),
        vmem((tall, 1024), WHOLE),
        vmem((3, 2, tall, width), LOW),
        vmem((2, tall, hidden), LOW),
        vmem((depths, 128, 512), WHOLE),
        vmem((2, 3) + left[1:], LOW),
        vmem((2, 4) + left[1:], LOW),
        *[vmem(exchange, LOW)] * 6,
        vmem((2, 2 * width), WHOLE),
        vmem((2, hidden), WHOLE),
        dma((total, depths - 1)),
        dma((total, depths - 1)),
        dma((total, half, 2)),
        dma((total, half, 2)),
        dma((total, 2 * half)),
        dma((total, 2 * half)),
        dma((total,)),
        dma(()),
        dma(()),
        dma(()),
        dma((total,)),
        dma((32,)),
        dma((2, 4)),
        dma((2, 4)),
        dma((1, peers - 1)),
        dma((1, peers - 1)),
        *[dma((4, peers - 1))] * 4,
    ]
    return pl.pallas_call(
        functools.partial(forward_kernel, chunks, depths, peers),
        out_shape=outs,
        in_specs=[ANY] * 4 + [VMEM] * 6 + [smem] * 4,
        out_specs=[ANY] * 8 + [VMEM] * 2 + [ANY] * 9 + [VMEM],
        scratch_shapes=scratch,
        compiler_params=pltpu.CompilerParams(
            collective_id=3, has_side_effects=True, vmem_limit_bytes=63 * 2**20
        ),
    )(*blocks, small, x0, grads, tables, index, mask, *moves)


SLOTS, Z_SLOTS, Z_WAIT = 6, 9, 3
DEEP = {3: (1, 7), 7: (6, 13), 15: (14, 20)}


class Reduce:
    def __init__(self, place, plan, product, keep, bufs, sems):
        self.place, self.plan, self.product, self.keep = place, plan, product, keep
        (self.half_send, self.half_recv, self.full_send, self.full_recv, self.z_out, self.z_in, self.own_part) = bufs
        self.r_send, self.r_recv, self.z_send, self.z_recv = sems
        self.half = place.half
        self.rows = self.z_out.shape[2]
        self.cut = place.depths * self.rows // 2

    def ring(self, i, step, way):
        slot = i % SLOTS
        if step == 1:
            source, target = self.half_send.at[slot, way], self.half_recv.at[slot, way]
        else:
            source = self.full_send.at[slot, step - 2, way]
            target = self.full_recv.at[slot, step - 2, way]
        return remote(
            source,
            target,
            self.r_send.at[slot, step - 1, way],
            self.r_recv.at[slot, step - 1, way],
            self.place.neighbour(1 if way == 0 else -1),
        )

    def deep(self, i, step):
        slot = i % Z_SLOTS
        return remote(
            self.z_out.at[slot, self.place.at_depth(step)],
            self.z_in.at[slot, step - 1],
            self.z_send.at[slot, step - 1],
            self.z_recv.at[slot, step - 1],
            self.place.deep(step),
        )

    def sent(self, i):
        for way in range(2):
            for step in range(1, self.half + 1):
                self.ring(i, step, way).wait_send()

    def deep_sent(self, i):
        for step in range(1, self.place.depths):
            self.deep(i, step).wait_send()

    def first(self, i):
        if i >= SLOTS:
            self.sent(i - SLOTS)
        slot = i % SLOTS
        found = self.product(self.plan[i], self.place.around(self.half)).astype(LOW)
        for way in range(2):
            self.half_send[slot, way] = found[: self.cut] if way == 0 else found[self.cut :]
            self.ring(i, 1, way).start()

    def next_step(self, i, step):
        slot = i % SLOTS
        cut = self.cut
        for way in range(2):
            turn = 1 if way == 0 else -1
            found = self.product(self.plan[i], self.place.around(turn * (self.half - step + 1)))
            self.ring(i, step - 1, way).wait_recv()
            target = self.full_send.at[slot, step - 2, way]
            if step == 2:
                came = self.half_recv[slot, way].astype(WHOLE)
                low = found[:cut] + came if way == 0 else found[:cut]
                high = found[cut:] if way == 0 else found[cut:] + came
                target[:cut] = low.astype(LOW)
                target[cut:] = high.astype(LOW)
            else:
                came = self.full_recv[slot, step - 3, way].astype(WHOLE)
                target[...] = (found + came).astype(LOW)
            self.ring(i, step, way).start()

    def plane(self, i):
        slot, rows = i % SLOTS, self.rows
        z_slot = i % Z_SLOTS
        if i >= Z_SLOTS:
            self.deep_sent(i - Z_SLOTS)
        found = self.product(self.plan[i], self.place.peer)
        for way in range(2):
            self.ring(i, self.half, way).wait_recv()
            found += self.full_recv[slot, self.half - 2, way].astype(WHOLE)
        for depth in range(self.place.depths):
            piece = found[depth * rows : (depth + 1) * rows]
            self.z_out[z_slot, depth] = piece.astype(LOW)

            @pl.when(depth == self.place.depth)
            def _():
                self.own_part[z_slot] = piece

        for step in range(1, self.place.depths):
            self.deep(i, step).start()

    def finish(self, i):
        slot = i % Z_SLOTS
        found = self.own_part[slot]
        for step in range(1, self.place.depths):
            self.deep(i, step).wait_recv()
            found += self.z_in[slot, step - 1].astype(WHOLE)
        self.keep(self.plan[i], found)


SMALL_ROWS = 96


class DeepFirst:
    def __init__(self, reduce, bufs, sems):
        self.reduce, self.place = reduce, reduce.place
        (self.out, self.into, self.kept, self.half_send, self.half_recv, self.full_send, self.full_recv) = bufs
        self.z_send, self.z_recv, self.r_send, self.r_recv = sems
        self.rows = self.kept.shape[2]
        self.cut = self.rows // 2

    def deep(self, k, step):
        return remote(
            self.out.at[k, self.place.at_depth(step)],
            self.into.at[k, step - 1],
            self.z_send.at[k, step - 1],
            self.z_recv.at[k, step - 1],
            self.place.deep(step),
        )

    def ring(self, k, step, way):
        if step == 1:
            source, target = self.half_send.at[k, way], self.half_recv.at[k, way]
        else:
            source = self.full_send.at[k, step - 2, way]
            target = self.full_recv.at[k, step - 2, way]
        return remote(
            source,
            target,
            self.r_send.at[k, step - 1, way],
            self.r_recv.at[k, step - 1, way],
            self.place.neighbour(1 if way == 0 else -1),
        )

    def start(self, k, entry):
        rows = self.rows
        for peer in range(self.place.peers):
            found = self.reduce.product(entry, peer)
            for depth in range(self.place.depths):
                piece = found[depth * rows : (depth + 1) * rows]
                self.out[k, depth, peer * rows : (peer + 1) * rows] = piece.astype(LOW)

                @pl.when(depth == self.place.depth)
                def _():
                    self.kept[k, peer] = piece

    def turn(self, k):
        place, rows = self.place, self.rows
        for step in range(1, place.depths):
            self.deep(k, step).wait_recv()
        for peer in range(place.peers):
            found = self.kept[k, peer]
            for step in range(1, place.depths):
                found += self.into[k, step - 1, peer * rows : (peer + 1) * rows].astype(WHOLE)
            self.kept[k, peer] = found
        found = self.kept[k, place.around(place.half)].astype(LOW)
        for way in range(2):
            self.half_send[k, way] = found[: self.cut] if way == 0 else found[self.cut :]
            self.ring(k, 1, way).start()

    def next_step(self, k, step):
        place, cut = self.place, self.cut
        for way in range(2):
            turn = 1 if way == 0 else -1
            found = self.kept[k, place.around(turn * (place.half - step + 1))]
            self.ring(k, step - 1, way).wait_recv()
            if step == 2:
                came = self.half_recv[k, way].astype(WHOLE)
                low = found[:cut] + came if way == 0 else found[:cut]
                high = found[cut:] if way == 0 else found[cut:] + came
                found = jnp.concatenate([low, high], axis=0)
            else:
                found += self.full_recv[k, step - 3, way].astype(WHOLE)
            self.full_send[k, step - 2, way] = found.astype(LOW)
            self.ring(k, step, way).start()

    def finish(self, k, entry):
        place = self.place
        found = self.kept[k, place.peer]
        for way in range(2):
            self.ring(k, place.half, way).wait_recv()
            found += self.full_recv[k, place.half - 2, way].astype(WHOLE)
        self.reduce.keep(entry, found)

    def sent(self, k):
        for way in range(2):
            for step in range(1, self.place.half + 1):
                self.ring(k, step, way).wait_send()
        for step in range(1, self.place.depths):
            self.deep(k, step).wait_send()


def backward_kernel(everything, depths, peers, *refs):
    r = types.SimpleNamespace()
    (
        r.f0, r.f1, r.f2, r.f3, r.f4, r.f5, r.f6, r.f7, r.moved_grad, r.left0, r.left1, r.left2, r.left3,
        r.low_x, r.middle, r.qkv, r.probs, r.slope, r.vec32, r.index, r.backward_send, r.backward_take,
        r.patches_grad, r.g_qkv, r.g_proj, r.g_up, r.g_down, r.o_gain, r.o_shift, r.o_qv, r.o_proj, r.o_up, r.o_down, r.o_table, r.small_all, r.half_send, r.half_recv,
        r.full_send, r.full_recv, r.z_out, r.z_in, r.own_part, r.left_a, r.left_b, r.right0, r.right1,
        r.right2, r.right3, r.wide_a, r.wide_b, r.slope_s, r.p_s, r.q_s, r.mid, r.x, r.grad, r.att_grad,
        r.total, r.g_mid, r.score_sum, r.tiles, r.e_out, r.e_in, r.small_mine, r.small_in, r.small_sum,
        r.r_send, r.r_recv, r.z_send, r.z_recv, r.swap_send, r.swap_recv, r.credit, r.load, r.state, r.e_send,
        r.e_recv, r.a_send, r.a_recv, r.a_own, r.b_send, r.b_recv, r.b_own,
        r.d_out, r.d_in, r.d_kept, r.d_half_send, r.d_half_recv, r.d_full_send, r.d_full_recv,
        r.dz_send, r.dz_recv, r.dr_send, r.dr_recv,
    ) = refs
    place = Place(depths, peers)
    fulls = (r.f0, r.f1, r.f2, r.f3, r.f4, r.f5, r.f6, r.f7)
    rights = (r.right0, r.right1, r.right2, r.right3)
    outs = (r.g_qkv, r.g_proj, r.g_up, r.g_down)
    windows, tall = 2, 2 * ROWS
    plan = [entry for i, entry in enumerate(everything) if i not in DEEP]
    total = len(plan)
    queue = Queue(B_BUDGET)
    done, used, loaded = set(), set(), []
    unit = r.z_out.shape[2]

    def product(entry, peer):
        layer, array, part, start = entry
        left = r.left_b[layer, part, peer] if array == 3 else r.left_a[layer, array, peer]
        return dot(left, rights[array][:, start : start + WIDE])

    def keep(entry, found):
        layer, array, part, start = entry
        outs[array][layer, part * unit : (part + 1) * unit, start : start + WIDE] = found

    reduce = Reduce(
        place,
        plan,
        product,
        keep,
        (r.half_send, r.half_recv, r.full_send, r.full_recv, r.z_out, r.z_in, r.own_part),
        (r.r_send, r.r_recv, r.z_send, r.z_recv),
    )
    deep_first = DeepFirst(
        reduce,
        (r.d_out, r.d_in, r.d_kept, r.d_half_send, r.d_half_recv, r.d_full_send, r.d_full_recv),
        (r.dz_send, r.dz_recv, r.dr_send, r.dr_recv),
    )
    exchange = Exchange(place, r.e_out, r.e_in, r.e_send, r.e_recv, 1)

    order = [(layer, array, part) for layer in (1, 0) for array, parts in ((3, 4), (2, 4), (1, 1), (0, 3)) for part in range(parts)]

    def slot_of(k):
        down = order[k][1] == 3
        return sum(1 for o in order[:k] if (o[1] == 3) == down) % 2

    def load(k):
        layer, array, part = order[k]
        full = fulls[layer * 4 + array]
        if array == 3:
            return pltpu.make_async_copy(full.at[part], r.wide_b.at[slot_of(k)], r.load.at[k])
        source = full.at[:, :, :, :, part * 1024 : (part + 1) * 1024]
        return pltpu.make_async_copy(source, r.wide_a.at[slot_of(k)], r.load.at[k])

    def pump():
        while len(loaded) < len(order):
            k = len(loaded)
            same = [j for j in range(k) if (order[j][1] == 3) == (order[k][1] == 3)]
            if len(same) > 1 and same[-2] not in used:
                break
            load(k).start()
            loaded.append(k)

    def weight(layer, array, part):
        k = order.index((layer, array, part))
        assert k in loaded
        used.add(k)
        load(k).wait()
        value = (r.wide_b if array == 3 else r.wide_a)[slot_of(k)]
        return value.reshape(-1, value.shape[-1])

    def swap(layer, array, part):
        columns = slice(part * 1024, (part + 1) * 1024)
        right = rights[array]
        return remote(
            right.at[0:tall, columns],
            right.at[256 : 256 + tall, columns],
            r.swap_send.at[array, part],
            r.swap_recv.at[array, part],
            place.sibling(),
        )

    def free(array):
        pl.semaphore_signal(r.credit.at[array], inc=1, device_id=place.sibling(), device_id_type=MESH)

    def hand_over(layer, array, part):
        if layer == 0 and part == 0:
            pl.semaphore_wait(r.credit.at[array], 1)
        swap(layer, array, part).start()

    def ready(layer, array, part):
        if layer == 0:
            assert (array, "freed") in done
            swap(1, array, part).wait_send()

    def put(layer, row, vector):
        for k in range(vector.shape[1] // 128):
            line = layer * SMALL_ROWS + row + k
            r.small_mine[line : line + 1, :] = vector[:, k * 128 : (k + 1) * 128]

    def column_sums(layer, row, value):
        ones = jnp.ones((8, tall), LOW)
        put(layer, row, dot(ones, value)[:1])

    states = ((r.slope_s, r.slope), (r.p_s, r.probs), (r.q_s, r.qkv), (r.mid, r.middle), (r.x, r.low_x))

    def state_copy(layer, k):
        here, there = states[k]
        return pltpu.make_async_copy(there.at[layer], here, r.state.at[layer, k])

    def left_copies(layer):
        sources = (r.left0, r.left1, r.left2)
        found = [
            pltpu.make_async_copy(
                sources[k].at[layer], r.left_a.at[layer, k], r.state.at[layer, 5 + k]
            )
            for k in range(3)
        ]
        return found + [
            pltpu.make_async_copy(r.left3.at[layer], r.left_b.at[layer], r.state.at[layer, 8])
        ]

    def vec(k):
        return r.vec32[k : k + 1, :]

    def take_grad(layer):
        if layer == 1:
            for w in range(windows):
                r.grad[w * ROWS : (w + 1) * ROWS, :] = r.moved_grad[w]
        else:
            exchange.await_part(0)
            for w in range(windows):
                r.grad[w * ROWS : (w + 1) * ROWS, :] = r.e_in[r.backward_take[w]]
        ready(layer, 3, 0)
        value = r.grad[...]
        r.right3[0:tall, :] = value
        hand_over(layer, 3, 0)
        column_sums(layer, 88, value)

    def hidden_grad(layer, part):
        if part == 0:
            state_copy(layer, 0).wait()
        columns = slice(part * 1024, (part + 1) * 1024)
        ready(layer, 2, part)
        found = dot(r.grad[...], weight(layer, 3, part), (1, 1))
        low = (found * r.slope_s[:, columns].astype(WHOLE)).astype(LOW)
        r.right2[0:tall, columns] = low
        hand_over(layer, 2, part)
        column_sums(layer, 56 + 8 * part, low)
        if part == 3 and layer == 1:
            state_copy(0, 0).start()

    def add_back(layer, array, part, columns):
        found = dot(rights[array][0:tall, columns], weight(layer, array, part), (1, 1))
        if part == 0:
            r.total[...] = found
        else:
            r.total[...] += found

    def up_back(layer, part):
        add_back(layer, 2, part, slice(part * 1024, (part + 1) * 1024))

    def norm_loop(source, layer, k, finish):
        gain = vec(2 * layer + k)

        def body(i, carry):
            start = pl.multiple_of(i * 16, 16)
            rows = pl.ds(start, 16)
            parts, inverse = normal_parts(source[rows, :].astype(WHOLE))
            g = r.total[rows, :]
            e = g * gain
            mean = jnp.mean(e, axis=1, keepdims=True)
            along = jnp.mean(e * parts, axis=1, keepdims=True)
            finish(rows, inverse * (e - mean - parts * along))
            by_gain, by_shift = carry
            return (
                by_gain + jnp.sum(g * parts, axis=0, keepdims=True),
                by_shift + jnp.sum(g, axis=0, keepdims=True),
            )

        zero = jnp.zeros((1, source.shape[-1]), WHOLE)
        by_gain, by_shift = lax.fori_loop(0, tall // 16, body, (zero, zero))
        put(layer, 8 * k, by_gain)
        put(layer, 16 + 8 * k, by_shift)

    def middle_grad(layer):
        state_copy(layer, 3).wait()
        ready(layer, 1, 0)

        def finish(rows, found):
            whole = r.grad[rows, :].astype(WHOLE) + found
            r.g_mid[rows, :] = whole
            r.right1[rows, :] = whole.astype(LOW)

        norm_loop(r.mid, layer, 1, finish)
        hand_over(layer, 1, 0)
        column_sums(layer, 48, r.right1[0:tall, :])
        if layer == 1:
            state_copy(0, 3).start()

    def attended_grad(layer):
        r.att_grad[...] = dot(r.right1[0:tall, :], weight(layer, 1, 0), (1, 1)).astype(LOW)

    def fold(value):
        return sum(
            jnp.where(lane_mask(KEYS, head), value[head * KEYS : (head + 1) * KEYS], 0.0)
            for head in range(GROUP)
        )[:ROWS]

    def attend_back(layer, w):
        if w == 0:
            state_copy(layer, 1).wait()
            state_copy(layer, 2).wait()
            for part in range(3):
                ready(layer, 0, part)

        def step(g, carry):
            rows = slice(w * ROWS, (w + 1) * ROWS)
            start = pl.multiple_of(g * 128, 128)
            q = r.q_s[rows, pl.ds(start, 128)]
            k = r.q_s[rows, pl.ds(start + 1024, 128)]
            v = r.q_s[rows, pl.ds(start + 2048, 128)]
            out_grad = r.att_grad[rows, pl.ds(start, 128)]
            low = r.p_s[w * 8 + g]
            prob_grad = dot(out_grad, per_head(v), (1, 1))
            pieces = []
            for head in range(GROUP):
                one = slice(head * KEYS, (head + 1) * KEYS)
                probs = low[:, one].astype(WHOLE)
                weighed = probs * prob_grad[:, one]
                pieces.append(weighed - probs * jnp.sum(weighed, axis=1, keepdims=True))
            score_grad = jnp.concatenate(pieces, axis=1).astype(LOW)
            for head in range(GROUP):
                lines = pl.ds(pl.multiple_of((head * 8 + g) * ROWS, 8), ROWS)
                one = score_grad[:, head * KEYS : (head + 1) * KEYS].astype(WHOLE)
                r.score_sum[lines, :] = one if w == 0 else r.score_sum[lines, :] + one
            by_query = dot(score_grad, per_head(k)) * SCALE
            by_key = fold(dot(score_grad, q, (0, 0))) * SCALE
            by_value = fold(dot(low, out_grad, (0, 0)))
            for part, found in enumerate((by_query, by_key, by_value)):
                r.right0[rows, pl.ds(start + part * 1024, 128)] = found.astype(LOW)
            return carry

        lax.fori_loop(0, 8, step, 0)
        if w == windows - 1:
            for part in range(3):
                hand_over(layer, 0, part)
            column_sums(layer, 32, r.right0[0:tall, 0:1024])
            column_sums(layer, 40, r.right0[0:tall, 2048:3072])
            if layer == 1:
                state_copy(0, 1).start()
                state_copy(0, 2).start()

    def qkv_back(layer, part):
        add_back(layer, 0, part, slice(part * 1024, (part + 1) * 1024))

    def input_grad(layer):
        state_copy(layer, 4).wait()

        def finish(rows, found):
            r.g_mid[rows, :] = r.g_mid[rows, :] + found

        norm_loop(r.x, layer, 0, finish)
        if layer == 1:
            state_copy(0, 4).start()
            for w in range(windows):
                r.tiles[w] = r.g_mid[w * ROWS : (w + 1) * ROWS, :].astype(LOW)
            exchange.give(0, r.tiles, r.backward_send)
        else:
            for w in range(windows):
                r.patches_grad[w * WIN : (w + 1) * WIN, :] = r.g_mid[w * ROWS : w * ROWS + WIN, :]

    def table_grad(layer):
        buckets = lax.broadcasted_iota(jnp.int32, (384, KEYS), 0)

        def step(i, found):
            start = pl.multiple_of(i * 8, 8)
            lines = r.index[pl.ds(start, 8), :]
            values, hots = [], []
            for row in range(8):
                hots.append(jnp.where(buckets == lines[row : row + 1], 1.0, 0.0).astype(LOW))
                values.append(r.score_sum[pl.ds(start + row, HEADS, stride=ROWS), :])
            value = jnp.concatenate(values, axis=1)
            high = value.astype(LOW)
            rest = (value - high.astype(WHOLE)).astype(LOW)
            both = jnp.concatenate([high, rest], axis=0)
            return found + dot(both, jnp.concatenate(hots, axis=1), (1, 1))

        found = lax.fori_loop(0, 13, step, jnp.zeros((64, 384), WHOLE))
        found = found[:32] + found[32:]
        base = 2 * SMALL_ROWS + layer * SMALL_ROWS
        for k in range(3):
            r.small_mine[base + 32 * k : base + 32 * (k + 1), :] = found[:, 128 * k : 128 * (k + 1)]

    def send_small():
        def step(k, carry):
            outer, peer = place.other(k)
            remote(
                r.small_mine.at[pl.ds(pl.multiple_of((outer * peers + peer) * 16, 16), 16)],
                r.small_in.at[place.index],
                r.a_send,
                r.a_recv,
                (outer, peer),
            ).start()
            return carry

        lax.fori_loop(1, place.total, step, 0)
        own_small().start()

    def own_small():
        mine = r.small_mine.at[pl.ds(pl.multiple_of(place.index * 16, 16), 16)]
        return pltpu.make_async_copy(mine, r.small_in.at[place.index], r.a_own)

    spread = Spread(place, r.small_sum, r.small_all, r.b_send, r.b_recv, r.b_own)

    def sum_small():
        rest = r.small_in.at[pl.ds(0, place.total - 1)]
        both = remote(rest, rest, r.a_send, r.a_recv, place.other(1))
        both.wait_send()
        both.wait_recv()
        own_small().wait()
        r.small_sum[...] = jnp.sum(r.small_in[...], axis=0)
        spread.start()

    def own_vectors():
        places = (
            (0, 4, r.o_gain, 0),
            (8, 4, r.o_gain, 1),
            (16, 4, r.o_shift, 0),
            (24, 4, r.o_shift, 1),
            (32, 2, r.o_qv, None),
            (48, 4, r.o_proj, None),
            (56, 1, r.o_up, None),
            (88, 4, r.o_down, None),
        )
        for layer in range(2):
            for row, each, target, k in places:
                line = layer * SMALL_ROWS + row + lax.div(place.index, each)
                found = r.small_all[lax.div(line, 16), pl.ds(lax.rem(line, 16), 1), :]
                back = lax.rem(each - lax.rem(place.index, each), each) * (128 // each)
                found = pltpu.roll(found, back, 1)[:, : 128 // each]
                if k is None:
                    target[layer : layer + 1, :] = found
                else:
                    target[layer, k : k + 1, :] = found
            first = (2 + layer) * SMALL_ROWS // 16
            parts = [
                r.small_all[first + 2 * k : first + 2 * k + 2].reshape(HEADS, 128) for k in range(3)
            ]
            rows = jnp.concatenate(parts, axis=1)
            order = [rows[h % GROUP * 8 + h // GROUP :][:1] for h in range(HEADS)]
            order.append(jnp.zeros((128 - HEADS, 384), WHOLE))
            turned = jnp.concatenate(order, axis=0).T
            r.o_table[layer] = turned[: r.o_table.shape[1], :HEADS]

    def note(work, *what):
        work(*what)
        done.add((work.__name__, *what))

    def add(tick, cost, work, *what):
        queue.add(tick, cost, note, work, *what)

    for k in range(5):
        state_copy(1, k).start()
    for layer in (1, 0):
        for copy in left_copies(layer):
            copy.start()
    for right in rights:
        zero = jnp.zeros((256 - tall, right.shape[1]), LOW)
        right[tall:256, :] = zero
        right[256 + tall : 512, :] = zero
    r.small_mine[...] = jnp.zeros(r.small_mine.shape, WHOLE)
    pump()
    place.greet()

    add(0, 1, take_grad, 1)
    last_use = {
        array: max(i for i, p in enumerate(plan) if p[0] == 1 and p[1] == array) for array in range(4)
    }
    after = {array: last_use[array] + GAP * place.half for array in range(4)}
    for layer in (1, 0):
        late = 9 if layer == 0 else 0
        if layer == 0:
            add(0, 5, table_grad, 1)
            add(late, 1, take_grad, 0)
        for part in range(4):
            add(late and after[2], 2, hidden_grad, layer, part)
        for part in range(4):
            add(late, 2, up_back, layer, part)
        add(late and after[1], 3, middle_grad, layer)
        add(late, 1.5, attended_grad, layer)
        for w in range(windows):
            add(late and after[0], 7, attend_back, layer, w)
        for part in range(3):
            add(late, 1.5, qkv_back, layer, part)
        add(late, 3, input_grad, layer)
    add(0, 5, table_grad, 0)
    add(0, 1, send_small)

    needs = {3: ("take_grad",), 2: ("hidden_grad",), 1: ("middle_grad",), 0: ("attend_back",)}

    def wanted(entry):
        layer, array, part, start = entry
        what = needs[array] + (layer,)
        if array == 2:
            what += (start // 1024,)
        if array == 0:
            what += (windows - 1,)
        return what

    received, lefts_in = set(), set()
    half = place.half

    def prepare(entry):
        layer, array, part, start = entry
        while wanted(entry) not in done:
            queue.step(pump)
        if layer not in lefts_in:
            lefts_in.add(layer)
            for copy in left_copies(layer):
                copy.wait()
        key = (layer, array, start // 1024)
        if key not in received:
            received.add(key)
            swap(*key).wait_recv()

    for tick in range(total + GAP * half + Z_WAIT):
        if tick < total:
            prepare(plan[tick])
            reduce.first(tick)
        for k, (i, (begin, middle)) in enumerate(DEEP.items()):
            assert place.depths == 4 and half == 2
            entry, slot = everything[i], k % 2
            if tick == begin:
                prepare(entry)
                if k >= 2:
                    deep_first.sent(slot)
                deep_first.start(slot, entry)
            if tick in (begin, begin + 2, begin + 4):
                deep_first.deep(slot, (tick - begin) // 2 + 1).start()
            if tick == middle:
                deep_first.turn(slot)
            if tick == middle + 3:
                deep_first.next_step(slot, 2)
            if tick == middle + 6:
                deep_first.finish(slot, entry)
        for step in range(2, half + 1):
            i = tick - GAP * (step - 1)
            if 0 <= i < total:
                reduce.next_step(i, step)
        i = tick - GAP * half
        if 0 <= i < total:
            reduce.plane(i)
            for array, last in last_use.items():
                if i == last:
                    free(array)
                    done.add((array, "freed"))
        i = tick - GAP * half - Z_WAIT
        if 0 <= i < total:
            reduce.finish(i)
        queue.run(tick, pump)
        if ("send_small",) in done and ("sum_small",) not in done and tick >= total - 1:
            note(sum_small)
    assert not queue.pieces
    if ("sum_small",) not in done:
        sum_small()
    spread.wait()
    own_vectors()
    exchange.finish(1)
    for array, parts in ((3, 1), (2, 4), (1, 1), (0, 3)):
        for part in range(parts):
            swap(0, array, part).wait_send()
    for i in range(total - SLOTS, total):
        reduce.sent(i)
    for i in range(total - Z_SLOTS, total):
        reduce.deep_sent(i)
    for k in range(2):
        deep_first.sent(k)


def backward_all(fulls, state, index, moves, depths, peers, buckets):
    moved_grad, left0, left1, left2, left3, low_x, middle, qkv, probs, slope, vec32 = state
    count = depths * 2 * peers
    tall, width = low_x.shape[1:]
    hidden = slope.shape[-1]
    unit = width // count
    half = peers // 2
    plan = []
    for layer in (1, 0):
        plan += [(layer, 3, part, 0) for part in range(4)]
        plan += [(layer, 2, 0, start) for start in range(0, hidden, WIDE)]
        plan += [(layer, 1, 0, 0)]
        plan += [(layer, 0, 0, start) for start in range(0, 3 * width, WIDE)]
    dma = pltpu.SemaphoreType.DMA
    vmem = pltpu.VMEM
    smem = pl.BlockSpec(memory_space=pltpu.SMEM)
    shape = jax.ShapeDtypeStruct
    flat = depths * unit
    outs = [
        shape((2 * WIN, width), WHOLE),
        shape((2, unit, 3 * width), WHOLE),
        shape((2, unit, width), WHOLE),
        shape((2, unit, hidden), WHOLE),
        shape((2, 4 * unit, width), WHOLE),
        shape((2, 2, unit), WHOLE),
        shape((2, 2, unit), WHOLE),
        shape((2, 2 * unit), WHOLE),
        shape((2, unit), WHOLE),
        shape((2, 4 * unit), WHOLE),
        shape((2, unit), WHOLE),
        shape((2, buckets, HEADS), WHOLE),
    ]
    scratch = [
        vmem((count, 16, 128), WHOLE),
        vmem((SLOTS, 2, flat // 2, WIDE), LOW),
        vmem((SLOTS, 2, flat // 2, WIDE), LOW),
        vmem((SLOTS, half - 1, 2, flat, WIDE), LOW),
        vmem((SLOTS, half - 1, 2, flat, WIDE), LOW),
        vmem((Z_SLOTS, depths, unit, WIDE), LOW),
        vmem((Z_SLOTS, depths - 1, unit, WIDE), LOW),
        vmem((Z_SLOTS, unit, WIDE), WHOLE),
        vmem((2, 3) + left0.shape[1:], LOW),
        vmem(left3.shape, LOW),
        vmem((512, 3 * width), LOW),
        vmem((512, width), LOW),
        vmem((512, hidden), LOW),
        vmem((512, width), LOW),
        vmem((2, depths, 2, peers, unit, 1024), LOW),
        vmem((2, 2, peers, 4 * unit, width), LOW),
        vmem((tall, hidden), LOW),
        vmem(probs.shape[1:], LOW),
        vmem((tall, 3 * width), LOW),
        vmem((tall, width), WHOLE),
        vmem((tall, width), LOW),
        vmem((tall, width), LOW),
        vmem((tall, width), LOW),
        vmem((tall, width), WHOLE),
        vmem((tall, width), WHOLE),
        vmem((HEADS * ROWS, KEYS), WHOLE),
        vmem((2, ROWS, width), LOW),
        vmem((peers, ROWS, width), LOW),
        vmem((peers, ROWS, width), LOW),
        vmem((count * 16, 128), WHOLE),
        vmem((count, 16, 128), WHOLE),
        vmem((16, 128), WHOLE),
        dma((SLOTS, half, 2)),
        dma((SLOTS, half, 2)),
        dma((Z_SLOTS, depths - 1)),
        dma((Z_SLOTS, depths - 1)),
        dma((4, 4)),
        dma((4, 4)),
        pltpu.SemaphoreType.REGULAR((4,)),
        dma((24,)),
        dma((2, 9)),
        dma((1, peers - 1)),
        dma((1, peers - 1)),
        *[dma(())] * 6,
        vmem((2, depths, peers * unit, WIDE), LOW),
        vmem((2, depths - 1, peers * unit, WIDE), LOW),
        vmem((2, peers, unit, WIDE), WHOLE),
        vmem((2, 2, unit // 2, WIDE), LOW),
        vmem((2, 2, unit // 2, WIDE), LOW),
        vmem((2, half - 1, 2, unit, WIDE), LOW),
        vmem((2, half - 1, 2, unit, WIDE), LOW),
        dma((2, depths - 1)),
        dma((2, depths - 1)),
        dma((2, half, 2)),
        dma((2, half, 2)),
    ]
    return pl.pallas_call(
        functools.partial(backward_kernel, plan, depths, peers),
        out_shape=outs,
        in_specs=[ANY] * 8 + [VMEM] + [ANY] * 9 + [VMEM] * 2 + [smem] * 2,
        out_specs=[VMEM] * 12,
        scratch_shapes=scratch,
        compiler_params=pltpu.CompilerParams(
            collective_id=4, has_side_effects=True, vmem_limit_bytes=63 * 2**20
        ),
    )(*fulls, *state, index, *moves)


def copy_kernel(count, *refs):
    sources, targets, held = refs[:count], refs[count : 2 * count], refs[2 * count : 3 * count]
    came, went = refs[3 * count :]
    loads = [pltpu.make_async_copy(sources[k], held[k], came.at[k]) for k in range(count)]
    stores = [pltpu.make_async_copy(held[k], targets[k], went.at[k]) for k in range(count)]
    for copy in loads:
        copy.start()
    for load, store in zip(loads, stores):
        load.wait()
        store.start()
    for copy in stores:
        copy.wait()


def copy_out(arrays):
    count = len(arrays)
    return pl.pallas_call(
        functools.partial(copy_kernel, count),
        out_shape=[jax.ShapeDtypeStruct(a.shape, a.dtype) for a in arrays],
        in_specs=[ANY] * count,
        out_specs=[ANY] * count,
        scratch_shapes=[
            *[pltpu.VMEM(a.shape, a.dtype) for a in arrays],
            pltpu.SemaphoreType.DMA((count,)),
            pltpu.SemaphoreType.DMA((count,)),
        ],
        compiler_params=pltpu.CompilerParams(vmem_limit_bytes=63 * 2**20),
    )(*arrays)


def whole_shards(
    outer_count,
    peer_count,
    patches,
    out_grad,
    norm_gain,
    norm_shift,
    qkv_weight,
    qv_bias,
    rel_table,
    proj_weight,
    proj_bias,
    up_weight,
    up_bias,
    down_weight,
    down_bias,
    tile_perm,
    window_slot,
    mask_ids,
    bias_index,
):
    windows = patches.shape[0] // WIN
    width = patches.shape[1]
    depths = outer_count // 2
    device_index = lax.axis_index(("dp", "fsdp"))
    slot_ids = jnp.arange(tile_perm.shape[0], dtype=jnp.int32)

    def one_hot_pick(keys, values):
        return jnp.sum(jnp.where(keys[None, :] == slot_ids[:, None], values[None, :], 0), axis=1)

    def look_up(values, at):
        hit = at[:, None] == jnp.arange(values.shape[0], dtype=jnp.int32)[None, :]
        return jnp.sum(jnp.where(hit, values[None, :], 0), axis=1)

    source_of = one_hot_pick(window_slot, look_up(window_slot, tile_perm))
    target_of = one_hot_pick(source_of, slot_ids)
    region_slot = one_hot_pick(window_slot, mask_ids)
    own_slots = device_index * windows + jnp.arange(windows, dtype=jnp.int32)
    forward_take = look_up(source_of, own_slots) // windows % peer_count
    backward_take = look_up(target_of, own_slots) // windows % peer_count
    spots = jnp.arange(peer_count, dtype=jnp.int32)
    numbers = jnp.arange(windows, dtype=jnp.int32)

    def window_for(peers):
        return jnp.sum(jnp.where(peers[None, :] == spots[:, None], numbers[None, :], 0), axis=1)

    moves = (window_for(backward_take), forward_take, window_for(forward_take), backward_take)
    mask = region_mask(look_up(region_slot, own_slots))[:, 0]
    mask = jnp.pad(mask, ((0, 0), (0, ROWS - WIN), (0, KEYS - WIN)))
    index = jnp.pad(
        bias_index, ((0, ROWS - WIN), (0, KEYS - WIN)), constant_values=rel_table.shape[1]
    )
    tables = rel_table.reshape(2, -1, HEADS // GROUP, GROUP).transpose(0, 3, 2, 1)
    tables = tables.reshape(2 * HEADS, -1)
    tables = jnp.pad(tables, ((0, 0), (0, 384 - tables.shape[1])), constant_values=NEVER)

    each = width // (outer_count * peer_count)
    small = jnp.concatenate(
        [
            norm_gain.reshape(1, 4 * each),
            norm_shift.reshape(1, 4 * each),
            jnp.concatenate([proj_bias, down_bias], axis=0).reshape(1, 4 * each),
            qv_bias.reshape(1, 4 * each),
            up_bias,
            jnp.zeros((2, 4 * each), LOW),
        ],
        axis=0,
    ).astype(jnp.float32)

    found = forward_all(
        (qkv_weight, proj_weight, up_weight, down_weight),
        small,
        patches,
        out_grad,
        tables,
        index,
        mask,
        moves,
        depths,
        peer_count,
    )
    fulls, moved_grad, result, state = found[:8], found[8], found[9], found[10:]
    (
        grad_patches,
        grad_qkv,
        grad_proj,
        grad_up,
        grad_down,
        gain_grad,
        shift_grad,
        qv_grad,
        proj_b_grad,
        up_b_grad,
        down_b_grad,
        table,
    ) = backward_all(
        fulls, (moved_grad, *state), index, moves[2:], depths, peer_count, rel_table.shape[1]
    )
    results = (
        result,
        grad_patches,
        gain_grad,
        shift_grad,
        grad_qkv,
        qv_grad,
        table,
        grad_proj,
        proj_b_grad,
        grad_up,
        up_b_grad,
        grad_down,
        down_b_grad,
    )
    return tuple(copy_out(results))


def solution(mesh):
    outer_count, peer_count = mesh.shape["dp"], mesh.shape["fsdp"]
    fused = outer_count == 8 and peer_count == 4
    placed = (
        P(("dp", "fsdp"), None),
        P(("dp", "fsdp"), None),
        P(None, None, ("dp", "fsdp")),
        P(None, None, ("dp", "fsdp")),
        P(None, ("dp", "fsdp"), None),
        P(None, ("dp", "fsdp")),
        P(),
        P(None, ("dp", "fsdp"), None),
        P(None, ("dp", "fsdp")),
        P(None, ("dp", "fsdp"), None),
        P(None, ("dp", "fsdp")),
        P(None, ("dp", "fsdp"), None),
        P(None, ("dp", "fsdp")),
        P(),
        P(),
        P(),
        P(),
    )
    return jax.shard_map(
        functools.partial(whole_shards if fused else shards, outer_count, peer_count),
        mesh=mesh,
        in_specs=placed,
        out_specs=(
            P(("dp", "fsdp"), None),
            P(("dp", "fsdp"), None),
            P(None, None, ("dp", "fsdp")),
            P(None, None, ("dp", "fsdp")),
            P(None, ("dp", "fsdp"), None),
            P(None, ("dp", "fsdp")),
            P(),
            P(None, ("dp", "fsdp"), None),
            P(None, ("dp", "fsdp")),
            P(None, ("dp", "fsdp"), None),
            P(None, ("dp", "fsdp")),
            P(None, ("dp", "fsdp"), None),
            P(None, ("dp", "fsdp")),
        ),
        check_vma=False,
    )
```

```python
import functools
import types

import jax
import jax.numpy as jnp
from jax import lax
from jax.experimental import pallas as pl
from jax.experimental.pallas import tpu as pltpu
from jax.sharding import PartitionSpec as P

HEADS = 32
SIDE = 10
WIN = 100


epsilon = 1e-05
masked_score = -1000000000.0


def layer_norm(inputs, gain, shift):
    mean_value = jnp.mean(inputs, axis=-1, keepdims=True)
    centered = inputs - mean_value
    inverse = lax.rsqrt(jnp.mean(centered * centered, axis=-1, keepdims=True) + epsilon)
    normal_part = centered * inverse
    return (normal_part * gain + shift, normal_part, inverse)


def norm_back(grad_out, normal_part, inverse, gain):
    scaled = grad_out * gain
    grad_in = inverse * (
        scaled
        - jnp.mean(scaled, axis=-1, keepdims=True)
        - normal_part * jnp.mean(scaled * normal_part, axis=-1, keepdims=True)
    )
    return (grad_in, jnp.sum(grad_out * normal_part, axis=0), jnp.sum(grad_out, axis=0))


def gelu_exact(hidden):
    return jax.nn.gelu(hidden, approximate=False)


def region_mask(region_ids):
    position = jnp.arange(WIN, dtype=jnp.int32)
    cut_point = SIDE - SIDE // 2
    right_half = (position % SIDE >= cut_point).astype(jnp.int32)
    lower_half = (position // SIDE >= cut_point).astype(jnp.int32)
    labels = (
        region_ids[:, None] % 2 * right_half[None]
        + 2 * (region_ids[:, None] // 2) * lower_half[None]
    )
    same_label = labels[:, :, None] == labels[:, None, :]
    return jnp.where(same_label, 0.0, masked_score).astype(jnp.float32)[:, None]


MESH = pl.DeviceIdType.MESH
ANY = pl.BlockSpec(memory_space=pl.ANY)
VMEM = pl.BlockSpec(memory_space=pltpu.VMEM)
WIDE = 1024
LOOK = 2


def ring_position(peer, peers):
    column, row = lax.rem(peer, 2), lax.div(peer, 2)
    return column * (peers - 1 - row) + (1 - column) * row


def ring_member(place, peers):
    place = lax.rem(place + peers, peers)
    far = lax.div(place, peers // 2)
    return (1 - far) * 2 * place + far * (2 * (peers - 1 - place) + 1)


class Place:
    def __init__(self, depths, peers):
        self.depths, self.peers, self.half = depths, peers, peers // 2
        outer = lax.axis_index("dp")
        self.depth, self.core = lax.div(outer, 2), lax.rem(outer, 2)
        self.peer = lax.axis_index("fsdp")
        self.spot = ring_position(self.peer, peers)
        self.index = outer * peers + self.peer
        self.total = depths * 2 * peers

    def sibling(self):
        return (self.depth * 2 + 1 - self.core, self.peer)

    def around(self, step):
        return ring_member(self.spot + step, self.peers)

    def neighbour(self, step):
        return (self.depth * 2 + self.core, self.around(step))

    def at_depth(self, step):
        return lax.rem(self.depth + step + self.depths, self.depths)

    def deep(self, step):
        return (self.at_depth(step) * 2 + self.core, self.peer)

    def other(self, step):
        index = lax.rem(self.index + step, self.total)
        return (lax.div(index, self.peers), lax.rem(index, self.peers))

    def greet(self):
        barrier = pltpu.get_barrier_semaphore()

        def signal(step, carry):
            pl.semaphore_signal(barrier, inc=1, device_id=self.other(step), device_id_type=MESH)
            return carry

        lax.fori_loop(1, self.total, signal, 0)
        pl.semaphore_wait(barrier, self.total - 1)

    def greet_near(self):
        barrier = pltpu.get_barrier_semaphore()
        near = [self.sibling(), self.neighbour(1), self.neighbour(-1)]
        near += [self.deep(step) for step in range(1, self.depths)]
        for device in near:
            pl.semaphore_signal(barrier, inc=1, device_id=device, device_id_type=MESH)
        pl.semaphore_wait(barrier, len(near))


def remote(source, target, send, receive, device):
    return pltpu.make_async_remote_copy(
        src_ref=source,
        dst_ref=target,
        send_sem=send,
        recv_sem=receive,
        device_id=device,
        device_id_type=MESH,
    )


class Spread:
    def __init__(self, place, source, target, send, receive, local):
        self.place, self.source, self.target = place, source, target
        self.send, self.receive, self.local = send, receive, local

    def own(self):
        return pltpu.make_async_copy(self.source, self.target.at[self.place.index], self.local)

    def start(self):
        def copy(step, carry):
            remote(
                self.source,
                self.target.at[self.place.index],
                self.send,
                self.receive,
                self.place.other(step),
            ).start()
            return carry

        lax.fori_loop(1, self.place.total, copy, 0)
        self.own().start()

    def wait(self):
        rest = self.target.at[pl.ds(0, self.place.total - 1)]
        both = remote(rest, rest, self.send, self.receive, self.place.other(1))
        both.wait_send()
        both.wait_recv()
        self.own().wait()


def gather_kernel(chunks, depths, peers, count, *refs):
    blocks, small = refs[:count], refs[count]
    fulls, small_full = refs[count + 1 : 2 * count + 1], refs[2 * count + 1]
    (z_send, z_recv, r_send, r_recv, c_send, c_recv, own_sem, s_send, s_recv, s_own) = refs[
        2 * count + 2 :
    ]
    place = Place(depths, peers)
    half = place.half
    core, cut = place.core, depths // 2

    def view(i, depth, peer):
        array, layer, rows, columns = chunks[i]
        return fulls[array].at[depth, core, peer, rows, columns]

    def block(i):
        array, layer, rows, columns = chunks[i]
        return blocks[array].at[layer, rows, columns]

    def own(i):
        return pltpu.make_async_copy(block(i), view(i, place.depth, place.peer), own_sem.at[i])

    def deep(i, step):
        return remote(
            block(i),
            view(i, place.depth, place.peer),
            z_send.at[i, step - 1],
            z_recv.at[i, step - 1],
            place.deep(step),
        )

    def part(step, way):
        if step < half:
            return slice(None)
        return slice(0, cut) if way == 0 else slice(cut, depths)

    def ring(i, step, way):
        turn = 1 if way == 0 else -1
        here = view(i, part(step, way), place.around(-turn * (step - 1)))
        return remote(
            here,
            here,
            r_send.at[i, step - 1, way],
            r_recv.at[i, step - 1, way],
            place.neighbour(turn),
        )

    def across(i, slot):
        step = (slot + 1) // 2
        turn = 1 if slot % 2 else -1
        here = view(i, slice(None), place.around(-turn * step))
        return remote(here, here, c_send.at[i, slot], c_recv.at[i, slot], place.sibling())

    slots = 2 * half
    total = len(chunks)

    def begin(i):
        for step in range(1, depths):
            deep(i, step).start()
        own(i).start()

    def first(i):
        own(i).wait()
        for step in range(1, depths):
            deep(i, step).wait_recv()
        ring(i, 1, 0).start()
        ring(i, 1, 1).start()
        across(i, 0).start()

    def later(i, step):
        ring(i, step, 0).wait_recv()
        ring(i, step, 1).wait_recv()
        if step < half:
            ring(i, step + 1, 0).start()
            ring(i, step + 1, 1).start()
            across(i, 2 * step - 1).start()
            across(i, 2 * step).start()
        else:
            across(i, 2 * step - 1).start()

    place.greet()
    begin(0)
    spread = Spread(place, small, small_full, s_send, s_recv, s_own)
    spread.start()
    for i in range(1, min(LOOK, total)):
        begin(i)
    for tick in range(total + half):
        if tick + LOOK < total:
            begin(tick + LOOK)
        if tick < total:
            first(tick)
        for step in range(1, half + 1):
            if 0 <= tick - step < total:
                later(tick - step, step)
    spread.wait()
    for i in range(total):
        for slot in range(slots):
            across(i, slot).wait()
        for step in range(1, depths):
            deep(i, step).wait_send()
        for step in range(1, half + 1):
            for way in range(2):
                ring(i, step, way).wait_send()


def chunk_list(shapes, layers):
    chunks = []
    for layer in layers:
        for which, (rows, columns) in enumerate(shapes):
            array = layer * len(shapes) + which
            if columns > WIDE:
                for start in range(0, columns, WIDE):
                    chunks.append((which, array, layer, slice(None), slice(start, start + WIDE)))
            else:
                size = rows // 4 if rows % 64 == 0 and rows > 64 else rows
                for start in range(0, rows, size):
                    chunks.append((which, array, layer, slice(start, start + size), slice(None)))
    return chunks


def gather_all(blocks, small, depths, peers):
    shapes = [b.shape[1:] for b in blocks]
    half = peers // 2
    count = 2 * len(blocks)
    plan = [(array, layer, rows, cols) for _, array, layer, rows, cols in chunk_list(shapes, (0, 1))]
    total = len(plan)

    outs = [
        jax.ShapeDtypeStruct((depths, 2, peers) + shape, jnp.bfloat16)
        for _ in range(2)
        for shape in shapes
    ]
    outs.append(jax.ShapeDtypeStruct((depths * 2 * peers,) + small.shape, small.dtype))
    dma = pltpu.SemaphoreType.DMA
    doubled = list(blocks) + list(blocks)
    return pl.pallas_call(
        functools.partial(gather_kernel, plan, depths, peers, count),
        out_shape=outs,
        in_specs=[ANY] * (count + 1),
        out_specs=[ANY] * (count + 1),
        scratch_shapes=[
            dma((total, depths - 1)),
            dma((total, depths - 1)),
            dma((total, half, 2)),
            dma((total, half, 2)),
            dma((total, 2 * half)),
            dma((total, 2 * half)),
            dma((total,)),
            dma(()),
            dma(()),
            dma(()),
        ],
        compiler_params=pltpu.CompilerParams(
            collective_id=0, has_side_effects=True, vmem_limit_bytes=60 * 2**20
        ),
    )(*doubled, small)


def sum_kernel(plan, depths, peers, count, with_small, *refs):
    lefts, rights, rest = refs[:count], refs[count : 2 * count], refs[2 * count :]
    if with_small:
        small, rest = rest[0], rest[1:]
    outs, rest = rest[:count], rest[count:]
    if with_small:
        small_all, rest = rest[0], rest[1:]
    left_bufs, right_bufs, rest = rest[:count], rest[count : 2 * count], rest[2 * count :]
    (half_send, half_recv, full_send, full_recv, z_out, z_in, own_part, x_send, x_recv, x_own) = rest[:10]
    (r_send, r_recv, z_send, z_recv) = rest[10:14]
    if with_small:
        small_in, small_sum, a_send, a_recv, a_own, b_send, b_recv, b_own = rest[14:]
    place = Place(depths, peers)
    half, core = place.half, place.core
    rows = z_out.shape[2]
    tall = depths * rows
    cut = tall // 2

    def swap(k):
        array = k // 2
        if k % 2 == 0:
            mine, theirs = lefts[array].at[core], lefts[array].at[1 - core]
            buf = left_bufs[array]
        else:
            mine = theirs = rights[array]
            buf = right_bufs[array]
        return (
            pltpu.make_async_copy(mine, buf.at[0], x_own.at[k]),
            remote(theirs, buf.at[1], x_send.at[k], x_recv.at[k], place.sibling()),
        )

    def product(i, peer):
        array, row_part, start, _ = plan[i]
        columns = pl.ds(start, WIDE)
        return jnp.dot(
            left_bufs[array][0, row_part, peer],
            right_bufs[array][0, :, columns],
            preferred_element_type=jnp.float32,
        ) + jnp.dot(
            left_bufs[array][1, row_part, peer],
            right_bufs[array][1, :, columns],
            preferred_element_type=jnp.float32,
        )

    def ring(i, step, way):
        if step == 1:
            source, target = half_send.at[i, way], half_recv.at[i, way]
        else:
            source, target = full_send.at[i, step - 2, way], full_recv.at[i, step - 2, way]
        return remote(
            source,
            target,
            r_send.at[i, step - 1, way],
            r_recv.at[i, step - 1, way],
            place.neighbour(1 if way == 0 else -1),
        )

    def deep(i, step):
        return remote(
            z_out.at[i, place.at_depth(step)],
            z_in.at[i, step - 1],
            z_send.at[i, step - 1],
            z_recv.at[i, step - 1],
            place.deep(step),
        )

    def first(i):
        found = product(i, place.around(half)).astype(jnp.bfloat16)
        half_send[i, 0] = found[:cut]
        half_send[i, 1] = found[cut:]
        ring(i, 1, 0).start()
        ring(i, 1, 1).start()

    def next_step(i, step):
        for way in range(2):
            turn = 1 if way == 0 else -1
            found = product(i, place.around(turn * (half - step + 1)))
            ring(i, step - 1, way).wait_recv()
            if step == 2:
                came = half_recv[i, way].astype(jnp.float32)
                low = found[:cut] + came if way == 0 else found[:cut]
                high = found[cut:] if way == 0 else found[cut:] + came
                full_send[i, 0, way, :cut] = low.astype(jnp.bfloat16)
                full_send[i, 0, way, cut:] = high.astype(jnp.bfloat16)
            else:
                came = full_recv[i, step - 3, way].astype(jnp.float32)
                full_send[i, step - 2, way] = (found + came).astype(jnp.bfloat16)
            ring(i, step, way).start()

    def plane(i):
        found = product(i, place.peer)
        for way in range(2):
            ring(i, half, way).wait_recv()
            found += full_recv[i, half - 2, way].astype(jnp.float32)
        for depth in range(depths):
            piece = found[depth * rows : (depth + 1) * rows]
            z_out[i, depth] = piece.astype(jnp.bfloat16)

            @pl.when(depth == place.depth)
            def _():
                own_part[i] = piece

        for step in range(1, depths):
            deep(i, step).start()

    def finish(i):
        array, _, start, out_rows = plan[i]
        found = own_part[i]
        for step in range(1, depths):
            deep(i, step).wait_recv()
            found += z_in[i, step - 1].astype(jnp.float32)
        outs[array][out_rows, pl.ds(start, WIDE)] = found

    if with_small:
        place.greet()
    else:
        place.greet_near()
    for k in reversed(range(2 * count)):
        for copy in swap(k):
            copy.start()
    if with_small:

        def send_small(step, carry):
            outer, peer = place.other(step)
            remote(
                small.at[outer * peers + peer],
                small_in.at[place.index],
                a_send,
                a_recv,
                (outer, peer),
            ).start()
            return carry

        lax.fori_loop(1, place.total, send_small, 0)
        own_small = pltpu.make_async_copy(small.at[place.index], small_in.at[place.index], a_own)
        own_small.start()
        spread = Spread(place, small_sum, small_all, b_send, b_recv, b_own)

    total = len(plan)
    ready = set()
    for tick in range(total + half + 1):
        if tick < total:
            array = plan[tick][0]
            if array not in ready:
                ready.add(array)
                for k in (2 * array + 1, 2 * array):
                    kept, sent = swap(k)
                    kept.wait()
                    sent.wait_recv()
            first(tick)
        for step in range(2, half + 1):
            if 0 <= tick - step + 1 < total:
                next_step(tick - step + 1, step)
        if 0 <= tick - half < total:
            plane(tick - half)
        if 0 <= tick - half - 1 < total:
            finish(tick - half - 1)
        if with_small and tick == 4:
            rest_in = small_in.at[pl.ds(0, place.total - 1)]
            both = remote(rest_in, rest_in, a_send, a_recv, place.other(1))
            both.wait_send()
            both.wait_recv()
            own_small.wait()
            small_sum[...] = jnp.sum(small_in[...], axis=0)
            spread.start()
    if with_small:
        spread.wait()
    for k in range(2 * count):
        swap(k)[1].wait_send()
    for i in range(total):
        for step in range(1, half + 1):
            for way in range(2):
                ring(i, step, way).wait_send()
        for step in range(1, depths):
            deep(i, step).wait_send()


def sum_all(pairs, shapes, depths, peers, call, small=None):
    half, count = peers // 2, len(pairs)
    tokens = pairs[0][0].shape[0]
    padded = -(-tokens // 128) * 128
    unit = min(shape[0] for shape in shapes)
    lefts, rights, plan = [], [], []
    for array, ((left, right), shape) in enumerate(zip(pairs, shapes)):
        parts = shape[0] // unit
        turned = jnp.pad(left, ((0, padded - tokens), (0, 0))).T
        turned = turned.reshape(depths, 2, peers, parts, unit, padded)
        lefts.append(
            turned.transpose(1, 3, 2, 0, 4, 5).reshape(2, parts, peers, depths * unit, padded)
        )
        rights.append(jnp.pad(right, ((0, padded - tokens), (0, 0))))
        for part in range(parts):
            for start in range(0, shape[1], WIDE):
                plan.append((array, part, start, pl.ds(part * unit, unit)))
    plan = plan[::-1]
    total, tall = len(plan), depths * unit
    dma = pltpu.SemaphoreType.DMA
    low = jnp.bfloat16
    scratch = [pltpu.VMEM((2,) + a.shape[1:], low) for a in lefts]
    scratch += [pltpu.VMEM((2,) + a.shape, low) for a in rights]
    scratch += [
        pltpu.VMEM((total, 2, tall // 2, WIDE), low),
        pltpu.VMEM((total, 2, tall // 2, WIDE), low),
        pltpu.VMEM((total, half - 1, 2, tall, WIDE), low),
        pltpu.VMEM((total, half - 1, 2, tall, WIDE), low),
        pltpu.VMEM((total, depths, unit, WIDE), low),
        pltpu.VMEM((total, depths - 1, unit, WIDE), low),
        pltpu.VMEM((total, unit, WIDE), jnp.float32),
        dma((2 * count,)),
        dma((2 * count,)),
        dma((2 * count,)),
        dma((total, half, 2)),
        dma((total, half, 2)),
        dma((total, depths - 1)),
        dma((total, depths - 1)),
    ]
    args = [*lefts, *rights]
    in_specs = [ANY] * (2 * count)
    out_shape = [jax.ShapeDtypeStruct(shape, jnp.float32) for shape in shapes]
    out_specs = [VMEM] * count
    if small is not None:
        args.append(small)
        in_specs.append(ANY)
        out_shape.append(jax.ShapeDtypeStruct(small.shape, jnp.float32))
        out_specs.append(VMEM)
        scratch += [
            pltpu.VMEM(small.shape, jnp.float32),
            pltpu.VMEM(small.shape[1:], jnp.float32),
        ] + [dma(())] * 6
    return pl.pallas_call(
        functools.partial(sum_kernel, plan, depths, peers, count, small is not None),
        out_shape=out_shape,
        in_specs=in_specs,
        out_specs=out_specs,
        scratch_shapes=scratch,
        compiler_params=pltpu.CompilerParams(
            collective_id=call, has_side_effects=True, vmem_limit_bytes=60 * 2**20
        ),
    )(*args)


def attention_scores(qkv_parts, position_bias, mask_add):
    head_scale = qkv_parts.shape[-1] ** (-0.5)
    scores = (
        jnp.einsum(
            "wqhd,wkhd->whqk",
            qkv_parts[:, :, 0],
            qkv_parts[:, :, 1],
            preferred_element_type=jnp.float32,
        )
        * head_scale
        + position_bias[None]
    )
    if mask_add is not None:
        scores = scores + mask_add
    return scores


def block_forward(inputs, weights, position_bias, mask_add, windows):
    norm_gains, norm_shifts, w_qkv, qv_bias, w_proj, b_proj, w_up, b_up, w_down, b_down = weights
    model_width = inputs.shape[1]
    norm_gains = norm_gains.astype(jnp.float32)
    norm_shifts = norm_shifts.astype(jnp.float32)
    normed, normal_one, inverse_one = layer_norm(inputs, norm_gains[0], norm_shifts[0])
    normed_low = normed.astype(jnp.bfloat16)
    qv_float = qv_bias.astype(jnp.float32)
    bias_full = jnp.concatenate(
        [qv_float[:model_width], jnp.zeros((model_width,), jnp.float32), qv_float[model_width:]]
    )
    qkv_low = (jnp.dot(normed_low, w_qkv, preferred_element_type=jnp.float32) + bias_full).astype(
        jnp.bfloat16
    )
    qkv_parts = qkv_low.reshape(windows, WIN, 3, HEADS, -1)
    scores = attention_scores(qkv_parts, position_bias, mask_add)
    row_max = jnp.max(scores, axis=-1, keepdims=True)
    shifted_exp = jnp.exp(scores - row_max)
    row_total = jnp.sum(shifted_exp, axis=-1, keepdims=True)
    soft_low = (shifted_exp / row_total).astype(jnp.bfloat16)
    log_total = row_max + jnp.log(row_total)
    attended = jnp.einsum(
        "whqk,wkhd->wqhd", soft_low, qkv_parts[:, :, 2], preferred_element_type=jnp.float32
    )
    attended_low = attended.reshape(inputs.shape).astype(jnp.bfloat16)
    middle = inputs + (
        jnp.dot(attended_low, w_proj, preferred_element_type=jnp.float32)
        + b_proj.astype(jnp.float32)
    )
    normed_two, normal_two, inverse_two = layer_norm(middle, norm_gains[1], norm_shifts[1])
    normed_two_low = normed_two.astype(jnp.bfloat16)
    hidden = jnp.dot(normed_two_low, w_up, preferred_element_type=jnp.float32) + b_up.astype(
        jnp.float32
    )
    activated_low = gelu_exact(hidden).astype(jnp.bfloat16)
    output = middle + (
        jnp.dot(activated_low, w_down, preferred_element_type=jnp.float32)
        + b_down.astype(jnp.float32)
    )
    kept_state = (
        normal_one,
        inverse_one,
        normed_low,
        qkv_low,
        log_total,
        attended_low,
        normal_two,
        inverse_two,
        normed_two_low,
        hidden,
        activated_low,
    )
    return (output, kept_state)


def block_backward(grad_out, weights, kept_state, position_bias, mask_add, bucket_table, windows):
    norm_gains, norm_shifts, w_qkv, qv_bias, w_proj, b_proj, w_up, b_up, w_down, b_down = weights
    (
        normal_one,
        inverse_one,
        normed_low,
        qkv_low,
        log_total,
        attended_low,
        normal_two,
        inverse_two,
        normed_two_low,
        hidden,
        activated_low,
    ) = kept_state
    model_width = grad_out.shape[1]
    norm_gains = norm_gains.astype(jnp.float32)
    grad_down_low = grad_out.astype(jnp.bfloat16)
    down_bias_grad = jnp.sum(grad_down_low, axis=0, dtype=jnp.float32)
    grad_act = jnp.einsum("rd,fd->rf", grad_down_low, w_down, preferred_element_type=jnp.float32)
    gelu_back = jax.vjp(gelu_exact, hidden)[1]
    grad_hidden_low = gelu_back(grad_act)[0].astype(jnp.bfloat16)
    up_bias_grad = jnp.sum(grad_hidden_low, axis=0, dtype=jnp.float32)
    grad_normed_two = jnp.einsum(
        "rf,df->rd", grad_hidden_low, w_up, preferred_element_type=jnp.float32
    )
    grad_mid_norm, gain_two_grad, shift_two_grad = norm_back(
        grad_normed_two, normal_two, inverse_two, norm_gains[1]
    )
    grad_middle = grad_out + grad_mid_norm
    grad_branch_low = grad_middle.astype(jnp.bfloat16)
    proj_bias_grad = jnp.sum(grad_branch_low, axis=0, dtype=jnp.float32)
    grad_attended_low = jnp.einsum(
        "rd,cd->rc", grad_branch_low, w_proj, preferred_element_type=jnp.float32
    ).astype(jnp.bfloat16)
    qkv_parts = qkv_low.reshape(windows, WIN, 3, HEADS, -1)
    scores = attention_scores(qkv_parts, position_bias, mask_add)
    soft = jnp.exp(scores - log_total)
    soft_low = soft.astype(jnp.bfloat16)
    grad_heads = grad_attended_low.reshape(windows, WIN, HEADS, -1)
    grad_value = jnp.einsum(
        "whqk,wqhd->wkhd", soft_low, grad_heads, preferred_element_type=jnp.float32
    )
    grad_soft = jnp.einsum(
        "wqhd,wkhd->whqk", grad_heads, qkv_parts[:, :, 2], preferred_element_type=jnp.float32
    )
    grad_scores_low = (
        soft * (grad_soft - jnp.sum(soft * grad_soft, axis=-1, keepdims=True))
    ).astype(jnp.bfloat16)
    head_scale = qkv_parts.shape[-1] ** (-0.5)
    grad_query = (
        jnp.einsum(
            "whqk,wkhd->wqhd",
            grad_scores_low,
            qkv_parts[:, :, 1],
            preferred_element_type=jnp.float32,
        )
        * head_scale
    )
    grad_key = (
        jnp.einsum(
            "whqk,wqhd->wkhd",
            grad_scores_low,
            qkv_parts[:, :, 0],
            preferred_element_type=jnp.float32,
        )
        * head_scale
    )
    score_sum = jnp.sum(grad_scores_low, axis=0, dtype=jnp.float32).reshape(HEADS, -1)
    table_grad = jnp.einsum("hn,nb->bh", score_sum, bucket_table, precision=lax.Precision.HIGHEST)
    grad_qkv_low = (
        jnp.stack([grad_query, grad_key, grad_value], axis=2)
        .reshape(qkv_low.shape)
        .astype(jnp.bfloat16)
    )
    column_sums = jnp.sum(grad_qkv_low, axis=0, dtype=jnp.float32)
    qv_grad = jnp.concatenate([column_sums[:model_width], column_sums[2 * model_width :]])
    grad_normed = jnp.einsum("re,de->rd", grad_qkv_low, w_qkv, preferred_element_type=jnp.float32)
    grad_in_norm, gain_one_grad, shift_one_grad = norm_back(
        grad_normed, normal_one, inverse_one, norm_gains[0]
    )
    grad_input = grad_middle + grad_in_norm
    grads = (
        jnp.stack([gain_one_grad, gain_two_grad]),
        jnp.stack([shift_one_grad, shift_two_grad]),
        qv_grad,
        proj_bias_grad,
        up_bias_grad,
        down_bias_grad,
    )
    pairs = (
        (normed_low, grad_qkv_low),
        (attended_low, grad_branch_low),
        (normed_two_low, grad_hidden_low),
        (activated_low, grad_down_low),
    )
    return (grad_input, grads, table_grad, pairs)


def shards(
    outer_count,
    peer_count,
    patches,
    out_grad,
    norm_gain,
    norm_shift,
    qkv_weight,
    qv_bias,
    rel_table,
    proj_weight,
    proj_bias,
    up_weight,
    up_bias,
    down_weight,
    down_bias,
    tile_perm,
    window_slot,
    mask_ids,
    bias_index,
):
    windows = patches.shape[0] // WIN
    model_width = patches.shape[1]
    depths = outer_count // 2
    devices = outer_count * peer_count
    capacity = (windows + peer_count - 1) // peer_count
    device_index = lax.axis_index(("dp", "fsdp"))
    total_windows = tile_perm.shape[0]
    slot_ids = jnp.arange(total_windows, dtype=jnp.int32)

    def one_hot_pick(keys, values):
        return jnp.sum(jnp.where(keys[None, :] == slot_ids[:, None], values[None, :], 0), axis=1)

    def look_up(values, at):
        hit = at[:, None] == jnp.arange(values.shape[0], dtype=jnp.int32)[None, :]
        return jnp.sum(jnp.where(hit, values[None, :], 0), axis=1)

    source_of = one_hot_pick(window_slot, look_up(window_slot, tile_perm))
    target_of = one_hot_pick(source_of, slot_ids)
    region_slot = one_hot_pick(window_slot, mask_ids)
    own_slots = device_index * windows + jnp.arange(windows, dtype=jnp.int32)

    def rank_of(slots, device_of):
        grid_view = device_of.reshape(-1, windows)
        earlier = jnp.arange(windows)[None, :] < jnp.arange(windows)[:, None]
        same_peer = grid_view[:, :, None] == grid_view[:, None, :]
        ranks = jnp.sum(same_peer & earlier[None], axis=2).reshape(-1)
        return look_up(ranks, slots)

    def peer_of(slots):
        return slots // windows % peer_count

    own_source = look_up(source_of, own_slots)
    own_target = look_up(target_of, own_slots)
    forward_send = peer_of(own_target) * capacity + rank_of(own_slots, target_of // windows)
    forward_take = peer_of(own_source) * capacity + rank_of(own_source, target_of // windows)
    backward_send = peer_of(own_source) * capacity + rank_of(own_slots, source_of // windows)
    backward_take = peer_of(own_target) * capacity + rank_of(own_target, source_of // windows)
    mask_add = region_mask(look_up(region_slot, own_slots))
    bucket_table = (
        bias_index.reshape(-1)[:, None] == jnp.arange(rel_table.shape[1], dtype=jnp.int32)[None, :]
    ).astype(jnp.float32)
    tables = rel_table.astype(jnp.float32)
    bias_one = jnp.einsum(
        "nb,bh->hn", bucket_table, tables[0], precision=lax.Precision.HIGHEST
    ).reshape(HEADS, WIN, WIN)
    bias_two = jnp.einsum(
        "nb,bh->hn", bucket_table, tables[1], precision=lax.Precision.HIGHEST
    ).reshape(HEADS, WIN, WIN)

    def choose(rows, at, count):
        spots = jnp.arange(count, dtype=jnp.int32)
        hit = spots[:, None] == at[None, :]
        return sum(
            jnp.where(hit[:, w][:, None, None], rows[w][None], jnp.zeros((), rows.dtype))
            for w in range(rows.shape[0])
        )

    def take(rows, at):
        hit = at[:, None] == jnp.arange(rows.shape[0], dtype=jnp.int32)[None, :]
        return sum(
            jnp.where(hit[:, w][:, None, None], rows[w][None], jnp.zeros((), rows.dtype))
            for w in range(rows.shape[0])
        )

    def move(rows_low, send, fetch):
        parts = rows_low.reshape(windows, WIN, model_width)
        sectioning = choose(parts, send, peer_count * capacity)
        arrived = lax.all_to_all(sectioning, "fsdp", split_axis=0, concat_axis=0, tiled=True)
        return take(arrived, fetch).reshape(rows_low.shape)

    def to_shifted(rows_low):
        return move(rows_low, forward_send, forward_take)

    def from_shifted(rows_low):
        return move(rows_low, backward_send, backward_take)

    vectors = (norm_gain, norm_shift, qv_bias, proj_bias, up_bias, down_bias)
    flat = jnp.concatenate([v.reshape(-1) for v in vectors])
    small = jnp.pad(flat, (0, -flat.shape[0] % 2048)).reshape(-1, 128)
    matrices = (qkv_weight, proj_weight, up_weight, down_weight)
    *fulls, small_full = gather_all(matrices, small, depths, peer_count)
    small_full = small_full.reshape(devices, -1)
    whole, offset = [], 0
    for v in vectors:
        size = v.size
        piece = small_full[:, offset : offset + size].reshape((devices,) + v.shape)
        offset += size
        piece = jnp.moveaxis(piece, 0, -2)
        whole.append(piece.reshape(v.shape[:-1] + (-1,)))

    def weights_of(layer):
        gains, shifts, qv, proj_b, up_b, down_b = [v[layer] for v in whole]
        w_qkv, w_proj, w_up, w_down = [
            fulls[4 * layer + k].reshape(-1, matrices[k].shape[-1]) for k in range(4)
        ]
        return (gains, shifts, w_qkv, qv, w_proj, proj_b, w_up, up_b, w_down, down_b)

    first_weights, second_weights = weights_of(0), weights_of(1)
    grad_two = to_shifted(out_grad)
    output_one, state_one = block_forward(
        patches.astype(jnp.float32), first_weights, bias_one, None, windows
    )
    second_input = to_shifted(output_one.astype(jnp.bfloat16))
    output_two, state_two = block_forward(
        second_input.astype(jnp.float32), second_weights, bias_two, mask_add, windows
    )
    block_out = from_shifted(output_two.astype(jnp.bfloat16))
    shapes = [m.shape[1:] for m in matrices]
    grad_input_two, grads_two, table_two, pairs_two = block_backward(
        grad_two.astype(jnp.float32), second_weights, state_two, bias_two, mask_add, bucket_table, windows
    )
    sums_two = sum_all(pairs_two, shapes, depths, peer_count, 1)
    grad_one = from_shifted(grad_input_two.astype(jnp.bfloat16))
    grad_patches, grads_one, table_one, pairs_one = block_backward(
        grad_one.astype(jnp.float32), first_weights, state_one, bias_one, None, bucket_table, windows
    )
    small_grads = []
    for one, two, v in zip(grads_one, grads_two, vectors):
        both = jnp.stack([one, two]).reshape(v.shape[:-1] + (devices, v.shape[-1]))
        small_grads.append(jnp.moveaxis(both, -2, 0).reshape(devices, -1))
    table = jnp.stack([table_one, table_two]).reshape(-1)
    table = jnp.pad(table, (0, -table.shape[0] % devices)).reshape(devices, -1)
    packed = jnp.concatenate(small_grads + [table], axis=1)
    width = packed.shape[1]
    packed = jnp.pad(packed, ((0, 0), (0, -width % 1024))).reshape(devices, -1, 128)
    *sums_one, small_all = sum_all(pairs_one, shapes, depths, peer_count, 2, packed)
    small_all = small_all.reshape(devices, -1)
    mine = lax.dynamic_index_in_dim(small_all, device_index, 0, keepdims=False)
    vector_grads, offset = [], 0
    for v in vectors:
        vector_grads.append(mine[offset : offset + v.size].reshape(v.shape))
        offset += v.size
    table_total = small_all[:, offset:width].reshape(-1)[: rel_table.size].reshape(rel_table.shape)
    grad_qkv, grad_proj, grad_up, grad_down = [
        jnp.stack([one, two]) for one, two in zip(sums_one, sums_two)
    ]
    return (
        block_out,
        grad_patches,
        vector_grads[0],
        vector_grads[1],
        grad_qkv,
        vector_grads[2],
        table_total,
        grad_proj,
        vector_grads[3],
        grad_up,
        vector_grads[4],
        grad_down,
        vector_grads[5],
    )


ROWS = 112
GAP, F_GAP = 2, 1
EARLY = {11: 1, 17: 6, 22: 10}
F_BUDGET, B_BUDGET = 5.0, 5.0
KEYS = 128
GROUP = 4
SCALE = 32**-0.5
LOW = jnp.bfloat16
WHOLE = jnp.float32
NEVER = -1e30


class Queue:
    def __init__(self, budget):
        self.pieces, self.budget = [], budget

    def add(self, tick, cost, work, *arguments):
        self.pieces.append((tick, cost, work, arguments))

    def run(self, tick, after, all_of_it=False):
        left = self.budget
        while self.pieces and self.pieces[0][0] <= tick and (left > 0 or all_of_it):
            left -= self.step(after)

    def step(self, after):
        _, cost, work, arguments = self.pieces.pop(0)
        work(*arguments)
        after()
        return cost


def row_loop(count, size, body):
    def step(i, carry):
        body(pl.multiple_of(i * size, size))
        return carry

    lax.fori_loop(0, count // size, step, 0)


def lane_mask(rows, head):
    lane = lax.broadcasted_iota(jnp.int32, (rows, 128), 1)
    return lane // 32 == head


def per_head(value):
    tall = jnp.concatenate([value, jnp.zeros((KEYS - ROWS, 128), value.dtype)], axis=0)
    zero = jnp.zeros((), value.dtype)
    return jnp.concatenate(
        [jnp.where(lane_mask(KEYS, head), tall, zero) for head in range(GROUP)], axis=0
    )


def dot(a, b, over=(1, 0)):
    return lax.dot_general(
        a, b, (((over[0],), (over[1],)), ((), ())), preferred_element_type=jnp.float32
    )


def normal_parts(block):
    mean = jnp.mean(block, axis=1, keepdims=True)
    centered = block - mean
    inverse = lax.rsqrt(jnp.mean(centered * centered, axis=1, keepdims=True) + epsilon)
    return centered * inverse, inverse


class Exchange:
    def __init__(self, place, out, into, send, receive, parts):
        self.place, self.out, self.into = place, out, into
        self.send, self.receive = send, receive
        self.width = out.shape[-1] // parts

    def columns(self, part):
        return slice(part * self.width, (part + 1) * self.width)

    def copy(self, part, step):
        place = self.place
        peer = lax.rem(place.peer + step, place.peers)
        return remote(
            self.out.at[peer, :, self.columns(part)],
            self.into.at[place.peer, :, self.columns(part)],
            self.send.at[part, step - 1],
            self.receive.at[part, step - 1],
            (place.depth * 2 + place.core, peer),
        )

    def give(self, part, tiles, chosen):
        columns = self.columns(part)
        for peer in range(self.place.peers):
            self.out[peer, :, columns] = tiles[chosen[peer], :, columns]
        self.into[self.place.peer, :, columns] = self.out[self.place.peer, :, columns]
        for step in range(1, self.place.peers):
            self.copy(part, step).start()

    def await_part(self, part):
        for step in range(1, self.place.peers):
            self.copy(part, step).wait_recv()

    def finish(self, parts):
        for part in range(parts):
            for step in range(1, self.place.peers):
                self.copy(part, step).wait_send()


class Gather:
    def __init__(self, place, chunks, early, blocks, fulls, sems):
        self.place, self.chunks, self.blocks, self.fulls = place, chunks, blocks, fulls
        (self.z_send, self.z_recv, self.r_send, self.r_recv, self.c_send, self.c_recv, self.own_sem, self.relay_send) = sems
        self.half, self.cut = place.half, place.depths // 2
        self.early = early
        self.late = [i for i in range(len(chunks)) if i not in early]
        self.begun = 0
        self.gone = len(self.late) - 1 + F_GAP * self.half
        assert place.depths == 2 * self.half == 4

    def whole_at(self, i):
        if i in self.early:
            return max(self.whole_at(i - 1), self.early[i] + 2 * self.half + 8)
        return self.late.index(i) + F_GAP * self.half

    def full(self, i):
        array, layer, columns = self.chunks[i]
        return self.fulls[layer * len(self.blocks) + array]

    def view(self, i, depth, peer, rows=slice(None)):
        return self.full(i).at[depth, self.place.core, peer, rows, self.chunks[i][2]]

    def plane(self, i, depth):
        return self.full(i).at[depth, self.place.core, :, :, self.chunks[i][2]]

    def block(self, i, rows=slice(None)):
        array, layer, columns = self.chunks[i]
        return self.blocks[array].at[layer, rows, columns]

    def own(self, i):
        place = self.place
        return pltpu.make_async_copy(
            self.block(i), self.view(i, place.depth, place.peer), self.own_sem.at[i]
        )

    def deep(self, i, step):
        place = self.place
        if i in self.early:
            source = target = self.plane(i, place.depth)
        else:
            source, target = self.block(i), self.view(i, place.depth, place.peer)
        return remote(
            source,
            target,
            self.z_send.at[i, step - 1],
            self.z_recv.at[i, step - 1],
            place.deep(step),
        )

    def unless_far(self, i, step, work):
        place = self.place
        far = {1: place.depths - 1, place.depths - 1: 0}
        if i in self.early and step in far:
            pl.when(place.depth != far[step])(work)
        else:
            work()

    def relay(self, i):
        place = self.place
        end = 3 * (place.depth - 1)
        here = self.plane(i, 3 - end)
        return remote(
            here,
            here,
            self.relay_send.at[i],
            self.z_recv.at[i, 2 * (place.depth - 1)],
            (end * 2 + place.core, place.peer),
        )

    def if_between(self, work):
        depth = self.place.depth
        pl.when(jnp.logical_and(depth > 0, depth < self.place.depths - 1))(work)

    def pass_on(self, i):
        self.deep(i, 2).wait_recv()
        self.if_between(lambda: self.relay(i).start())
        self.across(i, 2).start()

    def ring(self, i, step, way):
        place = self.place
        turn = 1 if way == 0 else -1
        peer = place.around(-turn * (step - 1))
        if i in self.early:
            rows = slice(None)
            if step == self.half:
                cut = self.full(i).shape[3] // 2
                rows = slice(0, cut) if way == 0 else slice(cut, 2 * cut)
            target = self.view(i, place.depth, peer, rows)
            source = self.block(i, rows) if step == 1 else target
        else:
            depths = slice(None)
            if step == self.half:
                depths = slice(0, self.cut) if way == 0 else slice(self.cut, place.depths)
            source = target = self.view(i, depths, peer)
        return remote(
            source,
            target,
            self.r_send.at[i, step - 1, way],
            self.r_recv.at[i, step - 1, way],
            place.neighbour(turn),
        )

    def across(self, i, slot):
        place = self.place
        if i in self.early:
            here = self.plane(i, place.at_depth(-slot))
        else:
            step = (slot + 1) // 2
            turn = 1 if slot % 2 else -1
            here = self.view(i, slice(None), place.around(-turn * step))
        return remote(here, here, self.c_send.at[i, slot], self.c_recv.at[i, slot], place.sibling())

    def begin(self, i):
        for step in range(1, self.place.depths):
            self.deep(i, step).start()
        self.own(i).start()

    def start_ring(self, i):
        self.ring(i, 1, 0).start()
        self.ring(i, 1, 1).start()

    def first(self, i):
        self.own(i).wait()
        for step in range(1, self.place.depths):
            self.deep(i, step).wait_recv()
        self.start_ring(i)
        self.across(i, 0).start()

    def later(self, i, step):
        self.ring(i, step, 0).wait_recv()
        self.ring(i, step, 1).wait_recv()
        early = i in self.early
        if step < self.half:
            self.ring(i, step + 1, 0).start()
            self.ring(i, step + 1, 1).start()
            if not early:
                self.across(i, 2 * step - 1).start()
                self.across(i, 2 * step).start()
        elif early:
            self.own(i).wait()
            self.across(i, 0).start()
        else:
            self.across(i, 2 * step - 1).start()

    def spread_planes(self, i):
        for step in (1, 3):
            self.deep(i, step).wait_recv()
            self.across(i, step).start()

    def tick(self, tick):
        late = self.late
        for i, start in self.early.items():
            if tick == start:
                self.own(i).start()
                self.start_ring(i)
            step, odd = divmod(tick - start, 2)
            if 1 <= step <= self.half and not odd:
                self.later(i, step)
            if 0 <= step - self.half < self.place.depths - 1 and not odd:
                deep = (2, 1, 3)[step - self.half]
                self.unless_far(i, deep, self.deep(i, deep).start)
            if tick == start + 2 * self.half + 3:
                self.pass_on(i)
            if tick == self.whole_at(i):
                self.spread_planes(i)
        while self.begun < min(len(late), tick + 1 + min(2 + (tick + 1) // 2, 6)):
            self.begin(late[self.begun])
            self.begun += 1
        if tick < len(late):
            self.first(late[tick])
        for step in range(1, self.half + 1):
            if 0 <= tick - step * F_GAP < len(late):
                self.later(late[tick - step * F_GAP], step)

    def await_across(self, i):
        for slot in range(2 * self.half):
            self.across(i, slot).wait_recv()

    def finish(self):
        for i in range(len(self.chunks)):
            for slot in range(2 * self.half):
                self.across(i, slot).wait_send()
            for step in range(1, self.place.depths):
                self.unless_far(i, step, self.deep(i, step).wait_send)
            if i in self.early:
                self.if_between(lambda i=i: self.relay(i).wait_send())
            for step in range(1, self.half + 1):
                for way in range(2):
                    self.ring(i, step, way).wait_send()


def forward_kernel(chunks, depths, peers, *refs):
    r = types.SimpleNamespace()
    (
        r.w0, r.w1, r.w2, r.w3, r.gain, r.shift, r.qv, r.proj_b, r.up_b, r.down_b, r.x0, r.grads, r.table, r.bias_index, r.region, r.forward_send,
        r.forward_take, r.backward_send, r.backward_take, r.f0, r.f1, r.f2, r.f3, r.f4, r.f5, r.f6, r.f7,
        r.moved_grad, r.result, r.left0, r.left1, r.left2, r.left3, r.low_x, r.middle, r.qkv, r.probs,
        r.slope, r.vec32, r.small_full, r.small, r.tables, r.index, r.mask, r.bias, r.x, r.x0w, r.normed, r.att, r.normed_two, r.act, r.mid,
        r.q_s, r.p_s, r.slope_s, r.wide_a, r.wide_b, r.total, r.sib_a, r.sib_b, r.turned, r.wide_t, r.left_a, r.left_b,
        r.g_out, r.g_in, r.x_out, r.x_in, r.y_out, r.y_in, r.vec64, r.vec128, r.z_send, r.z_recv, r.r_send,
        r.r_recv, r.c_send, r.c_recv, r.own_sem, r.relay_send, r.s_send, r.s_recv, r.s_own, r.load, r.save, r.swap_send,
        r.swap_recv, r.eg_send, r.eg_recv, r.ex_send, r.ex_recv, r.ey_send, r.ey_recv,
    ) = refs
    place = Place(depths, peers)
    gather = Gather(
        place,
        chunks,
        EARLY,
        (r.w0, r.w1, r.w2, r.w3),
        (r.f0, r.f1, r.f2, r.f3, r.f4, r.f5, r.f6, r.f7),
        (r.z_send, r.z_recv, r.r_send, r.r_recv, r.c_send, r.c_recv, r.own_sem, r.relay_send),
    )
    spread = Spread(place, r.small, r.small_full, r.s_send, r.s_recv, r.s_own)
    eg = Exchange(place, r.g_out, r.g_in, r.eg_send, r.eg_recv, 1)
    ex = Exchange(place, r.x_out, r.x_in, r.ex_send, r.ex_recv, 4)
    ey = Exchange(place, r.y_out, r.y_in, r.ey_send, r.ey_recv, 4)
    windows = 2
    tall = windows * ROWS
    per_layer = len(chunks) // 2
    total = len(chunks)
    queue = Queue(F_BUDGET)
    saved, loaded, used = [], [], set()

    def spill(source, target):
        copy = pltpu.make_async_copy(source, target, r.save.at[len(saved)])
        copy.start()
        saved.append(copy)

    def staged(i):
        array, layer, columns = chunks[i]
        count = sum(1 for c in chunks[:i] if (c[0] == 3) == (array == 3))
        return (r.wide_b if array == 3 else r.wide_a).at[count % 2]

    def load(i):
        array, layer, columns = chunks[i]
        source = gather.fulls[layer * 4 + array].at[:, :, :, :, columns]
        return pltpu.make_async_copy(source, staged(i), r.load.at[i])

    def weight(i):
        assert i in loaded
        used.add(i)
        load(i).wait()
        value = staged(i)[...]
        return value.reshape(-1, value.shape[-1])

    def fetch(i):
        gather.await_across(i)
        load(i).start()

    def unpack():
        spread.wait()
        count = place.total
        row = lax.broadcasted_iota(jnp.int32, (count, 128), 0)
        lane = lax.broadcasted_iota(jnp.int32, (count, 128), 1)

        def spread_lanes(line, member, size):
            each = 128 // size
            found = jnp.zeros((count, 128), WHOLE)
            for turn in range(each):
                spot = (member + turn) % each
                rolled = line if turn == 0 else pltpu.roll(line, turn * size, 1)
                found += jnp.where((lane // size == spot) & (row % each == spot), rolled, 0.0)
            blocks = [
                jnp.sum(found[each * b : each * (b + 1)], axis=0, keepdims=True)
                for b in range(count // each)
            ]
            return jnp.concatenate(blocks, axis=1)

        for k in range(3):
            line = r.small_full[:, k, :].astype(WHOLE)
            for member in range(4):
                r.vec32[4 * k + member : 4 * k + member + 1, :] = spread_lanes(line, member, 32)
        line = r.small_full[:, 3, :].astype(WHOLE)
        for member in range(2):
            r.vec64[member : member + 1, :] = spread_lanes(line, member, 64)
        for member in range(2):
            line = r.small_full[:, 4 + member, :].astype(WHOLE)
            r.vec128[member : member + 1, :] = jnp.concatenate(
                [line[d : d + 1] for d in range(count)], axis=1
            )

    def pack():
        r.small[...] = jnp.zeros(r.small.shape, WHOLE)
        gain, shift = r.gain[...].astype(WHOLE), r.shift[...].astype(WHOLE)
        proj_b, down_b = r.proj_b[...].astype(WHOLE), r.down_b[...].astype(WHOLE)
        qv, up_b = r.qv[...].astype(WHOLE), r.up_b[...].astype(WHOLE)
        each = proj_b.shape[1]
        for layer in range(2):
            for k in range(2):
                columns = slice((2 * layer + k) * each, (2 * layer + k + 1) * each)
                r.small[0:1, columns] = gain[layer, k : k + 1]
                r.small[1:2, columns] = shift[layer, k : k + 1]
            r.small[2:3, layer * each : (layer + 1) * each] = proj_b[layer : layer + 1]
            r.small[2:3, (2 + layer) * each : (3 + layer) * each] = down_b[layer : layer + 1]
            r.small[3:4, 2 * layer * each : 2 * (layer + 1) * each] = qv[layer : layer + 1]
            r.small[4 + layer : 5 + layer, :] = up_b[layer : layer + 1]

    def make_tables():
        count = r.table.shape[1]
        r.index[...] = jnp.full(r.index.shape, count, jnp.int32)
        r.index[:WIN, :WIN] = r.bias_index[...]
        for layer in range(2):
            r.wide_t[...] = jnp.full(r.wide_t.shape, NEVER, WHOLE)
            r.wide_t[:count, :HEADS] = r.table[layer].astype(WHOLE)
            turned = r.wide_t[...].T
            order = [turned[k % 8 * GROUP + k // 8 :][:1] for k in range(HEADS)]
            r.tables[layer * HEADS : (layer + 1) * HEADS, :] = jnp.concatenate(order, axis=0).astype(LOW)

        def label(axis, region):
            place = lax.broadcasted_iota(jnp.int32, (ROWS, KEYS), axis)
            row = lax.shift_right_logical(place * 6554, 16)
            right = jnp.where(place - 10 * row >= 5, 1, 0)
            lower = jnp.where(row >= 5, 1, 0)
            return lax.rem(region, 2) * right + 2 * lax.div(region, 2) * lower

        for w in range(windows):
            same = label(0, r.region[w]) == label(1, r.region[w])
            r.mask[w] = jnp.where(same, 0.0, masked_score)

    def bias_rows(start, stop):
        buckets = lax.broadcasted_iota(jnp.int32, (384, KEYS), 0)

        def step(i, carry):
            rows = pl.ds(pl.multiple_of(i * 8, 8), 8)
            lines = r.index[rows, :]
            found = []
            for row in range(8):
                hot = jnp.where(buckets == lines[row : row + 1], 1.0, 0.0).astype(LOW)
                found.append(dot(r.tables[...], hot))
            for k in range(2 * HEADS):
                layer, head, g = k // HEADS, k // 8 % GROUP, k % 8
                block = jnp.concatenate([one[k : k + 1] for one in found], axis=0)
                r.bias[layer, g, rows, head * KEYS : (head + 1) * KEYS] = block
            return carry

        lax.fori_loop(start, stop, step, 0)

    def vec(k):
        return r.vec32[k : k + 1, :]

    def pad_windows(source):
        flat = r.mid.at[1]
        flat[0 : windows * WIN, :] = source[...].astype(WHOLE)
        r.total[...] = jnp.zeros(r.total.shape, WHOLE)
        for w in range(windows):
            r.total[w * ROWS : w * ROWS + WIN, :] = flat[w * WIN : (w + 1) * WIN, :]

    def norm(source, target, layer, k):
        gain, shift = vec(2 * layer + k), vec(4 + 2 * layer + k)

        def body(start):
            rows = pl.ds(start, 32)
            parts, _ = normal_parts(source[rows, :].astype(WHOLE))
            target[rows, :] = (parts * gain + shift).astype(LOW)

        row_loop(tall, 32, body)

    def enter(layer):
        x = r.x.at[layer]
        if layer == 0:
            pad_windows(r.x0)
            x[...] = r.total[...].astype(LOW)
        else:
            for part in range(4):
                ex.await_part(part)
            for w in range(windows):
                x[w * ROWS : (w + 1) * ROWS, :] = r.x_in[r.forward_take[w]]
        spill(x, r.low_x.at[layer])
        norm(x, r.normed.at[layer], layer, 0)
        swap(layer, 0).start()

    def project(layer, i):
        part = i % per_layer
        found = dot(r.normed[layer], weight(i))
        if part != 1:
            half = part // 2
            found = found + r.vec64[layer : layer + 1, half * 1024 : (half + 1) * 1024]
        r.q_s[layer, :, part * 1024 : (part + 1) * 1024] = found.astype(LOW)

    def attend(layer, w):
        def step(g, carry):
            rows = slice(w * ROWS, (w + 1) * ROWS)
            start = pl.multiple_of(g * 128, 128)
            q = r.q_s[layer, rows, pl.ds(start, 128)]
            k = r.q_s[layer, rows, pl.ds(start + 1024, 128)]
            v = r.q_s[layer, rows, pl.ds(start + 2048, 128)]
            scores = dot(q, per_head(k), (1, 1)) * SCALE + r.bias[layer, g]
            heads = []
            for head in range(GROUP):
                one = scores[:, head * KEYS : (head + 1) * KEYS]
                if layer == 1:
                    one = one + r.mask[w]
                shifted = jnp.exp(one - jnp.max(one, axis=1, keepdims=True))
                heads.append(
                    (shifted * (1.0 / jnp.sum(shifted, axis=1, keepdims=True))).astype(LOW)
                )
            found = jnp.concatenate(heads, axis=1)
            r.p_s[layer, w * 8 + g] = found
            r.att[layer, rows, pl.ds(start, 128)] = dot(found, per_head(v)).astype(LOW)
            return carry

        lax.fori_loop(0, 8, step, 0)

    def branch(layer, i):
        spill(r.q_s.at[layer], r.qkv.at[layer])
        spill(r.p_s.at[layer], r.probs.at[layer])
        swap(layer, 1).start()
        found = dot(r.att[layer], weight(i)) + vec(8 + layer)
        r.mid[layer] = r.x[layer].astype(WHOLE) + found
        spill(r.mid.at[layer], r.middle.at[layer])

    def second_norm(layer):
        norm(r.mid.at[layer], r.normed_two.at[layer], layer, 1)
        swap(layer, 2).start()

    def widen(layer, i):
        part = i % per_layer - 4
        columns = slice(part * 1024, (part + 1) * 1024)
        r.total[...] = dot(r.normed_two[layer], weight(i)) + r.vec128[layer : layer + 1, columns]

        def body(start):
            rows = pl.ds(start, 16)
            v = r.total[rows, :]
            spread_half = 0.5 * (1.0 + lax.erf(v * (2.0**-0.5)))
            density = jnp.exp(-0.5 * v * v) * 0.3989422804014327
            r.act[layer, rows, columns] = (v * spread_half).astype(LOW)
            r.slope_s[layer, rows, columns] = (spread_half + v * density).astype(LOW)

        row_loop(tall, 16, body)
        if part == 3:
            spill(r.slope_s.at[layer], r.slope.at[layer])
            swap(layer, 3).start()

    def narrow(layer, i):
        part = i % per_layer - 8
        columns = slice(part * 256, (part + 1) * 256)
        found = dot(r.act[layer], weight(i)) + vec(10 + layer)[:, columns]
        found = (r.mid[layer, :, columns] + found).astype(LOW)
        for w in range(windows):
            r.x0w[w, :, columns] = found[w * ROWS : (w + 1) * ROWS]
        if layer == 0:
            ex.give(part, r.x0w, r.forward_send)
        else:
            ey.give(part, r.x0w, r.backward_send)

    sources = (r.normed, r.att, r.normed_two, r.act)

    def swap(layer, array):
        target = (r.sib_b if array == 3 else r.sib_a.at[array]).at[layer]
        return remote(
            sources[array].at[layer],
            target,
            r.swap_send.at[layer, array],
            r.swap_recv.at[layer, array],
            place.sibling(),
        )

    def turn(layer, array):
        swap(layer, array).wait_recv()
        mine = sources[array].at[layer]
        theirs = (r.sib_b if array == 3 else r.sib_a.at[array]).at[layer]
        unit = r.left0.shape[-2] // depths
        pad = jnp.zeros((256 - tall, 128), WHOLE)
        rounds = peers if array == 3 else 1
        for f in range(rounds):
            for depth in range(depths):
                start = (depth * 2 + place.core) * rounds * 128 + f * 128
                columns = pl.ds(pl.multiple_of(start, 128), 128)
                for side, ref in enumerate((mine, theirs)):
                    block = jnp.concatenate([ref[:, columns].astype(WHOLE), pad], axis=0)
                    r.turned[depth, :, side * 256 : (side + 1) * 256] = block.T
            for part in range(4):
                found = jnp.concatenate(
                    [r.turned[depth, part * unit : (part + 1) * unit] for depth in range(depths)],
                    axis=0,
                ).astype(LOW)
                if array == 3:
                    r.left_b[layer, part, f] = found
                else:
                    r.left_a[layer, array, part] = found
        if array == 3:
            spill(r.left_b.at[layer], r.left3.at[layer])
        else:
            spill(r.left_a.at[layer, array], (r.left0, r.left1, r.left2)[array].at[layer])

    pack()
    place.greet()
    gather.begin(gather.late[0])
    gather.begun = 1
    pad_windows(r.grads)
    for w in range(windows):
        r.x0w[w] = r.total[w * ROWS : (w + 1) * ROWS, :].astype(LOW)
    eg.give(0, r.x0w, r.forward_send)
    spread.start()

    def at(layer, part):
        return gather.whole_at(layer * per_layer + part) + 1

    queue.add(0, 1, make_tables)
    queue.add(0, 5, bias_rows, 0, 7)
    queue.add(0, 5, bias_rows, 7, ROWS // 8)
    queue.add(2, 1, unpack)
    for layer in range(2):
        base = layer * per_layer
        queue.add(2 if layer == 0 else at(0, 11) + 1, 2, enter, layer)
        for part in range(3):
            queue.add(at(layer, part), 1.5, project, layer, base + part)
        for w in range(windows):
            queue.add(at(layer, 2), 5, attend, layer, w)
        queue.add(at(layer, 3), 1.5, branch, layer, base + 3)
        queue.add(at(layer, 3), 1.5, second_norm, layer)
        for part in range(4):
            queue.add(at(layer, 4 + part), 3.5, widen, layer, base + 4 + part)
            if part < 3:
                queue.add(at(layer, 4 + part), 1, turn, layer, part)
        for part in range(4):
            queue.add(at(layer, 8 + part), 1.5, narrow, layer, base + 8 + part)
        queue.add(at(layer, 11) + 1, 4, turn, layer, 3)

    last = gather.gone + 1
    state = types.SimpleNamespace(tick=0)

    def pump():
        while len(loaded) < total and gather.whole_at(len(loaded)) <= state.tick:
            i = len(loaded)
            same = [j for j in range(i) if (chunks[j][0] == 3) == (chunks[i][0] == 3)]
            if len(same) > 1 and same[-2] not in used:
                break
            fetch(i)
            loaded.append(i)

    for tick in range(last + 1):
        state.tick = tick
        gather.tick(tick)
        pump()
        queue.run(tick, pump)
        if tick == 3:
            eg.await_part(0)
            for w in range(windows):
                r.moved_grad[w] = r.g_in[r.forward_take[w]]
    queue.run(last + total, pump, True)
    for part in range(4):
        ey.await_part(part)
    for w in range(windows):
        tile = r.y_in[r.backward_take[w]].astype(WHOLE)
        r.total[w * WIN : (w + 1) * WIN, :] = tile[:WIN]
    r.result[...] = r.total[0 : windows * WIN, :].astype(LOW)
    eg.finish(1)
    ex.finish(4)
    ey.finish(4)
    gather.finish()
    for layer in range(2):
        for array in range(4):
            swap(layer, array).wait_send()
    for copy in saved:
        copy.wait()


def forward_all(blocks, vectors, x0, grads, table, bias_index, region, moves, depths, peers):
    count = depths * 2 * peers
    width = x0.shape[-1]
    hidden = blocks[2].shape[-1]
    tall = 2 * ROWS
    half = peers // 2
    chunks = []
    for layer in range(2):
        for array, block in enumerate(blocks):
            size = 256 if array == 3 else 1024
            for start in range(0, block.shape[-1], size):
                chunks.append((array, layer, slice(start, start + size)))
    total = len(chunks)
    unit = blocks[0].shape[1]
    dma = pltpu.SemaphoreType.DMA
    vmem = pltpu.VMEM
    smem = pl.BlockSpec(memory_space=pltpu.SMEM)
    shape = jax.ShapeDtypeStruct
    tiles = (2, ROWS, width)
    left = (2, peers, depths * unit, 512)
    outs = [shape((depths, 2, peers) + b.shape[1:], LOW) for _ in range(2) for b in blocks]
    outs += [shape(tiles, LOW), shape(x0.shape, LOW)]
    outs += [shape(left, LOW)] * 3 + [shape((2, 4) + left[1:], LOW)]
    outs += [
        shape((2, tall, width), LOW),
        shape((2, tall, width), WHOLE),
        shape((2, tall, 3 * width), LOW),
        shape((2, 16, ROWS, GROUP * KEYS), LOW),
        shape((2, tall, hidden), LOW),
        shape((12, width), WHOLE),
    ]
    exchange = (peers,) + tiles[1:]
    scratch = [
        vmem((count, 8, 128), WHOLE),
        vmem((8, 128), WHOLE),
        vmem((2 * HEADS, 384), LOW),
        vmem((ROWS, KEYS), jnp.int32),
        vmem((2, ROWS, KEYS), WHOLE),
        vmem((2, 8, ROWS, GROUP * KEYS), WHOLE),
        vmem((2, tall, width), LOW),
        vmem(tiles, LOW),
        vmem((2, tall, width), LOW),
        vmem((2, tall, width), LOW),
        vmem((2, tall, width), LOW),
        vmem((2, tall, hidden), LOW),
        vmem((2, tall, width), WHOLE),
        vmem((2, tall, 3 * width), LOW),
        vmem((2, 16, ROWS, GROUP * KEYS), LOW),
        vmem((2, tall, hidden), LOW),
        vmem((2, depths, 2, peers, unit, 1024), LOW),
        vmem((2, depths, 2, peers, 4 * unit, 256), LOW),
        vmem((tall, 1024), WHOLE),
        vmem((3, 2, tall, width), LOW),
        vmem((2, tall, hidden), LOW),
        vmem((depths, 128, 512), WHOLE),
        vmem((384, 128), WHOLE),
        vmem((2, 3) + left[1:], LOW),
        vmem((2, 4) + left[1:], LOW),
        *[vmem(exchange, LOW)] * 6,
        vmem((2, 2 * width), WHOLE),
        vmem((2, hidden), WHOLE),
        dma((total, depths - 1)),
        dma((total, depths - 1)),
        dma((total, half, 2)),
        dma((total, half, 2)),
        dma((total, 2 * half)),
        dma((total, 2 * half)),
        dma((total,)),
        dma((total,)),
        dma(()),
        dma(()),
        dma(()),
        dma((total,)),
        dma((32,)),
        dma((2, 4)),
        dma((2, 4)),
        dma((1, peers - 1)),
        dma((1, peers - 1)),
        *[dma((4, peers - 1))] * 4,
    ]
    return pl.pallas_call(
        functools.partial(forward_kernel, chunks, depths, peers),
        out_shape=outs,
        in_specs=[ANY] * 4 + [VMEM] * 10 + [smem] * 5,
        out_specs=[ANY] * 8 + [VMEM] * 2 + [ANY] * 9 + [VMEM],
        scratch_shapes=scratch,
        compiler_params=pltpu.CompilerParams(
            collective_id=3, has_side_effects=True, vmem_limit_bytes=63 * 2**20
        ),
    )(*blocks, *vectors, x0, grads, table, bias_index, region, *moves)


SLOTS, Z_SLOTS, Z_WAIT = 6, 9, 3
DEEP = {3: (1, 7), 7: (6, 13), 15: (14, 20)}


class Reduce:
    def __init__(self, place, plan, product, keep, bufs, sems):
        self.place, self.plan, self.product, self.keep = place, plan, product, keep
        (self.half_send, self.half_recv, self.full_send, self.full_recv, self.z_out, self.z_in, self.own_part) = bufs
        self.r_send, self.r_recv, self.z_send, self.z_recv = sems
        self.half = place.half
        self.rows = self.z_out.shape[2]
        self.cut = place.depths * self.rows // 2

    def ring(self, i, step, way):
        slot = i % SLOTS
        if step == 1:
            source, target = self.half_send.at[slot, way], self.half_recv.at[slot, way]
        else:
            source = self.full_send.at[slot, step - 2, way]
            target = self.full_recv.at[slot, step - 2, way]
        return remote(
            source,
            target,
            self.r_send.at[slot, step - 1, way],
            self.r_recv.at[slot, step - 1, way],
            self.place.neighbour(1 if way == 0 else -1),
        )

    def deep(self, i, step):
        slot = i % Z_SLOTS
        return remote(
            self.z_out.at[slot, self.place.at_depth(step)],
            self.z_in.at[slot, step - 1],
            self.z_send.at[slot, step - 1],
            self.z_recv.at[slot, step - 1],
            self.place.deep(step),
        )

    def sent(self, i):
        for way in range(2):
            for step in range(1, self.half + 1):
                self.ring(i, step, way).wait_send()

    def deep_sent(self, i):
        for step in range(1, self.place.depths):
            self.deep(i, step).wait_send()

    def first(self, i):
        if i >= SLOTS:
            self.sent(i - SLOTS)
        slot = i % SLOTS
        found = self.product(self.plan[i], self.place.around(self.half)).astype(LOW)
        for way in range(2):
            self.half_send[slot, way] = found[: self.cut] if way == 0 else found[self.cut :]
            self.ring(i, 1, way).start()

    def next_step(self, i, step):
        slot = i % SLOTS
        cut = self.cut
        for way in range(2):
            turn = 1 if way == 0 else -1
            found = self.product(self.plan[i], self.place.around(turn * (self.half - step + 1)))
            self.ring(i, step - 1, way).wait_recv()
            target = self.full_send.at[slot, step - 2, way]
            if step == 2:
                came = self.half_recv[slot, way].astype(WHOLE)
                low = found[:cut] + came if way == 0 else found[:cut]
                high = found[cut:] if way == 0 else found[cut:] + came
                target[:cut] = low.astype(LOW)
                target[cut:] = high.astype(LOW)
            else:
                came = self.full_recv[slot, step - 3, way].astype(WHOLE)
                target[...] = (found + came).astype(LOW)
            self.ring(i, step, way).start()

    def plane(self, i):
        slot, rows = i % SLOTS, self.rows
        z_slot = i % Z_SLOTS
        if i >= Z_SLOTS:
            self.deep_sent(i - Z_SLOTS)
        found = self.product(self.plan[i], self.place.peer)
        for way in range(2):
            self.ring(i, self.half, way).wait_recv()
            found += self.full_recv[slot, self.half - 2, way].astype(WHOLE)
        for depth in range(self.place.depths):
            piece = found[depth * rows : (depth + 1) * rows]
            self.z_out[z_slot, depth] = piece.astype(LOW)

            @pl.when(depth == self.place.depth)
            def _():
                self.own_part[z_slot] = piece

        for step in range(1, self.place.depths):
            self.deep(i, step).start()

    def finish(self, i):
        slot = i % Z_SLOTS
        found = self.own_part[slot]
        for step in range(1, self.place.depths):
            self.deep(i, step).wait_recv()
            found += self.z_in[slot, step - 1].astype(WHOLE)
        self.keep(self.plan[i], found)


SMALL_ROWS = 96


class DeepFirst:
    def __init__(self, reduce, bufs, sems):
        self.reduce, self.place = reduce, reduce.place
        (self.out, self.into, self.kept, self.half_send, self.half_recv, self.full_send, self.full_recv) = bufs
        self.z_send, self.z_recv, self.r_send, self.r_recv = sems
        self.rows = self.kept.shape[2]
        self.cut = self.rows // 2

    def deep(self, k, step):
        return remote(
            self.out.at[k, self.place.at_depth(step)],
            self.into.at[k, step - 1],
            self.z_send.at[k, step - 1],
            self.z_recv.at[k, step - 1],
            self.place.deep(step),
        )

    def ring(self, k, step, way):
        if step == 1:
            source, target = self.half_send.at[k, way], self.half_recv.at[k, way]
        else:
            source = self.full_send.at[k, step - 2, way]
            target = self.full_recv.at[k, step - 2, way]
        return remote(
            source,
            target,
            self.r_send.at[k, step - 1, way],
            self.r_recv.at[k, step - 1, way],
            self.place.neighbour(1 if way == 0 else -1),
        )

    def start(self, k, entry):
        rows = self.rows
        for peer in range(self.place.peers):
            found = self.reduce.product(entry, peer)
            for depth in range(self.place.depths):
                piece = found[depth * rows : (depth + 1) * rows]
                self.out[k, depth, peer * rows : (peer + 1) * rows] = piece.astype(LOW)

                @pl.when(depth == self.place.depth)
                def _():
                    self.kept[k, peer] = piece

    def turn(self, k):
        place, rows = self.place, self.rows
        for step in range(1, place.depths):
            self.deep(k, step).wait_recv()
        for peer in range(place.peers):
            found = self.kept[k, peer]
            for step in range(1, place.depths):
                found += self.into[k, step - 1, peer * rows : (peer + 1) * rows].astype(WHOLE)
            self.kept[k, peer] = found
        found = self.kept[k, place.around(place.half)].astype(LOW)
        for way in range(2):
            self.half_send[k, way] = found[: self.cut] if way == 0 else found[self.cut :]
            self.ring(k, 1, way).start()

    def next_step(self, k, step):
        place, cut = self.place, self.cut
        for way in range(2):
            turn = 1 if way == 0 else -1
            found = self.kept[k, place.around(turn * (place.half - step + 1))]
            self.ring(k, step - 1, way).wait_recv()
            if step == 2:
                came = self.half_recv[k, way].astype(WHOLE)
                low = found[:cut] + came if way == 0 else found[:cut]
                high = found[cut:] if way == 0 else found[cut:] + came
                found = jnp.concatenate([low, high], axis=0)
            else:
                found += self.full_recv[k, step - 3, way].astype(WHOLE)
            self.full_send[k, step - 2, way] = found.astype(LOW)
            self.ring(k, step, way).start()

    def finish(self, k, entry):
        place = self.place
        found = self.kept[k, place.peer]
        for way in range(2):
            self.ring(k, place.half, way).wait_recv()
            found += self.full_recv[k, place.half - 2, way].astype(WHOLE)
        self.reduce.keep(entry, found)

    def sent(self, k):
        for way in range(2):
            for step in range(1, self.place.half + 1):
                self.ring(k, step, way).wait_send()
        for step in range(1, self.place.depths):
            self.deep(k, step).wait_send()


def backward_kernel(everything, depths, peers, *refs):
    r = types.SimpleNamespace()
    (
        r.f0, r.f1, r.f2, r.f3, r.f4, r.f5, r.f6, r.f7, r.moved_grad, r.left0, r.left1, r.left2, r.left3,
        r.low_x, r.middle, r.qkv, r.probs, r.slope, r.vec32, r.bias_index, r.backward_send, r.backward_take,
        r.patches_grad, r.g_qkv, r.g_proj, r.g_up, r.g_down, r.o_gain, r.o_shift, r.o_qv, r.o_proj, r.o_up, r.o_down, r.o_table, r.small_all, r.half_send, r.half_recv,
        r.full_send, r.full_recv, r.z_out, r.z_in, r.own_part, r.left_a, r.left_b, r.right0, r.right1,
        r.right2, r.right3, r.wide_a, r.wide_b, r.slope_s, r.p_s, r.q_s, r.mid, r.x, r.grad, r.att_grad,
        r.total, r.g_mid, r.score_sum, r.tiles, r.e_out, r.e_in, r.index, r.small_mine, r.small_in, r.small_sum,
        r.r_send, r.r_recv, r.z_send, r.z_recv, r.swap_send, r.swap_recv, r.credit, r.load, r.state, r.e_send,
        r.e_recv, r.a_send, r.a_recv, r.a_own, r.b_send, r.b_recv, r.b_own,
        r.d_out, r.d_in, r.d_kept, r.d_half_send, r.d_half_recv, r.d_full_send, r.d_full_recv,
        r.dz_send, r.dz_recv, r.dr_send, r.dr_recv,
    ) = refs
    place = Place(depths, peers)
    fulls = (r.f0, r.f1, r.f2, r.f3, r.f4, r.f5, r.f6, r.f7)
    rights = (r.right0, r.right1, r.right2, r.right3)
    outs = (r.g_qkv, r.g_proj, r.g_up, r.g_down)
    windows, tall = 2, 2 * ROWS
    plan = [entry for i, entry in enumerate(everything) if i not in DEEP]
    total = len(plan)
    queue = Queue(B_BUDGET)
    done, used, loaded = set(), set(), []
    unit = r.z_out.shape[2]

    def product(entry, peer):
        layer, array, part, start = entry
        left = r.left_b[layer, part, peer] if array == 3 else r.left_a[layer, array, peer]
        return dot(left, rights[array][:, start : start + WIDE])

    def keep(entry, found):
        layer, array, part, start = entry
        outs[array][layer, part * unit : (part + 1) * unit, start : start + WIDE] = found

    reduce = Reduce(
        place,
        plan,
        product,
        keep,
        (r.half_send, r.half_recv, r.full_send, r.full_recv, r.z_out, r.z_in, r.own_part),
        (r.r_send, r.r_recv, r.z_send, r.z_recv),
    )
    deep_first = DeepFirst(
        reduce,
        (r.d_out, r.d_in, r.d_kept, r.d_half_send, r.d_half_recv, r.d_full_send, r.d_full_recv),
        (r.dz_send, r.dz_recv, r.dr_send, r.dr_recv),
    )
    exchange = Exchange(place, r.e_out, r.e_in, r.e_send, r.e_recv, 1)

    order = [(layer, array, part) for layer in (1, 0) for array, parts in ((3, 4), (2, 4), (1, 1), (0, 3)) for part in range(parts)]

    def slot_of(k):
        down = order[k][1] == 3
        return sum(1 for o in order[:k] if (o[1] == 3) == down) % 2

    def load(k):
        layer, array, part = order[k]
        full = fulls[layer * 4 + array]
        if array == 3:
            return pltpu.make_async_copy(full.at[part], r.wide_b.at[slot_of(k)], r.load.at[k])
        source = full.at[:, :, :, :, part * 1024 : (part + 1) * 1024]
        return pltpu.make_async_copy(source, r.wide_a.at[slot_of(k)], r.load.at[k])

    def pump():
        while len(loaded) < len(order):
            k = len(loaded)
            same = [j for j in range(k) if (order[j][1] == 3) == (order[k][1] == 3)]
            if len(same) > 1 and same[-2] not in used:
                break
            load(k).start()
            loaded.append(k)

    def weight(layer, array, part):
        k = order.index((layer, array, part))
        assert k in loaded
        used.add(k)
        load(k).wait()
        value = (r.wide_b if array == 3 else r.wide_a)[slot_of(k)]
        return value.reshape(-1, value.shape[-1])

    def swap(layer, array, part):
        columns = slice(part * 1024, (part + 1) * 1024)
        right = rights[array]
        return remote(
            right.at[0:tall, columns],
            right.at[256 : 256 + tall, columns],
            r.swap_send.at[array, part],
            r.swap_recv.at[array, part],
            place.sibling(),
        )

    def free(array):
        pl.semaphore_signal(r.credit.at[array], inc=1, device_id=place.sibling(), device_id_type=MESH)

    def hand_over(layer, array, part):
        if layer == 0 and part == 0:
            pl.semaphore_wait(r.credit.at[array], 1)
        swap(layer, array, part).start()

    def ready(layer, array, part):
        if layer == 0:
            assert (array, "freed") in done
            swap(1, array, part).wait_send()

    def put(layer, row, vector):
        for k in range(vector.shape[1] // 128):
            line = layer * SMALL_ROWS + row + k
            r.small_mine[line : line + 1, :] = vector[:, k * 128 : (k + 1) * 128]

    def column_sums(layer, row, value):
        ones = jnp.ones((8, tall), LOW)
        put(layer, row, dot(ones, value)[:1])

    states = ((r.slope_s, r.slope), (r.p_s, r.probs), (r.q_s, r.qkv), (r.mid, r.middle), (r.x, r.low_x))

    def state_copy(layer, k):
        here, there = states[k]
        return pltpu.make_async_copy(there.at[layer], here, r.state.at[layer, k])

    def left_copies(layer):
        sources = (r.left0, r.left1, r.left2)
        found = [
            pltpu.make_async_copy(
                sources[k].at[layer], r.left_a.at[layer, k], r.state.at[layer, 5 + k]
            )
            for k in range(3)
        ]
        return found + [
            pltpu.make_async_copy(r.left3.at[layer], r.left_b.at[layer], r.state.at[layer, 8])
        ]

    def vec(k):
        return r.vec32[k : k + 1, :]

    def take_grad(layer):
        if layer == 1:
            for w in range(windows):
                r.grad[w * ROWS : (w + 1) * ROWS, :] = r.moved_grad[w]
        else:
            exchange.await_part(0)
            for w in range(windows):
                r.grad[w * ROWS : (w + 1) * ROWS, :] = r.e_in[r.backward_take[w]]
        ready(layer, 3, 0)
        value = r.grad[...]
        r.right3[0:tall, :] = value
        hand_over(layer, 3, 0)
        column_sums(layer, 88, value)

    def hidden_grad(layer, part):
        if part == 0:
            state_copy(layer, 0).wait()
        columns = slice(part * 1024, (part + 1) * 1024)
        ready(layer, 2, part)
        found = dot(r.grad[...], weight(layer, 3, part), (1, 1))
        low = (found * r.slope_s[:, columns].astype(WHOLE)).astype(LOW)
        r.right2[0:tall, columns] = low
        hand_over(layer, 2, part)
        column_sums(layer, 56 + 8 * part, low)
        if part == 3 and layer == 1:
            state_copy(0, 0).start()

    def add_back(layer, array, part, columns):
        found = dot(rights[array][0:tall, columns], weight(layer, array, part), (1, 1))
        if part == 0:
            r.total[...] = found
        else:
            r.total[...] += found

    def up_back(layer, part):
        add_back(layer, 2, part, slice(part * 1024, (part + 1) * 1024))

    def norm_loop(source, layer, k, finish):
        gain = vec(2 * layer + k)

        def body(i, carry):
            start = pl.multiple_of(i * 16, 16)
            rows = pl.ds(start, 16)
            parts, inverse = normal_parts(source[rows, :].astype(WHOLE))
            g = r.total[rows, :]
            e = g * gain
            mean = jnp.mean(e, axis=1, keepdims=True)
            along = jnp.mean(e * parts, axis=1, keepdims=True)
            finish(rows, inverse * (e - mean - parts * along))
            by_gain, by_shift = carry
            return (
                by_gain + jnp.sum(g * parts, axis=0, keepdims=True),
                by_shift + jnp.sum(g, axis=0, keepdims=True),
            )

        zero = jnp.zeros((1, source.shape[-1]), WHOLE)
        by_gain, by_shift = lax.fori_loop(0, tall // 16, body, (zero, zero))
        put(layer, 8 * k, by_gain)
        put(layer, 16 + 8 * k, by_shift)

    def middle_grad(layer):
        state_copy(layer, 3).wait()
        ready(layer, 1, 0)

        def finish(rows, found):
            whole = r.grad[rows, :].astype(WHOLE) + found
            r.g_mid[rows, :] = whole
            r.right1[rows, :] = whole.astype(LOW)

        norm_loop(r.mid, layer, 1, finish)
        hand_over(layer, 1, 0)
        column_sums(layer, 48, r.right1[0:tall, :])
        if layer == 1:
            state_copy(0, 3).start()

    def attended_grad(layer):
        r.att_grad[...] = dot(r.right1[0:tall, :], weight(layer, 1, 0), (1, 1)).astype(LOW)

    def fold(value):
        return sum(
            jnp.where(lane_mask(KEYS, head), value[head * KEYS : (head + 1) * KEYS], 0.0)
            for head in range(GROUP)
        )[:ROWS]

    def attend_back(layer, w):
        if w == 0:
            state_copy(layer, 1).wait()
            state_copy(layer, 2).wait()
            for part in range(3):
                ready(layer, 0, part)

        def step(g, carry):
            rows = slice(w * ROWS, (w + 1) * ROWS)
            start = pl.multiple_of(g * 128, 128)
            q = r.q_s[rows, pl.ds(start, 128)]
            k = r.q_s[rows, pl.ds(start + 1024, 128)]
            v = r.q_s[rows, pl.ds(start + 2048, 128)]
            out_grad = r.att_grad[rows, pl.ds(start, 128)]
            low = r.p_s[w * 8 + g]
            prob_grad = dot(out_grad, per_head(v), (1, 1))
            pieces = []
            for head in range(GROUP):
                one = slice(head * KEYS, (head + 1) * KEYS)
                probs = low[:, one].astype(WHOLE)
                weighed = probs * prob_grad[:, one]
                pieces.append(weighed - probs * jnp.sum(weighed, axis=1, keepdims=True))
            score_grad = jnp.concatenate(pieces, axis=1).astype(LOW)
            for head in range(GROUP):
                lines = pl.ds(pl.multiple_of((head * 8 + g) * ROWS, 8), ROWS)
                one = score_grad[:, head * KEYS : (head + 1) * KEYS].astype(WHOLE)
                r.score_sum[lines, :] = one if w == 0 else r.score_sum[lines, :] + one
            by_query = dot(score_grad, per_head(k)) * SCALE
            by_key = fold(dot(score_grad, q, (0, 0))) * SCALE
            by_value = fold(dot(low, out_grad, (0, 0)))
            for part, found in enumerate((by_query, by_key, by_value)):
                r.right0[rows, pl.ds(start + part * 1024, 128)] = found.astype(LOW)
            return carry

        lax.fori_loop(0, 8, step, 0)
        if w == windows - 1:
            for part in range(3):
                hand_over(layer, 0, part)
            column_sums(layer, 32, r.right0[0:tall, 0:1024])
            column_sums(layer, 40, r.right0[0:tall, 2048:3072])
            if layer == 1:
                state_copy(0, 1).start()
                state_copy(0, 2).start()

    def qkv_back(layer, part):
        add_back(layer, 0, part, slice(part * 1024, (part + 1) * 1024))

    def input_grad(layer):
        state_copy(layer, 4).wait()

        def finish(rows, found):
            r.g_mid[rows, :] = r.g_mid[rows, :] + found

        norm_loop(r.x, layer, 0, finish)
        if layer == 1:
            state_copy(0, 4).start()
            for w in range(windows):
                r.tiles[w] = r.g_mid[w * ROWS : (w + 1) * ROWS, :].astype(LOW)
            exchange.give(0, r.tiles, r.backward_send)
        else:
            for w in range(windows):
                r.patches_grad[w * WIN : (w + 1) * WIN, :] = r.g_mid[w * ROWS : w * ROWS + WIN, :]

    def table_grad(layer):
        buckets = lax.broadcasted_iota(jnp.int32, (384, KEYS), 0)

        def step(i, found):
            start = pl.multiple_of(i * 8, 8)
            lines = r.index[pl.ds(start, 8), :]
            values, hots = [], []
            for row in range(8):
                hots.append(jnp.where(buckets == lines[row : row + 1], 1.0, 0.0).astype(LOW))
                values.append(r.score_sum[pl.ds(start + row, HEADS, stride=ROWS), :])
            value = jnp.concatenate(values, axis=1)
            high = value.astype(LOW)
            rest = (value - high.astype(WHOLE)).astype(LOW)
            both = jnp.concatenate([high, rest], axis=0)
            return found + dot(both, jnp.concatenate(hots, axis=1), (1, 1))

        found = lax.fori_loop(0, 13, step, jnp.zeros((64, 384), WHOLE))
        found = found[:32] + found[32:]
        base = 2 * SMALL_ROWS + layer * SMALL_ROWS
        for k in range(3):
            r.small_mine[base + 32 * k : base + 32 * (k + 1), :] = found[:, 128 * k : 128 * (k + 1)]

    def send_small():
        def step(k, carry):
            outer, peer = place.other(k)
            remote(
                r.small_mine.at[pl.ds(pl.multiple_of((outer * peers + peer) * 16, 16), 16)],
                r.small_in.at[place.index],
                r.a_send,
                r.a_recv,
                (outer, peer),
            ).start()
            return carry

        lax.fori_loop(1, place.total, step, 0)
        own_small().start()

    def own_small():
        mine = r.small_mine.at[pl.ds(pl.multiple_of(place.index * 16, 16), 16)]
        return pltpu.make_async_copy(mine, r.small_in.at[place.index], r.a_own)

    spread = Spread(place, r.small_sum, r.small_all, r.b_send, r.b_recv, r.b_own)

    def sum_small():
        rest = r.small_in.at[pl.ds(0, place.total - 1)]
        both = remote(rest, rest, r.a_send, r.a_recv, place.other(1))
        both.wait_send()
        both.wait_recv()
        own_small().wait()
        r.small_sum[...] = jnp.sum(r.small_in[...], axis=0)
        spread.start()

    def own_vectors():
        places = (
            (0, 4, r.o_gain, 0),
            (8, 4, r.o_gain, 1),
            (16, 4, r.o_shift, 0),
            (24, 4, r.o_shift, 1),
            (32, 2, r.o_qv, None),
            (48, 4, r.o_proj, None),
            (56, 1, r.o_up, None),
            (88, 4, r.o_down, None),
        )
        for layer in range(2):
            for row, each, target, k in places:
                line = layer * SMALL_ROWS + row + lax.div(place.index, each)
                found = r.small_all[lax.div(line, 16), pl.ds(lax.rem(line, 16), 1), :]
                back = lax.rem(each - lax.rem(place.index, each), each) * (128 // each)
                found = pltpu.roll(found, back, 1)[:, : 128 // each]
                if k is None:
                    target[layer : layer + 1, :] = found
                else:
                    target[layer, k : k + 1, :] = found
            first = (2 + layer) * SMALL_ROWS // 16
            parts = [
                r.small_all[first + 2 * k : first + 2 * k + 2].reshape(HEADS, 128) for k in range(3)
            ]
            rows = jnp.concatenate(parts, axis=1)
            order = [rows[h % GROUP * 8 + h // GROUP :][:1] for h in range(HEADS)]
            order.append(jnp.zeros((128 - HEADS, 384), WHOLE))
            turned = jnp.concatenate(order, axis=0).T
            r.o_table[layer] = turned[: r.o_table.shape[1], :HEADS]

    def note(work, *what):
        work(*what)
        done.add((work.__name__, *what))

    def add(tick, cost, work, *what):
        queue.add(tick, cost, note, work, *what)

    for k in range(5):
        state_copy(1, k).start()
    for layer in (1, 0):
        for copy in left_copies(layer):
            copy.start()
    for right in rights:
        zero = jnp.zeros((256 - tall, right.shape[1]), LOW)
        right[tall:256, :] = zero
        right[256 + tall : 512, :] = zero
    r.index[...] = jnp.full(r.index.shape, r.o_table.shape[1], jnp.int32)
    r.index[:WIN, :WIN] = r.bias_index[...]
    r.small_mine[...] = jnp.zeros(r.small_mine.shape, WHOLE)
    pump()
    place.greet()

    add(0, 1, take_grad, 1)
    last_use = {
        array: max(i for i, p in enumerate(plan) if p[0] == 1 and p[1] == array) for array in range(4)
    }
    after = {array: last_use[array] + GAP * place.half for array in range(4)}
    for layer in (1, 0):
        late = 9 if layer == 0 else 0
        if layer == 0:
            add(0, 5, table_grad, 1)
            add(late, 1, take_grad, 0)
        for part in range(4):
            add(late and after[2], 2, hidden_grad, layer, part)
        for part in range(4):
            add(late, 2, up_back, layer, part)
        add(late and after[1], 3, middle_grad, layer)
        add(late, 1.5, attended_grad, layer)
        for w in range(windows):
            add(late and after[0], 7, attend_back, layer, w)
        for part in range(3):
            add(late, 1.5, qkv_back, layer, part)
        add(late, 3, input_grad, layer)
    add(0, 5, table_grad, 0)
    add(0, 1, send_small)

    needs = {3: ("take_grad",), 2: ("hidden_grad",), 1: ("middle_grad",), 0: ("attend_back",)}

    def wanted(entry):
        layer, array, part, start = entry
        what = needs[array] + (layer,)
        if array == 2:
            what += (start // 1024,)
        if array == 0:
            what += (windows - 1,)
        return what

    received, lefts_in = set(), set()
    half = place.half

    def prepare(entry):
        layer, array, part, start = entry
        while wanted(entry) not in done:
            queue.step(pump)
        if layer not in lefts_in:
            lefts_in.add(layer)
            for copy in left_copies(layer):
                copy.wait()
        key = (layer, array, start // 1024)
        if key not in received:
            received.add(key)
            swap(*key).wait_recv()

    for tick in range(total + GAP * half + Z_WAIT):
        if tick < total:
            prepare(plan[tick])
            reduce.first(tick)
        for k, (i, (begin, middle)) in enumerate(DEEP.items()):
            assert place.depths == 4 and half == 2
            entry, slot = everything[i], k % 2
            if tick == begin:
                prepare(entry)
                if k >= 2:
                    deep_first.sent(slot)
                deep_first.start(slot, entry)
            if tick in (begin, begin + 2, begin + 4):
                deep_first.deep(slot, (tick - begin) // 2 + 1).start()
            if tick == middle:
                deep_first.turn(slot)
            if tick == middle + 3:
                deep_first.next_step(slot, 2)
            if tick == middle + 6:
                deep_first.finish(slot, entry)
        for step in range(2, half + 1):
            i = tick - GAP * (step - 1)
            if 0 <= i < total:
                reduce.next_step(i, step)
        i = tick - GAP * half
        if 0 <= i < total:
            reduce.plane(i)
            for array, last in last_use.items():
                if i == last:
                    free(array)
                    done.add((array, "freed"))
        i = tick - GAP * half - Z_WAIT
        if 0 <= i < total:
            reduce.finish(i)
        queue.run(tick, pump)
        if ("send_small",) in done and ("sum_small",) not in done and tick >= total - 1:
            note(sum_small)
    assert not queue.pieces
    if ("sum_small",) not in done:
        sum_small()
    spread.wait()
    own_vectors()
    exchange.finish(1)
    for array, parts in ((3, 1), (2, 4), (1, 1), (0, 3)):
        for part in range(parts):
            swap(0, array, part).wait_send()
    for i in range(total - SLOTS, total):
        reduce.sent(i)
    for i in range(total - Z_SLOTS, total):
        reduce.deep_sent(i)
    for k in range(2):
        deep_first.sent(k)


def backward_all(fulls, state, index, moves, depths, peers, buckets):
    moved_grad, left0, left1, left2, left3, low_x, middle, qkv, probs, slope, vec32 = state
    count = depths * 2 * peers
    tall, width = low_x.shape[1:]
    hidden = slope.shape[-1]
    unit = width // count
    half = peers // 2
    plan = []
    for layer in (1, 0):
        plan += [(layer, 3, part, 0) for part in range(4)]
        plan += [(layer, 2, 0, start) for start in range(0, hidden, WIDE)]
        plan += [(layer, 1, 0, 0)]
        plan += [(layer, 0, 0, start) for start in range(0, 3 * width, WIDE)]
    dma = pltpu.SemaphoreType.DMA
    vmem = pltpu.VMEM
    smem = pl.BlockSpec(memory_space=pltpu.SMEM)
    shape = jax.ShapeDtypeStruct
    flat = depths * unit
    outs = [
        shape((2 * WIN, width), WHOLE),
        shape((2, unit, 3 * width), WHOLE),
        shape((2, unit, width), WHOLE),
        shape((2, unit, hidden), WHOLE),
        shape((2, 4 * unit, width), WHOLE),
        shape((2, 2, unit), WHOLE),
        shape((2, 2, unit), WHOLE),
        shape((2, 2 * unit), WHOLE),
        shape((2, unit), WHOLE),
        shape((2, 4 * unit), WHOLE),
        shape((2, unit), WHOLE),
        shape((2, buckets, HEADS), WHOLE),
    ]
    scratch = [
        vmem((count, 16, 128), WHOLE),
        vmem((SLOTS, 2, flat // 2, WIDE), LOW),
        vmem((SLOTS, 2, flat // 2, WIDE), LOW),
        vmem((SLOTS, half - 1, 2, flat, WIDE), LOW),
        vmem((SLOTS, half - 1, 2, flat, WIDE), LOW),
        vmem((Z_SLOTS, depths, unit, WIDE), LOW),
        vmem((Z_SLOTS, depths - 1, unit, WIDE), LOW),
        vmem((Z_SLOTS, unit, WIDE), WHOLE),
        vmem((2, 3) + left0.shape[1:], LOW),
        vmem(left3.shape, LOW),
        vmem((512, 3 * width), LOW),
        vmem((512, width), LOW),
        vmem((512, hidden), LOW),
        vmem((512, width), LOW),
        vmem((2, depths, 2, peers, unit, 1024), LOW),
        vmem((2, 2, peers, 4 * unit, width), LOW),
        vmem((tall, hidden), LOW),
        vmem(probs.shape[1:], LOW),
        vmem((tall, 3 * width), LOW),
        vmem((tall, width), WHOLE),
        vmem((tall, width), LOW),
        vmem((tall, width), LOW),
        vmem((tall, width), LOW),
        vmem((tall, width), WHOLE),
        vmem((tall, width), WHOLE),
        vmem((HEADS * ROWS, KEYS), WHOLE),
        vmem((2, ROWS, width), LOW),
        vmem((peers, ROWS, width), LOW),
        vmem((peers, ROWS, width), LOW),
        vmem((ROWS, KEYS), jnp.int32),
        vmem((count * 16, 128), WHOLE),
        vmem((count, 16, 128), WHOLE),
        vmem((16, 128), WHOLE),
        dma((SLOTS, half, 2)),
        dma((SLOTS, half, 2)),
        dma((Z_SLOTS, depths - 1)),
        dma((Z_SLOTS, depths - 1)),
        dma((4, 4)),
        dma((4, 4)),
        pltpu.SemaphoreType.REGULAR((4,)),
        dma((24,)),
        dma((2, 9)),
        dma((1, peers - 1)),
        dma((1, peers - 1)),
        *[dma(())] * 6,
        vmem((2, depths, peers * unit, WIDE), LOW),
        vmem((2, depths - 1, peers * unit, WIDE), LOW),
        vmem((2, peers, unit, WIDE), WHOLE),
        vmem((2, 2, unit // 2, WIDE), LOW),
        vmem((2, 2, unit // 2, WIDE), LOW),
        vmem((2, half - 1, 2, unit, WIDE), LOW),
        vmem((2, half - 1, 2, unit, WIDE), LOW),
        dma((2, depths - 1)),
        dma((2, depths - 1)),
        dma((2, half, 2)),
        dma((2, half, 2)),
    ]
    return pl.pallas_call(
        functools.partial(backward_kernel, plan, depths, peers),
        out_shape=outs,
        in_specs=[ANY] * 8 + [VMEM] + [ANY] * 9 + [VMEM] * 2 + [smem] * 2,
        out_specs=[VMEM] * 12,
        scratch_shapes=scratch,
        compiler_params=pltpu.CompilerParams(
            collective_id=4, has_side_effects=True, vmem_limit_bytes=63 * 2**20
        ),
    )(*fulls, *state, index, *moves)


def copy_kernel(count, *refs):
    sources, targets, held = refs[:count], refs[count : 2 * count], refs[2 * count : 3 * count]
    came, went = refs[3 * count :]
    loads = [pltpu.make_async_copy(sources[k], held[k], came.at[k]) for k in range(count)]
    stores = [pltpu.make_async_copy(held[k], targets[k], went.at[k]) for k in range(count)]
    for copy in loads:
        copy.start()
    for load, store in zip(loads, stores):
        load.wait()
        store.start()
    for copy in stores:
        copy.wait()


def copy_out(arrays):
    count = len(arrays)
    return pl.pallas_call(
        functools.partial(copy_kernel, count),
        out_shape=[jax.ShapeDtypeStruct(a.shape, a.dtype) for a in arrays],
        in_specs=[ANY] * count,
        out_specs=[ANY] * count,
        scratch_shapes=[
            *[pltpu.VMEM(a.shape, a.dtype) for a in arrays],
            pltpu.SemaphoreType.DMA((count,)),
            pltpu.SemaphoreType.DMA((count,)),
        ],
        compiler_params=pltpu.CompilerParams(vmem_limit_bytes=63 * 2**20),
    )(*arrays)


def whole_shards(
    outer_count,
    peer_count,
    patches,
    out_grad,
    norm_gain,
    norm_shift,
    qkv_weight,
    qv_bias,
    rel_table,
    proj_weight,
    proj_bias,
    up_weight,
    up_bias,
    down_weight,
    down_bias,
    tile_perm,
    window_slot,
    mask_ids,
    bias_index,
):
    windows = patches.shape[0] // WIN
    width = patches.shape[1]
    depths = outer_count // 2
    device_index = lax.axis_index(("dp", "fsdp"))
    slot_ids = jnp.arange(tile_perm.shape[0], dtype=jnp.int32)

    def one_hot_pick(keys, values):
        return jnp.sum(jnp.where(keys[None, :] == slot_ids[:, None], values[None, :], 0), axis=1)

    def look_up(values, at):
        hit = at[:, None] == jnp.arange(values.shape[0], dtype=jnp.int32)[None, :]
        return jnp.sum(jnp.where(hit, values[None, :], 0), axis=1)

    source_of = one_hot_pick(window_slot, look_up(window_slot, tile_perm))
    target_of = one_hot_pick(source_of, slot_ids)
    region_slot = one_hot_pick(window_slot, mask_ids)
    own_slots = device_index * windows + jnp.arange(windows, dtype=jnp.int32)
    forward_take = look_up(source_of, own_slots) // windows % peer_count
    backward_take = look_up(target_of, own_slots) // windows % peer_count
    spots = jnp.arange(peer_count, dtype=jnp.int32)
    numbers = jnp.arange(windows, dtype=jnp.int32)

    def window_for(peers):
        return jnp.sum(jnp.where(peers[None, :] == spots[:, None], numbers[None, :], 0), axis=1)

    moves = (window_for(backward_take), forward_take, window_for(forward_take), backward_take)
    region = look_up(region_slot, own_slots)
    found = forward_all(
        (qkv_weight, proj_weight, up_weight, down_weight),
        (norm_gain, norm_shift, qv_bias, proj_bias, up_bias, down_bias),
        patches,
        out_grad,
        rel_table,
        bias_index,
        region,
        moves,
        depths,
        peer_count,
    )
    fulls, moved_grad, result, state = found[:8], found[8], found[9], found[10:]
    (
        grad_patches,
        grad_qkv,
        grad_proj,
        grad_up,
        grad_down,
        gain_grad,
        shift_grad,
        qv_grad,
        proj_b_grad,
        up_b_grad,
        down_b_grad,
        table,
    ) = backward_all(
        fulls, (moved_grad, *state), bias_index, moves[2:], depths, peer_count, rel_table.shape[1]
    )
    results = (
        result,
        grad_patches,
        gain_grad,
        shift_grad,
        grad_qkv,
        qv_grad,
        table,
        grad_proj,
        proj_b_grad,
        grad_up,
        up_b_grad,
        grad_down,
        down_b_grad,
    )
    return tuple(copy_out(results))


def solution(mesh):
    outer_count, peer_count = mesh.shape["dp"], mesh.shape["fsdp"]
    fused = outer_count == 8 and peer_count == 4
    placed = (
        P(("dp", "fsdp"), None),
        P(("dp", "fsdp"), None),
        P(None, None, ("dp", "fsdp")),
        P(None, None, ("dp", "fsdp")),
        P(None, ("dp", "fsdp"), None),
        P(None, ("dp", "fsdp")),
        P(),
        P(None, ("dp", "fsdp"), None),
        P(None, ("dp", "fsdp")),
        P(None, ("dp", "fsdp"), None),
        P(None, ("dp", "fsdp")),
        P(None, ("dp", "fsdp"), None),
        P(None, ("dp", "fsdp")),
        P(),
        P(),
        P(),
        P(),
    )
    return jax.shard_map(
        functools.partial(whole_shards if fused else shards, outer_count, peer_count),
        mesh=mesh,
        in_specs=placed,
        out_specs=(
            P(("dp", "fsdp"), None),
            P(("dp", "fsdp"), None),
            P(None, None, ("dp", "fsdp")),
            P(None, None, ("dp", "fsdp")),
            P(None, ("dp", "fsdp"), None),
            P(None, ("dp", "fsdp")),
            P(),
            P(None, ("dp", "fsdp"), None),
            P(None, ("dp", "fsdp")),
            P(None, ("dp", "fsdp"), None),
            P(None, ("dp", "fsdp")),
            P(None, ("dp", "fsdp"), None),
            P(None, ("dp", "fsdp")),
        ),
        check_vma=False,
    )
```

```python
import functools
import types

import jax
import jax.numpy as jnp
from jax import lax
from jax.experimental import pallas as pl
from jax.experimental.pallas import tpu as pltpu
from jax.sharding import PartitionSpec as P

HEADS = 32
SIDE = 10
WIN = 100


epsilon = 1e-05
masked_score = -1000000000.0


def layer_norm(inputs, gain, shift):
    mean_value = jnp.mean(inputs, axis=-1, keepdims=True)
    centered = inputs - mean_value
    inverse = lax.rsqrt(jnp.mean(centered * centered, axis=-1, keepdims=True) + epsilon)
    normal_part = centered * inverse
    return (normal_part * gain + shift, normal_part, inverse)


def norm_back(grad_out, normal_part, inverse, gain):
    scaled = grad_out * gain
    grad_in = inverse * (
        scaled
        - jnp.mean(scaled, axis=-1, keepdims=True)
        - normal_part * jnp.mean(scaled * normal_part, axis=-1, keepdims=True)
    )
    return (grad_in, jnp.sum(grad_out * normal_part, axis=0), jnp.sum(grad_out, axis=0))


def gelu_exact(hidden):
    return jax.nn.gelu(hidden, approximate=False)


def region_mask(region_ids):
    position = jnp.arange(WIN, dtype=jnp.int32)
    cut_point = SIDE - SIDE // 2
    right_half = (position % SIDE >= cut_point).astype(jnp.int32)
    lower_half = (position // SIDE >= cut_point).astype(jnp.int32)
    labels = (
        region_ids[:, None] % 2 * right_half[None]
        + 2 * (region_ids[:, None] // 2) * lower_half[None]
    )
    same_label = labels[:, :, None] == labels[:, None, :]
    return jnp.where(same_label, 0.0, masked_score).astype(jnp.float32)[:, None]


MESH = pl.DeviceIdType.MESH
ANY = pl.BlockSpec(memory_space=pl.ANY)
VMEM = pl.BlockSpec(memory_space=pltpu.VMEM)
WIDE = 1024
LOOK = 2


def ring_position(peer, peers):
    column, row = lax.rem(peer, 2), lax.div(peer, 2)
    return column * (peers - 1 - row) + (1 - column) * row


def ring_member(place, peers):
    place = lax.rem(place + peers, peers)
    far = lax.div(place, peers // 2)
    return (1 - far) * 2 * place + far * (2 * (peers - 1 - place) + 1)


class Place:
    def __init__(self, depths, peers):
        self.depths, self.peers, self.half = depths, peers, peers // 2
        outer = lax.axis_index("dp")
        self.depth, self.core = lax.div(outer, 2), lax.rem(outer, 2)
        self.peer = lax.axis_index("fsdp")
        self.spot = ring_position(self.peer, peers)
        self.index = outer * peers + self.peer
        self.total = depths * 2 * peers

    def sibling(self):
        return (self.depth * 2 + 1 - self.core, self.peer)

    def around(self, step):
        return ring_member(self.spot + step, self.peers)

    def neighbour(self, step):
        return (self.depth * 2 + self.core, self.around(step))

    def at_depth(self, step):
        return lax.rem(self.depth + step + self.depths, self.depths)

    def deep(self, step):
        return (self.at_depth(step) * 2 + self.core, self.peer)

    def other(self, step):
        index = lax.rem(self.index + step, self.total)
        return (lax.div(index, self.peers), lax.rem(index, self.peers))

    def greet(self):
        barrier = pltpu.get_barrier_semaphore()

        def signal(step, carry):
            pl.semaphore_signal(barrier, inc=1, device_id=self.other(step), device_id_type=MESH)
            return carry

        lax.fori_loop(1, self.total, signal, 0)
        pl.semaphore_wait(barrier, self.total - 1)

    def greet_near(self):
        barrier = pltpu.get_barrier_semaphore()
        near = [self.sibling(), self.neighbour(1), self.neighbour(-1)]
        near += [self.deep(step) for step in range(1, self.depths)]
        for device in near:
            pl.semaphore_signal(barrier, inc=1, device_id=device, device_id_type=MESH)
        pl.semaphore_wait(barrier, len(near))


def remote(source, target, send, receive, device):
    return pltpu.make_async_remote_copy(
        src_ref=source,
        dst_ref=target,
        send_sem=send,
        recv_sem=receive,
        device_id=device,
        device_id_type=MESH,
    )


class Spread:
    def __init__(self, place, source, target, send, receive, local):
        self.place, self.source, self.target = place, source, target
        self.send, self.receive, self.local = send, receive, local

    def own(self):
        return pltpu.make_async_copy(self.source, self.target.at[self.place.index], self.local)

    def start(self):
        def copy(step, carry):
            remote(
                self.source,
                self.target.at[self.place.index],
                self.send,
                self.receive,
                self.place.other(step),
            ).start()
            return carry

        lax.fori_loop(1, self.place.total, copy, 0)
        self.own().start()

    def wait(self):
        rest = self.target.at[pl.ds(0, self.place.total - 1)]
        both = remote(rest, rest, self.send, self.receive, self.place.other(1))
        both.wait_send()
        both.wait_recv()
        self.own().wait()


def gather_kernel(chunks, depths, peers, count, *refs):
    blocks, small = refs[:count], refs[count]
    fulls, small_full = refs[count + 1 : 2 * count + 1], refs[2 * count + 1]
    (z_send, z_recv, r_send, r_recv, c_send, c_recv, own_sem, s_send, s_recv, s_own) = refs[
        2 * count + 2 :
    ]
    place = Place(depths, peers)
    half = place.half
    core, cut = place.core, depths // 2

    def view(i, depth, peer):
        array, layer, rows, columns = chunks[i]
        return fulls[array].at[depth, core, peer, rows, columns]

    def block(i):
        array, layer, rows, columns = chunks[i]
        return blocks[array].at[layer, rows, columns]

    def own(i):
        return pltpu.make_async_copy(block(i), view(i, place.depth, place.peer), own_sem.at[i])

    def deep(i, step):
        return remote(
            block(i),
            view(i, place.depth, place.peer),
            z_send.at[i, step - 1],
            z_recv.at[i, step - 1],
            place.deep(step),
        )

    def part(step, way):
        if step < half:
            return slice(None)
        return slice(0, cut) if way == 0 else slice(cut, depths)

    def ring(i, step, way):
        turn = 1 if way == 0 else -1
        here = view(i, part(step, way), place.around(-turn * (step - 1)))
        return remote(
            here,
            here,
            r_send.at[i, step - 1, way],
            r_recv.at[i, step - 1, way],
            place.neighbour(turn),
        )

    def across(i, slot):
        step = (slot + 1) // 2
        turn = 1 if slot % 2 else -1
        here = view(i, slice(None), place.around(-turn * step))
        return remote(here, here, c_send.at[i, slot], c_recv.at[i, slot], place.sibling())

    slots = 2 * half
    total = len(chunks)

    def begin(i):
        for step in range(1, depths):
            deep(i, step).start()
        own(i).start()

    def first(i):
        own(i).wait()
        for step in range(1, depths):
            deep(i, step).wait_recv()
        ring(i, 1, 0).start()
        ring(i, 1, 1).start()
        across(i, 0).start()

    def later(i, step):
        ring(i, step, 0).wait_recv()
        ring(i, step, 1).wait_recv()
        if step < half:
            ring(i, step + 1, 0).start()
            ring(i, step + 1, 1).start()
            across(i, 2 * step - 1).start()
            across(i, 2 * step).start()
        else:
            across(i, 2 * step - 1).start()

    place.greet()
    begin(0)
    spread = Spread(place, small, small_full, s_send, s_recv, s_own)
    spread.start()
    for i in range(1, min(LOOK, total)):
        begin(i)
    for tick in range(total + half):
        if tick + LOOK < total:
            begin(tick + LOOK)
        if tick < total:
            first(tick)
        for step in range(1, half + 1):
            if 0 <= tick - step < total:
                later(tick - step, step)
    spread.wait()
    for i in range(total):
        for slot in range(slots):
            across(i, slot).wait()
        for step in range(1, depths):
            deep(i, step).wait_send()
        for step in range(1, half + 1):
            for way in range(2):
                ring(i, step, way).wait_send()


def chunk_list(shapes, layers):
    chunks = []
    for layer in layers:
        for which, (rows, columns) in enumerate(shapes):
            array = layer * len(shapes) + which
            if columns > WIDE:
                for start in range(0, columns, WIDE):
                    chunks.append((which, array, layer, slice(None), slice(start, start + WIDE)))
            else:
                size = rows // 4 if rows % 64 == 0 and rows > 64 else rows
                for start in range(0, rows, size):
                    chunks.append((which, array, layer, slice(start, start + size), slice(None)))
    return chunks


def gather_all(blocks, small, depths, peers):
    shapes = [b.shape[1:] for b in blocks]
    half = peers // 2
    count = 2 * len(blocks)
    plan = [(array, layer, rows, cols) for _, array, layer, rows, cols in chunk_list(shapes, (0, 1))]
    total = len(plan)

    outs = [
        jax.ShapeDtypeStruct((depths, 2, peers) + shape, jnp.bfloat16)
        for _ in range(2)
        for shape in shapes
    ]
    outs.append(jax.ShapeDtypeStruct((depths * 2 * peers,) + small.shape, small.dtype))
    dma = pltpu.SemaphoreType.DMA
    doubled = list(blocks) + list(blocks)
    return pl.pallas_call(
        functools.partial(gather_kernel, plan, depths, peers, count),
        out_shape=outs,
        in_specs=[ANY] * (count + 1),
        out_specs=[ANY] * (count + 1),
        scratch_shapes=[
            dma((total, depths - 1)),
            dma((total, depths - 1)),
            dma((total, half, 2)),
            dma((total, half, 2)),
            dma((total, 2 * half)),
            dma((total, 2 * half)),
            dma((total,)),
            dma(()),
            dma(()),
            dma(()),
        ],
        compiler_params=pltpu.CompilerParams(
            collective_id=0, has_side_effects=True, vmem_limit_bytes=60 * 2**20
        ),
    )(*doubled, small)


def sum_kernel(plan, depths, peers, count, with_small, *refs):
    lefts, rights, rest = refs[:count], refs[count : 2 * count], refs[2 * count :]
    if with_small:
        small, rest = rest[0], rest[1:]
    outs, rest = rest[:count], rest[count:]
    if with_small:
        small_all, rest = rest[0], rest[1:]
    left_bufs, right_bufs, rest = rest[:count], rest[count : 2 * count], rest[2 * count :]
    (half_send, half_recv, full_send, full_recv, z_out, z_in, own_part, x_send, x_recv, x_own) = rest[:10]
    (r_send, r_recv, z_send, z_recv) = rest[10:14]
    if with_small:
        small_in, small_sum, a_send, a_recv, a_own, b_send, b_recv, b_own = rest[14:]
    place = Place(depths, peers)
    half, core = place.half, place.core
    rows = z_out.shape[2]
    tall = depths * rows
    cut = tall // 2

    def swap(k):
        array = k // 2
        if k % 2 == 0:
            mine, theirs = lefts[array].at[core], lefts[array].at[1 - core]
            buf = left_bufs[array]
        else:
            mine = theirs = rights[array]
            buf = right_bufs[array]
        return (
            pltpu.make_async_copy(mine, buf.at[0], x_own.at[k]),
            remote(theirs, buf.at[1], x_send.at[k], x_recv.at[k], place.sibling()),
        )

    def product(i, peer):
        array, row_part, start, _ = plan[i]
        columns = pl.ds(start, WIDE)
        return jnp.dot(
            left_bufs[array][0, row_part, peer],
            right_bufs[array][0, :, columns],
            preferred_element_type=jnp.float32,
        ) + jnp.dot(
            left_bufs[array][1, row_part, peer],
            right_bufs[array][1, :, columns],
            preferred_element_type=jnp.float32,
        )

    def ring(i, step, way):
        if step == 1:
            source, target = half_send.at[i, way], half_recv.at[i, way]
        else:
            source, target = full_send.at[i, step - 2, way], full_recv.at[i, step - 2, way]
        return remote(
            source,
            target,
            r_send.at[i, step - 1, way],
            r_recv.at[i, step - 1, way],
            place.neighbour(1 if way == 0 else -1),
        )

    def deep(i, step):
        return remote(
            z_out.at[i, place.at_depth(step)],
            z_in.at[i, step - 1],
            z_send.at[i, step - 1],
            z_recv.at[i, step - 1],
            place.deep(step),
        )

    def first(i):
        found = product(i, place.around(half)).astype(jnp.bfloat16)
        half_send[i, 0] = found[:cut]
        half_send[i, 1] = found[cut:]
        ring(i, 1, 0).start()
        ring(i, 1, 1).start()

    def next_step(i, step):
        for way in range(2):
            turn = 1 if way == 0 else -1
            found = product(i, place.around(turn * (half - step + 1)))
            ring(i, step - 1, way).wait_recv()
            if step == 2:
                came = half_recv[i, way].astype(jnp.float32)
                low = found[:cut] + came if way == 0 else found[:cut]
                high = found[cut:] if way == 0 else found[cut:] + came
                full_send[i, 0, way, :cut] = low.astype(jnp.bfloat16)
                full_send[i, 0, way, cut:] = high.astype(jnp.bfloat16)
            else:
                came = full_recv[i, step - 3, way].astype(jnp.float32)
                full_send[i, step - 2, way] = (found + came).astype(jnp.bfloat16)
            ring(i, step, way).start()

    def plane(i):
        found = product(i, place.peer)
        for way in range(2):
            ring(i, half, way).wait_recv()
            found += full_recv[i, half - 2, way].astype(jnp.float32)
        for depth in range(depths):
            piece = found[depth * rows : (depth + 1) * rows]
            z_out[i, depth] = piece.astype(jnp.bfloat16)

            @pl.when(depth == place.depth)
            def _():
                own_part[i] = piece

        for step in range(1, depths):
            deep(i, step).start()

    def finish(i):
        array, _, start, out_rows = plan[i]
        found = own_part[i]
        for step in range(1, depths):
            deep(i, step).wait_recv()
            found += z_in[i, step - 1].astype(jnp.float32)
        outs[array][out_rows, pl.ds(start, WIDE)] = found

    if with_small:
        place.greet()
    else:
        place.greet_near()
    for k in reversed(range(2 * count)):
        for copy in swap(k):
            copy.start()
    if with_small:

        def send_small(step, carry):
            outer, peer = place.other(step)
            remote(
                small.at[outer * peers + peer],
                small_in.at[place.index],
                a_send,
                a_recv,
                (outer, peer),
            ).start()
            return carry

        lax.fori_loop(1, place.total, send_small, 0)
        own_small = pltpu.make_async_copy(small.at[place.index], small_in.at[place.index], a_own)
        own_small.start()
        spread = Spread(place, small_sum, small_all, b_send, b_recv, b_own)

    total = len(plan)
    ready = set()
    for tick in range(total + half + 1):
        if tick < total:
            array = plan[tick][0]
            if array not in ready:
                ready.add(array)
                for k in (2 * array + 1, 2 * array):
                    kept, sent = swap(k)
                    kept.wait()
                    sent.wait_recv()
            first(tick)
        for step in range(2, half + 1):
            if 0 <= tick - step + 1 < total:
                next_step(tick - step + 1, step)
        if 0 <= tick - half < total:
            plane(tick - half)
        if 0 <= tick - half - 1 < total:
            finish(tick - half - 1)
        if with_small and tick == 4:
            rest_in = small_in.at[pl.ds(0, place.total - 1)]
            both = remote(rest_in, rest_in, a_send, a_recv, place.other(1))
            both.wait_send()
            both.wait_recv()
            own_small.wait()
            small_sum[...] = jnp.sum(small_in[...], axis=0)
            spread.start()
    if with_small:
        spread.wait()
    for k in range(2 * count):
        swap(k)[1].wait_send()
    for i in range(total):
        for step in range(1, half + 1):
            for way in range(2):
                ring(i, step, way).wait_send()
        for step in range(1, depths):
            deep(i, step).wait_send()


def sum_all(pairs, shapes, depths, peers, call, small=None):
    half, count = peers // 2, len(pairs)
    tokens = pairs[0][0].shape[0]
    padded = -(-tokens // 128) * 128
    unit = min(shape[0] for shape in shapes)
    lefts, rights, plan = [], [], []
    for array, ((left, right), shape) in enumerate(zip(pairs, shapes)):
        parts = shape[0] // unit
        turned = jnp.pad(left, ((0, padded - tokens), (0, 0))).T
        turned = turned.reshape(depths, 2, peers, parts, unit, padded)
        lefts.append(
            turned.transpose(1, 3, 2, 0, 4, 5).reshape(2, parts, peers, depths * unit, padded)
        )
        rights.append(jnp.pad(right, ((0, padded - tokens), (0, 0))))
        for part in range(parts):
            for start in range(0, shape[1], WIDE):
                plan.append((array, part, start, pl.ds(part * unit, unit)))
    plan = plan[::-1]
    total, tall = len(plan), depths * unit
    dma = pltpu.SemaphoreType.DMA
    low = jnp.bfloat16
    scratch = [pltpu.VMEM((2,) + a.shape[1:], low) for a in lefts]
    scratch += [pltpu.VMEM((2,) + a.shape, low) for a in rights]
    scratch += [
        pltpu.VMEM((total, 2, tall // 2, WIDE), low),
        pltpu.VMEM((total, 2, tall // 2, WIDE), low),
        pltpu.VMEM((total, half - 1, 2, tall, WIDE), low),
        pltpu.VMEM((total, half - 1, 2, tall, WIDE), low),
        pltpu.VMEM((total, depths, unit, WIDE), low),
        pltpu.VMEM((total, depths - 1, unit, WIDE), low),
        pltpu.VMEM((total, unit, WIDE), jnp.float32),
        dma((2 * count,)),
        dma((2 * count,)),
        dma((2 * count,)),
        dma((total, half, 2)),
        dma((total, half, 2)),
        dma((total, depths - 1)),
        dma((total, depths - 1)),
    ]
    args = [*lefts, *rights]
    in_specs = [ANY] * (2 * count)
    out_shape = [jax.ShapeDtypeStruct(shape, jnp.float32) for shape in shapes]
    out_specs = [VMEM] * count
    if small is not None:
        args.append(small)
        in_specs.append(ANY)
        out_shape.append(jax.ShapeDtypeStruct(small.shape, jnp.float32))
        out_specs.append(VMEM)
        scratch += [
            pltpu.VMEM(small.shape, jnp.float32),
            pltpu.VMEM(small.shape[1:], jnp.float32),
        ] + [dma(())] * 6
    return pl.pallas_call(
        functools.partial(sum_kernel, plan, depths, peers, count, small is not None),
        out_shape=out_shape,
        in_specs=in_specs,
        out_specs=out_specs,
        scratch_shapes=scratch,
        compiler_params=pltpu.CompilerParams(
            collective_id=call, has_side_effects=True, vmem_limit_bytes=60 * 2**20
        ),
    )(*args)


def attention_scores(qkv_parts, position_bias, mask_add):
    head_scale = qkv_parts.shape[-1] ** (-0.5)
    scores = (
        jnp.einsum(
            "wqhd,wkhd->whqk",
            qkv_parts[:, :, 0],
            qkv_parts[:, :, 1],
            preferred_element_type=jnp.float32,
        )
        * head_scale
        + position_bias[None]
    )
    if mask_add is not None:
        scores = scores + mask_add
    return scores


def block_forward(inputs, weights, position_bias, mask_add, windows):
    norm_gains, norm_shifts, w_qkv, qv_bias, w_proj, b_proj, w_up, b_up, w_down, b_down = weights
    model_width = inputs.shape[1]
    norm_gains = norm_gains.astype(jnp.float32)
    norm_shifts = norm_shifts.astype(jnp.float32)
    normed, normal_one, inverse_one = layer_norm(inputs, norm_gains[0], norm_shifts[0])
    normed_low = normed.astype(jnp.bfloat16)
    qv_float = qv_bias.astype(jnp.float32)
    bias_full = jnp.concatenate(
        [qv_float[:model_width], jnp.zeros((model_width,), jnp.float32), qv_float[model_width:]]
    )
    qkv_low = (jnp.dot(normed_low, w_qkv, preferred_element_type=jnp.float32) + bias_full).astype(
        jnp.bfloat16
    )
    qkv_parts = qkv_low.reshape(windows, WIN, 3, HEADS, -1)
    scores = attention_scores(qkv_parts, position_bias, mask_add)
    row_max = jnp.max(scores, axis=-1, keepdims=True)
    shifted_exp = jnp.exp(scores - row_max)
    row_total = jnp.sum(shifted_exp, axis=-1, keepdims=True)
    soft_low = (shifted_exp / row_total).astype(jnp.bfloat16)
    log_total = row_max + jnp.log(row_total)
    attended = jnp.einsum(
        "whqk,wkhd->wqhd", soft_low, qkv_parts[:, :, 2], preferred_element_type=jnp.float32
    )
    attended_low = attended.reshape(inputs.shape).astype(jnp.bfloat16)
    middle = inputs + (
        jnp.dot(attended_low, w_proj, preferred_element_type=jnp.float32)
        + b_proj.astype(jnp.float32)
    )
    normed_two, normal_two, inverse_two = layer_norm(middle, norm_gains[1], norm_shifts[1])
    normed_two_low = normed_two.astype(jnp.bfloat16)
    hidden = jnp.dot(normed_two_low, w_up, preferred_element_type=jnp.float32) + b_up.astype(
        jnp.float32
    )
    activated_low = gelu_exact(hidden).astype(jnp.bfloat16)
    output = middle + (
        jnp.dot(activated_low, w_down, preferred_element_type=jnp.float32)
        + b_down.astype(jnp.float32)
    )
    kept_state = (
        normal_one,
        inverse_one,
        normed_low,
        qkv_low,
        log_total,
        attended_low,
        normal_two,
        inverse_two,
        normed_two_low,
        hidden,
        activated_low,
    )
    return (output, kept_state)


def block_backward(grad_out, weights, kept_state, position_bias, mask_add, bucket_table, windows):
    norm_gains, norm_shifts, w_qkv, qv_bias, w_proj, b_proj, w_up, b_up, w_down, b_down = weights
    (
        normal_one,
        inverse_one,
        normed_low,
        qkv_low,
        log_total,
        attended_low,
        normal_two,
        inverse_two,
        normed_two_low,
        hidden,
        activated_low,
    ) = kept_state
    model_width = grad_out.shape[1]
    norm_gains = norm_gains.astype(jnp.float32)
    grad_down_low = grad_out.astype(jnp.bfloat16)
    down_bias_grad = jnp.sum(grad_down_low, axis=0, dtype=jnp.float32)
    grad_act = jnp.einsum("rd,fd->rf", grad_down_low, w_down, preferred_element_type=jnp.float32)
    gelu_back = jax.vjp(gelu_exact, hidden)[1]
    grad_hidden_low = gelu_back(grad_act)[0].astype(jnp.bfloat16)
    up_bias_grad = jnp.sum(grad_hidden_low, axis=0, dtype=jnp.float32)
    grad_normed_two = jnp.einsum(
        "rf,df->rd", grad_hidden_low, w_up, preferred_element_type=jnp.float32
    )
    grad_mid_norm, gain_two_grad, shift_two_grad = norm_back(
        grad_normed_two, normal_two, inverse_two, norm_gains[1]
    )
    grad_middle = grad_out + grad_mid_norm
    grad_branch_low = grad_middle.astype(jnp.bfloat16)
    proj_bias_grad = jnp.sum(grad_branch_low, axis=0, dtype=jnp.float32)
    grad_attended_low = jnp.einsum(
        "rd,cd->rc", grad_branch_low, w_proj, preferred_element_type=jnp.float32
    ).astype(jnp.bfloat16)
    qkv_parts = qkv_low.reshape(windows, WIN, 3, HEADS, -1)
    scores = attention_scores(qkv_parts, position_bias, mask_add)
    soft = jnp.exp(scores - log_total)
    soft_low = soft.astype(jnp.bfloat16)
    grad_heads = grad_attended_low.reshape(windows, WIN, HEADS, -1)
    grad_value = jnp.einsum(
        "whqk,wqhd->wkhd", soft_low, grad_heads, preferred_element_type=jnp.float32
    )
    grad_soft = jnp.einsum(
        "wqhd,wkhd->whqk", grad_heads, qkv_parts[:, :, 2], preferred_element_type=jnp.float32
    )
    grad_scores_low = (
        soft * (grad_soft - jnp.sum(soft * grad_soft, axis=-1, keepdims=True))
    ).astype(jnp.bfloat16)
    head_scale = qkv_parts.shape[-1] ** (-0.5)
    grad_query = (
        jnp.einsum(
            "whqk,wkhd->wqhd",
            grad_scores_low,
            qkv_parts[:, :, 1],
            preferred_element_type=jnp.float32,
        )
        * head_scale
    )
    grad_key = (
        jnp.einsum(
            "whqk,wqhd->wkhd",
            grad_scores_low,
            qkv_parts[:, :, 0],
            preferred_element_type=jnp.float32,
        )
        * head_scale
    )
    score_sum = jnp.sum(grad_scores_low, axis=0, dtype=jnp.float32).reshape(HEADS, -1)
    table_grad = jnp.einsum("hn,nb->bh", score_sum, bucket_table, precision=lax.Precision.HIGHEST)
    grad_qkv_low = (
        jnp.stack([grad_query, grad_key, grad_value], axis=2)
        .reshape(qkv_low.shape)
        .astype(jnp.bfloat16)
    )
    column_sums = jnp.sum(grad_qkv_low, axis=0, dtype=jnp.float32)
    qv_grad = jnp.concatenate([column_sums[:model_width], column_sums[2 * model_width :]])
    grad_normed = jnp.einsum("re,de->rd", grad_qkv_low, w_qkv, preferred_element_type=jnp.float32)
    grad_in_norm, gain_one_grad, shift_one_grad = norm_back(
        grad_normed, normal_one, inverse_one, norm_gains[0]
    )
    grad_input = grad_middle + grad_in_norm
    grads = (
        jnp.stack([gain_one_grad, gain_two_grad]),
        jnp.stack([shift_one_grad, shift_two_grad]),
        qv_grad,
        proj_bias_grad,
        up_bias_grad,
        down_bias_grad,
    )
    pairs = (
        (normed_low, grad_qkv_low),
        (attended_low, grad_branch_low),
        (normed_two_low, grad_hidden_low),
        (activated_low, grad_down_low),
    )
    return (grad_input, grads, table_grad, pairs)


def shards(
    outer_count,
    peer_count,
    patches,
    out_grad,
    norm_gain,
    norm_shift,
    qkv_weight,
    qv_bias,
    rel_table,
    proj_weight,
    proj_bias,
    up_weight,
    up_bias,
    down_weight,
    down_bias,
    tile_perm,
    window_slot,
    mask_ids,
    bias_index,
):
    windows = patches.shape[0] // WIN
    model_width = patches.shape[1]
    depths = outer_count // 2
    devices = outer_count * peer_count
    capacity = (windows + peer_count - 1) // peer_count
    device_index = lax.axis_index(("dp", "fsdp"))
    total_windows = tile_perm.shape[0]
    slot_ids = jnp.arange(total_windows, dtype=jnp.int32)

    def one_hot_pick(keys, values):
        return jnp.sum(jnp.where(keys[None, :] == slot_ids[:, None], values[None, :], 0), axis=1)

    def look_up(values, at):
        hit = at[:, None] == jnp.arange(values.shape[0], dtype=jnp.int32)[None, :]
        return jnp.sum(jnp.where(hit, values[None, :], 0), axis=1)

    source_of = one_hot_pick(window_slot, look_up(window_slot, tile_perm))
    target_of = one_hot_pick(source_of, slot_ids)
    region_slot = one_hot_pick(window_slot, mask_ids)
    own_slots = device_index * windows + jnp.arange(windows, dtype=jnp.int32)

    def rank_of(slots, device_of):
        grid_view = device_of.reshape(-1, windows)
        earlier = jnp.arange(windows)[None, :] < jnp.arange(windows)[:, None]
        same_peer = grid_view[:, :, None] == grid_view[:, None, :]
        ranks = jnp.sum(same_peer & earlier[None], axis=2).reshape(-1)
        return look_up(ranks, slots)

    def peer_of(slots):
        return slots // windows % peer_count

    own_source = look_up(source_of, own_slots)
    own_target = look_up(target_of, own_slots)
    forward_send = peer_of(own_target) * capacity + rank_of(own_slots, target_of // windows)
    forward_take = peer_of(own_source) * capacity + rank_of(own_source, target_of // windows)
    backward_send = peer_of(own_source) * capacity + rank_of(own_slots, source_of // windows)
    backward_take = peer_of(own_target) * capacity + rank_of(own_target, source_of // windows)
    mask_add = region_mask(look_up(region_slot, own_slots))
    bucket_table = (
        bias_index.reshape(-1)[:, None] == jnp.arange(rel_table.shape[1], dtype=jnp.int32)[None, :]
    ).astype(jnp.float32)
    tables = rel_table.astype(jnp.float32)
    bias_one = jnp.einsum(
        "nb,bh->hn", bucket_table, tables[0], precision=lax.Precision.HIGHEST
    ).reshape(HEADS, WIN, WIN)
    bias_two = jnp.einsum(
        "nb,bh->hn", bucket_table, tables[1], precision=lax.Precision.HIGHEST
    ).reshape(HEADS, WIN, WIN)

    def choose(rows, at, count):
        spots = jnp.arange(count, dtype=jnp.int32)
        hit = spots[:, None] == at[None, :]
        return sum(
            jnp.where(hit[:, w][:, None, None], rows[w][None], jnp.zeros((), rows.dtype))
            for w in range(rows.shape[0])
        )

    def take(rows, at):
        hit = at[:, None] == jnp.arange(rows.shape[0], dtype=jnp.int32)[None, :]
        return sum(
            jnp.where(hit[:, w][:, None, None], rows[w][None], jnp.zeros((), rows.dtype))
            for w in range(rows.shape[0])
        )

    def move(rows_low, send, fetch):
        parts = rows_low.reshape(windows, WIN, model_width)
        sectioning = choose(parts, send, peer_count * capacity)
        arrived = lax.all_to_all(sectioning, "fsdp", split_axis=0, concat_axis=0, tiled=True)
        return take(arrived, fetch).reshape(rows_low.shape)

    def to_shifted(rows_low):
        return move(rows_low, forward_send, forward_take)

    def from_shifted(rows_low):
        return move(rows_low, backward_send, backward_take)

    vectors = (norm_gain, norm_shift, qv_bias, proj_bias, up_bias, down_bias)
    flat = jnp.concatenate([v.reshape(-1) for v in vectors])
    small = jnp.pad(flat, (0, -flat.shape[0] % 2048)).reshape(-1, 128)
    matrices = (qkv_weight, proj_weight, up_weight, down_weight)
    *fulls, small_full = gather_all(matrices, small, depths, peer_count)
    small_full = small_full.reshape(devices, -1)
    whole, offset = [], 0
    for v in vectors:
        size = v.size
        piece = small_full[:, offset : offset + size].reshape((devices,) + v.shape)
        offset += size
        piece = jnp.moveaxis(piece, 0, -2)
        whole.append(piece.reshape(v.shape[:-1] + (-1,)))

    def weights_of(layer):
        gains, shifts, qv, proj_b, up_b, down_b = [v[layer] for v in whole]
        w_qkv, w_proj, w_up, w_down = [
            fulls[4 * layer + k].reshape(-1, matrices[k].shape[-1]) for k in range(4)
        ]
        return (gains, shifts, w_qkv, qv, w_proj, proj_b, w_up, up_b, w_down, down_b)

    first_weights, second_weights = weights_of(0), weights_of(1)
    grad_two = to_shifted(out_grad)
    output_one, state_one = block_forward(
        patches.astype(jnp.float32), first_weights, bias_one, None, windows
    )
    second_input = to_shifted(output_one.astype(jnp.bfloat16))
    output_two, state_two = block_forward(
        second_input.astype(jnp.float32), second_weights, bias_two, mask_add, windows
    )
    block_out = from_shifted(output_two.astype(jnp.bfloat16))
    shapes = [m.shape[1:] for m in matrices]
    grad_input_two, grads_two, table_two, pairs_two = block_backward(
        grad_two.astype(jnp.float32), second_weights, state_two, bias_two, mask_add, bucket_table, windows
    )
    sums_two = sum_all(pairs_two, shapes, depths, peer_count, 1)
    grad_one = from_shifted(grad_input_two.astype(jnp.bfloat16))
    grad_patches, grads_one, table_one, pairs_one = block_backward(
        grad_one.astype(jnp.float32), first_weights, state_one, bias_one, None, bucket_table, windows
    )
    small_grads = []
    for one, two, v in zip(grads_one, grads_two, vectors):
        both = jnp.stack([one, two]).reshape(v.shape[:-1] + (devices, v.shape[-1]))
        small_grads.append(jnp.moveaxis(both, -2, 0).reshape(devices, -1))
    table = jnp.stack([table_one, table_two]).reshape(-1)
    table = jnp.pad(table, (0, -table.shape[0] % devices)).reshape(devices, -1)
    packed = jnp.concatenate(small_grads + [table], axis=1)
    width = packed.shape[1]
    packed = jnp.pad(packed, ((0, 0), (0, -width % 1024))).reshape(devices, -1, 128)
    *sums_one, small_all = sum_all(pairs_one, shapes, depths, peer_count, 2, packed)
    small_all = small_all.reshape(devices, -1)
    mine = lax.dynamic_index_in_dim(small_all, device_index, 0, keepdims=False)
    vector_grads, offset = [], 0
    for v in vectors:
        vector_grads.append(mine[offset : offset + v.size].reshape(v.shape))
        offset += v.size
    table_total = small_all[:, offset:width].reshape(-1)[: rel_table.size].reshape(rel_table.shape)
    grad_qkv, grad_proj, grad_up, grad_down = [
        jnp.stack([one, two]) for one, two in zip(sums_one, sums_two)
    ]
    return (
        block_out,
        grad_patches,
        vector_grads[0],
        vector_grads[1],
        grad_qkv,
        vector_grads[2],
        table_total,
        grad_proj,
        vector_grads[3],
        grad_up,
        vector_grads[4],
        grad_down,
        vector_grads[5],
    )


ROWS = 112
GAP, F_GAP = 2, 1
EARLY = {11: 1, 17: 6, 22: 10}
F_BUDGET, B_BUDGET = 5.0, 5.0
KEYS = 128
GROUP = 4
SCALE = 32**-0.5
LOW = jnp.bfloat16
WHOLE = jnp.float32
NEVER = -1e30


class Queue:
    def __init__(self, budget):
        self.pieces, self.budget = [], budget

    def add(self, tick, cost, work, *arguments):
        self.pieces.append((tick, cost, work, arguments))

    def run(self, tick, after, all_of_it=False):
        left = self.budget
        while self.pieces and self.pieces[0][0] <= tick and (left > 0 or all_of_it):
            left -= self.step(after)

    def step(self, after):
        _, cost, work, arguments = self.pieces.pop(0)
        work(*arguments)
        after()
        return cost


def row_loop(count, size, body):
    def step(i, carry):
        body(pl.multiple_of(i * size, size))
        return carry

    lax.fori_loop(0, count // size, step, 0)


def lane_mask(rows, head):
    lane = lax.broadcasted_iota(jnp.int32, (rows, 128), 1)
    return lane // 32 == head


def per_head(value):
    tall = jnp.concatenate([value, jnp.zeros((KEYS - ROWS, 128), value.dtype)], axis=0)
    zero = jnp.zeros((), value.dtype)
    return jnp.concatenate(
        [jnp.where(lane_mask(KEYS, head), tall, zero) for head in range(GROUP)], axis=0
    )


def dot(a, b, over=(1, 0)):
    return lax.dot_general(
        a, b, (((over[0],), (over[1],)), ((), ())), preferred_element_type=jnp.float32
    )


def normal_parts(block):
    mean = jnp.mean(block, axis=1, keepdims=True)
    centered = block - mean
    inverse = lax.rsqrt(jnp.mean(centered * centered, axis=1, keepdims=True) + epsilon)
    return centered * inverse, inverse


class Exchange:
    def __init__(self, place, out, into, send, receive, parts):
        self.place, self.out, self.into = place, out, into
        self.send, self.receive = send, receive
        self.width = out.shape[-1] // parts

    def columns(self, part):
        return slice(part * self.width, (part + 1) * self.width)

    def copy(self, part, step):
        place = self.place
        peer = lax.rem(place.peer + step, place.peers)
        return remote(
            self.out.at[peer, :, self.columns(part)],
            self.into.at[place.peer, :, self.columns(part)],
            self.send.at[part, step - 1],
            self.receive.at[part, step - 1],
            (place.depth * 2 + place.core, peer),
        )

    def give(self, part, tiles, chosen):
        columns = self.columns(part)
        for peer in range(self.place.peers):
            self.out[peer, :, columns] = tiles[chosen[peer], :, columns]
        self.into[self.place.peer, :, columns] = self.out[self.place.peer, :, columns]
        for step in range(1, self.place.peers):
            self.copy(part, step).start()

    def await_part(self, part):
        for step in range(1, self.place.peers):
            self.copy(part, step).wait_recv()

    def finish(self, parts):
        for part in range(parts):
            for step in range(1, self.place.peers):
                self.copy(part, step).wait_send()


class Gather:
    def __init__(self, place, chunks, early, blocks, fulls, sems):
        self.place, self.chunks, self.blocks, self.fulls = place, chunks, blocks, fulls
        (self.z_send, self.z_recv, self.r_send, self.r_recv, self.c_send, self.c_recv, self.own_sem, self.relay_send) = sems
        self.half, self.cut = place.half, place.depths // 2
        self.early = early
        self.late = [i for i in range(len(chunks)) if i not in early]
        self.begun = 0
        self.gone = len(self.late) - 1 + F_GAP * self.half
        assert place.depths == 2 * self.half == 4

    def whole_at(self, i):
        if i in self.early:
            return max(self.whole_at(i - 1), self.early[i] + 2 * self.half + 8)
        return self.late.index(i) + F_GAP * self.half

    def full(self, i):
        array, layer, columns = self.chunks[i]
        return self.fulls[layer * len(self.blocks) + array]

    def view(self, i, depth, peer, rows=slice(None)):
        return self.full(i).at[depth, self.place.core, peer, rows, self.chunks[i][2]]

    def plane(self, i, depth):
        return self.full(i).at[depth, self.place.core, :, :, self.chunks[i][2]]

    def block(self, i, rows=slice(None)):
        array, layer, columns = self.chunks[i]
        return self.blocks[array].at[layer, rows, columns]

    def own(self, i):
        place = self.place
        return pltpu.make_async_copy(
            self.block(i), self.view(i, place.depth, place.peer), self.own_sem.at[i]
        )

    def deep(self, i, step):
        place = self.place
        if i in self.early:
            source = target = self.plane(i, place.depth)
        else:
            source, target = self.block(i), self.view(i, place.depth, place.peer)
        return remote(
            source,
            target,
            self.z_send.at[i, step - 1],
            self.z_recv.at[i, step - 1],
            place.deep(step),
        )

    def unless_far(self, i, step, work):
        place = self.place
        far = {1: place.depths - 1, place.depths - 1: 0}
        if i in self.early and step in far:
            pl.when(place.depth != far[step])(work)
        else:
            work()

    def relay(self, i):
        place = self.place
        end = 3 * (place.depth - 1)
        here = self.plane(i, 3 - end)
        return remote(
            here,
            here,
            self.relay_send.at[i],
            self.z_recv.at[i, 2 * (place.depth - 1)],
            (end * 2 + place.core, place.peer),
        )

    def if_between(self, work):
        depth = self.place.depth
        pl.when(jnp.logical_and(depth > 0, depth < self.place.depths - 1))(work)

    def pass_on(self, i):
        self.deep(i, 2).wait_recv()
        self.if_between(lambda: self.relay(i).start())
        self.across(i, 2).start()

    def ring(self, i, step, way):
        place = self.place
        turn = 1 if way == 0 else -1
        peer = place.around(-turn * (step - 1))
        if i in self.early:
            rows = slice(None)
            if step == self.half:
                cut = self.full(i).shape[3] // 2
                rows = slice(0, cut) if way == 0 else slice(cut, 2 * cut)
            target = self.view(i, place.depth, peer, rows)
            source = self.block(i, rows) if step == 1 else target
        else:
            depths = slice(None)
            if step == self.half:
                depths = slice(0, self.cut) if way == 0 else slice(self.cut, place.depths)
            source = target = self.view(i, depths, peer)
        return remote(
            source,
            target,
            self.r_send.at[i, step - 1, way],
            self.r_recv.at[i, step - 1, way],
            place.neighbour(turn),
        )

    def across(self, i, slot):
        place = self.place
        if i in self.early:
            here = self.plane(i, place.at_depth(-slot))
        else:
            step = (slot + 1) // 2
            turn = 1 if slot % 2 else -1
            here = self.view(i, slice(None), place.around(-turn * step))
        return remote(here, here, self.c_send.at[i, slot], self.c_recv.at[i, slot], place.sibling())

    def begin(self, i):
        for step in range(1, self.place.depths):
            self.deep(i, step).start()
        self.own(i).start()

    def start_ring(self, i):
        self.ring(i, 1, 0).start()
        self.ring(i, 1, 1).start()

    def first(self, i):
        self.own(i).wait()
        for step in range(1, self.place.depths):
            self.deep(i, step).wait_recv()
        self.start_ring(i)
        self.across(i, 0).start()

    def later(self, i, step):
        self.ring(i, step, 0).wait_recv()
        self.ring(i, step, 1).wait_recv()
        early = i in self.early
        if step < self.half:
            self.ring(i, step + 1, 0).start()
            self.ring(i, step + 1, 1).start()
            if not early:
                self.across(i, 2 * step - 1).start()
                self.across(i, 2 * step).start()
        elif early:
            self.own(i).wait()
            self.across(i, 0).start()
        else:
            self.across(i, 2 * step - 1).start()

    def spread_planes(self, i):
        for step in (1, 3):
            self.deep(i, step).wait_recv()
            self.across(i, step).start()

    def tick(self, tick):
        late = self.late
        for i, start in self.early.items():
            if tick == start:
                self.own(i).start()
                self.start_ring(i)
            step, odd = divmod(tick - start, 2)
            if 1 <= step <= self.half and not odd:
                self.later(i, step)
            if 0 <= step - self.half < self.place.depths - 1 and not odd:
                deep = (2, 1, 3)[step - self.half]
                self.unless_far(i, deep, self.deep(i, deep).start)
            if tick == start + 2 * self.half + 3:
                self.pass_on(i)
            if tick == self.whole_at(i):
                self.spread_planes(i)
        while self.begun < min(len(late), tick + 1 + min(2 + (tick + 1) // 2, 6)):
            self.begin(late[self.begun])
            self.begun += 1
        if tick < len(late):
            self.first(late[tick])
        for step in range(1, self.half + 1):
            if 0 <= tick - step * F_GAP < len(late):
                self.later(late[tick - step * F_GAP], step)

    def await_across(self, i):
        for slot in range(2 * self.half):
            self.across(i, slot).wait_recv()

    def finish(self):
        for i in range(len(self.chunks)):
            for slot in range(2 * self.half):
                self.across(i, slot).wait_send()
            for step in range(1, self.place.depths):
                self.unless_far(i, step, self.deep(i, step).wait_send)
            if i in self.early:
                self.if_between(lambda i=i: self.relay(i).wait_send())
            for step in range(1, self.half + 1):
                for way in range(2):
                    self.ring(i, step, way).wait_send()


def forward_kernel(chunks, depths, peers, *refs):
    r = types.SimpleNamespace()
    (
        r.w0, r.w1, r.w2, r.w3, r.gain, r.shift, r.qv, r.proj_b, r.up_b, r.down_b, r.x0, r.grads, r.table, r.bias_index, r.region, r.forward_send,
        r.forward_take, r.backward_send, r.backward_take, r.f0, r.f1, r.f2, r.f3, r.f4, r.f5, r.f6, r.f7,
        r.moved_grad, r.result, r.left0, r.left1, r.left2, r.left3, r.low_x, r.middle, r.qkv, r.probs,
        r.slope, r.vec32, r.small_full, r.small, r.tables, r.index, r.mask, r.bias, r.x, r.x0w, r.normed, r.att, r.normed_two, r.act, r.mid,
        r.q_s, r.p_s, r.slope_s, r.wide_a, r.wide_b, r.total, r.sib_a, r.sib_b, r.turned, r.wide_t, r.left_a, r.left_b,
        r.g_out, r.g_in, r.x_out, r.x_in, r.y_out, r.y_in, r.vec64, r.vec128, r.z_send, r.z_recv, r.r_send,
        r.r_recv, r.c_send, r.c_recv, r.own_sem, r.relay_send, r.s_send, r.s_recv, r.s_own, r.load, r.save, r.swap_send,
        r.swap_recv, r.eg_send, r.eg_recv, r.ex_send, r.ex_recv, r.ey_send, r.ey_recv,
    ) = refs
    place = Place(depths, peers)
    gather = Gather(
        place,
        chunks,
        EARLY,
        (r.w0, r.w1, r.w2, r.w3),
        (r.f0, r.f1, r.f2, r.f3, r.f4, r.f5, r.f6, r.f7),
        (r.z_send, r.z_recv, r.r_send, r.r_recv, r.c_send, r.c_recv, r.own_sem, r.relay_send),
    )
    spread = Spread(place, r.small, r.small_full, r.s_send, r.s_recv, r.s_own)
    eg = Exchange(place, r.g_out, r.g_in, r.eg_send, r.eg_recv, 1)
    ex = Exchange(place, r.x_out, r.x_in, r.ex_send, r.ex_recv, 4)
    ey = Exchange(place, r.y_out, r.y_in, r.ey_send, r.ey_recv, 4)
    windows = 2
    tall = windows * ROWS
    per_layer = len(chunks) // 2
    total = len(chunks)
    queue = Queue(F_BUDGET)
    saved, loaded, used = [], [], set()

    def spill(source, target):
        copy = pltpu.make_async_copy(source, target, r.save.at[len(saved)])
        copy.start()
        saved.append(copy)

    def staged(i):
        array, layer, columns = chunks[i]
        count = sum(1 for c in chunks[:i] if (c[0] == 3) == (array == 3))
        return (r.wide_b if array == 3 else r.wide_a).at[count % 2]

    def load(i):
        array, layer, columns = chunks[i]
        source = gather.fulls[layer * 4 + array].at[:, :, :, :, columns]
        return pltpu.make_async_copy(source, staged(i), r.load.at[i])

    def weight(i):
        assert i in loaded
        used.add(i)
        load(i).wait()
        value = staged(i)[...]
        return value.reshape(-1, value.shape[-1])

    def fetch(i):
        gather.await_across(i)
        load(i).start()

    def unpack():
        spread.wait()
        count = place.total
        row = lax.broadcasted_iota(jnp.int32, (count, 128), 0)
        lane = lax.broadcasted_iota(jnp.int32, (count, 128), 1)

        def spread_lanes(line, member, size):
            each = 128 // size
            found = jnp.zeros((count, 128), WHOLE)
            for turn in range(each):
                spot = (member + turn) % each
                rolled = line if turn == 0 else pltpu.roll(line, turn * size, 1)
                found += jnp.where((lane // size == spot) & (row % each == spot), rolled, 0.0)
            blocks = [
                jnp.sum(found[each * b : each * (b + 1)], axis=0, keepdims=True)
                for b in range(count // each)
            ]
            return jnp.concatenate(blocks, axis=1)

        for k in range(3):
            line = r.small_full[:, k, :].astype(WHOLE)
            for member in range(4):
                r.vec32[4 * k + member : 4 * k + member + 1, :] = spread_lanes(line, member, 32)
        line = r.small_full[:, 3, :].astype(WHOLE)
        for member in range(2):
            r.vec64[member : member + 1, :] = spread_lanes(line, member, 64)
        for member in range(2):
            line = r.small_full[:, 4 + member, :].astype(WHOLE)
            r.vec128[member : member + 1, :] = jnp.concatenate(
                [line[d : d + 1] for d in range(count)], axis=1
            )

    def pack():
        r.small[...] = jnp.zeros(r.small.shape, WHOLE)
        gain, shift = r.gain[...].astype(WHOLE), r.shift[...].astype(WHOLE)
        proj_b, down_b = r.proj_b[...].astype(WHOLE), r.down_b[...].astype(WHOLE)
        qv, up_b = r.qv[...].astype(WHOLE), r.up_b[...].astype(WHOLE)
        each = proj_b.shape[1]
        for layer in range(2):
            for k in range(2):
                columns = slice((2 * layer + k) * each, (2 * layer + k + 1) * each)
                r.small[0:1, columns] = gain[layer, k : k + 1]
                r.small[1:2, columns] = shift[layer, k : k + 1]
            r.small[2:3, layer * each : (layer + 1) * each] = proj_b[layer : layer + 1]
            r.small[2:3, (2 + layer) * each : (3 + layer) * each] = down_b[layer : layer + 1]
            r.small[3:4, 2 * layer * each : 2 * (layer + 1) * each] = qv[layer : layer + 1]
            r.small[4 + layer : 5 + layer, :] = up_b[layer : layer + 1]

    def make_tables():
        count = r.table.shape[2]
        r.index[...] = jnp.full(r.index.shape, count, jnp.int32)
        r.index[:WIN, :WIN] = r.bias_index[...]
        for layer in range(2):
            r.wide_t[...] = jnp.full(r.wide_t.shape, NEVER, WHOLE)
            r.wide_t[:, :count] = r.table[layer].astype(WHOLE)
            turned = r.wide_t[...]
            order = [turned[k % 8 * GROUP + k // 8 :][:1] for k in range(HEADS)]
            r.tables[layer * HEADS : (layer + 1) * HEADS, :] = jnp.concatenate(order, axis=0).astype(LOW)

        def label(axis, region):
            place = lax.broadcasted_iota(jnp.int32, (ROWS, KEYS), axis)
            row = lax.shift_right_logical(place * 6554, 16)
            right = jnp.where(place - 10 * row >= 5, 1, 0)
            lower = jnp.where(row >= 5, 1, 0)
            return lax.rem(region, 2) * right + 2 * lax.div(region, 2) * lower

        for w in range(windows):
            same = label(0, r.region[w]) == label(1, r.region[w])
            r.mask[w] = jnp.where(same, 0.0, masked_score)

    def bias_rows(start, stop):
        buckets = lax.broadcasted_iota(jnp.int32, (384, KEYS), 0)

        def step(i, carry):
            rows = pl.ds(pl.multiple_of(i * 8, 8), 8)
            lines = r.index[rows, :]
            found = []
            for row in range(8):
                hot = jnp.where(buckets == lines[row : row + 1], 1.0, 0.0).astype(LOW)
                found.append(dot(r.tables[...], hot))
            for k in range(2 * HEADS):
                layer, head, g = k // HEADS, k // 8 % GROUP, k % 8
                block = jnp.concatenate([one[k : k + 1] for one in found], axis=0)
                r.bias[layer, g, rows, head * KEYS : (head + 1) * KEYS] = block
            return carry

        lax.fori_loop(start, stop, step, 0)

    def vec(k):
        return r.vec32[k : k + 1, :]

    def pad_windows(source):
        flat = r.mid.at[1]
        flat[0 : windows * WIN, :] = source[...].astype(WHOLE)
        r.total[...] = jnp.zeros(r.total.shape, WHOLE)
        for w in range(windows):
            r.total[w * ROWS : w * ROWS + WIN, :] = flat[w * WIN : (w + 1) * WIN, :]

    def norm(source, target, layer, k):
        gain, shift = vec(2 * layer + k), vec(4 + 2 * layer + k)

        def body(start):
            rows = pl.ds(start, 32)
            parts, _ = normal_parts(source[rows, :].astype(WHOLE))
            target[rows, :] = (parts * gain + shift).astype(LOW)

        row_loop(tall, 32, body)

    def enter(layer):
        x = r.x.at[layer]
        if layer == 0:
            pad_windows(r.x0)
            x[...] = r.total[...].astype(LOW)
        else:
            for part in range(4):
                ex.await_part(part)
            for w in range(windows):
                x[w * ROWS : (w + 1) * ROWS, :] = r.x_in[r.forward_take[w]]
        spill(x, r.low_x.at[layer])
        norm(x, r.normed.at[layer], layer, 0)
        swap(layer, 0).start()

    def project(layer, i):
        part = i % per_layer
        found = dot(r.normed[layer], weight(i))
        if part != 1:
            half = part // 2
            found = found + r.vec64[layer : layer + 1, half * 1024 : (half + 1) * 1024]
        r.q_s[layer, :, part * 1024 : (part + 1) * 1024] = found.astype(LOW)

    def attend(layer, w):
        def step(g, carry):
            rows = slice(w * ROWS, (w + 1) * ROWS)
            start = pl.multiple_of(g * 128, 128)
            q = r.q_s[layer, rows, pl.ds(start, 128)]
            k = r.q_s[layer, rows, pl.ds(start + 1024, 128)]
            v = r.q_s[layer, rows, pl.ds(start + 2048, 128)]
            scores = dot(q, per_head(k), (1, 1)) * SCALE + r.bias[layer, g]
            heads = []
            for head in range(GROUP):
                one = scores[:, head * KEYS : (head + 1) * KEYS]
                if layer == 1:
                    one = one + r.mask[w]
                shifted = jnp.exp(one - jnp.max(one, axis=1, keepdims=True))
                heads.append(
                    (shifted * (1.0 / jnp.sum(shifted, axis=1, keepdims=True))).astype(LOW)
                )
            found = jnp.concatenate(heads, axis=1)
            r.p_s[layer, w * 8 + g] = found
            r.att[layer, rows, pl.ds(start, 128)] = dot(found, per_head(v)).astype(LOW)
            return carry

        lax.fori_loop(0, 8, step, 0)

    def branch(layer, i):
        spill(r.q_s.at[layer], r.qkv.at[layer])
        spill(r.p_s.at[layer], r.probs.at[layer])
        swap(layer, 1).start()
        found = dot(r.att[layer], weight(i)) + vec(8 + layer)
        r.mid[layer] = r.x[layer].astype(WHOLE) + found
        spill(r.mid.at[layer], r.middle.at[layer])

    def second_norm(layer):
        norm(r.mid.at[layer], r.normed_two.at[layer], layer, 1)
        swap(layer, 2).start()

    def widen(layer, i):
        part = i % per_layer - 4
        columns = slice(part * 1024, (part + 1) * 1024)
        r.total[...] = dot(r.normed_two[layer], weight(i)) + r.vec128[layer : layer + 1, columns]

        def body(start):
            rows = pl.ds(start, 16)
            v = r.total[rows, :]
            spread_half = 0.5 * (1.0 + lax.erf(v * (2.0**-0.5)))
            density = jnp.exp(-0.5 * v * v) * 0.3989422804014327
            r.act[layer, rows, columns] = (v * spread_half).astype(LOW)
            r.slope_s[layer, rows, columns] = (spread_half + v * density).astype(LOW)

        row_loop(tall, 16, body)
        if part == 3:
            spill(r.slope_s.at[layer], r.slope.at[layer])
            swap(layer, 3).start()

    def narrow(layer, i):
        part = i % per_layer - 8
        columns = slice(part * 256, (part + 1) * 256)
        found = dot(r.act[layer], weight(i)) + vec(10 + layer)[:, columns]
        found = (r.mid[layer, :, columns] + found).astype(LOW)
        for w in range(windows):
            r.x0w[w, :, columns] = found[w * ROWS : (w + 1) * ROWS]
        if layer == 0:
            ex.give(part, r.x0w, r.forward_send)
        else:
            ey.give(part, r.x0w, r.backward_send)

    sources = (r.normed, r.att, r.normed_two, r.act)

    def swap(layer, array):
        target = (r.sib_b if array == 3 else r.sib_a.at[array]).at[layer]
        return remote(
            sources[array].at[layer],
            target,
            r.swap_send.at[layer, array],
            r.swap_recv.at[layer, array],
            place.sibling(),
        )

    def turn(layer, array):
        swap(layer, array).wait_recv()
        mine = sources[array].at[layer]
        theirs = (r.sib_b if array == 3 else r.sib_a.at[array]).at[layer]
        unit = r.left0.shape[-2] // depths
        pad = jnp.zeros((256 - tall, 128), WHOLE)
        rounds = peers if array == 3 else 1
        for f in range(rounds):
            for depth in range(depths):
                start = (depth * 2 + place.core) * rounds * 128 + f * 128
                columns = pl.ds(pl.multiple_of(start, 128), 128)
                for side, ref in enumerate((mine, theirs)):
                    block = jnp.concatenate([ref[:, columns].astype(WHOLE), pad], axis=0)
                    r.turned[depth, :, side * 256 : (side + 1) * 256] = block.T
            for part in range(4):
                found = jnp.concatenate(
                    [r.turned[depth, part * unit : (part + 1) * unit] for depth in range(depths)],
                    axis=0,
                ).astype(LOW)
                if array == 3:
                    r.left_b[layer, part, f] = found
                else:
                    r.left_a[layer, array, part] = found
        if array == 3:
            spill(r.left_b.at[layer], r.left3.at[layer])
        else:
            spill(r.left_a.at[layer, array], (r.left0, r.left1, r.left2)[array].at[layer])

    pack()
    place.greet()
    gather.begin(gather.late[0])
    gather.begun = 1
    pad_windows(r.grads)
    for w in range(windows):
        r.x0w[w] = r.total[w * ROWS : (w + 1) * ROWS, :].astype(LOW)
    eg.give(0, r.x0w, r.forward_send)
    spread.start()

    def at(layer, part):
        return gather.whole_at(layer * per_layer + part) + 1

    queue.add(0, 1, make_tables)
    queue.add(0, 5, bias_rows, 0, 7)
    queue.add(0, 5, bias_rows, 7, ROWS // 8)
    queue.add(2, 1, unpack)
    for layer in range(2):
        base = layer * per_layer
        queue.add(2 if layer == 0 else at(0, 11) + 1, 2, enter, layer)
        for part in range(3):
            queue.add(at(layer, part), 1.5, project, layer, base + part)
        for w in range(windows):
            queue.add(at(layer, 2), 5, attend, layer, w)
        queue.add(at(layer, 3), 1.5, branch, layer, base + 3)
        queue.add(at(layer, 3), 1.5, second_norm, layer)
        for part in range(4):
            queue.add(at(layer, 4 + part), 3.5, widen, layer, base + 4 + part)
            if part < 3:
                queue.add(at(layer, 4 + part), 1, turn, layer, part)
        for part in range(4):
            queue.add(at(layer, 8 + part), 1.5, narrow, layer, base + 8 + part)
        queue.add(at(layer, 11) + 1, 4, turn, layer, 3)

    last = gather.gone + 1
    state = types.SimpleNamespace(tick=0)

    def pump():
        while len(loaded) < total and gather.whole_at(len(loaded)) <= state.tick:
            i = len(loaded)
            same = [j for j in range(i) if (chunks[j][0] == 3) == (chunks[i][0] == 3)]
            if len(same) > 1 and same[-2] not in used:
                break
            fetch(i)
            loaded.append(i)

    for tick in range(last + 1):
        state.tick = tick
        gather.tick(tick)
        pump()
        queue.run(tick, pump)
        if tick == 3:
            eg.await_part(0)
            for w in range(windows):
                r.moved_grad[w] = r.g_in[r.forward_take[w]]
    queue.run(last + total, pump, True)
    for part in range(4):
        ey.await_part(part)
    for w in range(windows):
        tile = r.y_in[r.backward_take[w]].astype(WHOLE)
        r.total[w * WIN : (w + 1) * WIN, :] = tile[:WIN]
    r.result[...] = r.total[0 : windows * WIN, :].astype(LOW)
    eg.finish(1)
    ex.finish(4)
    ey.finish(4)
    gather.finish()
    for layer in range(2):
        for array in range(4):
            swap(layer, array).wait_send()
    for copy in saved:
        copy.wait()


def forward_all(blocks, vectors, x0, grads, table, bias_index, region, moves, depths, peers):
    count = depths * 2 * peers
    width = x0.shape[-1]
    hidden = blocks[2].shape[-1]
    tall = 2 * ROWS
    half = peers // 2
    chunks = []
    for layer in range(2):
        for array, block in enumerate(blocks):
            size = 256 if array == 3 else 1024
            for start in range(0, block.shape[-1], size):
                chunks.append((array, layer, slice(start, start + size)))
    total = len(chunks)
    unit = blocks[0].shape[1]
    dma = pltpu.SemaphoreType.DMA
    vmem = pltpu.VMEM
    smem = pl.BlockSpec(memory_space=pltpu.SMEM)
    shape = jax.ShapeDtypeStruct
    tiles = (2, ROWS, width)
    left = (2, peers, depths * unit, 512)
    outs = [shape((depths, 2, peers) + b.shape[1:], LOW) for _ in range(2) for b in blocks]
    outs += [shape(tiles, LOW), shape(x0.shape, LOW)]
    outs += [shape(left, LOW)] * 3 + [shape((2, 4) + left[1:], LOW)]
    outs += [
        shape((2, tall, width), LOW),
        shape((2, tall, width), WHOLE),
        shape((2, tall, 3 * width), LOW),
        shape((2, 16, ROWS, GROUP * KEYS), LOW),
        shape((2, tall, hidden), LOW),
        shape((12, width), WHOLE),
    ]
    exchange = (peers,) + tiles[1:]
    scratch = [
        vmem((count, 8, 128), WHOLE),
        vmem((8, 128), WHOLE),
        vmem((2 * HEADS, 384), LOW),
        vmem((ROWS, KEYS), jnp.int32),
        vmem((2, ROWS, KEYS), WHOLE),
        vmem((2, 8, ROWS, GROUP * KEYS), WHOLE),
        vmem((2, tall, width), LOW),
        vmem(tiles, LOW),
        vmem((2, tall, width), LOW),
        vmem((2, tall, width), LOW),
        vmem((2, tall, width), LOW),
        vmem((2, tall, hidden), LOW),
        vmem((2, tall, width), WHOLE),
        vmem((2, tall, 3 * width), LOW),
        vmem((2, 16, ROWS, GROUP * KEYS), LOW),
        vmem((2, tall, hidden), LOW),
        vmem((2, depths, 2, peers, unit, 1024), LOW),
        vmem((2, depths, 2, peers, 4 * unit, 256), LOW),
        vmem((tall, 1024), WHOLE),
        vmem((3, 2, tall, width), LOW),
        vmem((2, tall, hidden), LOW),
        vmem((depths, 128, 512), WHOLE),
        vmem((HEADS, 384), WHOLE),
        vmem((2, 3) + left[1:], LOW),
        vmem((2, 4) + left[1:], LOW),
        *[vmem(exchange, LOW)] * 6,
        vmem((2, 2 * width), WHOLE),
        vmem((2, hidden), WHOLE),
        dma((total, depths - 1)),
        dma((total, depths - 1)),
        dma((total, half, 2)),
        dma((total, half, 2)),
        dma((total, 2 * half)),
        dma((total, 2 * half)),
        dma((total,)),
        dma((total,)),
        dma(()),
        dma(()),
        dma(()),
        dma((total,)),
        dma((32,)),
        dma((2, 4)),
        dma((2, 4)),
        dma((1, peers - 1)),
        dma((1, peers - 1)),
        *[dma((4, peers - 1))] * 4,
    ]
    return pl.pallas_call(
        functools.partial(forward_kernel, chunks, depths, peers),
        out_shape=outs,
        in_specs=[ANY] * 4 + [VMEM] * 10 + [smem] * 5,
        out_specs=[ANY] * 8 + [VMEM] * 2 + [ANY] * 9 + [VMEM],
        scratch_shapes=scratch,
        compiler_params=pltpu.CompilerParams(
            collective_id=3, has_side_effects=True, vmem_limit_bytes=63 * 2**20
        ),
    )(*blocks, *vectors, x0, grads, table, bias_index, region, *moves)


SLOTS, Z_SLOTS, Z_WAIT = 6, 9, 3
DEEP = {3: (1, 7), 7: (6, 13), 15: (14, 20)}


class Reduce:
    def __init__(self, place, plan, product, keep, bufs, sems):
        self.place, self.plan, self.product, self.keep = place, plan, product, keep
        (self.half_send, self.half_recv, self.full_send, self.full_recv, self.z_out, self.z_in, self.own_part) = bufs
        self.r_send, self.r_recv, self.z_send, self.z_recv = sems
        self.half = place.half
        self.rows = self.z_out.shape[2]
        self.cut = place.depths * self.rows // 2

    def ring(self, i, step, way):
        slot = i % SLOTS
        if step == 1:
            source, target = self.half_send.at[slot, way], self.half_recv.at[slot, way]
        else:
            source = self.full_send.at[slot, step - 2, way]
            target = self.full_recv.at[slot, step - 2, way]
        return remote(
            source,
            target,
            self.r_send.at[slot, step - 1, way],
            self.r_recv.at[slot, step - 1, way],
            self.place.neighbour(1 if way == 0 else -1),
        )

    def deep(self, i, step):
        slot = i % Z_SLOTS
        return remote(
            self.z_out.at[slot, self.place.at_depth(step)],
            self.z_in.at[slot, step - 1],
            self.z_send.at[slot, step - 1],
            self.z_recv.at[slot, step - 1],
            self.place.deep(step),
        )

    def sent(self, i):
        for way in range(2):
            for step in range(1, self.half + 1):
                self.ring(i, step, way).wait_send()

    def deep_sent(self, i):
        for step in range(1, self.place.depths):
            self.deep(i, step).wait_send()

    def first(self, i):
        if i >= SLOTS:
            self.sent(i - SLOTS)
        slot = i % SLOTS
        found = self.product(self.plan[i], self.place.around(self.half)).astype(LOW)
        for way in range(2):
            self.half_send[slot, way] = found[: self.cut] if way == 0 else found[self.cut :]
            self.ring(i, 1, way).start()

    def next_step(self, i, step):
        slot = i % SLOTS
        cut = self.cut
        for way in range(2):
            turn = 1 if way == 0 else -1
            found = self.product(self.plan[i], self.place.around(turn * (self.half - step + 1)))
            self.ring(i, step - 1, way).wait_recv()
            target = self.full_send.at[slot, step - 2, way]
            if step == 2:
                came = self.half_recv[slot, way].astype(WHOLE)
                low = found[:cut] + came if way == 0 else found[:cut]
                high = found[cut:] if way == 0 else found[cut:] + came
                target[:cut] = low.astype(LOW)
                target[cut:] = high.astype(LOW)
            else:
                came = self.full_recv[slot, step - 3, way].astype(WHOLE)
                target[...] = (found + came).astype(LOW)
            self.ring(i, step, way).start()

    def plane(self, i):
        slot, rows = i % SLOTS, self.rows
        z_slot = i % Z_SLOTS
        if i >= Z_SLOTS:
            self.deep_sent(i - Z_SLOTS)
        found = self.product(self.plan[i], self.place.peer)
        for way in range(2):
            self.ring(i, self.half, way).wait_recv()
            found += self.full_recv[slot, self.half - 2, way].astype(WHOLE)
        for depth in range(self.place.depths):
            piece = found[depth * rows : (depth + 1) * rows]
            self.z_out[z_slot, depth] = piece.astype(LOW)

            @pl.when(depth == self.place.depth)
            def _():
                self.own_part[z_slot] = piece

        for step in range(1, self.place.depths):
            self.deep(i, step).start()

    def finish(self, i):
        slot = i % Z_SLOTS
        found = self.own_part[slot]
        for step in range(1, self.place.depths):
            self.deep(i, step).wait_recv()
            found += self.z_in[slot, step - 1].astype(WHOLE)
        self.keep(self.plan[i], found)


SMALL_ROWS = 96


class DeepFirst:
    def __init__(self, reduce, bufs, sems):
        self.reduce, self.place = reduce, reduce.place
        (self.out, self.into, self.kept, self.half_send, self.half_recv, self.full_send, self.full_recv) = bufs
        self.z_send, self.z_recv, self.r_send, self.r_recv = sems
        self.rows = self.kept.shape[2]
        self.cut = self.rows // 2

    def deep(self, k, step):
        return remote(
            self.out.at[k, self.place.at_depth(step)],
            self.into.at[k, step - 1],
            self.z_send.at[k, step - 1],
            self.z_recv.at[k, step - 1],
            self.place.deep(step),
        )

    def ring(self, k, step, way):
        if step == 1:
            source, target = self.half_send.at[k, way], self.half_recv.at[k, way]
        else:
            source = self.full_send.at[k, step - 2, way]
            target = self.full_recv.at[k, step - 2, way]
        return remote(
            source,
            target,
            self.r_send.at[k, step - 1, way],
            self.r_recv.at[k, step - 1, way],
            self.place.neighbour(1 if way == 0 else -1),
        )

    def start(self, k, entry):
        rows = self.rows
        for peer in range(self.place.peers):
            found = self.reduce.product(entry, peer)
            for depth in range(self.place.depths):
                piece = found[depth * rows : (depth + 1) * rows]
                self.out[k, depth, peer * rows : (peer + 1) * rows] = piece.astype(LOW)

                @pl.when(depth == self.place.depth)
                def _():
                    self.kept[k, peer] = piece

    def turn(self, k):
        place, rows = self.place, self.rows
        for step in range(1, place.depths):
            self.deep(k, step).wait_recv()
        for peer in range(place.peers):
            found = self.kept[k, peer]
            for step in range(1, place.depths):
                found += self.into[k, step - 1, peer * rows : (peer + 1) * rows].astype(WHOLE)
            self.kept[k, peer] = found
        found = self.kept[k, place.around(place.half)].astype(LOW)
        for way in range(2):
            self.half_send[k, way] = found[: self.cut] if way == 0 else found[self.cut :]
            self.ring(k, 1, way).start()

    def next_step(self, k, step):
        place, cut = self.place, self.cut
        for way in range(2):
            turn = 1 if way == 0 else -1
            found = self.kept[k, place.around(turn * (place.half - step + 1))]
            self.ring(k, step - 1, way).wait_recv()
            if step == 2:
                came = self.half_recv[k, way].astype(WHOLE)
                low = found[:cut] + came if way == 0 else found[:cut]
                high = found[cut:] if way == 0 else found[cut:] + came
                found = jnp.concatenate([low, high], axis=0)
            else:
                found += self.full_recv[k, step - 3, way].astype(WHOLE)
            self.full_send[k, step - 2, way] = found.astype(LOW)
            self.ring(k, step, way).start()

    def finish(self, k, entry):
        place = self.place
        found = self.kept[k, place.peer]
        for way in range(2):
            self.ring(k, place.half, way).wait_recv()
            found += self.full_recv[k, place.half - 2, way].astype(WHOLE)
        self.reduce.keep(entry, found)

    def sent(self, k):
        for way in range(2):
            for step in range(1, self.place.half + 1):
                self.ring(k, step, way).wait_send()
        for step in range(1, self.place.depths):
            self.deep(k, step).wait_send()


def backward_kernel(everything, depths, peers, *refs):
    r = types.SimpleNamespace()
    (
        r.f0, r.f1, r.f2, r.f3, r.f4, r.f5, r.f6, r.f7, r.moved_grad, r.left0, r.left1, r.left2, r.left3,
        r.low_x, r.middle, r.qkv, r.probs, r.slope, r.vec32, r.bias_index, r.backward_send, r.backward_take,
        r.patches_grad, r.g_qkv, r.g_proj, r.g_up, r.g_down, r.o_gain, r.o_shift, r.o_qv, r.o_proj, r.o_up, r.o_down, r.o_table, r.small_all, r.half_send, r.half_recv,
        r.full_send, r.full_recv, r.z_out, r.z_in, r.own_part, r.left_a, r.left_b, r.right0, r.right1,
        r.right2, r.right3, r.wide_a, r.wide_b, r.slope_s, r.p_s, r.q_s, r.mid, r.x, r.grad, r.att_grad,
        r.total, r.g_mid, r.score_sum, r.tiles, r.e_out, r.e_in, r.index, r.small_mine, r.small_in, r.small_sum,
        r.r_send, r.r_recv, r.z_send, r.z_recv, r.swap_send, r.swap_recv, r.credit, r.load, r.state, r.e_send,
        r.e_recv, r.a_send, r.a_recv, r.a_own, r.b_send, r.b_recv, r.b_own,
        r.d_out, r.d_in, r.d_kept, r.d_half_send, r.d_half_recv, r.d_full_send, r.d_full_recv,
        r.dz_send, r.dz_recv, r.dr_send, r.dr_recv,
    ) = refs
    place = Place(depths, peers)
    fulls = (r.f0, r.f1, r.f2, r.f3, r.f4, r.f5, r.f6, r.f7)
    rights = (r.right0, r.right1, r.right2, r.right3)
    outs = (r.g_qkv, r.g_proj, r.g_up, r.g_down)
    windows, tall = 2, 2 * ROWS
    plan = [entry for i, entry in enumerate(everything) if i not in DEEP]
    total = len(plan)
    queue = Queue(B_BUDGET)
    done, used, loaded = set(), set(), []
    unit = r.z_out.shape[2]

    def product(entry, peer):
        layer, array, part, start = entry
        left = r.left_b[layer, part, peer] if array == 3 else r.left_a[layer, array, peer]
        return dot(left, rights[array][:, start : start + WIDE])

    def keep(entry, found):
        layer, array, part, start = entry
        outs[array][layer, part * unit : (part + 1) * unit, start : start + WIDE] = found

    reduce = Reduce(
        place,
        plan,
        product,
        keep,
        (r.half_send, r.half_recv, r.full_send, r.full_recv, r.z_out, r.z_in, r.own_part),
        (r.r_send, r.r_recv, r.z_send, r.z_recv),
    )
    deep_first = DeepFirst(
        reduce,
        (r.d_out, r.d_in, r.d_kept, r.d_half_send, r.d_half_recv, r.d_full_send, r.d_full_recv),
        (r.dz_send, r.dz_recv, r.dr_send, r.dr_recv),
    )
    exchange = Exchange(place, r.e_out, r.e_in, r.e_send, r.e_recv, 1)

    order = [(layer, array, part) for layer in (1, 0) for array, parts in ((3, 4), (2, 4), (1, 1), (0, 3)) for part in range(parts)]

    def slot_of(k):
        down = order[k][1] == 3
        return sum(1 for o in order[:k] if (o[1] == 3) == down) % 2

    def load(k):
        layer, array, part = order[k]
        full = fulls[layer * 4 + array]
        if array == 3:
            return pltpu.make_async_copy(full.at[part], r.wide_b.at[slot_of(k)], r.load.at[k])
        source = full.at[:, :, :, :, part * 1024 : (part + 1) * 1024]
        return pltpu.make_async_copy(source, r.wide_a.at[slot_of(k)], r.load.at[k])

    def pump():
        while len(loaded) < len(order):
            k = len(loaded)
            same = [j for j in range(k) if (order[j][1] == 3) == (order[k][1] == 3)]
            if len(same) > 1 and same[-2] not in used:
                break
            load(k).start()
            loaded.append(k)

    def weight(layer, array, part):
        k = order.index((layer, array, part))
        assert k in loaded
        used.add(k)
        load(k).wait()
        value = (r.wide_b if array == 3 else r.wide_a)[slot_of(k)]
        return value.reshape(-1, value.shape[-1])

    def swap(layer, array, part):
        columns = slice(part * 1024, (part + 1) * 1024)
        right = rights[array]
        return remote(
            right.at[0:tall, columns],
            right.at[256 : 256 + tall, columns],
            r.swap_send.at[array, part],
            r.swap_recv.at[array, part],
            place.sibling(),
        )

    def free(array):
        pl.semaphore_signal(r.credit.at[array], inc=1, device_id=place.sibling(), device_id_type=MESH)

    def hand_over(layer, array, part):
        if layer == 0 and part == 0:
            pl.semaphore_wait(r.credit.at[array], 1)
        swap(layer, array, part).start()

    def ready(layer, array, part):
        if layer == 0:
            assert (array, "freed") in done
            swap(1, array, part).wait_send()

    def put(layer, row, vector):
        for k in range(vector.shape[1] // 128):
            line = layer * SMALL_ROWS + row + k
            r.small_mine[line : line + 1, :] = vector[:, k * 128 : (k + 1) * 128]

    def column_sums(layer, row, value):
        ones = jnp.ones((8, tall), LOW)
        put(layer, row, dot(ones, value)[:1])

    states = ((r.slope_s, r.slope), (r.p_s, r.probs), (r.q_s, r.qkv), (r.mid, r.middle), (r.x, r.low_x))

    def state_copy(layer, k):
        here, there = states[k]
        return pltpu.make_async_copy(there.at[layer], here, r.state.at[layer, k])

    def left_copies(layer):
        sources = (r.left0, r.left1, r.left2)
        found = [
            pltpu.make_async_copy(
                sources[k].at[layer], r.left_a.at[layer, k], r.state.at[layer, 5 + k]
            )
            for k in range(3)
        ]
        return found + [
            pltpu.make_async_copy(r.left3.at[layer], r.left_b.at[layer], r.state.at[layer, 8])
        ]

    def vec(k):
        return r.vec32[k : k + 1, :]

    def take_grad(layer):
        if layer == 1:
            for w in range(windows):
                r.grad[w * ROWS : (w + 1) * ROWS, :] = r.moved_grad[w]
        else:
            exchange.await_part(0)
            for w in range(windows):
                r.grad[w * ROWS : (w + 1) * ROWS, :] = r.e_in[r.backward_take[w]]
        ready(layer, 3, 0)
        value = r.grad[...]
        r.right3[0:tall, :] = value
        hand_over(layer, 3, 0)
        column_sums(layer, 88, value)

    def hidden_grad(layer, part):
        if part == 0:
            state_copy(layer, 0).wait()
        columns = slice(part * 1024, (part + 1) * 1024)
        ready(layer, 2, part)
        found = dot(r.grad[...], weight(layer, 3, part), (1, 1))
        low = (found * r.slope_s[:, columns].astype(WHOLE)).astype(LOW)
        r.right2[0:tall, columns] = low
        hand_over(layer, 2, part)
        column_sums(layer, 56 + 8 * part, low)
        if part == 3 and layer == 1:
            state_copy(0, 0).start()

    def add_back(layer, array, part, columns):
        found = dot(rights[array][0:tall, columns], weight(layer, array, part), (1, 1))
        if part == 0:
            r.total[...] = found
        else:
            r.total[...] += found

    def up_back(layer, part):
        add_back(layer, 2, part, slice(part * 1024, (part + 1) * 1024))

    def norm_loop(source, layer, k, finish):
        gain = vec(2 * layer + k)

        def body(i, carry):
            start = pl.multiple_of(i * 16, 16)
            rows = pl.ds(start, 16)
            parts, inverse = normal_parts(source[rows, :].astype(WHOLE))
            g = r.total[rows, :]
            e = g * gain
            mean = jnp.mean(e, axis=1, keepdims=True)
            along = jnp.mean(e * parts, axis=1, keepdims=True)
            finish(rows, inverse * (e - mean - parts * along))
            by_gain, by_shift = carry
            return (
                by_gain + jnp.sum(g * parts, axis=0, keepdims=True),
                by_shift + jnp.sum(g, axis=0, keepdims=True),
            )

        zero = jnp.zeros((1, source.shape[-1]), WHOLE)
        by_gain, by_shift = lax.fori_loop(0, tall // 16, body, (zero, zero))
        put(layer, 8 * k, by_gain)
        put(layer, 16 + 8 * k, by_shift)

    def middle_grad(layer):
        state_copy(layer, 3).wait()
        ready(layer, 1, 0)

        def finish(rows, found):
            whole = r.grad[rows, :].astype(WHOLE) + found
            r.g_mid[rows, :] = whole
            r.right1[rows, :] = whole.astype(LOW)

        norm_loop(r.mid, layer, 1, finish)
        hand_over(layer, 1, 0)
        column_sums(layer, 48, r.right1[0:tall, :])
        if layer == 1:
            state_copy(0, 3).start()

    def attended_grad(layer):
        r.att_grad[...] = dot(r.right1[0:tall, :], weight(layer, 1, 0), (1, 1)).astype(LOW)

    def fold(value):
        return sum(
            jnp.where(lane_mask(KEYS, head), value[head * KEYS : (head + 1) * KEYS], 0.0)
            for head in range(GROUP)
        )[:ROWS]

    def attend_back(layer, w):
        if w == 0:
            state_copy(layer, 1).wait()
            state_copy(layer, 2).wait()
            for part in range(3):
                ready(layer, 0, part)

        def step(g, carry):
            rows = slice(w * ROWS, (w + 1) * ROWS)
            start = pl.multiple_of(g * 128, 128)
            q = r.q_s[rows, pl.ds(start, 128)]
            k = r.q_s[rows, pl.ds(start + 1024, 128)]
            v = r.q_s[rows, pl.ds(start + 2048, 128)]
            out_grad = r.att_grad[rows, pl.ds(start, 128)]
            low = r.p_s[w * 8 + g]
            prob_grad = dot(out_grad, per_head(v), (1, 1))
            pieces = []
            for head in range(GROUP):
                one = slice(head * KEYS, (head + 1) * KEYS)
                probs = low[:, one].astype(WHOLE)
                weighed = probs * prob_grad[:, one]
                pieces.append(weighed - probs * jnp.sum(weighed, axis=1, keepdims=True))
            score_grad = jnp.concatenate(pieces, axis=1).astype(LOW)
            for head in range(GROUP):
                lines = pl.ds(pl.multiple_of((head * 8 + g) * ROWS, 8), ROWS)
                one = score_grad[:, head * KEYS : (head + 1) * KEYS].astype(WHOLE)
                r.score_sum[lines, :] = one if w == 0 else r.score_sum[lines, :] + one
            by_query = dot(score_grad, per_head(k)) * SCALE
            by_key = fold(dot(score_grad, q, (0, 0))) * SCALE
            by_value = fold(dot(low, out_grad, (0, 0)))
            for part, found in enumerate((by_query, by_key, by_value)):
                r.right0[rows, pl.ds(start + part * 1024, 128)] = found.astype(LOW)
            return carry

        lax.fori_loop(0, 8, step, 0)
        if w == windows - 1:
            for part in range(3):
                hand_over(layer, 0, part)
            column_sums(layer, 32, r.right0[0:tall, 0:1024])
            column_sums(layer, 40, r.right0[0:tall, 2048:3072])
            if layer == 1:
                state_copy(0, 1).start()
                state_copy(0, 2).start()

    def qkv_back(layer, part):
        add_back(layer, 0, part, slice(part * 1024, (part + 1) * 1024))

    def input_grad(layer):
        state_copy(layer, 4).wait()

        def finish(rows, found):
            r.g_mid[rows, :] = r.g_mid[rows, :] + found

        norm_loop(r.x, layer, 0, finish)
        if layer == 1:
            state_copy(0, 4).start()
            for w in range(windows):
                r.tiles[w] = r.g_mid[w * ROWS : (w + 1) * ROWS, :].astype(LOW)
            exchange.give(0, r.tiles, r.backward_send)
        else:
            for w in range(windows):
                r.patches_grad[w * WIN : (w + 1) * WIN, :] = r.g_mid[w * ROWS : w * ROWS + WIN, :]

    def table_grad(layer):
        buckets = lax.broadcasted_iota(jnp.int32, (384, KEYS), 0)

        def step(i, found):
            start = pl.multiple_of(i * 8, 8)
            lines = r.index[pl.ds(start, 8), :]
            values, hots = [], []
            for row in range(8):
                hots.append(jnp.where(buckets == lines[row : row + 1], 1.0, 0.0).astype(LOW))
                values.append(r.score_sum[pl.ds(start + row, HEADS, stride=ROWS), :])
            value = jnp.concatenate(values, axis=1)
            high = value.astype(LOW)
            rest = (value - high.astype(WHOLE)).astype(LOW)
            both = jnp.concatenate([high, rest], axis=0)
            return found + dot(both, jnp.concatenate(hots, axis=1), (1, 1))

        found = lax.fori_loop(0, 13, step, jnp.zeros((64, 384), WHOLE))
        found = found[:32] + found[32:]
        base = 2 * SMALL_ROWS + layer * SMALL_ROWS
        for k in range(3):
            r.small_mine[base + 32 * k : base + 32 * (k + 1), :] = found[:, 128 * k : 128 * (k + 1)]

    def send_small():
        def step(k, carry):
            outer, peer = place.other(k)
            remote(
                r.small_mine.at[pl.ds(pl.multiple_of((outer * peers + peer) * 16, 16), 16)],
                r.small_in.at[place.index],
                r.a_send,
                r.a_recv,
                (outer, peer),
            ).start()
            return carry

        lax.fori_loop(1, place.total, step, 0)
        own_small().start()

    def own_small():
        mine = r.small_mine.at[pl.ds(pl.multiple_of(place.index * 16, 16), 16)]
        return pltpu.make_async_copy(mine, r.small_in.at[place.index], r.a_own)

    spread = Spread(place, r.small_sum, r.small_all, r.b_send, r.b_recv, r.b_own)

    def sum_small():
        rest = r.small_in.at[pl.ds(0, place.total - 1)]
        both = remote(rest, rest, r.a_send, r.a_recv, place.other(1))
        both.wait_send()
        both.wait_recv()
        own_small().wait()
        r.small_sum[...] = jnp.sum(r.small_in[...], axis=0)
        spread.start()

    def own_vectors():
        places = (
            (0, 4, r.o_gain, 0),
            (8, 4, r.o_gain, 1),
            (16, 4, r.o_shift, 0),
            (24, 4, r.o_shift, 1),
            (32, 2, r.o_qv, None),
            (48, 4, r.o_proj, None),
            (56, 1, r.o_up, None),
            (88, 4, r.o_down, None),
        )
        for layer in range(2):
            for row, each, target, k in places:
                line = layer * SMALL_ROWS + row + lax.div(place.index, each)
                found = r.small_all[lax.div(line, 16), pl.ds(lax.rem(line, 16), 1), :]
                back = lax.rem(each - lax.rem(place.index, each), each) * (128 // each)
                found = pltpu.roll(found, back, 1)[:, : 128 // each]
                if k is None:
                    target[layer : layer + 1, :] = found
                else:
                    target[layer, k : k + 1, :] = found
            first = (2 + layer) * SMALL_ROWS // 16
            parts = [
                r.small_all[first + 2 * k : first + 2 * k + 2].reshape(HEADS, 128) for k in range(3)
            ]
            rows = jnp.concatenate(parts, axis=1)
            order = [rows[h % GROUP * 8 + h // GROUP :][:1] for h in range(HEADS)]
            r.o_table[layer] = jnp.concatenate(order, axis=0)[:, : r.o_table.shape[2]]

    def note(work, *what):
        work(*what)
        done.add((work.__name__, *what))

    def add(tick, cost, work, *what):
        queue.add(tick, cost, note, work, *what)

    for k in range(5):
        state_copy(1, k).start()
    for layer in (1, 0):
        for copy in left_copies(layer):
            copy.start()
    for right in rights:
        zero = jnp.zeros((256 - tall, right.shape[1]), LOW)
        right[tall:256, :] = zero
        right[256 + tall : 512, :] = zero
    r.index[...] = jnp.full(r.index.shape, r.o_table.shape[2], jnp.int32)
    r.index[:WIN, :WIN] = r.bias_index[...]
    r.small_mine[...] = jnp.zeros(r.small_mine.shape, WHOLE)
    pump()
    place.greet()

    add(0, 1, take_grad, 1)
    last_use = {
        array: max(i for i, p in enumerate(plan) if p[0] == 1 and p[1] == array) for array in range(4)
    }
    after = {array: last_use[array] + GAP * place.half for array in range(4)}
    for layer in (1, 0):
        late = 9 if layer == 0 else 0
        if layer == 0:
            add(0, 5, table_grad, 1)
            add(late, 1, take_grad, 0)
        for part in range(4):
            add(late and after[2], 2, hidden_grad, layer, part)
        for part in range(4):
            add(late, 2, up_back, layer, part)
        add(late and after[1], 3, middle_grad, layer)
        add(late, 1.5, attended_grad, layer)
        for w in range(windows):
            add(late and after[0], 7, attend_back, layer, w)
        for part in range(3):
            add(late, 1.5, qkv_back, layer, part)
        add(late, 3, input_grad, layer)
    add(0, 5, table_grad, 0)
    add(0, 1, send_small)

    needs = {3: ("take_grad",), 2: ("hidden_grad",), 1: ("middle_grad",), 0: ("attend_back",)}

    def wanted(entry):
        layer, array, part, start = entry
        what = needs[array] + (layer,)
        if array == 2:
            what += (start // 1024,)
        if array == 0:
            what += (windows - 1,)
        return what

    received, lefts_in = set(), set()
    half = place.half

    def prepare(entry):
        layer, array, part, start = entry
        while wanted(entry) not in done:
            queue.step(pump)
        if layer not in lefts_in:
            lefts_in.add(layer)
            for copy in left_copies(layer):
                copy.wait()
        key = (layer, array, start // 1024)
        if key not in received:
            received.add(key)
            swap(*key).wait_recv()

    for tick in range(total + GAP * half + Z_WAIT):
        if tick < total:
            prepare(plan[tick])
            reduce.first(tick)
        for k, (i, (begin, middle)) in enumerate(DEEP.items()):
            assert place.depths == 4 and half == 2
            entry, slot = everything[i], k % 2
            if tick == begin:
                prepare(entry)
                if k >= 2:
                    deep_first.sent(slot)
                deep_first.start(slot, entry)
            if tick in (begin, begin + 2, begin + 4):
                deep_first.deep(slot, (tick - begin) // 2 + 1).start()
            if tick == middle:
                deep_first.turn(slot)
            if tick == middle + 3:
                deep_first.next_step(slot, 2)
            if tick == middle + 6:
                deep_first.finish(slot, entry)
        for step in range(2, half + 1):
            i = tick - GAP * (step - 1)
            if 0 <= i < total:
                reduce.next_step(i, step)
        i = tick - GAP * half
        if 0 <= i < total:
            reduce.plane(i)
            for array, last in last_use.items():
                if i == last:
                    free(array)
                    done.add((array, "freed"))
        i = tick - GAP * half - Z_WAIT
        if 0 <= i < total:
            reduce.finish(i)
        queue.run(tick, pump)
        if ("send_small",) in done and ("sum_small",) not in done and tick >= total - 1:
            note(sum_small)
    assert not queue.pieces
    if ("sum_small",) not in done:
        sum_small()
    spread.wait()
    own_vectors()
    exchange.finish(1)
    for array, parts in ((3, 1), (2, 4), (1, 1), (0, 3)):
        for part in range(parts):
            swap(0, array, part).wait_send()
    for i in range(total - SLOTS, total):
        reduce.sent(i)
    for i in range(total - Z_SLOTS, total):
        reduce.deep_sent(i)
    for k in range(2):
        deep_first.sent(k)


def backward_all(fulls, state, index, moves, depths, peers, buckets):
    moved_grad, left0, left1, left2, left3, low_x, middle, qkv, probs, slope, vec32 = state
    count = depths * 2 * peers
    tall, width = low_x.shape[1:]
    hidden = slope.shape[-1]
    unit = width // count
    half = peers // 2
    plan = []
    for layer in (1, 0):
        plan += [(layer, 3, part, 0) for part in range(4)]
        plan += [(layer, 2, 0, start) for start in range(0, hidden, WIDE)]
        plan += [(layer, 1, 0, 0)]
        plan += [(layer, 0, 0, start) for start in range(0, 3 * width, WIDE)]
    dma = pltpu.SemaphoreType.DMA
    vmem = pltpu.VMEM
    smem = pl.BlockSpec(memory_space=pltpu.SMEM)
    shape = jax.ShapeDtypeStruct
    flat = depths * unit
    outs = [
        shape((2 * WIN, width), WHOLE),
        shape((2, unit, 3 * width), WHOLE),
        shape((2, unit, width), WHOLE),
        shape((2, unit, hidden), WHOLE),
        shape((2, 4 * unit, width), WHOLE),
        shape((2, 2, unit), WHOLE),
        shape((2, 2, unit), WHOLE),
        shape((2, 2 * unit), WHOLE),
        shape((2, unit), WHOLE),
        shape((2, 4 * unit), WHOLE),
        shape((2, unit), WHOLE),
        shape((2, HEADS, buckets), WHOLE),
    ]
    scratch = [
        vmem((count, 16, 128), WHOLE),
        vmem((SLOTS, 2, flat // 2, WIDE), LOW),
        vmem((SLOTS, 2, flat // 2, WIDE), LOW),
        vmem((SLOTS, half - 1, 2, flat, WIDE), LOW),
        vmem((SLOTS, half - 1, 2, flat, WIDE), LOW),
        vmem((Z_SLOTS, depths, unit, WIDE), LOW),
        vmem((Z_SLOTS, depths - 1, unit, WIDE), LOW),
        vmem((Z_SLOTS, unit, WIDE), WHOLE),
        vmem((2, 3) + left0.shape[1:], LOW),
        vmem(left3.shape, LOW),
        vmem((512, 3 * width), LOW),
        vmem((512, width), LOW),
        vmem((512, hidden), LOW),
        vmem((512, width), LOW),
        vmem((2, depths, 2, peers, unit, 1024), LOW),
        vmem((2, 2, peers, 4 * unit, width), LOW),
        vmem((tall, hidden), LOW),
        vmem(probs.shape[1:], LOW),
        vmem((tall, 3 * width), LOW),
        vmem((tall, width), WHOLE),
        vmem((tall, width), LOW),
        vmem((tall, width), LOW),
        vmem((tall, width), LOW),
        vmem((tall, width), WHOLE),
        vmem((tall, width), WHOLE),
        vmem((HEADS * ROWS, KEYS), WHOLE),
        vmem((2, ROWS, width), LOW),
        vmem((peers, ROWS, width), LOW),
        vmem((peers, ROWS, width), LOW),
        vmem((ROWS, KEYS), jnp.int32),
        vmem((count * 16, 128), WHOLE),
        vmem((count, 16, 128), WHOLE),
        vmem((16, 128), WHOLE),
        dma((SLOTS, half, 2)),
        dma((SLOTS, half, 2)),
        dma((Z_SLOTS, depths - 1)),
        dma((Z_SLOTS, depths - 1)),
        dma((4, 4)),
        dma((4, 4)),
        pltpu.SemaphoreType.REGULAR((4,)),
        dma((24,)),
        dma((2, 9)),
        dma((1, peers - 1)),
        dma((1, peers - 1)),
        *[dma(())] * 6,
        vmem((2, depths, peers * unit, WIDE), LOW),
        vmem((2, depths - 1, peers * unit, WIDE), LOW),
        vmem((2, peers, unit, WIDE), WHOLE),
        vmem((2, 2, unit // 2, WIDE), LOW),
        vmem((2, 2, unit // 2, WIDE), LOW),
        vmem((2, half - 1, 2, unit, WIDE), LOW),
        vmem((2, half - 1, 2, unit, WIDE), LOW),
        dma((2, depths - 1)),
        dma((2, depths - 1)),
        dma((2, half, 2)),
        dma((2, half, 2)),
    ]
    return pl.pallas_call(
        functools.partial(backward_kernel, plan, depths, peers),
        out_shape=outs,
        in_specs=[ANY] * 8 + [VMEM] + [ANY] * 9 + [VMEM] * 2 + [smem] * 2,
        out_specs=[VMEM] * 12,
        scratch_shapes=scratch,
        compiler_params=pltpu.CompilerParams(
            collective_id=4, has_side_effects=True, vmem_limit_bytes=63 * 2**20
        ),
    )(*fulls, *state, index, *moves)


def copy_kernel(count, *refs):
    sources, targets, held = refs[:count], refs[count : 2 * count], refs[2 * count : 3 * count]
    came, went = refs[3 * count :]
    loads = [pltpu.make_async_copy(sources[k], held[k], came.at[k]) for k in range(count)]
    stores = [pltpu.make_async_copy(held[k], targets[k], went.at[k]) for k in range(count)]
    for copy in loads:
        copy.start()
    for load, store in zip(loads, stores):
        load.wait()
        store.start()
    for copy in stores:
        copy.wait()


def copy_out(arrays):
    count = len(arrays)
    return pl.pallas_call(
        functools.partial(copy_kernel, count),
        out_shape=[jax.ShapeDtypeStruct(a.shape, a.dtype) for a in arrays],
        in_specs=[ANY] * count,
        out_specs=[ANY] * count,
        scratch_shapes=[
            *[pltpu.VMEM(a.shape, a.dtype) for a in arrays],
            pltpu.SemaphoreType.DMA((count,)),
            pltpu.SemaphoreType.DMA((count,)),
        ],
        compiler_params=pltpu.CompilerParams(vmem_limit_bytes=63 * 2**20),
    )(*arrays)


def whole_shards(
    outer_count,
    peer_count,
    patches,
    out_grad,
    norm_gain,
    norm_shift,
    qkv_weight,
    qv_bias,
    rel_table,
    proj_weight,
    proj_bias,
    up_weight,
    up_bias,
    down_weight,
    down_bias,
    tile_perm,
    window_slot,
    mask_ids,
    bias_index,
):
    windows = patches.shape[0] // WIN
    width = patches.shape[1]
    depths = outer_count // 2
    device_index = lax.axis_index(("dp", "fsdp"))
    slot_ids = jnp.arange(tile_perm.shape[0], dtype=jnp.int32)

    def one_hot_pick(keys, values):
        return jnp.sum(jnp.where(keys[None, :] == slot_ids[:, None], values[None, :], 0), axis=1)

    def look_up(values, at):
        hit = at[:, None] == jnp.arange(values.shape[0], dtype=jnp.int32)[None, :]
        return jnp.sum(jnp.where(hit, values[None, :], 0), axis=1)

    source_of = one_hot_pick(window_slot, look_up(window_slot, tile_perm))
    target_of = one_hot_pick(source_of, slot_ids)
    region_slot = one_hot_pick(window_slot, mask_ids)
    own_slots = device_index * windows + jnp.arange(windows, dtype=jnp.int32)
    forward_take = look_up(source_of, own_slots) // windows % peer_count
    backward_take = look_up(target_of, own_slots) // windows % peer_count
    spots = jnp.arange(peer_count, dtype=jnp.int32)
    numbers = jnp.arange(windows, dtype=jnp.int32)

    def window_for(peers):
        return jnp.sum(jnp.where(peers[None, :] == spots[:, None], numbers[None, :], 0), axis=1)

    moves = (window_for(backward_take), forward_take, window_for(forward_take), backward_take)
    region = look_up(region_slot, own_slots)
    found = forward_all(
        (qkv_weight, proj_weight, up_weight, down_weight),
        (norm_gain, norm_shift, qv_bias, proj_bias, up_bias, down_bias),
        patches,
        out_grad,
        rel_table.transpose(0, 2, 1),
        bias_index,
        region,
        moves,
        depths,
        peer_count,
    )
    fulls, moved_grad, result, state = found[:8], found[8], found[9], found[10:]
    (
        grad_patches,
        grad_qkv,
        grad_proj,
        grad_up,
        grad_down,
        gain_grad,
        shift_grad,
        qv_grad,
        proj_b_grad,
        up_b_grad,
        down_b_grad,
        table,
    ) = backward_all(
        fulls, (moved_grad, *state), bias_index, moves[2:], depths, peer_count, rel_table.shape[1]
    )
    results = (
        result,
        grad_patches,
        gain_grad,
        shift_grad,
        grad_qkv,
        qv_grad,
        table,
        grad_proj,
        proj_b_grad,
        grad_up,
        up_b_grad,
        grad_down,
        down_b_grad,
    )
    results = list(copy_out(results))
    results[6] = results[6].transpose(0, 2, 1)
    return tuple(results)


def solution(mesh):
    outer_count, peer_count = mesh.shape["dp"], mesh.shape["fsdp"]
    fused = outer_count == 8 and peer_count == 4
    placed = (
        P(("dp", "fsdp"), None),
        P(("dp", "fsdp"), None),
        P(None, None, ("dp", "fsdp")),
        P(None, None, ("dp", "fsdp")),
        P(None, ("dp", "fsdp"), None),
        P(None, ("dp", "fsdp")),
        P(),
        P(None, ("dp", "fsdp"), None),
        P(None, ("dp", "fsdp")),
        P(None, ("dp", "fsdp"), None),
        P(None, ("dp", "fsdp")),
        P(None, ("dp", "fsdp"), None),
        P(None, ("dp", "fsdp")),
        P(),
        P(),
        P(),
        P(),
    )
    return jax.shard_map(
        functools.partial(whole_shards if fused else shards, outer_count, peer_count),
        mesh=mesh,
        in_specs=placed,
        out_specs=(
            P(("dp", "fsdp"), None),
            P(("dp", "fsdp"), None),
            P(None, None, ("dp", "fsdp")),
            P(None, None, ("dp", "fsdp")),
            P(None, ("dp", "fsdp"), None),
            P(None, ("dp", "fsdp")),
            P(),
            P(None, ("dp", "fsdp"), None),
            P(None, ("dp", "fsdp")),
            P(None, ("dp", "fsdp"), None),
            P(None, ("dp", "fsdp")),
            P(None, ("dp", "fsdp"), None),
            P(None, ("dp", "fsdp")),
        ),
        check_vma=False,
    )
```
